32 devices in a mesh: ctx: 16 (over z, y, x), wsh: 2 (over core).
Axes of the slice: x: 2, y: 2, z: 4, core: 2. Of those that a mesh axis runs over, the one named last changes fastest.
Arguments:
- inputs: bfloat16 [2, 2048, 1024], P('wsh', 'ctx'), may hold values from -6 to 6
- encoder: bfloat16 [2, 256, 1024], P('wsh', 'ctx'), may hold values from -6 to 6
- cotangent: bfloat16 [2, 2048, 1024], P('wsh', 'ctx'), may hold values from -6 to 6
- block_order: int32 [32], replicated, may hold values from 0 to 31, as said below
- bucket_of: int32 [2048], replicated, may hold values from 0 to 31, as said below
- self_gain: bfloat16 [1024], P('wsh'), may hold values from 0.5 to 1.5
- query_weight: bfloat16 [1024, 1024], P('wsh'), may hold values from -0.0234375 to 0.0234375
- key_weight: bfloat16 [1024, 1024], P('wsh'), may hold values from -0.1875 to 0.1875
- value_weight: bfloat16 [1024, 1024], P('wsh'), may hold values from -0.1875 to 0.1875
- out_weight: bfloat16 [1024, 1024], P('wsh'), may hold values from -6 to 6
- bias_table: bfloat16 [32, 16], P('wsh'), may hold values from -6 to 6
- cross_gain: bfloat16 [1024], P('wsh'), may hold values from 0.5 to 1.5
- cross_query: bfloat16 [1024, 1024], P('wsh'), may hold values from -0.0234375 to 0.0234375
- cross_key: bfloat16 [1024, 1024], P('wsh'), may hold values from -0.1875 to 0.1875
- cross_value: bfloat16 [1024, 1024], P('wsh'), may hold values from -0.1875 to 0.1875
- cross_out: bfloat16 [1024, 1024], P('wsh'), may hold values from -6 to 6
- mlp_gain: bfloat16 [1024], P('wsh'), may hold values from 0.5 to 1.5
- gate_weight: bfloat16 [1024, 2816], P('wsh'), may hold values from -0.1875 to 0.1875
- up_weight: bfloat16 [1024, 2816], P('wsh'), may hold values from -0.1875 to 0.1875
- down_weight: bfloat16 [2816, 1024], P('wsh'), may hold values from -0.109375 to 0.109375
Outputs:
- output: bfloat16 [2, 2048, 1024], P('wsh', 'ctx')
- input_grad: bfloat16 [2, 2048, 1024], P('wsh', 'ctx')
- encoder_grad: bfloat16 [2, 256, 1024], P('wsh', 'ctx')
- self_gain_grad: float32 [1024], P('wsh')
- query_weight_grad: float32 [1024, 1024], P('wsh')
- key_weight_grad: float32 [1024, 1024], P('wsh')
- value_weight_grad: float32 [1024, 1024], P('wsh')
- out_weight_grad: float32 [1024, 1024], P('wsh')
- bias_table_grad: float32 [32, 16], P('wsh')
- cross_gain_grad: float32 [1024], P('wsh')
- cross_query_grad: float32 [1024, 1024], P('wsh')
- cross_key_grad: float32 [1024, 1024], P('wsh')
- cross_value_grad: float32 [1024, 1024], P('wsh')
- cross_out_grad: float32 [1024, 1024], P('wsh')
- mlp_gain_grad: float32 [1024], P('wsh')
- gate_weight_grad: float32 [1024, 2816], P('wsh')
- up_weight_grad: float32 [1024, 2816], P('wsh')
- down_weight_grad: float32 [2816, 1024], P('wsh')
The draws below stay inside these ranges and needn't reach their ends.
Inputs may be any that keep to these rules, and one draw needn't show every extreme that they name: The device at index c of ctx holds stored blocks 2c and 2c + 1; their position blocks are j and 31 - j for one j, each j of 0 to 15 at one device; block_order is a permutation. `bucket_of`: nondecreasing in the offset, 0 at offset 0, every bucket used.
All inputs are finite; a program needn't handle non-finite values.
Results may differ from the reference program's by a relative error of at most 0.024.
Values may be sent and summed in bfloat16 or wider, within the bound.
A program may use at most 448 MiB of HBM per device.

```python
import math
import jax
import jax.numpy as jnp
from jax import lax

D = 1024
HEADS = 16
HEAD_DIM = 64
FF = 2816
BUCKETS = 32
TOK_DEV = 128
HD = 1024
SEQ = 2048
ENC = 256
SEQS = 2
NBLOCKS = 32


def draw_block_order(key, part):
    key = jax.random.fold_in(key, 11)
    pair_key, flip_key = jax.random.split(key)
    pair_count = NBLOCKS // 2
    chosen = jax.random.permutation(pair_key, pair_count).astype(jnp.int32)
    flip_bits = jax.random.randint(flip_key, (pair_count,), 0, 2).astype(jnp.int32)
    leading = jnp.where(flip_bits == 1, NBLOCKS - 1 - chosen, chosen)
    trailing = NBLOCKS - 1 - leading
    return jnp.stack([leading, trailing], axis=1).reshape(NBLOCKS).astype(jnp.int32)


def draw_bucket_of(key, part):
    key = jax.random.fold_in(key, 23)
    boundaries = jax.random.permutation(key, SEQ - 1)[:BUCKETS - 1].astype(jnp.int32) + 1
    offsets = jnp.arange(SEQ, dtype=jnp.int32)
    return jnp.sum((offsets[:, None] >= boundaries[None, :]).astype(jnp.int32), axis=1).astype(jnp.int32)


def level_of(key, extent, cuts, smallest, largest):
    factor_of = 1.0
    for axis_at, blocks in cuts:
        heights = jax.random.uniform(jax.random.fold_in(jax.random.fold_in(key, 6), axis_at), (blocks,), jnp.float32, smallest / len(cuts), largest / len(cuts))
        factor_of = factor_of * jnp.repeat(jnp.exp(heights), extent[axis_at] // blocks).reshape((-1,) + (1,) * (len(extent) - 1 - axis_at))
    return factor_of


def normal_values(rng, shape, scale, limit, cuts=(), held_as=jnp.bfloat16):
    drawn = scale * jax.random.normal(rng, shape, jnp.float32)
    if cuts:
        drawn = drawn * level_of(rng, shape, cuts, -0.22, 0.18)
    return jnp.clip(drawn, -limit, limit).astype(held_as)


def setup_inputs(seed: int = 0) -> dict:
    streams_of = jax.random.split(jax.random.key(seed), 21)
    inputs = normal_values(streams_of[0], (SEQS, SEQ, D), 1.0, 6.0, ((0, 2), (1, 16)))
    encoder = normal_values(streams_of[1], (SEQS, ENC, D), 1.0, 6.0, ((0, 2), (1, 16)))
    cotangent = normal_values(streams_of[2], (SEQS, SEQ, D), 1.0, 6.0, ((0, 2), (1, 16)))
    block_order = draw_block_order(jax.random.fold_in(streams_of[20], 71), 0)
    bucket_of = draw_bucket_of(jax.random.fold_in(streams_of[20], 71), 0)
    self_gain = jnp.clip(1.0 + 0.1 * jax.random.normal(streams_of[5], (D,), jnp.float32), 0.5, 1.5).astype(jnp.bfloat16)
    query_weight = normal_values(streams_of[6], (D, HD), (D * HEAD_DIM) ** -0.5, 0.0234375, ((0, 2),))
    key_weight = normal_values(streams_of[7], (D, HD), D ** -0.5, 0.1875, ((0, 2),))
    value_weight = normal_values(streams_of[8], (D, HD), D ** -0.5, 0.1875, ((0, 2),))
    out_weight = normal_values(streams_of[9], (HD, D), 1.0, 6.0, ((0, 2),))
    bias_table = normal_values(streams_of[10], (BUCKETS, HEADS), 1.0, 6.0, ((0, 2),))
    cross_gain = jnp.clip(1.0 + 0.1 * jax.random.normal(streams_of[11], (D,), jnp.float32), 0.5, 1.5).astype(jnp.bfloat16)
    cross_query = normal_values(streams_of[12], (D, HD), (D * HEAD_DIM) ** -0.5, 0.0234375, ((0, 2),))
    cross_key = normal_values(streams_of[13], (D, HD), D ** -0.5, 0.1875, ((0, 2),))
    cross_value = normal_values(streams_of[14], (D, HD), D ** -0.5, 0.1875, ((0, 2),))
    cross_out = normal_values(streams_of[15], (HD, D), 0.7, 6.0, ((0, 2),))
    mlp_gain = jnp.clip(1.0 + 0.1 * jax.random.normal(streams_of[16], (D,), jnp.float32), 0.5, 1.5).astype(jnp.bfloat16)
    gate_weight = normal_values(streams_of[17], (D, FF), D ** -0.5, 0.1875, ((0, 2),))
    up_weight = normal_values(streams_of[18], (D, FF), D ** -0.5, 0.1875, ((0, 2),))
    down_weight = normal_values(streams_of[19], (FF, D), FF ** -0.5, 0.109375, ((0, 2),))
    return {"inputs": inputs, "encoder": encoder, "cotangent": cotangent, "block_order": block_order, "bucket_of": bucket_of, "self_gain": self_gain, "query_weight": query_weight, "key_weight": key_weight, "value_weight": value_weight, "out_weight": out_weight, "bias_table": bias_table, "cross_gain": cross_gain, "cross_query": cross_query, "cross_key": cross_key, "cross_value": cross_value, "cross_out": cross_out, "mlp_gain": mlp_gain, "gate_weight": gate_weight, "up_weight": up_weight, "down_weight": down_weight}


EPSILON = 1e-06
NEG_BIG = -1e+30
HIGHEST = lax.Precision.HIGHEST

@jax.custom_vjp
def low(v):
    return lax.optimization_barrier(v.astype(jnp.bfloat16)).astype(jnp.float32)

@jax.custom_vjp
def low_back(v):
    return v

def low_keep(v):
    return (low(v), None)

def low_pass(kept, grad):
    return (grad,)

def back_keep(v):
    return (v, None)

def back_low(kept, grad):
    return (low(grad),)
low.defvjp(low_keep, low_pass)
low_back.defvjp(back_keep, back_low)

def matmul_high(left, right):
    return jnp.dot(left, right, precision=HIGHEST, preferred_element_type=jnp.float32)

def rms_norm(values, gain):
    return values * lax.rsqrt(lax.optimization_barrier(jnp.mean(values * values, axis=-1, keepdims=True)) + EPSILON) * gain

def softmax_low(logits):
    log_norm = jax.nn.logsumexp(logits, axis=-1, keepdims=True)
    return low(jnp.exp(logits - log_norm))

def self_attention(queries, keys_all, every_value_row, positions, table, bucket_of):
    length = queries.shape[0]
    block_rows = math.gcd(length, 512)
    key_heads = keys_all.reshape(length, HEADS, HEAD_DIM)
    value_heads = every_value_row.reshape(length, HEADS, HEAD_DIM)

    def one_block(pieces):
        query_block, query_pos = pieces
        query_heads = query_block.reshape(block_rows, HEADS, HEAD_DIM)
        logits = jnp.einsum('qhe,khe->hqk', query_heads, key_heads, precision=HIGHEST)
        offset = query_pos[:, None] - positions[None, :]
        bucket = bucket_of[jnp.maximum(offset, 0)]
        rel_bias = jnp.transpose(table[bucket], (2, 0, 1))
        logits = low_back(logits + rel_bias)
        logits = jnp.where(offset[None] >= 0, logits, NEG_BIG)
        attn_probs = softmax_low(logits)
        mixture = jnp.einsum('hqk,khe->qhe', attn_probs, value_heads, precision=HIGHEST)
        return mixture.reshape(block_rows, HEADS * HEAD_DIM)
    blocks = (queries.reshape(length // block_rows, block_rows, HEADS * HEAD_DIM), positions.reshape(length // block_rows, block_rows))
    return lax.map(jax.checkpoint(one_block), blocks).reshape(length, HEADS * HEAD_DIM)

def cross_attention(queries, keys_all, every_value_row):
    length = queries.shape[0]
    block_rows = math.gcd(length, 512)
    key_count = keys_all.shape[0]
    key_heads = keys_all.reshape(key_count, HEADS, HEAD_DIM)
    value_heads = every_value_row.reshape(key_count, HEADS, HEAD_DIM)

    def one_block(query_block):
        query_heads = query_block.reshape(block_rows, HEADS, HEAD_DIM)
        logits = low_back(jnp.einsum('qhe,khe->hqk', query_heads, key_heads, precision=HIGHEST))
        attn_probs = softmax_low(logits)
        mixture = jnp.einsum('hqk,khe->qhe', attn_probs, value_heads, precision=HIGHEST)
        return mixture.reshape(block_rows, HEADS * HEAD_DIM)
    blocks = queries.reshape(length // block_rows, block_rows, HEADS * HEAD_DIM)
    return lax.map(jax.checkpoint(one_block), blocks).reshape(length, HEADS * HEAD_DIM)

def decoder_layer(hidden_in, encoder_rows, positions, bucket_of, params):
    self_gain, query_weight, key_weight, value_weight, out_weight, bias_table, cross_gain, cross_query, cross_key, cross_value, cross_out, mlp_gain, gate_weight, up_weight, down_weight = params
    normed = low(rms_norm(hidden_in, self_gain))
    queries = low_back(low(matmul_high(normed, query_weight)))
    key_rows = low_back(low(matmul_high(normed, key_weight)))
    value_rows = low_back(low(matmul_high(normed, value_weight)))
    attended = low_back(low(self_attention(queries, key_rows, value_rows, positions, bias_table, bucket_of)))
    after_self = hidden_in + low_back(matmul_high(attended, out_weight))
    cross_normed = low(rms_norm(after_self, cross_gain))
    cross_queries = low_back(low(matmul_high(cross_normed, cross_query)))
    encoder_key_rows = low_back(low(matmul_high(encoder_rows, cross_key)))
    cross_values = low_back(low(matmul_high(encoder_rows, cross_value)))
    cross_mix = low_back(low(cross_attention(cross_queries, encoder_key_rows, cross_values)))
    after_cross = after_self + low_back(matmul_high(cross_mix, cross_out))
    mlp_normed = low(rms_norm(after_cross, mlp_gain))
    gate_act = low_back(matmul_high(mlp_normed, gate_weight))
    up_act = low_back(matmul_high(mlp_normed, up_weight))
    hidden = low(jax.nn.gelu(gate_act, approximate=True) * up_act)
    return after_cross + low_back(matmul_high(hidden, down_weight))

def reference(inputs, encoder, cotangent, block_order, bucket_of, self_gain, query_weight, key_weight, value_weight, out_weight, bias_table, cross_gain, cross_query, cross_key, cross_value, cross_out, mlp_gain, gate_weight, up_weight, down_weight):
    block_len = TOK_DEV // 2
    token_ids = jnp.arange(SEQ, dtype=jnp.int32)
    positions = (block_order[token_ids // block_len] * block_len + token_ids % block_len).astype(jnp.int32)
    params = tuple((weight.astype(jnp.float32) for weight in (self_gain, query_weight, key_weight, value_weight, out_weight, bias_table, cross_gain, cross_query, cross_key, cross_value, cross_out, mlp_gain, gate_weight, up_weight, down_weight)))

    def forward(hidden_all, encoder_all, param_list):
        return jnp.stack([decoder_layer(hidden_all[sequence], encoder_all[sequence], positions, bucket_of, param_list) for sequence in range(SEQS)])
    result, pullback = jax.vjp(forward, inputs.astype(jnp.float32), encoder.astype(jnp.float32), params)
    input_grad, encoder_grad, param_grads = pullback(cotangent.astype(jnp.float32))
    return (result.astype(jnp.bfloat16), input_grad.astype(jnp.bfloat16), encoder_grad.astype(jnp.bfloat16), param_grads[0], param_grads[1], param_grads[2], param_grads[3], param_grads[4], param_grads[5], param_grads[6], param_grads[7], param_grads[8], param_grads[9], param_grads[10], param_grads[11], param_grads[12], param_grads[13], param_grads[14])
```

```python
import functools

import jax
import jax.numpy as jnp
from jax import lax
from jax.experimental import pallas as pl
from jax.experimental.pallas import tpu as pltpu
from jax.sharding import PartitionSpec as P

HEADS = 16
HEAD_DIM = 64
BUCKETS = 32


EPSILON = 1e-06
NEG_BIG = -1e30


def rms_norm(values, gain):
    return values * lax.rsqrt(jnp.mean(values * values, axis=-1, keepdims=True) + EPSILON) * gain


def plain_dot(left, right):
    return jnp.dot(left, right, preferred_element_type=jnp.float32)


def left_contract(left, right):
    return lax.dot_general(
        left, right, (((0,), (0,)), ((), ())), preferred_element_type=jnp.float32
    )


def right_contract(left, right):
    return lax.dot_general(
        left, right, (((1,), (1,)), ((), ())), preferred_element_type=jnp.float32
    )


def gelu_product(gate_vals, up_vals):
    return jax.nn.gelu(gate_vals, approximate=True) * up_vals


def norm_back(values, gain, cotan):
    normed, pullback = jax.vjp(rms_norm, values, gain)
    return pullback(cotan)


def lookup_positions(block_order, first_row, row_count, block_len):
    token_ids = first_row + jnp.arange(row_count, dtype=jnp.int32)
    block_ids = token_ids // block_len
    matches = block_ids[:, None] == jnp.arange(block_order.shape[0], dtype=jnp.int32)[None, :]
    starts = jnp.sum(jnp.where(matches, block_order[None, :], 0), axis=1)
    return starts * block_len + token_ids % block_len


def fold_groups(step_fn, carried, pieces, shard_rows):
    piece_rows = pieces[0].shape[0]
    shards = max(1, piece_rows // shard_rows)
    group_limit = max(1, 1152 // shard_rows)
    group_size = max(
        (divisor for divisor in range(1, min(shards, group_limit) + 1) if shards % divisor == 0)
    )
    group_rows = group_size * shard_rows

    def group_step(group_idx, inner_state):
        sub_pieces = tuple(
            (
                lax.dynamic_slice_in_dim(member, group_idx * group_rows, group_rows, 0)
                for member in pieces
            )
        )
        return step_fn(inner_state, sub_pieces, group_idx * group_rows)

    return lax.fori_loop(0, shards // group_size, group_step, carried)


def on_device(
    inputs,
    encoder,
    cotangent,
    block_order,
    bucket_of,
    self_gain,
    query_weight,
    key_weight,
    value_weight,
    out_weight,
    bias_table,
    cross_gain,
    cross_query,
    cross_key,
    cross_value,
    cross_out,
    mlp_gain,
    gate_weight,
    up_weight,
    down_weight,
):
    (
        gain_one,
        query_full,
        key_full,
        value_full,
        out_full,
        bias_rows,
        gain_two,
        cross_query_full,
        cross_key_full,
        cross_value_full,
        cross_out_full,
        gain_three,
        gate_full,
        up_full,
        down_full,
    ) = (
        lax.all_gather(self_gain, "wsh", axis=0, tiled=True),
        lax.all_gather(query_weight, "wsh", axis=0, tiled=True),
        lax.all_gather(key_weight, "wsh", axis=0, tiled=True),
        lax.all_gather(value_weight, "wsh", axis=0, tiled=True),
        lax.all_gather(out_weight, "wsh", axis=0, tiled=True),
        lax.all_gather(bias_table, "wsh", axis=0, tiled=True),
        lax.all_gather(cross_gain, "wsh", axis=0, tiled=True),
        lax.all_gather(cross_query, "wsh", axis=0, tiled=True),
        lax.all_gather(cross_key, "wsh", axis=0, tiled=True),
        lax.all_gather(cross_value, "wsh", axis=0, tiled=True),
        lax.all_gather(cross_out, "wsh", axis=0, tiled=True),
        lax.all_gather(mlp_gain, "wsh", axis=0, tiled=True),
        lax.all_gather(gate_weight, "wsh", axis=0, tiled=True),
        lax.all_gather(up_weight, "wsh", axis=0, tiled=True),
        lax.all_gather(down_weight, "wsh", axis=0, tiled=True),
    )
    gain_one = gain_one.astype(jnp.float32)
    gain_two = gain_two.astype(jnp.float32)
    gain_three = gain_three.astype(jnp.float32)
    resid_in = inputs[0].astype(jnp.float32)
    tokens = resid_in.shape[0]
    block_len = tokens // 2
    head_width = HEADS * HEAD_DIM
    total_rows = tokens * lax.axis_size("ctx")
    own_pos = lookup_positions(block_order, lax.axis_index("ctx") * tokens, tokens, block_len)
    bucket_ids = jnp.arange(BUCKETS, dtype=jnp.int32)
    boundaries = jnp.sum((bucket_of[None, :] < bucket_ids[1:, None]).astype(jnp.int32), axis=1)

    def bucket_indicator_of(clipped):
        bucket = jnp.sum((clipped[None] >= boundaries[:, None, None]).astype(jnp.int32), axis=0)
        return (bucket[None] == bucket_ids[:, None, None]).astype(jnp.bfloat16)

    def query_key_logits(query_heads, key_heads, query_pos, key_pos):
        logits = jnp.einsum(
            "qhe,khe->hqk", query_heads, key_heads, preferred_element_type=jnp.float32
        )
        offset = query_pos[:, None] - key_pos[None, :]
        clipped = jnp.maximum(offset, 0)
        indicator = bucket_indicator_of(clipped)
        rel_bias = jnp.einsum(
            "ouw,om->muw", indicator, bias_rows, preferred_element_type=jnp.float32
        )
        allowed = (offset >= 0)[None]
        return (jnp.where(allowed, logits + rel_bias, NEG_BIG), allowed, indicator)

    normed_one = rms_norm(resid_in, gain_one).astype(jnp.bfloat16)
    query_heads = (
        plain_dot(normed_one, query_full).astype(jnp.bfloat16).reshape(tokens, HEADS, HEAD_DIM)
    )
    key_heads = (
        plain_dot(normed_one, key_full).astype(jnp.bfloat16).reshape(tokens, HEADS, HEAD_DIM)
    )
    value_heads = (
        plain_dot(normed_one, value_full).astype(jnp.bfloat16).reshape(tokens, HEADS, HEAD_DIM)
    )

    def norm_step(carried, pieces, first_row):
        running_max, running_sum = carried
        key_pos = lookup_positions(block_order, first_row, pieces[0].shape[0], block_len)
        logits, allowed, indicator = query_key_logits(query_heads, pieces[0], own_pos, key_pos)
        new_max = jnp.maximum(running_max, jnp.max(logits, axis=-1))
        kept = jnp.where(allowed, jnp.exp(logits - new_max[..., None]), 0.0)
        return (new_max, running_sum * jnp.exp(running_max - new_max) + jnp.sum(kept, axis=-1))

    start_state = (
        jnp.full((HEADS, tokens), NEG_BIG, jnp.float32),
        jnp.zeros((HEADS, tokens), jnp.float32),
    )
    running_max, running_sum = fold_groups(
        norm_step, start_state, (lax.all_gather(key_heads, "ctx", axis=0, tiled=True),), tokens
    )
    log_norm = running_max + jnp.log(running_sum)

    def output_step(carried, pieces, first_row):
        key_pos = lookup_positions(block_order, first_row, pieces[0].shape[0], block_len)
        logits, allowed, indicator = query_key_logits(query_heads, pieces[0], own_pos, key_pos)
        attn_probs = jnp.exp(logits - log_norm[..., None]).astype(jnp.bfloat16)
        return carried + jnp.einsum(
            "hqk,khe->qhe", attn_probs, pieces[1], preferred_element_type=jnp.float32
        )

    zero_heads = jnp.zeros((tokens, HEADS, HEAD_DIM), jnp.float32)
    attn_sum = fold_groups(
        output_step,
        zero_heads,
        (
            lax.all_gather(key_heads, "ctx", axis=0, tiled=True),
            lax.all_gather(value_heads, "ctx", axis=0, tiled=True),
        ),
        tokens,
    )
    attended = attn_sum.reshape(tokens, head_width).astype(jnp.bfloat16)
    after_self = resid_in + plain_dot(attended, out_full)
    normed_two = rms_norm(after_self, gain_two).astype(jnp.bfloat16)
    cross_q_heads = (
        plain_dot(normed_two, cross_query_full)
        .astype(jnp.bfloat16)
        .reshape(tokens, HEADS, HEAD_DIM)
    )
    encoder_rows = encoder[0]
    encoder_key_rows, cross_values = (
        lax.all_gather(
            plain_dot(encoder_rows, cross_key_full).astype(jnp.bfloat16), "ctx", axis=0, tiled=True
        ),
        lax.all_gather(
            plain_dot(encoder_rows, cross_value_full).astype(jnp.bfloat16),
            "ctx",
            axis=0,
            tiled=True,
        ),
    )
    cross_k_heads = encoder_key_rows.reshape(encoder_key_rows.shape[0], HEADS, HEAD_DIM)
    cross_v_heads = cross_values.reshape(cross_values.shape[0], HEADS, HEAD_DIM)
    cross_logits = jnp.einsum(
        "qhe,khe->hqk", cross_q_heads, cross_k_heads, preferred_element_type=jnp.float32
    )
    cross_exact = jnp.exp(cross_logits - jax.nn.logsumexp(cross_logits, axis=-1, keepdims=True))
    cross_probs = cross_exact.astype(jnp.bfloat16)
    cross_mixed = (
        jnp.einsum("hqk,khe->qhe", cross_probs, cross_v_heads, preferred_element_type=jnp.float32)
        .reshape(tokens, head_width)
        .astype(jnp.bfloat16)
    )
    after_cross = after_self + plain_dot(cross_mixed, cross_out_full)
    normed_three = rms_norm(after_cross, gain_three).astype(jnp.bfloat16)
    gate_act = plain_dot(normed_three, gate_full)
    up_act = plain_dot(normed_three, up_full)
    hidden_float, mlp_pull = jax.vjp(gelu_product, gate_act, up_act)
    hidden = hidden_float.astype(jnp.bfloat16)
    result = after_cross + plain_dot(hidden, down_full)
    resid_grad = cotangent[0].astype(jnp.float32)
    branch_three = resid_grad.astype(jnp.bfloat16)
    down_grad = left_contract(hidden, branch_three)
    hidden_state_gradient = right_contract(branch_three, down_full)
    gate_grad, up_grad = mlp_pull(hidden_state_gradient)
    gate_grad = gate_grad.astype(jnp.bfloat16)
    up_grad = up_grad.astype(jnp.bfloat16)
    gate_w_grad = left_contract(normed_three, gate_grad)
    up_w_grad = left_contract(normed_three, up_grad)
    normed_three_grad = right_contract(gate_grad, gate_full) + right_contract(up_grad, up_full)
    part_grad, gain_three_grad = norm_back(after_cross, gain_three, normed_three_grad)
    after_cross_grad = resid_grad + part_grad
    branch_two = after_cross_grad.astype(jnp.bfloat16)
    cross_out_grad = left_contract(cross_mixed, branch_two)
    mix_grad = (
        right_contract(branch_two, cross_out_full)
        .astype(jnp.bfloat16)
        .reshape(tokens, HEADS, HEAD_DIM)
    )
    cross_score_grad = jnp.einsum(
        "qhe,khe->hqk", mix_grad, cross_v_heads, preferred_element_type=jnp.float32
    )
    cross_delta = jnp.sum(cross_exact * cross_score_grad, axis=-1, keepdims=True)
    cross_dlogits = (cross_exact * (cross_score_grad - cross_delta)).astype(jnp.bfloat16)
    cross_q_grad = (
        jnp.einsum("hqk,khe->qhe", cross_dlogits, cross_k_heads, preferred_element_type=jnp.float32)
        .reshape(tokens, head_width)
        .astype(jnp.bfloat16)
    )
    cross_k_part = jnp.einsum(
        "hqk,qhe->khe", cross_dlogits, cross_q_heads, preferred_element_type=jnp.float32
    ).reshape(-1, head_width)
    cross_v_part = jnp.einsum(
        "hqk,qhe->khe", cross_probs, mix_grad, preferred_element_type=jnp.float32
    ).reshape(-1, head_width)
    cross_k_grad, cross_v_grad = (
        lax.psum_scatter(cross_k_part, "ctx", scatter_dimension=0, tiled=True),
        lax.psum_scatter(cross_v_part, "ctx", scatter_dimension=0, tiled=True),
    )
    cross_k_grad = cross_k_grad.astype(jnp.bfloat16)
    cross_v_grad = cross_v_grad.astype(jnp.bfloat16)
    cross_query_grad = left_contract(normed_two, cross_q_grad)
    cross_key_grad = left_contract(encoder_rows, cross_k_grad)
    cross_value_grad = left_contract(encoder_rows, cross_v_grad)
    encoder_grad = (
        right_contract(cross_k_grad, cross_key_full)
        + right_contract(cross_v_grad, cross_value_full)
    ).astype(jnp.bfloat16)
    normed_two_grad = right_contract(cross_q_grad, cross_query_full)
    part_grad, gain_two_grad = norm_back(after_self, gain_two, normed_two_grad)
    after_self_grad = after_cross_grad + part_grad
    branch_one = after_self_grad.astype(jnp.bfloat16)
    out_w_grad = left_contract(attended, branch_one)
    dattn_heads = (
        right_contract(branch_one, out_full).astype(jnp.bfloat16).reshape(tokens, HEADS, HEAD_DIM)
    )
    row_delta = jnp.einsum("qhe,qhe->hq", dattn_heads.astype(jnp.float32), attn_sum)

    def block_grads(
        query_side, grad_side, norm_side, delta_side, query_pos, key_side, value_side, key_pos
    ):
        logits, allowed, indicator = query_key_logits(query_side, key_side, query_pos, key_pos)
        exact = jnp.exp(logits - norm_side[..., None])
        score_grad = jnp.einsum(
            "qhe,khe->hqk", grad_side, value_side, preferred_element_type=jnp.float32
        )
        logits_gradient = (exact * (score_grad - delta_side[..., None])).astype(jnp.bfloat16)
        grad_query = jnp.einsum(
            "hqk,khe->qhe", logits_gradient, key_side, preferred_element_type=jnp.float32
        )
        grad_key = jnp.einsum(
            "hqk,qhe->khe", logits_gradient, query_side, preferred_element_type=jnp.float32
        )
        grad_value = jnp.einsum(
            "hqk,qhe->khe",
            exact.astype(jnp.bfloat16),
            grad_side,
            preferred_element_type=jnp.float32,
        )
        bucket_table_gradient = jnp.einsum(
            "ouw,muw->om", indicator, logits_gradient, preferred_element_type=jnp.float32
        )
        return (grad_query, grad_key, grad_value, bucket_table_gradient)

    zero_table = jnp.zeros((BUCKETS, HEADS), jnp.float32)
    full_zero = jnp.zeros((total_rows, HEADS, HEAD_DIM), jnp.float32)

    def key_grad_step(carried, pieces, first_row):
        query_total, table_total, key_total, value_total = carried
        key_pos = lookup_positions(block_order, first_row, pieces[0].shape[0], block_len)
        grad_query, grad_key, grad_value, bucket_table_gradient = block_grads(
            query_heads, dattn_heads, log_norm, row_delta, own_pos, pieces[0], pieces[1], key_pos
        )
        key_total = lax.dynamic_update_slice_in_dim(key_total, grad_key, first_row, 0)
        value_total = lax.dynamic_update_slice_in_dim(value_total, grad_value, first_row, 0)
        return (
            query_total + grad_query,
            table_total + bucket_table_gradient,
            key_total,
            value_total,
        )

    query_sum, table_grad, key_partial, value_partial = fold_groups(
        key_grad_step,
        (zero_heads, zero_table, full_zero, full_zero),
        (
            lax.all_gather(key_heads, "ctx", axis=0, tiled=True),
            lax.all_gather(value_heads, "ctx", axis=0, tiled=True),
        ),
        tokens,
    )
    key_sum, value_accumulated = (
        lax.psum_scatter(key_partial, "ctx", scatter_dimension=0, tiled=True),
        lax.psum_scatter(value_partial, "ctx", scatter_dimension=0, tiled=True),
    )
    query_grad = query_sum.reshape(tokens, head_width).astype(jnp.bfloat16)
    key_grad = key_sum.reshape(tokens, head_width).astype(jnp.bfloat16)
    value_grad = value_accumulated.reshape(tokens, head_width).astype(jnp.bfloat16)
    query_w_grad = left_contract(normed_one, query_grad)
    key_w_grad = left_contract(normed_one, key_grad)
    value_w_grad = left_contract(normed_one, value_grad)
    normed_one_grad = (
        right_contract(query_grad, query_full)
        + right_contract(key_grad, key_full)
        + right_contract(value_grad, value_full)
    )
    part_grad, gain_one_grad = norm_back(resid_in, gain_one, normed_one_grad)
    input_grad = (after_self_grad + part_grad).astype(jnp.bfloat16)
    (
        sum_gain_one,
        sum_query,
        sum_key,
        sum_value,
        sum_out,
        sum_table,
        sum_gain_two,
        sum_cross_query,
        sum_cross_key,
        sum_cross_value,
        sum_cross_out,
        sum_gain_three,
        sum_gate,
        sum_up,
        sum_down,
    ) = (
        lax.psum_scatter(
            gain_one_grad.astype(jnp.bfloat16), "wsh", scatter_dimension=0, tiled=True
        ).astype(jnp.float32),
        lax.psum_scatter(
            query_w_grad.astype(jnp.bfloat16), "wsh", scatter_dimension=0, tiled=True
        ).astype(jnp.float32),
        lax.psum_scatter(
            key_w_grad.astype(jnp.bfloat16), "wsh", scatter_dimension=0, tiled=True
        ).astype(jnp.float32),
        lax.psum_scatter(
            value_w_grad.astype(jnp.bfloat16), "wsh", scatter_dimension=0, tiled=True
        ).astype(jnp.float32),
        lax.psum_scatter(
            out_w_grad.astype(jnp.bfloat16), "wsh", scatter_dimension=0, tiled=True
        ).astype(jnp.float32),
        lax.psum_scatter(
            table_grad.astype(jnp.bfloat16), "wsh", scatter_dimension=0, tiled=True
        ).astype(jnp.float32),
        lax.psum_scatter(
            gain_two_grad.astype(jnp.bfloat16), "wsh", scatter_dimension=0, tiled=True
        ).astype(jnp.float32),
        lax.psum_scatter(
            cross_query_grad.astype(jnp.bfloat16), "wsh", scatter_dimension=0, tiled=True
        ).astype(jnp.float32),
        lax.psum_scatter(
            cross_key_grad.astype(jnp.bfloat16), "wsh", scatter_dimension=0, tiled=True
        ).astype(jnp.float32),
        lax.psum_scatter(
            cross_value_grad.astype(jnp.bfloat16), "wsh", scatter_dimension=0, tiled=True
        ).astype(jnp.float32),
        lax.psum_scatter(
            cross_out_grad.astype(jnp.bfloat16), "wsh", scatter_dimension=0, tiled=True
        ).astype(jnp.float32),
        lax.psum_scatter(
            gain_three_grad.astype(jnp.bfloat16), "wsh", scatter_dimension=0, tiled=True
        ).astype(jnp.float32),
        lax.psum_scatter(
            gate_w_grad.astype(jnp.bfloat16), "wsh", scatter_dimension=0, tiled=True
        ).astype(jnp.float32),
        lax.psum_scatter(
            up_w_grad.astype(jnp.bfloat16), "wsh", scatter_dimension=0, tiled=True
        ).astype(jnp.float32),
        lax.psum_scatter(
            down_grad.astype(jnp.bfloat16), "wsh", scatter_dimension=0, tiled=True
        ).astype(jnp.float32),
    )
    total_grads = lax.psum(
        (
            sum_gain_one,
            sum_query,
            sum_key,
            sum_value,
            sum_out,
            sum_table,
            sum_gain_two,
            sum_cross_query,
            sum_cross_key,
            sum_cross_value,
            sum_cross_out,
            sum_gain_three,
            sum_gate,
            sum_up,
            sum_down,
        ),
        "ctx",
    )
    return (result.astype(jnp.bfloat16)[None], input_grad[None], encoder_grad[None]) + tuple(
        total_grads
    )


F32 = jnp.float32
BF16 = jnp.bfloat16
MESH = pl.DeviceIdType.MESH
TILE = 256
BLOCK = 64
MIB = 2**20


def dot_nt(left, right):
    return lax.dot_general(left, right, (((1,), (1,)), ((), ())), preferred_element_type=F32)


def vmem_spec():
    return pl.BlockSpec(memory_space=pltpu.VMEM)


def any_spec():
    return pl.BlockSpec(memory_space=pl.ANY)


def greet_all(peers):
    me, core = lax.axis_index("ctx"), lax.axis_index("wsh")
    barrier = pltpu.get_barrier_semaphore()
    for step in range(1, peers):
        pl.semaphore_signal(
            barrier, inc=1, device_id=(lax.rem(me + step, peers), core), device_id_type=MESH
        )
    pl.semaphore_wait(barrier, peers - 1)


def exchange_all(packed, landed, send_sem, recv_sem, own_sem):
    peers = packed.shape[0]
    me, core = lax.axis_index("ctx"), lax.axis_index("wsh")

    def copy(step):
        peer = lax.rem(me + step, peers)
        return pltpu.make_async_remote_copy(
            src_ref=packed.at[peer],
            dst_ref=landed.at[me],
            send_sem=send_sem.at[step],
            recv_sem=recv_sem.at[step],
            device_id=(peer, core),
            device_id_type=MESH,
        )

    copies = [copy(step) for step in range(1, peers)]
    for each in copies:
        each.start()
    own = pltpu.make_async_copy(packed.at[me], landed.at[me], own_sem)
    own.start()
    own.wait()
    for each in copies:
        each.wait()


def exchange_scratch(peers):
    return [
        pltpu.SemaphoreType.DMA((peers,)),
        pltpu.SemaphoreType.DMA((peers,)),
        pltpu.SemaphoreType.DMA,
    ]


def to_heads_kernel(q_ref, k_ref, v_ref, landed, packed, *sems):
    peers = packed.shape[0]
    greet_all(peers)
    for head in range(peers):
        cols = slice(head * HEAD_DIM, (head + 1) * HEAD_DIM)
        packed[head, : 2 * BLOCK, :] = jnp.concatenate([q_ref[:, cols], k_ref[:, cols]], axis=1)
        packed[head, 2 * BLOCK :, :] = jnp.concatenate(
            [v_ref[:BLOCK, cols], v_ref[BLOCK:, cols]], axis=1
        )
    exchange_all(packed, landed, *sems)


def to_heads(queries, keys, values):
    shape = (HEADS, 3 * BLOCK, 2 * HEAD_DIM)
    return pl.pallas_call(
        to_heads_kernel,
        out_shape=jax.ShapeDtypeStruct(shape, BF16),
        in_specs=[vmem_spec()] * 3,
        out_specs=vmem_spec(),
        scratch_shapes=[pltpu.VMEM(shape, BF16)] + exchange_scratch(HEADS),
        compiler_params=pltpu.CompilerParams(
            collective_id=1, has_side_effects=True, vmem_limit_bytes=16 * MIB
        ),
        name="to_heads",
    )(queries, keys, values)


def rows_to_heads_kernel(g_ref, landed, packed, *sems):
    peers = packed.shape[0]
    greet_all(peers)
    for head in range(peers):
        cols = slice(head * HEAD_DIM, (head + 1) * HEAD_DIM)
        packed[head] = jnp.concatenate([g_ref[:BLOCK, cols], g_ref[BLOCK:, cols]], axis=1)
    exchange_all(packed, landed, *sems)


def rows_to_heads(rows):
    shape = (HEADS, BLOCK, 2 * HEAD_DIM)
    return pl.pallas_call(
        rows_to_heads_kernel,
        out_shape=jax.ShapeDtypeStruct(shape, BF16),
        in_specs=[vmem_spec()],
        out_specs=vmem_spec(),
        scratch_shapes=[pltpu.VMEM(shape, BF16)] + exchange_scratch(HEADS),
        compiler_params=pltpu.CompilerParams(
            collective_id=2, has_side_effects=True, vmem_limit_bytes=16 * MIB
        ),
        name="rows_to_heads",
    )(rows)


def unpack_pair(landed, pair, rows):
    left, right = landed[2 * pair, rows, :], landed[2 * pair + 1, rows, :]
    return (
        jnp.concatenate([left[:, :HEAD_DIM], right[:, :HEAD_DIM]], axis=1),
        jnp.concatenate([left[:, HEAD_DIM:], right[:, HEAD_DIM:]], axis=1),
    )


def from_heads_kernel(packed, out_ref, landed, *sems):
    peers = packed.shape[0]
    greet_all(peers)
    exchange_all(packed, landed, *sems)
    for pair in range(peers // 2):
        cols = slice(pair * 2 * HEAD_DIM, (pair + 1) * 2 * HEAD_DIM)
        first, second = unpack_pair(landed, pair, slice(0, BLOCK))
        out_ref[:BLOCK, cols] = first
        out_ref[BLOCK:, cols] = second


def from_heads(packed):
    return pl.pallas_call(
        from_heads_kernel,
        out_shape=jax.ShapeDtypeStruct((2 * BLOCK, HEADS * HEAD_DIM), BF16),
        in_specs=[vmem_spec()],
        out_specs=vmem_spec(),
        scratch_shapes=[pltpu.VMEM(packed.shape, BF16)] + exchange_scratch(HEADS),
        compiler_params=pltpu.CompilerParams(
            collective_id=3, has_side_effects=True, vmem_limit_bytes=16 * MIB
        ),
        name="from_heads",
    )(packed)


def grads_from_heads_kernel(packed, q_ref, k_ref, v_ref, landed, *sems):
    peers = packed.shape[0]
    greet_all(peers)
    exchange_all(packed, landed, *sems)
    for pair in range(peers // 2):
        cols = slice(pair * 2 * HEAD_DIM, (pair + 1) * 2 * HEAD_DIM)
        q_ref[:, cols], k_ref[:, cols] = unpack_pair(landed, pair, slice(0, 2 * BLOCK))
        first, second = unpack_pair(landed, pair, slice(2 * BLOCK, 3 * BLOCK))
        v_ref[:BLOCK, cols] = first
        v_ref[BLOCK:, cols] = second


def grads_from_heads(packed):
    return pl.pallas_call(
        grads_from_heads_kernel,
        out_shape=[jax.ShapeDtypeStruct((2 * BLOCK, HEADS * HEAD_DIM), BF16)] * 3,
        in_specs=[vmem_spec()],
        out_specs=[vmem_spec()] * 3,
        scratch_shapes=[pltpu.VMEM(packed.shape, BF16)] + exchange_scratch(HEADS),
        compiler_params=pltpu.CompilerParams(
            collective_id=4, has_side_effects=True, vmem_limit_bytes=16 * MIB
        ),
        name="grads_from_heads",
    )(packed)


def place_tiles(bias_lines, tiles):
    for apart in range(tiles.shape[0]):
        line = jnp.broadcast_to(bias_lines[apart : apart + 1, :], (TILE, 2 * TILE))
        tiles[apart] = pltpu.roll(line, 0, 1, stride=1, stride_axis=0)[:, :TILE]


def attend_kernel(order, landed, bias_lines, out_ref, sum_ref, norm_ref, q_s, k_s, vt_s, tiles, ot_s, o_s):
    blocks = order.shape[0]
    spans = blocks * BLOCK // TILE
    for stored in range(blocks):
        device, half = stored // 2, stored % 2
        at = pl.ds(pl.multiple_of(order[stored] * BLOCK, BLOCK), BLOCK)
        pair = landed[device, half * BLOCK : (half + 1) * BLOCK, :]
        q_s[at, :] = pair[:, :HEAD_DIM]
        k_s[at, :] = pair[:, HEAD_DIM:]
        values = landed[device, 2 * BLOCK :, half * HEAD_DIM : (half + 1) * HEAD_DIM]
        o_s[at, :] = values.astype(F32)
    vt_s[...] = jnp.transpose(o_s[...], (1, 0)).astype(BF16)
    place_tiles(bias_lines, tiles)
    for i in range(spans):
        at_i = slice(i * TILE, (i + 1) * TILE)
        queries = q_s[at_i, :]
        scores = [
            dot_nt(k_s[j * TILE : (j + 1) * TILE, :], queries) + tiles[i - j] for j in range(i + 1)
        ]
        top = functools.reduce(
            jnp.maximum, [jnp.max(each, axis=0, keepdims=True) for each in scores]
        )
        total = jnp.zeros((1, TILE), F32)
        mixed = jnp.zeros((HEAD_DIM, TILE), F32)
        for j in range(i + 1):
            weights = jnp.exp(scores[j] - top)
            total = total + jnp.sum(weights, axis=0, keepdims=True)
            mixed = mixed + plain_dot(
                vt_s[:, j * TILE : (j + 1) * TILE], weights.astype(BF16)
            )
        norm_ref[0:1, at_i] = top + jnp.log(total)
        ot_s[:, at_i] = mixed / total
    sum_ref[...] = ot_s[...]
    o_s[...] = jnp.transpose(ot_s[...], (1, 0))
    for stored in range(blocks):
        device, half = stored // 2, stored % 2
        at = pl.ds(pl.multiple_of(order[stored] * BLOCK, BLOCK), BLOCK)
        out_ref[device, :, half * HEAD_DIM : (half + 1) * HEAD_DIM] = o_s[at, :].astype(BF16)


def attend(order, landed, bias_lines):
    blocks = order.shape[0]
    length = blocks * BLOCK
    vmem = pltpu.VMEM
    return pl.pallas_call(
        attend_kernel,
        grid_spec=pltpu.PrefetchScalarGridSpec(
            num_scalar_prefetch=1,
            grid=(),
            in_specs=[vmem_spec()] * 2,
            out_specs=[vmem_spec()] * 3,
            scratch_shapes=[
                vmem((length, HEAD_DIM), BF16),
                vmem((length, HEAD_DIM), BF16),
                vmem((HEAD_DIM, length), BF16),
                vmem((length // TILE, TILE, TILE), F32),
                vmem((HEAD_DIM, length), F32),
                vmem((length, HEAD_DIM), F32),
            ],
        ),
        out_shape=[
            jax.ShapeDtypeStruct((blocks // 2, BLOCK, 2 * HEAD_DIM), BF16),
            jax.ShapeDtypeStruct((HEAD_DIM, length), F32),
            jax.ShapeDtypeStruct((1, length), F32),
        ],
        compiler_params=pltpu.CompilerParams(vmem_limit_bytes=32 * MIB),
        cost_estimate=pl.CostEstimate(
            flops=4 * length * length * HEAD_DIM, bytes_accessed=4 * MIB, transcendentals=length * length // 2
        ),
        name="attend",
    )(order, landed, bias_lines)


def attend_back_kernel(
    order, landed, grad_landed, sums, norm, bias_lines, out_ref, lines_ref,
    q_s, k_s, v_s, do_s, kt_s, tiles, by_offset, dq_s, dk_s, dv_s, delta_s, dqt_s,
):
    blocks = order.shape[0]
    spans = blocks * BLOCK // TILE
    for stored in range(blocks):
        device, half = stored // 2, stored % 2
        at = pl.ds(pl.multiple_of(order[stored] * BLOCK, BLOCK), BLOCK)
        cols = slice(half * HEAD_DIM, (half + 1) * HEAD_DIM)
        pair = landed[device, half * BLOCK : (half + 1) * BLOCK, :]
        q_s[at, :] = pair[:, :HEAD_DIM]
        k_s[at, :] = pair[:, HEAD_DIM:]
        v_s[at, :] = landed[device, 2 * BLOCK :, cols]
        do_s[at, :] = grad_landed[device, :, cols]
    place_tiles(bias_lines, tiles)
    kt_s[...] = jnp.transpose(k_s[...].astype(F32), (1, 0)).astype(BF16)
    grad_t = jnp.transpose(do_s[...].astype(F32), (1, 0))
    delta_s[...] = jnp.sum(grad_t * sums[...], axis=0, keepdims=True)
    by_offset[...] = jnp.zeros_like(by_offset)
    dk_s[...] = jnp.zeros_like(dk_s)
    dv_s[...] = jnp.zeros_like(dv_s)
    for i in range(spans):
        at_i = slice(i * TILE, (i + 1) * TILE)
        queries, grads = q_s[at_i, :], do_s[at_i, :]
        norm_i, delta_i = norm[0:1, at_i], delta_s[0:1, at_i]
        dqt = jnp.zeros((HEAD_DIM, TILE), F32)
        for j in range(i + 1):
            at_j = slice(j * TILE, (j + 1) * TILE)
            exact = jnp.exp(dot_nt(k_s[at_j, :], queries) + tiles[i - j] - norm_i)
            dscore = exact * (dot_nt(v_s[at_j, :], grads) - delta_i)
            by_offset[i - j] += dscore
            rounded = dscore.astype(BF16)
            dv_s[at_j, :] += plain_dot(exact.astype(BF16), grads)
            dk_s[at_j, :] += plain_dot(rounded, queries)
            dqt = dqt + plain_dot(kt_s[:, at_j], rounded)
        dqt_s[:, at_i] = dqt
    dq_s[...] = jnp.transpose(dqt_s[...], (1, 0))
    for stored in range(blocks):
        device, half = stored // 2, stored % 2
        at = pl.ds(pl.multiple_of(order[stored] * BLOCK, BLOCK), BLOCK)
        rows = slice(half * BLOCK, (half + 1) * BLOCK)
        out_ref[device, rows, :HEAD_DIM] = dq_s[at, :].astype(BF16)
        out_ref[device, rows, HEAD_DIM:] = dk_s[at, :].astype(BF16)
        cols = slice(half * HEAD_DIM, (half + 1) * HEAD_DIM)
        out_ref[device, 2 * BLOCK :, cols] = dv_s[at, :].astype(BF16)
    for apart in range(spans):
        folded = jnp.zeros((8, 2 * TILE), F32)
        for group in range(TILE // 8):
            rows = by_offset[apart, 8 * group : 8 * group + 8, :]
            wide = jnp.concatenate([rows, jnp.zeros((8, TILE), F32)], axis=1)
            folded = folded + (pltpu.roll(wide, 2 * TILE - 8 * group, 1) if group else wide)
        line = folded[0:1]
        for row in range(1, 8):
            line = line + pltpu.roll(folded[row : row + 1], 2 * TILE - row, 1)
        lines_ref[apart : apart + 1, :] = line


def attend_back(order, landed, grad_landed, sums, norm, bias_lines):
    blocks = order.shape[0]
    length = blocks * BLOCK
    spans = length // TILE
    vmem = pltpu.VMEM
    return pl.pallas_call(
        attend_back_kernel,
        grid_spec=pltpu.PrefetchScalarGridSpec(
            num_scalar_prefetch=1,
            grid=(),
            in_specs=[vmem_spec()] * 5,
            out_specs=[vmem_spec()] * 2,
            scratch_shapes=[vmem((length, HEAD_DIM), BF16)] * 4
            + [vmem((HEAD_DIM, length), BF16)]
            + [vmem((spans, TILE, TILE), F32)] * 2
            + [vmem((length, HEAD_DIM), F32)] * 3
            + [vmem((1, length), F32), vmem((HEAD_DIM, length), F32)],
        ),
        out_shape=[
            jax.ShapeDtypeStruct((blocks // 2, 3 * BLOCK, 2 * HEAD_DIM), BF16),
            jax.ShapeDtypeStruct((spans, 2 * TILE), F32),
        ],
        compiler_params=pltpu.CompilerParams(vmem_limit_bytes=32 * MIB),
        cost_estimate=pl.CostEstimate(
            flops=10 * length * length * HEAD_DIM, bytes_accessed=4 * MIB, transcendentals=length * length // 2
        ),
        name="attend_back",
    )(order, landed, grad_landed, sums, norm, bias_lines)


BIT_X, BIT_Y, BIT_Z0, BIT_Z1 = 0, 1, 2, 3
X_FIRST = (BIT_X, BIT_Y, BIT_Z0, BIT_Z1)
Y_FIRST = (BIT_Y, BIT_X, BIT_Z0, BIT_Z1)
Z_FIRST = (BIT_Z0, BIT_Z1, BIT_X, BIT_Y)


def flip_pairs(bit, size):
    return [(at, at ^ (1 << bit)) for at in range(size)]


def pick(flag, when_set, when_clear):
    return jnp.where(flag == 1, when_set, when_clear)


def reduce_pieces(left, right, order):
    peers = lax.axis_size("ctx")
    me = lax.axis_index("ctx")
    bits = [(me >> bit) & 1 for bit in order]
    half = left.shape[1] // 2
    low, high = left[:, :half], left[:, half:]
    away = left_contract(pick(bits[0], low, high), right).astype(BF16)
    came = lax.ppermute(away, "ctx", flip_pairs(order[0], peers))
    held = (left_contract(pick(bits[0], high, low), right) + came.astype(F32)).astype(BF16)
    for bit, name in zip(bits[1:3], order[1:3]):
        half = held.shape[0] // 2
        low, high = held[:half], held[half:]
        came = lax.ppermute(pick(bit, low, high), "ctx", flip_pairs(name, peers))
        held = (pick(bit, high, low).astype(F32) + came.astype(F32)).astype(BF16)
    half = held.shape[1] // 2
    low, high = held[:, :half], held[:, half:]
    came = lax.ppermute(pick(bits[3], low, high), "ctx", flip_pairs(order[3], peers))
    return (pick(bits[3], high, low).astype(F32) + came.astype(F32)).astype(BF16)


def gather_kernel(orders, *refs):
    count = len(orders)
    pieces, vec_in = refs[:count], refs[count]
    wholes, vec_out = refs[count + 1 : 2 * count + 1], refs[2 * count + 1]
    send_sem, recv_sem, own_sem, vec_send, vec_recv = refs[2 * count + 2 :]
    me, core = lax.axis_index("ctx"), lax.axis_index("wsh")
    peers = vec_out.shape[0]
    x, y, z = lax.rem(me, 2), lax.rem(me // 2, 2), me // 4
    greet_all(peers)

    def place(zz, yy, xx):
        return zz * 4 + yy * 2 + xx

    def window(array, at):
        rows, cols = pieces[array].shape
        bits = [lax.rem(at // (1 << bit), 2) for bit in orders[array]]
        block = bits[0] * 4 + bits[1] * 2 + bits[2]
        return wholes[array].at[
            pl.ds(pl.multiple_of(block * rows, 16), rows),
            pl.ds(pl.multiple_of(bits[3] * cols, 128), cols),
        ]

    UP, DOWN, ACROSS_Y, ACROSS_X = 0, 1, 2, 3
    targets = {
        UP: place(lax.rem(z + 1, 4), y, x),
        DOWN: place(lax.rem(z + 3, 4), y, x),
        ACROSS_Y: place(z, 1 - y, x),
        ACROSS_X: place(z, y, 1 - x),
    }
    sent = []

    def send(array, at, way, slot, only=None, own=False):
        def act(what):
            copy = pltpu.make_async_remote_copy(
                src_ref=pieces[array] if own else window(array, at),
                dst_ref=window(array, at),
                send_sem=send_sem.at[array, way, slot],
                recv_sem=recv_sem.at[array, at],
                device_id=(targets[way], core),
                device_id_type=MESH,
            )
            if what == "start":
                copy.start()
            else:
                copy.wait_send()

        def guarded(what):
            if only is None:
                act(what)
            else:
                pl.when(only)(functools.partial(act, what))

        guarded("start")
        sent.append(functools.partial(guarded, "end"))

    def arrive(array, at):
        pltpu.make_async_remote_copy(
            src_ref=window(array, at),
            dst_ref=window(array, at),
            send_sem=own_sem.at[array],
            recv_sem=recv_sem.at[array, at],
            device_id=(targets[ACROSS_X], core),
            device_id_type=MESH,
        ).wait_recv()

    def along_z(array, zz, at, slot, own=False):
        send(array, at, UP, slot, only=jnp.logical_and(zz <= z, z < 3), own=own)
        send(array, at, DOWN, slot, only=jnp.logical_and(zz >= z, z > 0), own=own)

    late_z = [array for array in range(count) if orders[array] == Z_FIRST]
    early_z = [array for array in range(count) if orders[array] != Z_FIRST]

    def planar(array):
        if orders[array] == X_FIRST:
            return ACROSS_Y, ACROSS_X, lambda zz: place(zz, 1 - y, x), lambda zz: place(zz, y, 1 - x)
        return ACROSS_X, ACROSS_Y, lambda zz: place(zz, y, 1 - x), lambda zz: place(zz, 1 - y, x)

    opposite = lambda zz: place(zz, 1 - y, 1 - x)

    own_copies = [
        pltpu.make_async_copy(pieces[array], window(array, me), own_sem.at[array])
        for array in range(count)
    ]
    for each in own_copies:
        each.start()
    vec_copies = []
    for step in range(1, peers):
        peer = lax.rem(me + step, peers)
        vec_copies.append(
            pltpu.make_async_remote_copy(
                src_ref=vec_in,
                dst_ref=vec_out.at[me],
                send_sem=vec_send.at[step],
                recv_sem=vec_recv.at[step],
                device_id=(peer, core),
                device_id_type=MESH,
            )
        )
    vec_copies.append(pltpu.make_async_copy(vec_in, vec_out.at[me], vec_recv.at[0]))
    for each in vec_copies:
        each.start()

    for array in early_z:
        along_z(array, z, me, 0, own=True)
        second, third, _, _ = planar(array)
        send(array, me, second, 0, own=True)
        send(array, me, third, 0, own=True)
    for array in late_z:
        send(array, me, ACROSS_Y, 0, own=True)
        send(array, me, ACROSS_X, 0, own=True)
        along_z(array, z, me, 0, own=True)
    for array in late_z:
        at = place(z, 1 - y, x)
        arrive(array, at)
        send(array, at, ACROSS_X, 1)
        along_z(array, z, at, 1)
    for step in range(1, 4):
        if step <= 2:
            for array in late_z:
                at = place(z, y, 1 - x) if step == 1 else opposite(z)
                arrive(array, at)
                along_z(array, z, at, 1 + step)
        for array in early_z:
            zz = z ^ step
            at = place(zz, y, x)
            second, third, _, _ = planar(array)
            arrive(array, at)
            along_z(array, zz, at, step)
            send(array, at, second, step)
            send(array, at, third, step)
    for step in range(4):
        for array in early_z:
            second, third, near, _ = planar(array)
            at = near(z ^ step)
            arrive(array, at)
            send(array, at, third, 4 + step)
        if step:
            for array in late_z:
                zz = z ^ step
                for slot, at in enumerate(
                    (place(zz, y, x), place(zz, 1 - y, x), place(zz, y, 1 - x), opposite(zz))
                ):
                    arrive(array, at)
                    along_z(array, zz, at, 4 * step + slot)
    for step in range(4):
        for array in early_z:
            _, _, _, far = planar(array)
            arrive(array, far(z ^ step))
            arrive(array, opposite(z ^ step))
    for each in sent:
        each()
    for each in own_copies + vec_copies:
        each.wait()


def gather_pieces(pieces, orders, vector):
    count, peers = len(pieces), lax.axis_size("ctx")
    dma = pltpu.SemaphoreType.DMA
    return pl.pallas_call(
        functools.partial(gather_kernel, orders),
        out_shape=[
            jax.ShapeDtypeStruct((8 * piece.shape[0], 2 * piece.shape[1]), BF16) for piece in pieces
        ]
        + [jax.ShapeDtypeStruct((peers,) + vector.shape, F32)],
        in_specs=[any_spec()] * (count + 1),
        out_specs=[any_spec()] * (count + 1),
        scratch_shapes=[
            dma((count, 4, 16)),
            dma((count, peers)),
            dma((count,)),
            dma((peers,)),
            dma((peers,)),
        ],
        compiler_params=pltpu.CompilerParams(collective_id=5, has_side_effects=True),
        name="gather_pieces",
    )(*pieces, vector)


def on_device_by_heads(
    inputs,
    encoder,
    cotangent,
    block_order,
    bucket_of,
    self_gain,
    query_weight,
    key_weight,
    value_weight,
    out_weight,
    bias_table,
    cross_gain,
    cross_query,
    cross_key,
    cross_value,
    cross_out,
    mlp_gain,
    gate_weight,
    up_weight,
    down_weight,
):
    core, me = lax.axis_index("wsh"), lax.axis_index("ctx")

    def swap(values):
        return lax.ppermute(values, "wsh", [(0, 1), (1, 0)])

    def own_half(values):
        half = values.shape[-1] // 2
        return pick(core, values[..., half:], values[..., :half])

    def other_half(values):
        half = values.shape[-1] // 2
        return pick(core, values[..., :half], values[..., half:])

    def join(own, other, axis):
        return pick(
            core,
            jnp.concatenate([other, own], axis=axis),
            jnp.concatenate([own, other], axis=axis),
        )

    def times(values, pair):
        return plain_dot(own_half(values), pair[0]) + plain_dot(other_half(values), pair[1])

    def times_back(values, pair):
        return join(right_contract(values, pair[0]), right_contract(values, pair[1]), 1)

    def both_cores(values):
        return jnp.concatenate([own_half(values), swap(other_half(values))], axis=0)

    def both_whole(values):
        return jnp.concatenate([values, swap(values)], axis=0)

    small = jnp.concatenate([self_gain, cross_gain, mlp_gain, bias_table.reshape(-1)])
    small_other = swap(small)
    width = self_gain.shape[0]
    gain_one, gain_two, gain_three = (
        join(small[at * width : (at + 1) * width], small_other[at * width : (at + 1) * width], 0).astype(F32)
        for at in range(3)
    )
    bias_rows = join(bias_table, small_other[3 * width :].reshape(bias_table.shape), 0).astype(F32)
    query_pair, key_pair, value_pair = (
        (member, swap(member)) for member in (query_weight, key_weight, value_weight)
    )
    out_pair, cross_query_pair, cross_key_pair, cross_value_pair, cross_out_pair = (
        (member, swap(member))
        for member in (out_weight, cross_query, cross_key, cross_value, cross_out)
    )
    gate_pair, up_pair, down_pair = (
        (member, swap(member)) for member in (gate_weight, up_weight, down_weight)
    )

    resid_in = inputs[0].astype(F32)
    tokens = resid_in.shape[0]
    head_width = HEADS * HEAD_DIM
    length = bucket_of.shape[0]

    normed_one = rms_norm(resid_in, gain_one).astype(BF16)
    queries = times(normed_one, query_pair).astype(BF16)
    keys = times(normed_one, key_pair).astype(BF16)
    values = times(normed_one, value_pair).astype(BF16)
    landed = to_heads(queries, keys, values)

    own_column = jnp.sum(
        jnp.where(jnp.arange(HEADS)[None, :] == me, bias_rows, 0.0), axis=1, keepdims=True
    )
    in_bucket = bucket_of[None, :] == jnp.arange(BUCKETS, dtype=jnp.int32)[:, None]
    by_offset = jnp.sum(jnp.where(in_bucket, own_column, 0.0), axis=0).reshape(-1, TILE)
    before = jnp.concatenate([jnp.full((1, TILE), NEG_BIG, F32), by_offset[:-1]], axis=0)
    bias_lines = jnp.concatenate([by_offset, before], axis=1)

    mixed_packed, attn_sum, log_norm = attend(block_order, landed, bias_lines)
    attended = from_heads(mixed_packed)

    after_self = resid_in + times(attended, out_pair)
    normed_two = rms_norm(after_self, gain_two).astype(BF16)
    cross_q_heads = times(normed_two, cross_query_pair).astype(BF16).reshape(tokens, HEADS, HEAD_DIM)
    encoder_all = lax.all_gather(encoder[0], "ctx", axis=0, tiled=True)
    cross_k_heads = times(encoder_all, cross_key_pair).astype(BF16).reshape(-1, HEADS, HEAD_DIM)
    cross_v_heads = times(encoder_all, cross_value_pair).astype(BF16).reshape(-1, HEADS, HEAD_DIM)
    cross_logits = jnp.einsum(
        "qhe,khe->hqk", cross_q_heads, cross_k_heads, preferred_element_type=F32
    )
    cross_exact = jnp.exp(cross_logits - jax.nn.logsumexp(cross_logits, axis=-1, keepdims=True))
    cross_probs = cross_exact.astype(BF16)
    cross_mixed = (
        jnp.einsum("hqk,khe->qhe", cross_probs, cross_v_heads, preferred_element_type=F32)
        .reshape(tokens, head_width)
        .astype(BF16)
    )
    after_cross = after_self + times(cross_mixed, cross_out_pair)
    normed_three = rms_norm(after_cross, gain_three).astype(BF16)
    gate_act = times(normed_three, gate_pair)
    up_act = times(normed_three, up_pair)
    hidden_float, mlp_pull = jax.vjp(gelu_product, gate_act, up_act)
    hidden = hidden_float.astype(BF16)
    result = (after_cross + times(hidden, down_pair)).astype(BF16)

    resid_grad = cotangent[0].astype(F32)
    branch_three = cotangent[0]
    down_piece = reduce_pieces(both_cores(hidden), both_whole(branch_three), X_FIRST)
    gate_grad, up_grad = mlp_pull(times_back(branch_three, down_pair))
    gate_grad, up_grad = gate_grad.astype(BF16), up_grad.astype(BF16)
    normed_three_both = both_cores(normed_three)
    gate_piece = reduce_pieces(normed_three_both, both_whole(gate_grad), Y_FIRST)
    up_piece = reduce_pieces(normed_three_both, both_whole(up_grad), Z_FIRST)
    normed_three_grad = times_back(gate_grad, gate_pair) + times_back(up_grad, up_pair)
    part_grad, gain_three_grad = norm_back(after_cross, gain_three, normed_three_grad)
    after_cross_grad = resid_grad + part_grad
    branch_two = after_cross_grad.astype(BF16)
    cross_out_piece = reduce_pieces(both_cores(cross_mixed), both_whole(branch_two), X_FIRST)
    mix_grad = times_back(branch_two, cross_out_pair).astype(BF16).reshape(tokens, HEADS, HEAD_DIM)
    cross_score_grad = jnp.einsum(
        "qhe,khe->hqk", mix_grad, cross_v_heads, preferred_element_type=F32
    )
    cross_delta = jnp.sum(cross_exact * cross_score_grad, axis=-1, keepdims=True)
    cross_dlogits = (cross_exact * (cross_score_grad - cross_delta)).astype(BF16)
    cross_q_grad = (
        jnp.einsum("hqk,khe->qhe", cross_dlogits, cross_k_heads, preferred_element_type=F32)
        .reshape(tokens, head_width)
        .astype(BF16)
    )
    cross_k_part = jnp.einsum(
        "hqk,qhe->khe", cross_dlogits, cross_q_heads, preferred_element_type=F32
    ).reshape(-1, head_width)
    cross_v_part = jnp.einsum(
        "hqk,qhe->khe", cross_probs, mix_grad, preferred_element_type=F32
    ).reshape(-1, head_width)
    cross_kv_part = jnp.concatenate([cross_k_part, cross_v_part], axis=1).astype(BF16)
    cross_kv_grad = lax.psum_scatter(cross_kv_part, "ctx", scatter_dimension=0, tiled=True)
    cross_kv_all = lax.all_gather(cross_kv_grad, "ctx", axis=0, tiled=True)
    encoder_grad = (
        times_back(cross_kv_grad[:, :head_width], cross_key_pair)
        + times_back(cross_kv_grad[:, head_width:], cross_value_pair)
    ).astype(BF16)
    cross_kv_w_grad = left_contract(both_cores(encoder_all), both_whole(cross_kv_all))
    cross_query_piece = reduce_pieces(both_cores(normed_two), both_whole(cross_q_grad), Y_FIRST)
    normed_two_grad = times_back(cross_q_grad, cross_query_pair)
    part_grad, gain_two_grad = norm_back(after_self, gain_two, normed_two_grad)
    after_self_grad = after_cross_grad + part_grad
    branch_one = after_self_grad.astype(BF16)
    out_piece = reduce_pieces(both_cores(attended), both_whole(branch_one), Z_FIRST)
    grad_landed = rows_to_heads(times_back(branch_one, out_pair).astype(BF16))
    packed_grads, offset_lines = attend_back(
        block_order, landed, grad_landed, attn_sum, log_norm, bias_lines
    )
    query_grad, key_grad, value_grad = grads_from_heads(packed_grads)

    offset_sums = offset_lines[:, :TILE] + jnp.concatenate(
        [offset_lines[1:, TILE:], jnp.zeros((1, TILE), F32)], axis=0
    )
    table_column = jnp.sum(jnp.where(in_bucket, offset_sums.reshape(1, length), 0.0), axis=1)
    table_grad = jnp.where(jnp.arange(HEADS)[None, :] == me, table_column[:, None], 0.0)

    normed_one_both = both_cores(normed_one)
    query_piece = reduce_pieces(normed_one_both, both_whole(query_grad), X_FIRST)
    key_piece = reduce_pieces(normed_one_both, both_whole(key_grad), Y_FIRST)
    value_piece = reduce_pieces(normed_one_both, both_whole(value_grad), Z_FIRST)
    normed_one_grad = (
        times_back(query_grad, query_pair)
        + times_back(key_grad, key_pair)
        + times_back(value_grad, value_pair)
    )
    part_grad, gain_one_grad = norm_back(resid_in, gain_one, normed_one_grad)
    input_grad = (after_self_grad + part_grad).astype(BF16)

    vector = jnp.concatenate(
        [
            gain_one_grad,
            gain_two_grad,
            gain_three_grad,
            table_grad.reshape(-1),
            jnp.zeros((512,), F32),
        ]
    ).reshape(8, 512)
    vector = vector + swap(vector)
    pieces = (
        down_piece,
        gate_piece,
        up_piece,
        cross_out_piece,
        cross_query_piece,
        out_piece,
        query_piece,
        key_piece,
        value_piece,
    )
    orders = (X_FIRST, Y_FIRST, Z_FIRST) * 3
    *wholes, vectors = gather_pieces(pieces, orders, vector)
    (
        sum_down,
        sum_gate,
        sum_up,
        sum_cross_out,
        sum_cross_query,
        sum_out,
        sum_query,
        sum_key,
        sum_value,
    ) = (member.astype(F32) for member in wholes)
    totals = jnp.sum(vectors, axis=0)
    sum_gain_one, sum_gain_two, sum_gain_three = (
        own_half(totals[2 * at : 2 * at + 2].reshape(1, -1))[0] for at in range(3)
    )
    sum_table = own_half(totals[6:7])[0].reshape(BUCKETS // 2, HEADS)
    return (
        result[None],
        input_grad[None],
        encoder_grad[None],
        sum_gain_one,
        sum_query,
        sum_key,
        sum_value,
        sum_out,
        sum_table,
        sum_gain_two,
        sum_cross_query,
        cross_kv_w_grad[:, :head_width],
        cross_kv_w_grad[:, head_width:],
        sum_cross_out,
        sum_gain_three,
        sum_gate,
        sum_up,
        sum_down,
    )


def solution(mesh):
    by_heads = mesh.shape["ctx"] == HEADS and mesh.shape["wsh"] == 2
    return jax.shard_map(
        on_device_by_heads if by_heads else on_device,
        mesh=mesh,
        in_specs=(
            P("wsh", "ctx", None),
            P("wsh", "ctx", None),
            P("wsh", "ctx", None),
            P(),
            P(),
            P("wsh"),
            P("wsh", None),
            P("wsh", None),
            P("wsh", None),
            P("wsh", None),
            P("wsh", None),
            P("wsh"),
            P("wsh", None),
            P("wsh", None),
            P("wsh", None),
            P("wsh", None),
            P("wsh"),
            P("wsh", None),
            P("wsh", None),
            P("wsh", None),
        ),
        out_specs=(
            P("wsh", "ctx", None),
            P("wsh", "ctx", None),
            P("wsh", "ctx", None),
            P("wsh"),
            P("wsh", None),
            P("wsh", None),
            P("wsh", None),
            P("wsh", None),
            P("wsh", None),
            P("wsh"),
            P("wsh", None),
            P("wsh", None),
            P("wsh", None),
            P("wsh", None),
            P("wsh"),
            P("wsh", None),
            P("wsh", None),
            P("wsh", None),
        ),
        check_vma=False,
    )
```

```python
import functools

import jax
import jax.numpy as jnp
from jax import lax
from jax.experimental import pallas as pl
from jax.experimental.pallas import tpu as pltpu
from jax.sharding import PartitionSpec as P

HEADS = 16
HEAD_DIM = 64
BUCKETS = 32


EPSILON = 1e-06
NEG_BIG = -1e30


def rms_norm(values, gain):
    return values * lax.rsqrt(jnp.mean(values * values, axis=-1, keepdims=True) + EPSILON) * gain


def plain_dot(left, right):
    return jnp.dot(left, right, preferred_element_type=jnp.float32)


def left_contract(left, right):
    return lax.dot_general(
        left, right, (((0,), (0,)), ((), ())), preferred_element_type=jnp.float32
    )


def right_contract(left, right):
    return lax.dot_general(
        left, right, (((1,), (1,)), ((), ())), preferred_element_type=jnp.float32
    )


def gelu_product(gate_vals, up_vals):
    return jax.nn.gelu(gate_vals, approximate=True) * up_vals


def norm_back(values, gain, cotan):
    normed, pullback = jax.vjp(rms_norm, values, gain)
    return pullback(cotan)


def lookup_positions(block_order, first_row, row_count, block_len):
    token_ids = first_row + jnp.arange(row_count, dtype=jnp.int32)
    block_ids = token_ids // block_len
    matches = block_ids[:, None] == jnp.arange(block_order.shape[0], dtype=jnp.int32)[None, :]
    starts = jnp.sum(jnp.where(matches, block_order[None, :], 0), axis=1)
    return starts * block_len + token_ids % block_len


def fold_groups(step_fn, carried, pieces, shard_rows):
    piece_rows = pieces[0].shape[0]
    shards = max(1, piece_rows // shard_rows)
    group_limit = max(1, 1152 // shard_rows)
    group_size = max(
        (divisor for divisor in range(1, min(shards, group_limit) + 1) if shards % divisor == 0)
    )
    group_rows = group_size * shard_rows

    def group_step(group_idx, inner_state):
        sub_pieces = tuple(
            (
                lax.dynamic_slice_in_dim(member, group_idx * group_rows, group_rows, 0)
                for member in pieces
            )
        )
        return step_fn(inner_state, sub_pieces, group_idx * group_rows)

    return lax.fori_loop(0, shards // group_size, group_step, carried)


def on_device(
    inputs,
    encoder,
    cotangent,
    block_order,
    bucket_of,
    self_gain,
    query_weight,
    key_weight,
    value_weight,
    out_weight,
    bias_table,
    cross_gain,
    cross_query,
    cross_key,
    cross_value,
    cross_out,
    mlp_gain,
    gate_weight,
    up_weight,
    down_weight,
):
    (
        gain_one,
        query_full,
        key_full,
        value_full,
        out_full,
        bias_rows,
        gain_two,
        cross_query_full,
        cross_key_full,
        cross_value_full,
        cross_out_full,
        gain_three,
        gate_full,
        up_full,
        down_full,
    ) = (
        lax.all_gather(self_gain, "wsh", axis=0, tiled=True),
        lax.all_gather(query_weight, "wsh", axis=0, tiled=True),
        lax.all_gather(key_weight, "wsh", axis=0, tiled=True),
        lax.all_gather(value_weight, "wsh", axis=0, tiled=True),
        lax.all_gather(out_weight, "wsh", axis=0, tiled=True),
        lax.all_gather(bias_table, "wsh", axis=0, tiled=True),
        lax.all_gather(cross_gain, "wsh", axis=0, tiled=True),
        lax.all_gather(cross_query, "wsh", axis=0, tiled=True),
        lax.all_gather(cross_key, "wsh", axis=0, tiled=True),
        lax.all_gather(cross_value, "wsh", axis=0, tiled=True),
        lax.all_gather(cross_out, "wsh", axis=0, tiled=True),
        lax.all_gather(mlp_gain, "wsh", axis=0, tiled=True),
        lax.all_gather(gate_weight, "wsh", axis=0, tiled=True),
        lax.all_gather(up_weight, "wsh", axis=0, tiled=True),
        lax.all_gather(down_weight, "wsh", axis=0, tiled=True),
    )
    gain_one = gain_one.astype(jnp.float32)
    gain_two = gain_two.astype(jnp.float32)
    gain_three = gain_three.astype(jnp.float32)
    resid_in = inputs[0].astype(jnp.float32)
    tokens = resid_in.shape[0]
    block_len = tokens // 2
    head_width = HEADS * HEAD_DIM
    total_rows = tokens * lax.axis_size("ctx")
    own_pos = lookup_positions(block_order, lax.axis_index("ctx") * tokens, tokens, block_len)
    bucket_ids = jnp.arange(BUCKETS, dtype=jnp.int32)
    boundaries = jnp.sum((bucket_of[None, :] < bucket_ids[1:, None]).astype(jnp.int32), axis=1)

    def bucket_indicator_of(clipped):
        bucket = jnp.sum((clipped[None] >= boundaries[:, None, None]).astype(jnp.int32), axis=0)
        return (bucket[None] == bucket_ids[:, None, None]).astype(jnp.bfloat16)

    def query_key_logits(query_heads, key_heads, query_pos, key_pos):
        logits = jnp.einsum(
            "qhe,khe->hqk", query_heads, key_heads, preferred_element_type=jnp.float32
        )
        offset = query_pos[:, None] - key_pos[None, :]
        clipped = jnp.maximum(offset, 0)
        indicator = bucket_indicator_of(clipped)
        rel_bias = jnp.einsum(
            "ouw,om->muw", indicator, bias_rows, preferred_element_type=jnp.float32
        )
        allowed = (offset >= 0)[None]
        return (jnp.where(allowed, logits + rel_bias, NEG_BIG), allowed, indicator)

    normed_one = rms_norm(resid_in, gain_one).astype(jnp.bfloat16)
    query_heads = (
        plain_dot(normed_one, query_full).astype(jnp.bfloat16).reshape(tokens, HEADS, HEAD_DIM)
    )
    key_heads = (
        plain_dot(normed_one, key_full).astype(jnp.bfloat16).reshape(tokens, HEADS, HEAD_DIM)
    )
    value_heads = (
        plain_dot(normed_one, value_full).astype(jnp.bfloat16).reshape(tokens, HEADS, HEAD_DIM)
    )

    def norm_step(carried, pieces, first_row):
        running_max, running_sum = carried
        key_pos = lookup_positions(block_order, first_row, pieces[0].shape[0], block_len)
        logits, allowed, indicator = query_key_logits(query_heads, pieces[0], own_pos, key_pos)
        new_max = jnp.maximum(running_max, jnp.max(logits, axis=-1))
        kept = jnp.where(allowed, jnp.exp(logits - new_max[..., None]), 0.0)
        return (new_max, running_sum * jnp.exp(running_max - new_max) + jnp.sum(kept, axis=-1))

    start_state = (
        jnp.full((HEADS, tokens), NEG_BIG, jnp.float32),
        jnp.zeros((HEADS, tokens), jnp.float32),
    )
    running_max, running_sum = fold_groups(
        norm_step, start_state, (lax.all_gather(key_heads, "ctx", axis=0, tiled=True),), tokens
    )
    log_norm = running_max + jnp.log(running_sum)

    def output_step(carried, pieces, first_row):
        key_pos = lookup_positions(block_order, first_row, pieces[0].shape[0], block_len)
        logits, allowed, indicator = query_key_logits(query_heads, pieces[0], own_pos, key_pos)
        attn_probs = jnp.exp(logits - log_norm[..., None]).astype(jnp.bfloat16)
        return carried + jnp.einsum(
            "hqk,khe->qhe", attn_probs, pieces[1], preferred_element_type=jnp.float32
        )

    zero_heads = jnp.zeros((tokens, HEADS, HEAD_DIM), jnp.float32)
    attn_sum = fold_groups(
        output_step,
        zero_heads,
        (
            lax.all_gather(key_heads, "ctx", axis=0, tiled=True),
            lax.all_gather(value_heads, "ctx", axis=0, tiled=True),
        ),
        tokens,
    )
    attended = attn_sum.reshape(tokens, head_width).astype(jnp.bfloat16)
    after_self = resid_in + plain_dot(attended, out_full)
    normed_two = rms_norm(after_self, gain_two).astype(jnp.bfloat16)
    cross_q_heads = (
        plain_dot(normed_two, cross_query_full)
        .astype(jnp.bfloat16)
        .reshape(tokens, HEADS, HEAD_DIM)
    )
    encoder_rows = encoder[0]
    encoder_key_rows, cross_values = (
        lax.all_gather(
            plain_dot(encoder_rows, cross_key_full).astype(jnp.bfloat16), "ctx", axis=0, tiled=True
        ),
        lax.all_gather(
            plain_dot(encoder_rows, cross_value_full).astype(jnp.bfloat16),
            "ctx",
            axis=0,
            tiled=True,
        ),
    )
    cross_k_heads = encoder_key_rows.reshape(encoder_key_rows.shape[0], HEADS, HEAD_DIM)
    cross_v_heads = cross_values.reshape(cross_values.shape[0], HEADS, HEAD_DIM)
    cross_logits = jnp.einsum(
        "qhe,khe->hqk", cross_q_heads, cross_k_heads, preferred_element_type=jnp.float32
    )
    cross_exact = jnp.exp(cross_logits - jax.nn.logsumexp(cross_logits, axis=-1, keepdims=True))
    cross_probs = cross_exact.astype(jnp.bfloat16)
    cross_mixed = (
        jnp.einsum("hqk,khe->qhe", cross_probs, cross_v_heads, preferred_element_type=jnp.float32)
        .reshape(tokens, head_width)
        .astype(jnp.bfloat16)
    )
    after_cross = after_self + plain_dot(cross_mixed, cross_out_full)
    normed_three = rms_norm(after_cross, gain_three).astype(jnp.bfloat16)
    gate_act = plain_dot(normed_three, gate_full)
    up_act = plain_dot(normed_three, up_full)
    hidden_float, mlp_pull = jax.vjp(gelu_product, gate_act, up_act)
    hidden = hidden_float.astype(jnp.bfloat16)
    result = after_cross + plain_dot(hidden, down_full)
    resid_grad = cotangent[0].astype(jnp.float32)
    branch_three = resid_grad.astype(jnp.bfloat16)
    down_grad = left_contract(hidden, branch_three)
    hidden_state_gradient = right_contract(branch_three, down_full)
    gate_grad, up_grad = mlp_pull(hidden_state_gradient)
    gate_grad = gate_grad.astype(jnp.bfloat16)
    up_grad = up_grad.astype(jnp.bfloat16)
    gate_w_grad = left_contract(normed_three, gate_grad)
    up_w_grad = left_contract(normed_three, up_grad)
    normed_three_grad = right_contract(gate_grad, gate_full) + right_contract(up_grad, up_full)
    part_grad, gain_three_grad = norm_back(after_cross, gain_three, normed_three_grad)
    after_cross_grad = resid_grad + part_grad
    branch_two = after_cross_grad.astype(jnp.bfloat16)
    cross_out_grad = left_contract(cross_mixed, branch_two)
    mix_grad = (
        right_contract(branch_two, cross_out_full)
        .astype(jnp.bfloat16)
        .reshape(tokens, HEADS, HEAD_DIM)
    )
    cross_score_grad = jnp.einsum(
        "qhe,khe->hqk", mix_grad, cross_v_heads, preferred_element_type=jnp.float32
    )
    cross_delta = jnp.sum(cross_exact * cross_score_grad, axis=-1, keepdims=True)
    cross_dlogits = (cross_exact * (cross_score_grad - cross_delta)).astype(jnp.bfloat16)
    cross_q_grad = (
        jnp.einsum("hqk,khe->qhe", cross_dlogits, cross_k_heads, preferred_element_type=jnp.float32)
        .reshape(tokens, head_width)
        .astype(jnp.bfloat16)
    )
    cross_k_part = jnp.einsum(
        "hqk,qhe->khe", cross_dlogits, cross_q_heads, preferred_element_type=jnp.float32
    ).reshape(-1, head_width)
    cross_v_part = jnp.einsum(
        "hqk,qhe->khe", cross_probs, mix_grad, preferred_element_type=jnp.float32
    ).reshape(-1, head_width)
    cross_k_grad, cross_v_grad = (
        lax.psum_scatter(cross_k_part, "ctx", scatter_dimension=0, tiled=True),
        lax.psum_scatter(cross_v_part, "ctx", scatter_dimension=0, tiled=True),
    )
    cross_k_grad = cross_k_grad.astype(jnp.bfloat16)
    cross_v_grad = cross_v_grad.astype(jnp.bfloat16)
    cross_query_grad = left_contract(normed_two, cross_q_grad)
    cross_key_grad = left_contract(encoder_rows, cross_k_grad)
    cross_value_grad = left_contract(encoder_rows, cross_v_grad)
    encoder_grad = (
        right_contract(cross_k_grad, cross_key_full)
        + right_contract(cross_v_grad, cross_value_full)
    ).astype(jnp.bfloat16)
    normed_two_grad = right_contract(cross_q_grad, cross_query_full)
    part_grad, gain_two_grad = norm_back(after_self, gain_two, normed_two_grad)
    after_self_grad = after_cross_grad + part_grad
    branch_one = after_self_grad.astype(jnp.bfloat16)
    out_w_grad = left_contract(attended, branch_one)
    dattn_heads = (
        right_contract(branch_one, out_full).astype(jnp.bfloat16).reshape(tokens, HEADS, HEAD_DIM)
    )
    row_delta = jnp.einsum("qhe,qhe->hq", dattn_heads.astype(jnp.float32), attn_sum)

    def block_grads(
        query_side, grad_side, norm_side, delta_side, query_pos, key_side, value_side, key_pos
    ):
        logits, allowed, indicator = query_key_logits(query_side, key_side, query_pos, key_pos)
        exact = jnp.exp(logits - norm_side[..., None])
        score_grad = jnp.einsum(
            "qhe,khe->hqk", grad_side, value_side, preferred_element_type=jnp.float32
        )
        logits_gradient = (exact * (score_grad - delta_side[..., None])).astype(jnp.bfloat16)
        grad_query = jnp.einsum(
            "hqk,khe->qhe", logits_gradient, key_side, preferred_element_type=jnp.float32
        )
        grad_key = jnp.einsum(
            "hqk,qhe->khe", logits_gradient, query_side, preferred_element_type=jnp.float32
        )
        grad_value = jnp.einsum(
            "hqk,qhe->khe",
            exact.astype(jnp.bfloat16),
            grad_side,
            preferred_element_type=jnp.float32,
        )
        bucket_table_gradient = jnp.einsum(
            "ouw,muw->om", indicator, logits_gradient, preferred_element_type=jnp.float32
        )
        return (grad_query, grad_key, grad_value, bucket_table_gradient)

    zero_table = jnp.zeros((BUCKETS, HEADS), jnp.float32)
    full_zero = jnp.zeros((total_rows, HEADS, HEAD_DIM), jnp.float32)

    def key_grad_step(carried, pieces, first_row):
        query_total, table_total, key_total, value_total = carried
        key_pos = lookup_positions(block_order, first_row, pieces[0].shape[0], block_len)
        grad_query, grad_key, grad_value, bucket_table_gradient = block_grads(
            query_heads, dattn_heads, log_norm, row_delta, own_pos, pieces[0], pieces[1], key_pos
        )
        key_total = lax.dynamic_update_slice_in_dim(key_total, grad_key, first_row, 0)
        value_total = lax.dynamic_update_slice_in_dim(value_total, grad_value, first_row, 0)
        return (
            query_total + grad_query,
            table_total + bucket_table_gradient,
            key_total,
            value_total,
        )

    query_sum, table_grad, key_partial, value_partial = fold_groups(
        key_grad_step,
        (zero_heads, zero_table, full_zero, full_zero),
        (
            lax.all_gather(key_heads, "ctx", axis=0, tiled=True),
            lax.all_gather(value_heads, "ctx", axis=0, tiled=True),
        ),
        tokens,
    )
    key_sum, value_accumulated = (
        lax.psum_scatter(key_partial, "ctx", scatter_dimension=0, tiled=True),
        lax.psum_scatter(value_partial, "ctx", scatter_dimension=0, tiled=True),
    )
    query_grad = query_sum.reshape(tokens, head_width).astype(jnp.bfloat16)
    key_grad = key_sum.reshape(tokens, head_width).astype(jnp.bfloat16)
    value_grad = value_accumulated.reshape(tokens, head_width).astype(jnp.bfloat16)
    query_w_grad = left_contract(normed_one, query_grad)
    key_w_grad = left_contract(normed_one, key_grad)
    value_w_grad = left_contract(normed_one, value_grad)
    normed_one_grad = (
        right_contract(query_grad, query_full)
        + right_contract(key_grad, key_full)
        + right_contract(value_grad, value_full)
    )
    part_grad, gain_one_grad = norm_back(resid_in, gain_one, normed_one_grad)
    input_grad = (after_self_grad + part_grad).astype(jnp.bfloat16)
    (
        sum_gain_one,
        sum_query,
        sum_key,
        sum_value,
        sum_out,
        sum_table,
        sum_gain_two,
        sum_cross_query,
        sum_cross_key,
        sum_cross_value,
        sum_cross_out,
        sum_gain_three,
        sum_gate,
        sum_up,
        sum_down,
    ) = (
        lax.psum_scatter(
            gain_one_grad.astype(jnp.bfloat16), "wsh", scatter_dimension=0, tiled=True
        ).astype(jnp.float32),
        lax.psum_scatter(
            query_w_grad.astype(jnp.bfloat16), "wsh", scatter_dimension=0, tiled=True
        ).astype(jnp.float32),
        lax.psum_scatter(
            key_w_grad.astype(jnp.bfloat16), "wsh", scatter_dimension=0, tiled=True
        ).astype(jnp.float32),
        lax.psum_scatter(
            value_w_grad.astype(jnp.bfloat16), "wsh", scatter_dimension=0, tiled=True
        ).astype(jnp.float32),
        lax.psum_scatter(
            out_w_grad.astype(jnp.bfloat16), "wsh", scatter_dimension=0, tiled=True
        ).astype(jnp.float32),
        lax.psum_scatter(
            table_grad.astype(jnp.bfloat16), "wsh", scatter_dimension=0, tiled=True
        ).astype(jnp.float32),
        lax.psum_scatter(
            gain_two_grad.astype(jnp.bfloat16), "wsh", scatter_dimension=0, tiled=True
        ).astype(jnp.float32),
        lax.psum_scatter(
            cross_query_grad.astype(jnp.bfloat16), "wsh", scatter_dimension=0, tiled=True
        ).astype(jnp.float32),
        lax.psum_scatter(
            cross_key_grad.astype(jnp.bfloat16), "wsh", scatter_dimension=0, tiled=True
        ).astype(jnp.float32),
        lax.psum_scatter(
            cross_value_grad.astype(jnp.bfloat16), "wsh", scatter_dimension=0, tiled=True
        ).astype(jnp.float32),
        lax.psum_scatter(
            cross_out_grad.astype(jnp.bfloat16), "wsh", scatter_dimension=0, tiled=True
        ).astype(jnp.float32),
        lax.psum_scatter(
            gain_three_grad.astype(jnp.bfloat16), "wsh", scatter_dimension=0, tiled=True
        ).astype(jnp.float32),
        lax.psum_scatter(
            gate_w_grad.astype(jnp.bfloat16), "wsh", scatter_dimension=0, tiled=True
        ).astype(jnp.float32),
        lax.psum_scatter(
            up_w_grad.astype(jnp.bfloat16), "wsh", scatter_dimension=0, tiled=True
        ).astype(jnp.float32),
        lax.psum_scatter(
            down_grad.astype(jnp.bfloat16), "wsh", scatter_dimension=0, tiled=True
        ).astype(jnp.float32),
    )
    total_grads = lax.psum(
        (
            sum_gain_one,
            sum_query,
            sum_key,
            sum_value,
            sum_out,
            sum_table,
            sum_gain_two,
            sum_cross_query,
            sum_cross_key,
            sum_cross_value,
            sum_cross_out,
            sum_gain_three,
            sum_gate,
            sum_up,
            sum_down,
        ),
        "ctx",
    )
    return (result.astype(jnp.bfloat16)[None], input_grad[None], encoder_grad[None]) + tuple(
        total_grads
    )


F32 = jnp.float32
BF16 = jnp.bfloat16
MESH = pl.DeviceIdType.MESH
TILE = 256
BLOCK = 64
MIB = 2**20


def dot_nt(left, right):
    return lax.dot_general(left, right, (((1,), (1,)), ((), ())), preferred_element_type=F32)


def vmem_spec():
    return pl.BlockSpec(memory_space=pltpu.VMEM)


def any_spec():
    return pl.BlockSpec(memory_space=pl.ANY)


def greet_all(peers):
    me, core = lax.axis_index("ctx"), lax.axis_index("wsh")
    barrier = pltpu.get_barrier_semaphore()
    for step in range(1, peers):
        pl.semaphore_signal(
            barrier, inc=1, device_id=(lax.rem(me + step, peers), core), device_id_type=MESH
        )
    pl.semaphore_wait(barrier, peers - 1)


def exchange_all(packed, landed, send_sem, recv_sem, own_sem):
    peers = packed.shape[0]
    me, core = lax.axis_index("ctx"), lax.axis_index("wsh")

    def copy(step):
        peer = lax.rem(me + step, peers)
        return pltpu.make_async_remote_copy(
            src_ref=packed.at[peer],
            dst_ref=landed.at[me],
            send_sem=send_sem.at[step],
            recv_sem=recv_sem.at[step],
            device_id=(peer, core),
            device_id_type=MESH,
        )

    copies = [copy(step) for step in range(1, peers)]
    for each in copies:
        each.start()
    own = pltpu.make_async_copy(packed.at[me], landed.at[me], own_sem)
    own.start()
    own.wait()
    for each in copies:
        each.wait()


def exchange_scratch(peers):
    return [
        pltpu.SemaphoreType.DMA((peers,)),
        pltpu.SemaphoreType.DMA((peers,)),
        pltpu.SemaphoreType.DMA,
    ]


def to_heads_kernel(q_ref, k_ref, v_ref, rows_ref, landed, rows_out, packed, rows_send, rows_recv, rows_own, *sems):
    peers = packed.shape[0]
    me, core = lax.axis_index("ctx"), lax.axis_index("wsh")
    greet_all(peers)
    copies = []
    for step in range(1, peers):
        copies.append(
            pltpu.make_async_remote_copy(
                src_ref=rows_ref,
                dst_ref=rows_out.at[me],
                send_sem=rows_send.at[step],
                recv_sem=rows_recv.at[step],
                device_id=(lax.rem(me + step, peers), core),
                device_id_type=MESH,
            )
        )
    copies.append(pltpu.make_async_copy(rows_ref, rows_out.at[me], rows_own))
    for head in range(peers):
        cols = slice(head * HEAD_DIM, (head + 1) * HEAD_DIM)
        packed[head, : 2 * BLOCK, :] = jnp.concatenate([q_ref[:, cols], k_ref[:, cols]], axis=1)
        packed[head, 2 * BLOCK :, :] = jnp.concatenate(
            [v_ref[:BLOCK, cols], v_ref[BLOCK:, cols]], axis=1
        )
    for each in copies:
        each.start()
    exchange_all(packed, landed, *sems)
    for each in copies:
        each.wait()


def to_heads(queries, keys, values, rows):
    shape = (HEADS, 3 * BLOCK, 2 * HEAD_DIM)
    return pl.pallas_call(
        to_heads_kernel,
        out_shape=[
            jax.ShapeDtypeStruct(shape, BF16),
            jax.ShapeDtypeStruct((HEADS,) + rows.shape, BF16),
        ],
        in_specs=[vmem_spec()] * 4,
        out_specs=[vmem_spec()] * 2,
        scratch_shapes=[pltpu.VMEM(shape, BF16)] + exchange_scratch(HEADS) * 2,
        compiler_params=pltpu.CompilerParams(
            collective_id=1, has_side_effects=True, vmem_limit_bytes=16 * MIB
        ),
        name="to_heads",
    )(queries, keys, values, rows)


def rows_to_heads_kernel(g_ref, landed, packed, *sems):
    peers = packed.shape[0]
    greet_all(peers)
    for head in range(peers):
        cols = slice(head * HEAD_DIM, (head + 1) * HEAD_DIM)
        packed[head] = jnp.concatenate([g_ref[:BLOCK, cols], g_ref[BLOCK:, cols]], axis=1)
    exchange_all(packed, landed, *sems)


def rows_to_heads(rows):
    shape = (HEADS, BLOCK, 2 * HEAD_DIM)
    return pl.pallas_call(
        rows_to_heads_kernel,
        out_shape=jax.ShapeDtypeStruct(shape, BF16),
        in_specs=[vmem_spec()],
        out_specs=vmem_spec(),
        scratch_shapes=[pltpu.VMEM(shape, BF16)] + exchange_scratch(HEADS),
        compiler_params=pltpu.CompilerParams(
            collective_id=2, has_side_effects=True, vmem_limit_bytes=16 * MIB
        ),
        name="rows_to_heads",
    )(rows)


def unpack_pair(landed, pair, rows):
    left, right = landed[2 * pair, rows, :], landed[2 * pair + 1, rows, :]
    return (
        jnp.concatenate([left[:, :HEAD_DIM], right[:, :HEAD_DIM]], axis=1),
        jnp.concatenate([left[:, HEAD_DIM:], right[:, HEAD_DIM:]], axis=1),
    )


def from_heads_kernel(packed, out_ref, landed, *sems):
    peers = packed.shape[0]
    greet_all(peers)
    exchange_all(packed, landed, *sems)
    for pair in range(peers // 2):
        cols = slice(pair * 2 * HEAD_DIM, (pair + 1) * 2 * HEAD_DIM)
        first, second = unpack_pair(landed, pair, slice(0, BLOCK))
        out_ref[:BLOCK, cols] = first
        out_ref[BLOCK:, cols] = second


def from_heads(packed):
    return pl.pallas_call(
        from_heads_kernel,
        out_shape=jax.ShapeDtypeStruct((2 * BLOCK, HEADS * HEAD_DIM), BF16),
        in_specs=[vmem_spec()],
        out_specs=vmem_spec(),
        scratch_shapes=[pltpu.VMEM(packed.shape, BF16)] + exchange_scratch(HEADS),
        compiler_params=pltpu.CompilerParams(
            collective_id=3, has_side_effects=True, vmem_limit_bytes=16 * MIB
        ),
        name="from_heads",
    )(packed)


def grads_from_heads_kernel(packed, q_ref, k_ref, v_ref, landed, *sems):
    peers = packed.shape[0]
    greet_all(peers)
    exchange_all(packed, landed, *sems)
    for pair in range(peers // 2):
        cols = slice(pair * 2 * HEAD_DIM, (pair + 1) * 2 * HEAD_DIM)
        q_ref[:, cols], k_ref[:, cols] = unpack_pair(landed, pair, slice(0, 2 * BLOCK))
        first, second = unpack_pair(landed, pair, slice(2 * BLOCK, 3 * BLOCK))
        v_ref[:BLOCK, cols] = first
        v_ref[BLOCK:, cols] = second


def grads_from_heads(packed):
    return pl.pallas_call(
        grads_from_heads_kernel,
        out_shape=[jax.ShapeDtypeStruct((2 * BLOCK, HEADS * HEAD_DIM), BF16)] * 3,
        in_specs=[vmem_spec()],
        out_specs=[vmem_spec()] * 3,
        scratch_shapes=[pltpu.VMEM(packed.shape, BF16)] + exchange_scratch(HEADS),
        compiler_params=pltpu.CompilerParams(
            collective_id=4, has_side_effects=True, vmem_limit_bytes=16 * MIB
        ),
        name="grads_from_heads",
    )(packed)


def place_tiles(bias_lines, tiles):
    for apart in range(tiles.shape[0]):
        line = jnp.broadcast_to(bias_lines[apart : apart + 1, :], (TILE, 2 * TILE))
        tiles[apart] = pltpu.roll(line, 0, 1, stride=1, stride_axis=0)[:, :TILE]


def attend_kernel(order, landed, bias_lines, out_ref, sum_ref, norm_ref, q_s, k_s, vt_s, tiles, ot_s, o_s):
    blocks = order.shape[0]
    spans = blocks * BLOCK // TILE
    for stored in range(blocks):
        device, half = stored // 2, stored % 2
        at = pl.ds(pl.multiple_of(order[stored] * BLOCK, BLOCK), BLOCK)
        pair = landed[device, half * BLOCK : (half + 1) * BLOCK, :]
        q_s[at, :] = pair[:, :HEAD_DIM]
        k_s[at, :] = pair[:, HEAD_DIM:]
        values = landed[device, 2 * BLOCK :, half * HEAD_DIM : (half + 1) * HEAD_DIM]
        o_s[at, :] = values.astype(F32)
    vt_s[...] = jnp.transpose(o_s[...], (1, 0)).astype(BF16)
    place_tiles(bias_lines, tiles)
    for i in range(spans):
        at_i = slice(i * TILE, (i + 1) * TILE)
        queries = q_s[at_i, :]
        scores = [
            dot_nt(k_s[j * TILE : (j + 1) * TILE, :], queries) + tiles[i - j] for j in range(i + 1)
        ]
        top = functools.reduce(
            jnp.maximum, [jnp.max(each, axis=0, keepdims=True) for each in scores]
        )
        total = jnp.zeros((1, TILE), F32)
        mixed = jnp.zeros((HEAD_DIM, TILE), F32)
        for j in range(i + 1):
            weights = jnp.exp(scores[j] - top)
            total = total + jnp.sum(weights, axis=0, keepdims=True)
            mixed = mixed + plain_dot(
                vt_s[:, j * TILE : (j + 1) * TILE], weights.astype(BF16)
            )
        norm_ref[0:1, at_i] = top + jnp.log(total)
        ot_s[:, at_i] = mixed / total
    sum_ref[...] = ot_s[...]
    o_s[...] = jnp.transpose(ot_s[...], (1, 0))
    for stored in range(blocks):
        device, half = stored // 2, stored % 2
        at = pl.ds(pl.multiple_of(order[stored] * BLOCK, BLOCK), BLOCK)
        out_ref[device, :, half * HEAD_DIM : (half + 1) * HEAD_DIM] = o_s[at, :].astype(BF16)


def attend(order, landed, bias_lines):
    blocks = order.shape[0]
    length = blocks * BLOCK
    vmem = pltpu.VMEM
    return pl.pallas_call(
        attend_kernel,
        grid_spec=pltpu.PrefetchScalarGridSpec(
            num_scalar_prefetch=1,
            grid=(),
            in_specs=[vmem_spec()] * 2,
            out_specs=[vmem_spec()] * 3,
            scratch_shapes=[
                vmem((length, HEAD_DIM), BF16),
                vmem((length, HEAD_DIM), BF16),
                vmem((HEAD_DIM, length), BF16),
                vmem((length // TILE, TILE, TILE), F32),
                vmem((HEAD_DIM, length), F32),
                vmem((length, HEAD_DIM), F32),
            ],
        ),
        out_shape=[
            jax.ShapeDtypeStruct((blocks // 2, BLOCK, 2 * HEAD_DIM), BF16),
            jax.ShapeDtypeStruct((HEAD_DIM, length), F32),
            jax.ShapeDtypeStruct((1, length), F32),
        ],
        compiler_params=pltpu.CompilerParams(vmem_limit_bytes=32 * MIB),
        cost_estimate=pl.CostEstimate(
            flops=4 * length * length * HEAD_DIM, bytes_accessed=4 * MIB, transcendentals=length * length // 2
        ),
        name="attend",
    )(order, landed, bias_lines)


def attend_back_kernel(
    order, landed, grad_landed, sums, norm, bias_lines, out_ref, lines_ref,
    q_s, k_s, v_s, do_s, kt_s, tiles, by_offset, dq_s, dk_s, dv_s, delta_s, dqt_s,
):
    blocks = order.shape[0]
    spans = blocks * BLOCK // TILE
    for stored in range(blocks):
        device, half = stored // 2, stored % 2
        at = pl.ds(pl.multiple_of(order[stored] * BLOCK, BLOCK), BLOCK)
        cols = slice(half * HEAD_DIM, (half + 1) * HEAD_DIM)
        pair = landed[device, half * BLOCK : (half + 1) * BLOCK, :]
        q_s[at, :] = pair[:, :HEAD_DIM]
        k_s[at, :] = pair[:, HEAD_DIM:]
        v_s[at, :] = landed[device, 2 * BLOCK :, cols]
        do_s[at, :] = grad_landed[device, :, cols]
    place_tiles(bias_lines, tiles)
    kt_s[...] = jnp.transpose(k_s[...].astype(F32), (1, 0)).astype(BF16)
    grad_t = jnp.transpose(do_s[...].astype(F32), (1, 0))
    delta_s[...] = jnp.sum(grad_t * sums[...], axis=0, keepdims=True)
    by_offset[...] = jnp.zeros_like(by_offset)
    dk_s[...] = jnp.zeros_like(dk_s)
    dv_s[...] = jnp.zeros_like(dv_s)
    for i in range(spans):
        at_i = slice(i * TILE, (i + 1) * TILE)
        queries, grads = q_s[at_i, :], do_s[at_i, :]
        norm_i, delta_i = norm[0:1, at_i], delta_s[0:1, at_i]
        dqt = jnp.zeros((HEAD_DIM, TILE), F32)
        for j in range(i + 1):
            at_j = slice(j * TILE, (j + 1) * TILE)
            exact = jnp.exp(dot_nt(k_s[at_j, :], queries) + tiles[i - j] - norm_i)
            dscore = exact * (dot_nt(v_s[at_j, :], grads) - delta_i)
            by_offset[i - j] += dscore
            rounded = dscore.astype(BF16)
            dv_s[at_j, :] += plain_dot(exact.astype(BF16), grads)
            dk_s[at_j, :] += plain_dot(rounded, queries)
            dqt = dqt + plain_dot(kt_s[:, at_j], rounded)
        dqt_s[:, at_i] = dqt
    dq_s[...] = jnp.transpose(dqt_s[...], (1, 0))
    for stored in range(blocks):
        device, half = stored // 2, stored % 2
        at = pl.ds(pl.multiple_of(order[stored] * BLOCK, BLOCK), BLOCK)
        rows = slice(half * BLOCK, (half + 1) * BLOCK)
        out_ref[device, rows, :HEAD_DIM] = dq_s[at, :].astype(BF16)
        out_ref[device, rows, HEAD_DIM:] = dk_s[at, :].astype(BF16)
        cols = slice(half * HEAD_DIM, (half + 1) * HEAD_DIM)
        out_ref[device, 2 * BLOCK :, cols] = dv_s[at, :].astype(BF16)
    for apart in range(spans):
        folded = jnp.zeros((8, 2 * TILE), F32)
        for group in range(TILE // 8):
            rows = by_offset[apart, 8 * group : 8 * group + 8, :]
            wide = jnp.concatenate([rows, jnp.zeros((8, TILE), F32)], axis=1)
            folded = folded + (pltpu.roll(wide, 2 * TILE - 8 * group, 1) if group else wide)
        line = folded[0:1]
        for row in range(1, 8):
            line = line + pltpu.roll(folded[row : row + 1], 2 * TILE - row, 1)
        lines_ref[apart : apart + 1, :] = line


def attend_back(order, landed, grad_landed, sums, norm, bias_lines):
    blocks = order.shape[0]
    length = blocks * BLOCK
    spans = length // TILE
    vmem = pltpu.VMEM
    return pl.pallas_call(
        attend_back_kernel,
        grid_spec=pltpu.PrefetchScalarGridSpec(
            num_scalar_prefetch=1,
            grid=(),
            in_specs=[vmem_spec()] * 5,
            out_specs=[vmem_spec()] * 2,
            scratch_shapes=[vmem((length, HEAD_DIM), BF16)] * 4
            + [vmem((HEAD_DIM, length), BF16)]
            + [vmem((spans, TILE, TILE), F32)] * 2
            + [vmem((length, HEAD_DIM), F32)] * 3
            + [vmem((1, length), F32), vmem((HEAD_DIM, length), F32)],
        ),
        out_shape=[
            jax.ShapeDtypeStruct((blocks // 2, 3 * BLOCK, 2 * HEAD_DIM), BF16),
            jax.ShapeDtypeStruct((spans, 2 * TILE), F32),
        ],
        compiler_params=pltpu.CompilerParams(vmem_limit_bytes=32 * MIB),
        cost_estimate=pl.CostEstimate(
            flops=10 * length * length * HEAD_DIM, bytes_accessed=4 * MIB, transcendentals=length * length // 2
        ),
        name="attend_back",
    )(order, landed, grad_landed, sums, norm, bias_lines)


BIT_X, BIT_Y = 0, 1


def pick(flag, when_set, when_clear):
    return jnp.where(flag == 1, when_set, when_clear)


UP, DOWN, ACROSS_Y, ACROSS_X = 0, 1, 2, 3


class Product:
    def __init__(self, left, right, first, tall, route):
        self.left, self.right, self.first, self.tall, self.route = left, right, first, tall, route


def weight_grad_kernel(products, left_count, *refs):
    count = len(products)
    refs = list(refs)

    def take(number):
        taken = refs[:number]
        del refs[:number]
        return taken

    lefts, rights, (vec_in,) = take(left_count), take(count), take(1)
    wholes, (vec_out,) = take(count), take(1)
    left_all, left_pass, left_t = take(left_count), take(left_count), take(left_count)
    right_all, away, came, held, up_in, down_in = (take(count) for _ in range(6))
    (
        left_send,
        left_recv,
        right_send,
        right_recv,
        pair_send,
        pair_recv,
        line_send,
        line_recv,
        out_send,
        out_recv,
        own_sem,
        vec_send,
        vec_recv,
    ) = refs
    me, core = lax.axis_index("ctx"), lax.axis_index("wsh")
    peers = lax.axis_size("ctx")
    tokens = lefts[0].shape[0]
    x, y, z = lax.rem(me, 2), lax.rem(me // 2, 2), me // 4

    barrier = pltpu.get_barrier_semaphore()
    for step in range(1, peers):
        for side in (core, 1 - core):
            pl.semaphore_signal(
                barrier, inc=1, device_id=(lax.rem(me + step, peers), side), device_id_type=MESH
            )
    pl.semaphore_signal(barrier, inc=1, device_id=(me, 1 - core), device_id_type=MESH)
    pl.semaphore_wait(barrier, 2 * peers - 1)

    def place(zz, yy, xx):
        return zz * 4 + yy * 2 + xx

    targets = {
        UP: place(lax.rem(z + 1, 4), y, x),
        DOWN: place(lax.rem(z + 3, 4), y, x),
        ACROSS_Y: place(z, 1 - y, x),
        ACROSS_X: place(z, y, 1 - x),
    }
    finish = []

    def remote(src, dst, send_sem, recv_sem, ctx, side):
        return pltpu.make_async_remote_copy(
            src_ref=src,
            dst_ref=dst,
            send_sem=send_sem,
            recv_sem=recv_sem,
            device_id=(ctx, side),
            device_id_type=MESH,
        )

    def launch(copy, only=None):
        if only is None:
            copy.start()
            finish.append(copy.wait_send)
        else:
            pl.when(only)(copy.start)
            finish.append(lambda: pl.when(only)(copy.wait_send))

    def arrived(dst, recv_sem):
        remote(dst, dst, own_sem.at[0], recv_sem, me, 1 - core).wait_recv()

    def lanes(ref, at, width):
        return ref.at[:, pl.ds(pl.multiple_of(at * width, 128), width)]

    def rows(ref, at, height):
        return ref.at[pl.ds(pl.multiple_of(at * height, 16), height)]

    def slot(ref, index):
        return ref.at[pl.ds(index * tokens, tokens)]

    def axes(product):
        along_x, along_y = (x, ACROSS_X), (y, ACROSS_Y)
        return (along_x, along_y) if product.first == BIT_X else (along_y, along_x)

    left_axis = {product.left: product for product in products}

    def send_left(at):
        (_, way), _ = axes(left_axis[at])
        half = left_all[at].shape[1]
        launch(remote(lanes(lefts[at], core, half), slot(left_all[at], 1), left_send.at[at, 0], left_recv.at[at, 0], targets[way], core))
        launch(remote(lanes(lefts[at], 1 - core, half), left_pass[at], left_send.at[at, 1], left_recv.at[at, 1], targets[way], core))
        launch(remote(lanes(lefts[at], 1 - core, half), slot(left_all[at], 2), left_send.at[at, 2], left_recv.at[at, 2], me, 1 - core))
        own = pltpu.make_async_copy(lanes(lefts[at], core, half), slot(left_all[at], 0), left_send.at[at, 4])
        own.start()
        return own

    def send_right(at):
        (mine, way), _ = axes(products[at])
        half = right_all[at].shape[1]
        launch(remote(lanes(rights[at], 1 - mine, half), slot(right_all[at], 1), right_send.at[at, 0], right_recv.at[at, 0], targets[way], core))
        launch(remote(lanes(rights[at], mine, half), slot(right_all[at], 2), right_send.at[at, 1], right_recv.at[at, 1], me, 1 - core))
        own = pltpu.make_async_copy(lanes(rights[at], mine, half), slot(right_all[at], 0), right_send.at[at, 3])
        own.start()
        return own

    seen = set()
    owns = {}
    for at, product in enumerate(products):
        if product.left not in seen:
            seen.add(product.left)
            owns["left", product.left] = send_left(product.left)
        owns["right", at] = send_right(at)

    for step in range(1, peers):
        peer = lax.rem(me + step, peers)
        for offset, side in ((0, core), (peers, 1 - core)):
            launch(remote(vec_in, vec_out.at[core * peers + me], vec_send.at[offset + step], vec_recv.at[core * peers + me], peer, side))
    launch(remote(vec_in, vec_out.at[core * peers + me], vec_send.at[peers], vec_recv.at[core * peers + me], me, 1 - core))
    own_vec = pltpu.make_async_copy(vec_in, vec_out.at[core * peers + me], vec_send.at[0])
    own_vec.start()

    passed = set()

    def pass_on(at):
        left = products[at].left
        if left not in passed:
            passed.add(left)
            arrived(slot(left_all[left], 1), left_recv.at[left, 0])
            arrived(left_pass[left], left_recv.at[left, 1])
            launch(remote(left_pass[left], slot(left_all[left], 3), left_send.at[left, 3], left_recv.at[left, 3], me, 1 - core))
        arrived(slot(right_all[at], 1), right_recv.at[at, 0])
        launch(remote(slot(right_all[at], 1), slot(right_all[at], 3), right_send.at[at, 2], right_recv.at[at, 2], me, 1 - core))

    def multiply(at, out, half):
        product = products[at]
        left, right = left_t[product.left], right_all[at]
        height, width = out.shape
        step = 256 if height <= 256 else 128 if height % 256 else 256
        if product.tall:
            columns = pl.ds(pl.multiple_of(half * width, 128), width)

            def strip(index, carry):
                band = pl.ds(pl.multiple_of(index * 176, 16), 176)
                out[band, :] = plain_dot(left[band, :], right[:, columns]).astype(BF16)
                return carry

            lax.fori_loop(0, height // 176, strip, 0)
        else:
            band = pl.ds(pl.multiple_of(half * height, 16), height)

            def strip(index, carry):
                columns = pl.ds(pl.multiple_of(index * 256, 128), 256)
                out[:, columns] = plain_dot(left[band, :], right[:, columns]).astype(BF16)
                return carry

            lax.fori_loop(0, width // 256, strip, 0)
            if width % 256:
                out[:, width - 128 :] = plain_dot(left[band, :], right[:, width - 128 :]).astype(BF16)

    turned = set()

    def product_away(at):
        left = products[at].left
        if left not in turned:
            turned.add(left)
            arrived(slot(left_all[left], 2), left_recv.at[left, 2])
            arrived(slot(left_all[left], 3), left_recv.at[left, 3])
            owns["left", left].wait()
            height = left_t[left].shape[0]

            def turn(index, carry):
                band = pl.ds(pl.multiple_of(index * 128, 128), 128)
                left_t[left][band, :] = jnp.transpose(left_all[left][:, band], (1, 0))
                return carry

            lax.fori_loop(0, height // 128, turn, 0)
        arrived(slot(right_all[at], 2), right_recv.at[at, 1])
        arrived(slot(right_all[at], 3), right_recv.at[at, 2])
        owns["right", at].wait()
        _, (mine, way) = axes(products[at])
        multiply(at, away[at], 1 - mine)
        launch(remote(away[at], came[at], pair_send.at[at], pair_recv.at[at], targets[way], core))
        multiply(at, held[at], mine)

    def add(into, more):
        into[...] = (into[...].astype(F32) + more[...].astype(F32)).astype(BF16)

    def add_pair(at):
        arrived(came[at], pair_recv.at[at])
        add(held[at], came[at])

    def line_step(at, step):
        height = held[at].shape[0] // 4
        for side, buffer, behind, chunk, way in (
            (0, up_in[at], z, lax.rem(z + 3 - step, 4), UP),
            (1, down_in[at], 3 - z, lax.rem(z + step + 1, 4), DOWN),
        ):
            recv_sem = line_recv.at[at, side, chunk]

            def land(buffer=buffer, chunk=chunk, recv_sem=recv_sem):
                arrived(rows(buffer, chunk, height), recv_sem)
                add(rows(held[at], chunk, height), rows(buffer, chunk, height))

            pl.when(jnp.logical_and(behind > 0, behind <= step))(land)
            if step < 3:
                launch(
                    remote(
                        rows(held[at], chunk, height),
                        rows(buffer, chunk, height),
                        line_send.at[at, side, chunk],
                        recv_sem,
                        targets[way],
                        core,
                    ),
                    only=behind <= step,
                )

    def own_piece(at):
        return rows(held[at], z, held[at].shape[0] // 4)

    def window(at, where):
        product = products[at]
        height, width = held[at].shape
        height //= 4
        xx, yy, zz = lax.rem(where, 2), lax.rem(where // 2, 2), where // 4
        one, two = (xx, yy) if product.first == BIT_X else (yy, xx)
        row, column = (zz, one * 2 + two) if product.tall else (two * 4 + zz, one)
        return wholes[at].at[
            pl.ds(pl.multiple_of(row * height, 16), height),
            pl.ds(pl.multiple_of(column * width, 128), width),
        ]

    def send(at, where, way, index, only=None, own=False):
        launch(
            remote(
                own_piece(at) if own else window(at, where),
                window(at, where),
                out_send.at[at, way, index],
                out_recv.at[at, where],
                targets[way],
                core,
            ),
            only,
        )

    def arrive(at, where, only=None):
        def act():
            arrived(window(at, where), out_recv.at[at, where])

        if only is None:
            act()
        else:
            pl.when(only)(act)

    def near(way, zz):
        return place(zz, 1 - y, x) if way == ACROSS_Y else place(zz, y, 1 - x)

    def opposite(zz):
        return place(zz, 1 - y, 1 - x)

    def from_line(apart):
        return (
            (z >= apart, lax.rem(z + 4 - apart, 4), UP, jnp.logical_and(z >= apart, z < 3)),
            (z + apart <= 3, lax.rem(z + apart, 4), DOWN, jnp.logical_and(z + apart <= 3, z > 0)),
        )

    def gather_step(at, step):
        z_first, second, third = products[at].route
        if step == 0:
            own = pltpu.make_async_copy(own_piece(at), window(at, me), own_sem.at[at])
            own.start()
            finish.append(own.wait)
            if not z_first:
                send(at, me, second, 0, own=True)
                send(at, me, third, 0, own=True)
            send(at, me, UP, 0, only=z < 3, own=True)
            send(at, me, DOWN, 0, only=z > 0, own=True)
            if z_first:
                send(at, me, second, 0, own=True)
                send(at, me, third, 0, own=True)
        elif z_first:
            if step <= 3:
                for side, (there, zz, way, on) in enumerate(from_line(step)):
                    where = place(zz, y, x)
                    arrive(at, where, there)
                    send(at, where, way, step, on)
                    send(at, where, second, 2 * step + side, there)
                    send(at, where, third, 2 * step + side, there)
            elif step <= 7:
                where = near(second, z ^ (step - 4))
                arrive(at, where)
                send(at, where, third, 4 + step)
            elif step == 8:
                for turn in range(4):
                    arrive(at, near(third, z ^ turn))
                    arrive(at, opposite(z ^ turn))
        else:
            if step == 1:
                where = near(second, z)
                arrive(at, where)
                send(at, where, third, 1)
                send(at, where, UP, 1, z < 3)
                send(at, where, DOWN, 1, z > 0)
            elif step == 2:
                for index, where in ((2, near(third, z)), (3, opposite(z))):
                    arrive(at, where)
                    send(at, where, UP, index, z < 3)
                    send(at, where, DOWN, index, z > 0)
            elif step <= 5:
                for there, zz, way, on in from_line(step - 2):
                    for index, where in enumerate(
                        (place(zz, y, x), near(second, zz), near(third, zz), opposite(zz))
                    ):
                        arrive(at, where, there)
                        send(at, where, way, 4 * (step - 2) + index, on)

    for at in range(count):
        pass_on(at)
        if at:
            product_away(at - 1)
    product_away(count - 1)
    for time in range(count + 4):
        if time < count:
            add_pair(time)
        for step in range(4):
            if 0 <= time - step < count:
                line_step(time - step, step)
        if time >= 4:
            gather_step(time - 4, 0)
    for step in range(1, 9):
        for at in range(count):
            gather_step(at, step)

    for step in range(1, peers):
        peer = lax.rem(me + step, peers)
        for side in (core, 1 - core):
            arrived(vec_out.at[side * peers + peer], vec_recv.at[side * peers + peer])
    arrived(vec_out.at[(1 - core) * peers + me], vec_recv.at[(1 - core) * peers + me])
    own_vec.wait()
    for each in finish:
        each()


def weight_grads(products, lefts, rights, vector):
    count, peers = len(products), lax.axis_size("ctx")
    tokens = lefts[0].shape[0]
    dma = pltpu.SemaphoreType.DMA
    vmem = pltpu.VMEM
    halves = [left.shape[1] // 2 for left in lefts]
    helds = []
    for product, right in zip(products, rights):
        height, width = halves[product.left], right.shape[1] // 2
        helds.append((height, width // 2) if product.tall else (height // 2, width))
    lands = [vmem(shape, BF16) for shape in helds]
    return pl.pallas_call(
        functools.partial(weight_grad_kernel, products, len(lefts)),
        out_shape=[
            jax.ShapeDtypeStruct((halves[product.left], right.shape[1]), BF16)
            for product, right in zip(products, rights)
        ]
        + [jax.ShapeDtypeStruct((2 * peers,) + vector.shape, F32)],
        in_specs=[vmem_spec()] * (len(lefts) + count + 1),
        out_specs=[any_spec()] * count + [vmem_spec()],
        scratch_shapes=[vmem((4 * tokens, half), BF16) for half in halves]
        + [vmem((tokens, half), BF16) for half in halves]
        + [vmem((half, 4 * tokens), BF16) for half in halves]
        + [vmem((4 * tokens, right.shape[1] // 2), BF16) for right in rights]
        + lands * 5
        + [
            dma((len(lefts), 5)),
            dma((len(lefts), 4)),
            dma((count, 4)),
            dma((count, 3)),
            dma((count,)),
            dma((count,)),
            dma((count, 2, 4)),
            dma((count, 2, 4)),
            dma((count, 4, 16)),
            dma((count, peers)),
            dma((count,)),
            dma((2 * peers,)),
            dma((2 * peers,)),
        ],
        compiler_params=pltpu.CompilerParams(
            collective_id=5, has_side_effects=True, vmem_limit_bytes=52 * MIB
        ),
        name="weight_grads",
    )(*lefts, *rights, vector)


def on_device_by_heads(
    inputs,
    encoder,
    cotangent,
    block_order,
    bucket_of,
    self_gain,
    query_weight,
    key_weight,
    value_weight,
    out_weight,
    bias_table,
    cross_gain,
    cross_query,
    cross_key,
    cross_value,
    cross_out,
    mlp_gain,
    gate_weight,
    up_weight,
    down_weight,
):
    core, me = lax.axis_index("wsh"), lax.axis_index("ctx")

    def swap(values):
        return lax.ppermute(values, "wsh", [(0, 1), (1, 0)])

    def own_half(values):
        half = values.shape[-1] // 2
        return pick(core, values[..., half:], values[..., :half])

    def other_half(values):
        half = values.shape[-1] // 2
        return pick(core, values[..., :half], values[..., half:])

    def join(own, other, axis):
        return pick(
            core,
            jnp.concatenate([other, own], axis=axis),
            jnp.concatenate([own, other], axis=axis),
        )

    def times(values, pair):
        return plain_dot(own_half(values), pair[0]) + plain_dot(other_half(values), pair[1])

    def times_back(values, pair):
        return join(right_contract(values, pair[0]), right_contract(values, pair[1]), 1)

    def both_cores(values):
        return jnp.concatenate([own_half(values), swap(other_half(values))], axis=0)

    def both_whole(values):
        return jnp.concatenate([values, swap(values)], axis=0)

    small = jnp.concatenate([self_gain, cross_gain, mlp_gain, bias_table.reshape(-1)])
    small_other = swap(small)
    width = self_gain.shape[0]
    gain_one, gain_two, gain_three = (
        join(small[at * width : (at + 1) * width], small_other[at * width : (at + 1) * width], 0).astype(F32)
        for at in range(3)
    )
    bias_rows = join(bias_table, small_other[3 * width :].reshape(bias_table.shape), 0).astype(F32)
    query_pair, key_pair, value_pair = (
        (member, swap(member)) for member in (query_weight, key_weight, value_weight)
    )
    out_pair, cross_query_pair, cross_key_pair, cross_value_pair, cross_out_pair = (
        (member, swap(member))
        for member in (out_weight, cross_query, cross_key, cross_value, cross_out)
    )
    gate_pair, up_pair, down_pair = (
        (member, swap(member)) for member in (gate_weight, up_weight, down_weight)
    )

    resid_in = inputs[0].astype(F32)
    tokens = resid_in.shape[0]
    head_width = HEADS * HEAD_DIM
    length = bucket_of.shape[0]

    normed_one = rms_norm(resid_in, gain_one).astype(BF16)
    queries = times(normed_one, query_pair).astype(BF16)
    keys = times(normed_one, key_pair).astype(BF16)
    values = times(normed_one, value_pair).astype(BF16)
    landed, encoder_all = to_heads(queries, keys, values, encoder[0])
    encoder_all = encoder_all.reshape(-1, encoder.shape[2])

    own_column = jnp.sum(
        jnp.where(jnp.arange(HEADS)[None, :] == me, bias_rows, 0.0), axis=1, keepdims=True
    )
    in_bucket = bucket_of[None, :] == jnp.arange(BUCKETS, dtype=jnp.int32)[:, None]
    by_offset = jnp.sum(jnp.where(in_bucket, own_column, 0.0), axis=0).reshape(-1, TILE)
    before = jnp.concatenate([jnp.full((1, TILE), NEG_BIG, F32), by_offset[:-1]], axis=0)
    bias_lines = jnp.concatenate([by_offset, before], axis=1)

    mixed_packed, attn_sum, log_norm = attend(block_order, landed, bias_lines)
    attended = from_heads(mixed_packed)

    after_self = resid_in + times(attended, out_pair)
    normed_two = rms_norm(after_self, gain_two).astype(BF16)
    cross_q_heads = times(normed_two, cross_query_pair).astype(BF16).reshape(tokens, HEADS, HEAD_DIM)
    cross_k_heads = times(encoder_all, cross_key_pair).astype(BF16).reshape(-1, HEADS, HEAD_DIM)
    cross_v_heads = times(encoder_all, cross_value_pair).astype(BF16).reshape(-1, HEADS, HEAD_DIM)
    cross_logits = jnp.einsum(
        "qhe,khe->hqk", cross_q_heads, cross_k_heads, preferred_element_type=F32
    )
    cross_exact = jnp.exp(cross_logits - jax.nn.logsumexp(cross_logits, axis=-1, keepdims=True))
    cross_probs = cross_exact.astype(BF16)
    cross_mixed = (
        jnp.einsum("hqk,khe->qhe", cross_probs, cross_v_heads, preferred_element_type=F32)
        .reshape(tokens, head_width)
        .astype(BF16)
    )
    after_cross = after_self + times(cross_mixed, cross_out_pair)
    normed_three = rms_norm(after_cross, gain_three).astype(BF16)
    gate_act = times(normed_three, gate_pair)
    up_act = times(normed_three, up_pair)
    hidden_float, mlp_pull = jax.vjp(gelu_product, gate_act, up_act)
    hidden = hidden_float.astype(BF16)
    result = (after_cross + times(hidden, down_pair)).astype(BF16)

    resid_grad = cotangent[0].astype(F32)
    branch_three = cotangent[0]
    gate_grad, up_grad = mlp_pull(times_back(branch_three, down_pair))
    gate_grad, up_grad = gate_grad.astype(BF16), up_grad.astype(BF16)
    normed_three_grad = times_back(gate_grad, gate_pair) + times_back(up_grad, up_pair)
    part_grad, gain_three_grad = norm_back(after_cross, gain_three, normed_three_grad)
    after_cross_grad = resid_grad + part_grad
    branch_two = after_cross_grad.astype(BF16)
    mix_grad = times_back(branch_two, cross_out_pair).astype(BF16).reshape(tokens, HEADS, HEAD_DIM)
    cross_score_grad = jnp.einsum(
        "qhe,khe->hqk", mix_grad, cross_v_heads, preferred_element_type=F32
    )
    cross_delta = jnp.sum(cross_exact * cross_score_grad, axis=-1, keepdims=True)
    cross_dlogits = (cross_exact * (cross_score_grad - cross_delta)).astype(BF16)
    cross_q_grad = (
        jnp.einsum("hqk,khe->qhe", cross_dlogits, cross_k_heads, preferred_element_type=F32)
        .reshape(tokens, head_width)
        .astype(BF16)
    )
    cross_k_part = jnp.einsum(
        "hqk,qhe->khe", cross_dlogits, cross_q_heads, preferred_element_type=F32
    ).reshape(-1, head_width)
    cross_v_part = jnp.einsum(
        "hqk,qhe->khe", cross_probs, mix_grad, preferred_element_type=F32
    ).reshape(-1, head_width)
    cross_kv_part = jnp.concatenate([cross_k_part, cross_v_part], axis=1).astype(BF16)
    cross_kv_grad = lax.psum_scatter(cross_kv_part, "ctx", scatter_dimension=0, tiled=True)
    cross_kv_all = lax.all_gather(cross_kv_grad, "ctx", axis=0, tiled=True)
    encoder_grad = (
        times_back(cross_kv_grad[:, :head_width], cross_key_pair)
        + times_back(cross_kv_grad[:, head_width:], cross_value_pair)
    ).astype(BF16)
    cross_kv_w_grad = left_contract(both_cores(encoder_all), both_whole(cross_kv_all))
    normed_two_grad = times_back(cross_q_grad, cross_query_pair)
    part_grad, gain_two_grad = norm_back(after_self, gain_two, normed_two_grad)
    after_self_grad = after_cross_grad + part_grad
    branch_one = after_self_grad.astype(BF16)
    grad_landed = rows_to_heads(times_back(branch_one, out_pair).astype(BF16))
    packed_grads, offset_lines = attend_back(
        block_order, landed, grad_landed, attn_sum, log_norm, bias_lines
    )
    query_grad, key_grad, value_grad = grads_from_heads(packed_grads)

    offset_sums = offset_lines[:, :TILE] + jnp.concatenate(
        [offset_lines[1:, TILE:], jnp.zeros((1, TILE), F32)], axis=0
    )
    table_column = jnp.sum(jnp.where(in_bucket, offset_sums.reshape(1, length), 0.0), axis=1)
    table_grad = jnp.where(jnp.arange(HEADS)[None, :] == me, table_column[:, None], 0.0)

    normed_one_grad = (
        times_back(query_grad, query_pair)
        + times_back(key_grad, key_pair)
        + times_back(value_grad, value_pair)
    )
    part_grad, gain_one_grad = norm_back(resid_in, gain_one, normed_one_grad)
    input_grad = (after_self_grad + part_grad).astype(BF16)

    vector = jnp.concatenate(
        [
            gain_one_grad,
            gain_two_grad,
            gain_three_grad,
            table_grad.reshape(-1),
            jnp.zeros((512,), F32),
        ]
    ).reshape(8, 512)
    z_then_yx, z_then_xy, z_last = (
        (True, ACROSS_Y, ACROSS_X),
        (True, ACROSS_X, ACROSS_Y),
        (False, ACROSS_Y, ACROSS_X),
    )
    lefts = (normed_three, hidden, cross_mixed, normed_two, attended, normed_one)
    products = (
        Product(0, gate_grad, BIT_Y, False, z_then_yx),
        Product(1, branch_three, BIT_X, True, z_then_yx),
        Product(0, up_grad, BIT_Y, False, z_then_xy),
        Product(5, query_grad, BIT_X, False, z_then_xy),
        Product(2, branch_two, BIT_Y, False, z_last),
        Product(5, key_grad, BIT_X, False, z_then_xy),
        Product(3, cross_q_grad, BIT_Y, False, z_last),
        Product(5, value_grad, BIT_X, False, z_then_xy),
        Product(4, branch_one, BIT_Y, False, z_last),
    )
    *wholes, vectors = weight_grads(
        products, lefts, [product.right for product in products], vector
    )
    (
        sum_gate,
        sum_down,
        sum_up,
        sum_query,
        sum_cross_out,
        sum_key,
        sum_cross_query,
        sum_value,
        sum_out,
    ) = (member.astype(F32) for member in wholes)
    totals = jnp.sum(vectors, axis=0)
    sum_gain_one, sum_gain_two, sum_gain_three = (
        own_half(totals[2 * at : 2 * at + 2].reshape(1, -1))[0] for at in range(3)
    )
    sum_table = own_half(totals[6:7])[0].reshape(BUCKETS // 2, HEADS)
    return (
        result[None],
        input_grad[None],
        encoder_grad[None],
        sum_gain_one,
        sum_query,
        sum_key,
        sum_value,
        sum_out,
        sum_table,
        sum_gain_two,
        sum_cross_query,
        cross_kv_w_grad[:, :head_width],
        cross_kv_w_grad[:, head_width:],
        sum_cross_out,
        sum_gain_three,
        sum_gate,
        sum_up,
        sum_down,
    )


def solution(mesh):
    by_heads = mesh.shape["ctx"] == HEADS and mesh.shape["wsh"] == 2
    return jax.shard_map(
        on_device_by_heads if by_heads else on_device,
        mesh=mesh,
        in_specs=(
            P("wsh", "ctx", None),
            P("wsh", "ctx", None),
            P("wsh", "ctx", None),
            P(),
            P(),
            P("wsh"),
            P("wsh", None),
            P("wsh", None),
            P("wsh", None),
            P("wsh", None),
            P("wsh", None),
            P("wsh"),
            P("wsh", None),
            P("wsh", None),
            P("wsh", None),
            P("wsh", None),
            P("wsh"),
            P("wsh", None),
            P("wsh", None),
            P("wsh", None),
        ),
        out_specs=(
            P("wsh", "ctx", None),
            P("wsh", "ctx", None),
            P("wsh", "ctx", None),
            P("wsh"),
            P("wsh", None),
            P("wsh", None),
            P("wsh", None),
            P("wsh", None),
            P("wsh", None),
            P("wsh"),
            P("wsh", None),
            P("wsh", None),
            P("wsh", None),
            P("wsh", None),
            P("wsh"),
            P("wsh", None),
            P("wsh", None),
            P("wsh", None),
        ),
        check_vma=False,
    )
```

```python
import functools

import jax
import jax.numpy as jnp
from jax import lax
from jax.experimental import pallas as pl
from jax.experimental.pallas import tpu as pltpu
from jax.sharding import PartitionSpec as P

HEADS = 16
HEAD_DIM = 64
BUCKETS = 32


EPSILON = 1e-06
NEG_BIG = -1e30


def rms_norm(values, gain):
    return values * lax.rsqrt(jnp.mean(values * values, axis=-1, keepdims=True) + EPSILON) * gain


def plain_dot(left, right):
    return jnp.dot(left, right, preferred_element_type=jnp.float32)


def left_contract(left, right):
    return lax.dot_general(
        left, right, (((0,), (0,)), ((), ())), preferred_element_type=jnp.float32
    )


def right_contract(left, right):
    return lax.dot_general(
        left, right, (((1,), (1,)), ((), ())), preferred_element_type=jnp.float32
    )


def gelu_product(gate_vals, up_vals):
    return jax.nn.gelu(gate_vals, approximate=True) * up_vals


def norm_back(values, gain, cotan):
    normed, pullback = jax.vjp(rms_norm, values, gain)
    return pullback(cotan)


def lookup_positions(block_order, first_row, row_count, block_len):
    token_ids = first_row + jnp.arange(row_count, dtype=jnp.int32)
    block_ids = token_ids // block_len
    matches = block_ids[:, None] == jnp.arange(block_order.shape[0], dtype=jnp.int32)[None, :]
    starts = jnp.sum(jnp.where(matches, block_order[None, :], 0), axis=1)
    return starts * block_len + token_ids % block_len


def fold_groups(step_fn, carried, pieces, shard_rows):
    piece_rows = pieces[0].shape[0]
    shards = max(1, piece_rows // shard_rows)
    group_limit = max(1, 1152 // shard_rows)
    group_size = max(
        (divisor for divisor in range(1, min(shards, group_limit) + 1) if shards % divisor == 0)
    )
    group_rows = group_size * shard_rows

    def group_step(group_idx, inner_state):
        sub_pieces = tuple(
            (
                lax.dynamic_slice_in_dim(member, group_idx * group_rows, group_rows, 0)
                for member in pieces
            )
        )
        return step_fn(inner_state, sub_pieces, group_idx * group_rows)

    return lax.fori_loop(0, shards // group_size, group_step, carried)


def on_device(
    inputs,
    encoder,
    cotangent,
    block_order,
    bucket_of,
    self_gain,
    query_weight,
    key_weight,
    value_weight,
    out_weight,
    bias_table,
    cross_gain,
    cross_query,
    cross_key,
    cross_value,
    cross_out,
    mlp_gain,
    gate_weight,
    up_weight,
    down_weight,
):
    (
        gain_one,
        query_full,
        key_full,
        value_full,
        out_full,
        bias_rows,
        gain_two,
        cross_query_full,
        cross_key_full,
        cross_value_full,
        cross_out_full,
        gain_three,
        gate_full,
        up_full,
        down_full,
    ) = (
        lax.all_gather(self_gain, "wsh", axis=0, tiled=True),
        lax.all_gather(query_weight, "wsh", axis=0, tiled=True),
        lax.all_gather(key_weight, "wsh", axis=0, tiled=True),
        lax.all_gather(value_weight, "wsh", axis=0, tiled=True),
        lax.all_gather(out_weight, "wsh", axis=0, tiled=True),
        lax.all_gather(bias_table, "wsh", axis=0, tiled=True),
        lax.all_gather(cross_gain, "wsh", axis=0, tiled=True),
        lax.all_gather(cross_query, "wsh", axis=0, tiled=True),
        lax.all_gather(cross_key, "wsh", axis=0, tiled=True),
        lax.all_gather(cross_value, "wsh", axis=0, tiled=True),
        lax.all_gather(cross_out, "wsh", axis=0, tiled=True),
        lax.all_gather(mlp_gain, "wsh", axis=0, tiled=True),
        lax.all_gather(gate_weight, "wsh", axis=0, tiled=True),
        lax.all_gather(up_weight, "wsh", axis=0, tiled=True),
        lax.all_gather(down_weight, "wsh", axis=0, tiled=True),
    )
    gain_one = gain_one.astype(jnp.float32)
    gain_two = gain_two.astype(jnp.float32)
    gain_three = gain_three.astype(jnp.float32)
    resid_in = inputs[0].astype(jnp.float32)
    tokens = resid_in.shape[0]
    block_len = tokens // 2
    head_width = HEADS * HEAD_DIM
    total_rows = tokens * lax.axis_size("ctx")
    own_pos = lookup_positions(block_order, lax.axis_index("ctx") * tokens, tokens, block_len)
    bucket_ids = jnp.arange(BUCKETS, dtype=jnp.int32)
    boundaries = jnp.sum((bucket_of[None, :] < bucket_ids[1:, None]).astype(jnp.int32), axis=1)

    def bucket_indicator_of(clipped):
        bucket = jnp.sum((clipped[None] >= boundaries[:, None, None]).astype(jnp.int32), axis=0)
        return (bucket[None] == bucket_ids[:, None, None]).astype(jnp.bfloat16)

    def query_key_logits(query_heads, key_heads, query_pos, key_pos):
        logits = jnp.einsum(
            "qhe,khe->hqk", query_heads, key_heads, preferred_element_type=jnp.float32
        )
        offset = query_pos[:, None] - key_pos[None, :]
        clipped = jnp.maximum(offset, 0)
        indicator = bucket_indicator_of(clipped)
        rel_bias = jnp.einsum(
            "ouw,om->muw", indicator, bias_rows, preferred_element_type=jnp.float32
        )
        allowed = (offset >= 0)[None]
        return (jnp.where(allowed, logits + rel_bias, NEG_BIG), allowed, indicator)

    normed_one = rms_norm(resid_in, gain_one).astype(jnp.bfloat16)
    query_heads = (
        plain_dot(normed_one, query_full).astype(jnp.bfloat16).reshape(tokens, HEADS, HEAD_DIM)
    )
    key_heads = (
        plain_dot(normed_one, key_full).astype(jnp.bfloat16).reshape(tokens, HEADS, HEAD_DIM)
    )
    value_heads = (
        plain_dot(normed_one, value_full).astype(jnp.bfloat16).reshape(tokens, HEADS, HEAD_DIM)
    )

    def norm_step(carried, pieces, first_row):
        running_max, running_sum = carried
        key_pos = lookup_positions(block_order, first_row, pieces[0].shape[0], block_len)
        logits, allowed, indicator = query_key_logits(query_heads, pieces[0], own_pos, key_pos)
        new_max = jnp.maximum(running_max, jnp.max(logits, axis=-1))
        kept = jnp.where(allowed, jnp.exp(logits - new_max[..., None]), 0.0)
        return (new_max, running_sum * jnp.exp(running_max - new_max) + jnp.sum(kept, axis=-1))

    start_state = (
        jnp.full((HEADS, tokens), NEG_BIG, jnp.float32),
        jnp.zeros((HEADS, tokens), jnp.float32),
    )
    running_max, running_sum = fold_groups(
        norm_step, start_state, (lax.all_gather(key_heads, "ctx", axis=0, tiled=True),), tokens
    )
    log_norm = running_max + jnp.log(running_sum)

    def output_step(carried, pieces, first_row):
        key_pos = lookup_positions(block_order, first_row, pieces[0].shape[0], block_len)
        logits, allowed, indicator = query_key_logits(query_heads, pieces[0], own_pos, key_pos)
        attn_probs = jnp.exp(logits - log_norm[..., None]).astype(jnp.bfloat16)
        return carried + jnp.einsum(
            "hqk,khe->qhe", attn_probs, pieces[1], preferred_element_type=jnp.float32
        )

    zero_heads = jnp.zeros((tokens, HEADS, HEAD_DIM), jnp.float32)
    attn_sum = fold_groups(
        output_step,
        zero_heads,
        (
            lax.all_gather(key_heads, "ctx", axis=0, tiled=True),
            lax.all_gather(value_heads, "ctx", axis=0, tiled=True),
        ),
        tokens,
    )
    attended = attn_sum.reshape(tokens, head_width).astype(jnp.bfloat16)
    after_self = resid_in + plain_dot(attended, out_full)
    normed_two = rms_norm(after_self, gain_two).astype(jnp.bfloat16)
    cross_q_heads = (
        plain_dot(normed_two, cross_query_full)
        .astype(jnp.bfloat16)
        .reshape(tokens, HEADS, HEAD_DIM)
    )
    encoder_rows = encoder[0]
    encoder_key_rows, cross_values = (
        lax.all_gather(
            plain_dot(encoder_rows, cross_key_full).astype(jnp.bfloat16), "ctx", axis=0, tiled=True
        ),
        lax.all_gather(
            plain_dot(encoder_rows, cross_value_full).astype(jnp.bfloat16),
            "ctx",
            axis=0,
            tiled=True,
        ),
    )
    cross_k_heads = encoder_key_rows.reshape(encoder_key_rows.shape[0], HEADS, HEAD_DIM)
    cross_v_heads = cross_values.reshape(cross_values.shape[0], HEADS, HEAD_DIM)
    cross_logits = jnp.einsum(
        "qhe,khe->hqk", cross_q_heads, cross_k_heads, preferred_element_type=jnp.float32
    )
    cross_exact = jnp.exp(cross_logits - jax.nn.logsumexp(cross_logits, axis=-1, keepdims=True))
    cross_probs = cross_exact.astype(jnp.bfloat16)
    cross_mixed = (
        jnp.einsum("hqk,khe->qhe", cross_probs, cross_v_heads, preferred_element_type=jnp.float32)
        .reshape(tokens, head_width)
        .astype(jnp.bfloat16)
    )
    after_cross = after_self + plain_dot(cross_mixed, cross_out_full)
    normed_three = rms_norm(after_cross, gain_three).astype(jnp.bfloat16)
    gate_act = plain_dot(normed_three, gate_full)
    up_act = plain_dot(normed_three, up_full)
    hidden_float, mlp_pull = jax.vjp(gelu_product, gate_act, up_act)
    hidden = hidden_float.astype(jnp.bfloat16)
    result = after_cross + plain_dot(hidden, down_full)
    resid_grad = cotangent[0].astype(jnp.float32)
    branch_three = resid_grad.astype(jnp.bfloat16)
    down_grad = left_contract(hidden, branch_three)
    hidden_state_gradient = right_contract(branch_three, down_full)
    gate_grad, up_grad = mlp_pull(hidden_state_gradient)
    gate_grad = gate_grad.astype(jnp.bfloat16)
    up_grad = up_grad.astype(jnp.bfloat16)
    gate_w_grad = left_contract(normed_three, gate_grad)
    up_w_grad = left_contract(normed_three, up_grad)
    normed_three_grad = right_contract(gate_grad, gate_full) + right_contract(up_grad, up_full)
    part_grad, gain_three_grad = norm_back(after_cross, gain_three, normed_three_grad)
    after_cross_grad = resid_grad + part_grad
    branch_two = after_cross_grad.astype(jnp.bfloat16)
    cross_out_grad = left_contract(cross_mixed, branch_two)
    mix_grad = (
        right_contract(branch_two, cross_out_full)
        .astype(jnp.bfloat16)
        .reshape(tokens, HEADS, HEAD_DIM)
    )
    cross_score_grad = jnp.einsum(
        "qhe,khe->hqk", mix_grad, cross_v_heads, preferred_element_type=jnp.float32
    )
    cross_delta = jnp.sum(cross_exact * cross_score_grad, axis=-1, keepdims=True)
    cross_dlogits = (cross_exact * (cross_score_grad - cross_delta)).astype(jnp.bfloat16)
    cross_q_grad = (
        jnp.einsum("hqk,khe->qhe", cross_dlogits, cross_k_heads, preferred_element_type=jnp.float32)
        .reshape(tokens, head_width)
        .astype(jnp.bfloat16)
    )
    cross_k_part = jnp.einsum(
        "hqk,qhe->khe", cross_dlogits, cross_q_heads, preferred_element_type=jnp.float32
    ).reshape(-1, head_width)
    cross_v_part = jnp.einsum(
        "hqk,qhe->khe", cross_probs, mix_grad, preferred_element_type=jnp.float32
    ).reshape(-1, head_width)
    cross_k_grad, cross_v_grad = (
        lax.psum_scatter(cross_k_part, "ctx", scatter_dimension=0, tiled=True),
        lax.psum_scatter(cross_v_part, "ctx", scatter_dimension=0, tiled=True),
    )
    cross_k_grad = cross_k_grad.astype(jnp.bfloat16)
    cross_v_grad = cross_v_grad.astype(jnp.bfloat16)
    cross_query_grad = left_contract(normed_two, cross_q_grad)
    cross_key_grad = left_contract(encoder_rows, cross_k_grad)
    cross_value_grad = left_contract(encoder_rows, cross_v_grad)
    encoder_grad = (
        right_contract(cross_k_grad, cross_key_full)
        + right_contract(cross_v_grad, cross_value_full)
    ).astype(jnp.bfloat16)
    normed_two_grad = right_contract(cross_q_grad, cross_query_full)
    part_grad, gain_two_grad = norm_back(after_self, gain_two, normed_two_grad)
    after_self_grad = after_cross_grad + part_grad
    branch_one = after_self_grad.astype(jnp.bfloat16)
    out_w_grad = left_contract(attended, branch_one)
    dattn_heads = (
        right_contract(branch_one, out_full).astype(jnp.bfloat16).reshape(tokens, HEADS, HEAD_DIM)
    )
    row_delta = jnp.einsum("qhe,qhe->hq", dattn_heads.astype(jnp.float32), attn_sum)

    def block_grads(
        query_side, grad_side, norm_side, delta_side, query_pos, key_side, value_side, key_pos
    ):
        logits, allowed, indicator = query_key_logits(query_side, key_side, query_pos, key_pos)
        exact = jnp.exp(logits - norm_side[..., None])
        score_grad = jnp.einsum(
            "qhe,khe->hqk", grad_side, value_side, preferred_element_type=jnp.float32
        )
        logits_gradient = (exact * (score_grad - delta_side[..., None])).astype(jnp.bfloat16)
        grad_query = jnp.einsum(
            "hqk,khe->qhe", logits_gradient, key_side, preferred_element_type=jnp.float32
        )
        grad_key = jnp.einsum(
            "hqk,qhe->khe", logits_gradient, query_side, preferred_element_type=jnp.float32
        )
        grad_value = jnp.einsum(
            "hqk,qhe->khe",
            exact.astype(jnp.bfloat16),
            grad_side,
            preferred_element_type=jnp.float32,
        )
        bucket_table_gradient = jnp.einsum(
            "ouw,muw->om", indicator, logits_gradient, preferred_element_type=jnp.float32
        )
        return (grad_query, grad_key, grad_value, bucket_table_gradient)

    zero_table = jnp.zeros((BUCKETS, HEADS), jnp.float32)
    full_zero = jnp.zeros((total_rows, HEADS, HEAD_DIM), jnp.float32)

    def key_grad_step(carried, pieces, first_row):
        query_total, table_total, key_total, value_total = carried
        key_pos = lookup_positions(block_order, first_row, pieces[0].shape[0], block_len)
        grad_query, grad_key, grad_value, bucket_table_gradient = block_grads(
            query_heads, dattn_heads, log_norm, row_delta, own_pos, pieces[0], pieces[1], key_pos
        )
        key_total = lax.dynamic_update_slice_in_dim(key_total, grad_key, first_row, 0)
        value_total = lax.dynamic_update_slice_in_dim(value_total, grad_value, first_row, 0)
        return (
            query_total + grad_query,
            table_total + bucket_table_gradient,
            key_total,
            value_total,
        )

    query_sum, table_grad, key_partial, value_partial = fold_groups(
        key_grad_step,
        (zero_heads, zero_table, full_zero, full_zero),
        (
            lax.all_gather(key_heads, "ctx", axis=0, tiled=True),
            lax.all_gather(value_heads, "ctx", axis=0, tiled=True),
        ),
        tokens,
    )
    key_sum, value_accumulated = (
        lax.psum_scatter(key_partial, "ctx", scatter_dimension=0, tiled=True),
        lax.psum_scatter(value_partial, "ctx", scatter_dimension=0, tiled=True),
    )
    query_grad = query_sum.reshape(tokens, head_width).astype(jnp.bfloat16)
    key_grad = key_sum.reshape(tokens, head_width).astype(jnp.bfloat16)
    value_grad = value_accumulated.reshape(tokens, head_width).astype(jnp.bfloat16)
    query_w_grad = left_contract(normed_one, query_grad)
    key_w_grad = left_contract(normed_one, key_grad)
    value_w_grad = left_contract(normed_one, value_grad)
    normed_one_grad = (
        right_contract(query_grad, query_full)
        + right_contract(key_grad, key_full)
        + right_contract(value_grad, value_full)
    )
    part_grad, gain_one_grad = norm_back(resid_in, gain_one, normed_one_grad)
    input_grad = (after_self_grad + part_grad).astype(jnp.bfloat16)
    (
        sum_gain_one,
        sum_query,
        sum_key,
        sum_value,
        sum_out,
        sum_table,
        sum_gain_two,
        sum_cross_query,
        sum_cross_key,
        sum_cross_value,
        sum_cross_out,
        sum_gain_three,
        sum_gate,
        sum_up,
        sum_down,
    ) = (
        lax.psum_scatter(
            gain_one_grad.astype(jnp.bfloat16), "wsh", scatter_dimension=0, tiled=True
        ).astype(jnp.float32),
        lax.psum_scatter(
            query_w_grad.astype(jnp.bfloat16), "wsh", scatter_dimension=0, tiled=True
        ).astype(jnp.float32),
        lax.psum_scatter(
            key_w_grad.astype(jnp.bfloat16), "wsh", scatter_dimension=0, tiled=True
        ).astype(jnp.float32),
        lax.psum_scatter(
            value_w_grad.astype(jnp.bfloat16), "wsh", scatter_dimension=0, tiled=True
        ).astype(jnp.float32),
        lax.psum_scatter(
            out_w_grad.astype(jnp.bfloat16), "wsh", scatter_dimension=0, tiled=True
        ).astype(jnp.float32),
        lax.psum_scatter(
            table_grad.astype(jnp.bfloat16), "wsh", scatter_dimension=0, tiled=True
        ).astype(jnp.float32),
        lax.psum_scatter(
            gain_two_grad.astype(jnp.bfloat16), "wsh", scatter_dimension=0, tiled=True
        ).astype(jnp.float32),
        lax.psum_scatter(
            cross_query_grad.astype(jnp.bfloat16), "wsh", scatter_dimension=0, tiled=True
        ).astype(jnp.float32),
        lax.psum_scatter(
            cross_key_grad.astype(jnp.bfloat16), "wsh", scatter_dimension=0, tiled=True
        ).astype(jnp.float32),
        lax.psum_scatter(
            cross_value_grad.astype(jnp.bfloat16), "wsh", scatter_dimension=0, tiled=True
        ).astype(jnp.float32),
        lax.psum_scatter(
            cross_out_grad.astype(jnp.bfloat16), "wsh", scatter_dimension=0, tiled=True
        ).astype(jnp.float32),
        lax.psum_scatter(
            gain_three_grad.astype(jnp.bfloat16), "wsh", scatter_dimension=0, tiled=True
        ).astype(jnp.float32),
        lax.psum_scatter(
            gate_w_grad.astype(jnp.bfloat16), "wsh", scatter_dimension=0, tiled=True
        ).astype(jnp.float32),
        lax.psum_scatter(
            up_w_grad.astype(jnp.bfloat16), "wsh", scatter_dimension=0, tiled=True
        ).astype(jnp.float32),
        lax.psum_scatter(
            down_grad.astype(jnp.bfloat16), "wsh", scatter_dimension=0, tiled=True
        ).astype(jnp.float32),
    )
    total_grads = lax.psum(
        (
            sum_gain_one,
            sum_query,
            sum_key,
            sum_value,
            sum_out,
            sum_table,
            sum_gain_two,
            sum_cross_query,
            sum_cross_key,
            sum_cross_value,
            sum_cross_out,
            sum_gain_three,
            sum_gate,
            sum_up,
            sum_down,
        ),
        "ctx",
    )
    return (result.astype(jnp.bfloat16)[None], input_grad[None], encoder_grad[None]) + tuple(
        total_grads
    )


F32 = jnp.float32
BF16 = jnp.bfloat16
MESH = pl.DeviceIdType.MESH
TILE = 256
BLOCK = 64
MIB = 2**20


def dot_nt(left, right):
    return lax.dot_general(left, right, (((1,), (1,)), ((), ())), preferred_element_type=F32)


def vmem_spec():
    return pl.BlockSpec(memory_space=pltpu.VMEM)


def any_spec():
    return pl.BlockSpec(memory_space=pl.ANY)


def greet_all(peers):
    me, core = lax.axis_index("ctx"), lax.axis_index("wsh")
    barrier = pltpu.get_barrier_semaphore()
    for step in range(1, peers):
        pl.semaphore_signal(
            barrier, inc=1, device_id=(lax.rem(me + step, peers), core), device_id_type=MESH
        )
    pl.semaphore_wait(barrier, peers - 1)


def exchange_all(packed, landed, send_sem, recv_sem, own_sem):
    peers = packed.shape[0]
    me, core = lax.axis_index("ctx"), lax.axis_index("wsh")

    def copy(step):
        peer = lax.rem(me + step, peers)
        return pltpu.make_async_remote_copy(
            src_ref=packed.at[peer],
            dst_ref=landed.at[me],
            send_sem=send_sem.at[step],
            recv_sem=recv_sem.at[step],
            device_id=(peer, core),
            device_id_type=MESH,
        )

    copies = [copy(step) for step in range(1, peers)]
    for each in copies:
        each.start()
    own = pltpu.make_async_copy(packed.at[me], landed.at[me], own_sem)
    own.start()
    own.wait()
    for each in copies:
        each.wait()


def exchange_scratch(peers):
    return [
        pltpu.SemaphoreType.DMA((peers,)),
        pltpu.SemaphoreType.DMA((peers,)),
        pltpu.SemaphoreType.DMA,
    ]


def to_heads_kernel(q_ref, k_ref, v_ref, rows_ref, landed, rows_out, packed, rows_send, rows_recv, rows_own, *sems):
    peers = packed.shape[0]
    me, core = lax.axis_index("ctx"), lax.axis_index("wsh")
    greet_all(peers)
    copies = []
    for step in range(1, peers):
        copies.append(
            pltpu.make_async_remote_copy(
                src_ref=rows_ref,
                dst_ref=rows_out.at[me],
                send_sem=rows_send.at[step],
                recv_sem=rows_recv.at[step],
                device_id=(lax.rem(me + step, peers), core),
                device_id_type=MESH,
            )
        )
    copies.append(pltpu.make_async_copy(rows_ref, rows_out.at[me], rows_own))
    for head in range(peers):
        cols = slice(head * HEAD_DIM, (head + 1) * HEAD_DIM)
        packed[head, : 2 * BLOCK, :] = jnp.concatenate([q_ref[:, cols], k_ref[:, cols]], axis=1)
        packed[head, 2 * BLOCK :, :] = jnp.concatenate(
            [v_ref[:BLOCK, cols], v_ref[BLOCK:, cols]], axis=1
        )
    for each in copies:
        each.start()
    exchange_all(packed, landed, *sems)
    for each in copies:
        each.wait()


def to_heads(queries, keys, values, rows):
    shape = (HEADS, 3 * BLOCK, 2 * HEAD_DIM)
    return pl.pallas_call(
        to_heads_kernel,
        out_shape=[
            jax.ShapeDtypeStruct(shape, BF16),
            jax.ShapeDtypeStruct((HEADS,) + rows.shape, BF16),
        ],
        in_specs=[vmem_spec()] * 4,
        out_specs=[vmem_spec()] * 2,
        scratch_shapes=[pltpu.VMEM(shape, BF16)] + exchange_scratch(HEADS) * 2,
        compiler_params=pltpu.CompilerParams(
            collective_id=1, has_side_effects=True, vmem_limit_bytes=16 * MIB
        ),
        name="to_heads",
    )(queries, keys, values, rows)


def unpack_pair(landed, pair, rows):
    left, right = landed[2 * pair, rows, :], landed[2 * pair + 1, rows, :]
    return (
        jnp.concatenate([left[:, :HEAD_DIM], right[:, :HEAD_DIM]], axis=1),
        jnp.concatenate([left[:, HEAD_DIM:], right[:, HEAD_DIM:]], axis=1),
    )


def from_heads_kernel(packed, out_ref, landed, *sems):
    peers = packed.shape[0]
    greet_all(peers)
    exchange_all(packed, landed, *sems)
    for pair in range(peers // 2):
        cols = slice(pair * 2 * HEAD_DIM, (pair + 1) * 2 * HEAD_DIM)
        first, second = unpack_pair(landed, pair, slice(0, BLOCK))
        out_ref[:BLOCK, cols] = first
        out_ref[BLOCK:, cols] = second


def from_heads(packed):
    return pl.pallas_call(
        from_heads_kernel,
        out_shape=jax.ShapeDtypeStruct((2 * BLOCK, HEADS * HEAD_DIM), BF16),
        in_specs=[vmem_spec()],
        out_specs=vmem_spec(),
        scratch_shapes=[pltpu.VMEM(packed.shape, BF16)] + exchange_scratch(HEADS),
        compiler_params=pltpu.CompilerParams(
            collective_id=3, has_side_effects=True, vmem_limit_bytes=16 * MIB
        ),
        name="from_heads",
    )(packed)


def place_tiles(bias_lines, tiles):
    for apart in range(tiles.shape[0]):
        line = jnp.broadcast_to(bias_lines[apart : apart + 1, :], (TILE, 2 * TILE))
        tiles[apart] = pltpu.roll(line, 0, 1, stride=1, stride_axis=0)[:, :TILE]


def attend_kernel(order, landed, bias_lines, out_ref, sum_ref, norm_ref, q_s, k_s, vt_s, tiles, ot_s, o_s):
    blocks = order.shape[0]
    spans = blocks * BLOCK // TILE
    for stored in range(blocks):
        device, half = stored // 2, stored % 2
        at = pl.ds(pl.multiple_of(order[stored] * BLOCK, BLOCK), BLOCK)
        pair = landed[device, half * BLOCK : (half + 1) * BLOCK, :]
        q_s[at, :] = pair[:, :HEAD_DIM]
        k_s[at, :] = pair[:, HEAD_DIM:]
        values = landed[device, 2 * BLOCK :, half * HEAD_DIM : (half + 1) * HEAD_DIM]
        o_s[at, :] = values.astype(F32)
    vt_s[...] = jnp.transpose(o_s[...], (1, 0)).astype(BF16)
    place_tiles(bias_lines, tiles)
    for i in range(spans):
        at_i = slice(i * TILE, (i + 1) * TILE)
        queries = q_s[at_i, :]
        scores = [
            dot_nt(k_s[j * TILE : (j + 1) * TILE, :], queries) + tiles[i - j] for j in range(i + 1)
        ]
        top = functools.reduce(
            jnp.maximum, [jnp.max(each, axis=0, keepdims=True) for each in scores]
        )
        total = jnp.zeros((1, TILE), F32)
        mixed = jnp.zeros((HEAD_DIM, TILE), F32)
        for j in range(i + 1):
            weights = jnp.exp(scores[j] - top)
            total = total + jnp.sum(weights, axis=0, keepdims=True)
            mixed = mixed + plain_dot(
                vt_s[:, j * TILE : (j + 1) * TILE], weights.astype(BF16)
            )
        norm_ref[0:1, at_i] = top + jnp.log(total)
        ot_s[:, at_i] = mixed / total
    sum_ref[...] = ot_s[...]
    o_s[...] = jnp.transpose(ot_s[...], (1, 0))
    for stored in range(blocks):
        device, half = stored // 2, stored % 2
        at = pl.ds(pl.multiple_of(order[stored] * BLOCK, BLOCK), BLOCK)
        out_ref[device, :, half * HEAD_DIM : (half + 1) * HEAD_DIM] = o_s[at, :].astype(BF16)


def attend(order, landed, bias_lines):
    blocks = order.shape[0]
    length = blocks * BLOCK
    vmem = pltpu.VMEM
    return pl.pallas_call(
        attend_kernel,
        grid_spec=pltpu.PrefetchScalarGridSpec(
            num_scalar_prefetch=1,
            grid=(),
            in_specs=[vmem_spec()] * 2,
            out_specs=[vmem_spec()] * 3,
            scratch_shapes=[
                vmem((length, HEAD_DIM), BF16),
                vmem((length, HEAD_DIM), BF16),
                vmem((HEAD_DIM, length), BF16),
                vmem((length // TILE, TILE, TILE), F32),
                vmem((HEAD_DIM, length), F32),
                vmem((length, HEAD_DIM), F32),
            ],
        ),
        out_shape=[
            jax.ShapeDtypeStruct((blocks // 2, BLOCK, 2 * HEAD_DIM), BF16),
            jax.ShapeDtypeStruct((HEAD_DIM, length), F32),
            jax.ShapeDtypeStruct((1, length), F32),
        ],
        compiler_params=pltpu.CompilerParams(vmem_limit_bytes=32 * MIB),
        cost_estimate=pl.CostEstimate(
            flops=4 * length * length * HEAD_DIM, bytes_accessed=4 * MIB, transcendentals=length * length // 2
        ),
        name="attend",
    )(order, landed, bias_lines)


def attend_back(
    order, held_at, landed, grad_landed, sums, norm, bias_lines, out_ref, lines_ref,
    q_s, k_s, v_s, do_s, kt_s, tiles, by_offset, dq_s, dk_s, dv_s, delta_s, dqt_s,
):
    blocks = order.shape[0]
    spans = blocks * BLOCK // TILE
    def stored_rows(stored):
        return slice(stored * BLOCK, (stored + 1) * BLOCK), stored // 2, slice(
            stored % 2 * HEAD_DIM, (stored % 2 + 1) * HEAD_DIM
        )

    def in_order(into, staged):
        for block in range(blocks):
            at = slice(block * BLOCK, (block + 1) * BLOCK)
            into[at, :] = staged[pl.ds(held_at[block] * BLOCK, BLOCK), :].astype(BF16)

    for stored in range(blocks):
        at, device, cols = stored_rows(stored)
        pair = landed[device, stored % 2 * BLOCK : (stored % 2 + 1) * BLOCK, :].astype(F32)
        dq_s[at, :] = pair[:, :HEAD_DIM]
        dk_s[at, :] = pair[:, HEAD_DIM:]
        dv_s[at, :] = landed[device, 2 * BLOCK :, cols].astype(F32)
    in_order(q_s, dq_s)
    in_order(k_s, dk_s)
    in_order(v_s, dv_s)
    for stored in range(blocks):
        at, device, cols = stored_rows(stored)
        dq_s[at, :] = grad_landed[device, :, cols].astype(F32)
    in_order(do_s, dq_s)
    place_tiles(bias_lines, tiles)
    kt_s[...] = jnp.transpose(k_s[...].astype(F32), (1, 0)).astype(BF16)
    grad_t = jnp.transpose(do_s[...].astype(F32), (1, 0))
    delta_s[...] = jnp.sum(grad_t * sums[...], axis=0, keepdims=True)
    by_offset[...] = jnp.zeros_like(by_offset)
    dk_s[...] = jnp.zeros_like(dk_s)
    dv_s[...] = jnp.zeros_like(dv_s)
    for i in range(spans):
        at_i = slice(i * TILE, (i + 1) * TILE)
        queries, grads = q_s[at_i, :], do_s[at_i, :]
        norm_i, delta_i = norm[0:1, at_i], delta_s[0:1, at_i]
        dqt = jnp.zeros((HEAD_DIM, TILE), F32)
        for j in range(i + 1):
            at_j = slice(j * TILE, (j + 1) * TILE)
            exact = jnp.exp(dot_nt(k_s[at_j, :], queries) + tiles[i - j] - norm_i)
            dscore = exact * (dot_nt(v_s[at_j, :], grads) - delta_i)
            by_offset[i - j] += dscore
            rounded = dscore.astype(BF16)
            dv_s[at_j, :] += plain_dot(exact.astype(BF16), grads)
            dk_s[at_j, :] += plain_dot(rounded, queries)
            dqt = dqt + plain_dot(kt_s[:, at_j], rounded)
        dqt_s[:, at_i] = dqt
    dq_s[...] = jnp.transpose(dqt_s[...], (1, 0))
    for stored in range(blocks):
        device, half = stored // 2, stored % 2
        at = pl.ds(order[stored] * BLOCK, BLOCK)
        rows = slice(half * BLOCK, (half + 1) * BLOCK)
        cols = slice(half * HEAD_DIM, (half + 1) * HEAD_DIM)
        out_ref[device, rows, :HEAD_DIM] = dq_s[at, :].astype(BF16)
        out_ref[device, rows, HEAD_DIM:] = dk_s[at, :].astype(BF16)
        out_ref[device, 2 * BLOCK :, cols] = dv_s[at, :].astype(BF16)
    for apart in range(spans):
        folded = jnp.zeros((8, 2 * TILE), F32)
        for group in range(TILE // 8):
            rows = by_offset[apart, 8 * group : 8 * group + 8, :]
            wide = jnp.concatenate([rows, jnp.zeros((8, TILE), F32)], axis=1)
            folded = folded + (pltpu.roll(wide, 2 * TILE - 8 * group, 1) if group else wide)
        line = folded[0:1]
        for row in range(1, 8):
            line = line + pltpu.roll(folded[row : row + 1], 2 * TILE - row, 1)
        lines_ref[apart : apart + 1, :] = line


BIT_X, BIT_Y = 0, 1
FAR_LEFTS, FAR_RIGHTS = 2, 3


def pick(flag, when_set, when_clear):
    return jnp.where(flag == 1, when_set, when_clear)


UP, DOWN, ACROSS_Y, ACROSS_X = 0, 1, 2, 3


class Product:
    def __init__(self, left, right, first, tall, route):
        self.left, self.right, self.first, self.tall, self.route = left, right, first, tall, route


SUMMED = -1


def weight_grad_kernel(products, left_count, *refs):
    count = len(products)
    refs = list(refs)

    def take(number):
        taken = refs[:number]
        del refs[:number]
        return taken

    lefts, rights = take(left_count), take(count - 3)
    left_far, right_far = take(FAR_LEFTS), take(FAR_RIGHTS)
    (
        order,
        held_at,
        grad_rows,
        landed,
        attn_sum,
        log_norm,
        bias_lines,
        in_bucket,
        resid_in,
        gain_one,
        resid_grad,
        gains,
    ) = take(12)
    weights = take(10)
    wholes, (vec_out, input_grad, encoder_grad, kv_both) = take(count - 1), take(4)
    kv_at = [product.left for product in products].index(SUMMED)
    wholes.insert(kv_at, kv_both.at[0])
    left_all, left_pass, left_t = take(left_count), take(left_count), take(left_count)
    right_all, away, came, held, line_in = (take(count) for _ in range(5))
    rights += take(3)
    grad_packed, grad_landed, back_packed, back_landed, lines = take(5)
    attention_scratch = take(12)
    vec_in, vec_sums, vec_landed, weight_buffer, normed_grad = take(5)
    (
        left_send,
        left_recv,
        right_send,
        right_recv,
        pair_send,
        pair_recv,
        line_send,
        line_recv,
        out_send,
        out_recv,
        own_sem,
        vec_send,
        vec_recv,
        all_send,
        all_recv,
        all_own,
        weight_sem,
    ) = refs
    me, core = lax.axis_index("ctx"), lax.axis_index("wsh")
    peers = lax.axis_size("ctx")
    tokens = lefts[0].shape[0]
    x, y, z = lax.rem(me, 2), lax.rem(me // 2, 2), me // 4

    barrier = pltpu.get_barrier_semaphore()
    for step in range(1, peers):
        for side in (core, 1 - core):
            pl.semaphore_signal(
                barrier, inc=1, device_id=(lax.rem(me + step, peers), side), device_id_type=MESH
            )
    pl.semaphore_signal(barrier, inc=1, device_id=(me, 1 - core), device_id_type=MESH)
    for head in range(peers):
        cols = slice(head * HEAD_DIM, (head + 1) * HEAD_DIM)
        grad_packed[head] = jnp.concatenate(
            [grad_rows[:BLOCK, cols], grad_rows[BLOCK:, cols]], axis=1
        )
    pl.semaphore_wait(barrier, 2 * peers - 1)

    def place(zz, yy, xx):
        return zz * 4 + yy * 2 + xx

    targets = {
        UP: place(lax.rem(z + 1, 4), y, x),
        DOWN: place(lax.rem(z + 3, 4), y, x),
        ACROSS_Y: place(z, 1 - y, x),
        ACROSS_X: place(z, y, 1 - x),
    }
    finish = []

    def remote(src, dst, send_sem, recv_sem, ctx, side):
        return pltpu.make_async_remote_copy(
            src_ref=src,
            dst_ref=dst,
            send_sem=send_sem,
            recv_sem=recv_sem,
            device_id=(ctx, side),
            device_id_type=MESH,
        )

    def launch(copy, only=None):
        if only is None:
            copy.start()
            finish.append(copy.wait_send)
        else:
            pl.when(only)(copy.start)
            finish.append(lambda: pl.when(only)(copy.wait_send))

    def arrived(dst, recv_sem):
        remote(dst, dst, own_sem.at[0], recv_sem, me, 1 - core).wait_recv()

    def lanes(ref, at, width):
        return ref.at[:, pl.ds(pl.multiple_of(at * width, 128), width)]

    def rows(ref, at, height):
        return ref.at[pl.ds(pl.multiple_of(at * height, 16), height)]

    def slot(ref, index):
        return ref.at[pl.ds(index * tokens, tokens)]

    def axes(product):
        along_x, along_y = (x, ACROSS_X), (y, ACROSS_Y)
        return (along_x, along_y) if product.first == BIT_X else (along_y, along_x)

    left_axis = {product.left: product for product in products}
    far_rights = [at for at in range(count) if 0 <= products[at].left < FAR_LEFTS]

    def local(src, dst, sem):
        copy = pltpu.make_async_copy(src, dst, sem)
        copy.start()
        return copy

    def send_left(at):
        (_, way), _ = axes(left_axis[at])
        half = left_all[at].shape[1]
        copies = [local(lanes(lefts[at], core, half), slot(left_all[at], 0), left_send.at[at, 4])]
        launch(remote(lanes(lefts[at], 1 - core, half), slot(left_all[at], 2), left_send.at[at, 2], left_recv.at[at, 2], me, 1 - core))
        if at < FAR_LEFTS:
            copies.append(local(lanes(left_far[at], core, half), slot(left_all[at], 1), left_send.at[at, 5]))
            launch(remote(lanes(left_far[at], 1 - core, half), slot(left_all[at], 3), left_send.at[at, 3], left_recv.at[at, 3], me, 1 - core))
        else:
            launch(remote(lanes(lefts[at], core, half), slot(left_all[at], 1), left_send.at[at, 0], left_recv.at[at, 0], targets[way], core))
            launch(remote(lanes(lefts[at], 1 - core, half), left_pass[at], left_send.at[at, 1], left_recv.at[at, 1], targets[way], core))
        return copies

    def send_right(at):
        (mine, way), _ = axes(products[at])
        half = right_all[at].shape[1]
        if products[at].left == SUMMED:
            launch(remote(lanes(rights[at], 1 - mine, half), right_all[at], right_send.at[at, 0], right_recv.at[at, 0], targets[way], core))
            return []
        copies = [local(lanes(rights[at], mine, half), slot(right_all[at], 0), right_send.at[at, 3])]
        launch(remote(lanes(rights[at], mine, half), slot(right_all[at], 2), right_send.at[at, 1], right_recv.at[at, 1], me, 1 - core))
        if at in far_rights:
            far = right_far[far_rights.index(at)]
            copies.append(local(far, slot(right_all[at], 1), right_send.at[at, 4]))
            launch(remote(far, slot(right_all[at], 3), right_send.at[at, 2], right_recv.at[at, 2], me, 1 - core))
        else:
            launch(remote(lanes(rights[at], 1 - mine, half), slot(right_all[at], 1), right_send.at[at, 0], right_recv.at[at, 0], targets[way], core))
        return copies

    def to_all(which, source, target):
        copies = []
        for step in range(1, peers):
            peer = lax.rem(me + step, peers)
            copies.append(
                remote(source(peer), target(me), all_send.at[which, step], all_recv.at[which, step], peer, core)
            )
            launch(copies[-1])
        own = pltpu.make_async_copy(source(me), target(me), all_own.at[which])
        own.start()

        def wait():
            own.wait()
            for each in copies:
                each.wait_recv()

        return wait

    seen = set()
    owns = {}

    def send_operands(some):
        for at in some:
            left = products[at].left
            if left not in seen and left != SUMMED:
                seen.add(left)
                owns["left", left] = send_left(left)
            owns["right", at] = send_right(at)

    def vector_step(step):
        if step == 0:
            source, ctx, side = vec_in.at[1 - core], me, 1 - core
        else:
            source, ctx, side = vec_sums.at[step - 1], me ^ (1 << (step - 1)), core
        launch(remote(source, vec_landed.at[step], vec_send.at[step], vec_recv.at[step], ctx, side))

    def vector_add(step):
        arrived(vec_landed.at[step], vec_recv.at[step])
        total = (vec_sums[step - 1] if step else vec_in[core]) + vec_landed[step]
        if step < 4:
            vec_sums[step] = total
            vector_step(step + 1)
        else:
            vec_out[...] = total

    passed = set()

    def pass_on(at):
        left = products[at].left
        if left == SUMMED or at in far_rights:
            return
        if left not in passed:
            passed.add(left)
            arrived(slot(left_all[left], 1), left_recv.at[left, 0])
            arrived(left_pass[left], left_recv.at[left, 1])
            launch(remote(left_pass[left], slot(left_all[left], 3), left_send.at[left, 3], left_recv.at[left, 3], me, 1 - core))
        arrived(slot(right_all[at], 1), right_recv.at[at, 0])
        launch(remote(slot(right_all[at], 1), slot(right_all[at], 3), right_send.at[at, 2], right_recv.at[at, 2], me, 1 - core))

    def multiply(at, out, half):
        product = products[at]
        left, right = left_t[product.left], right_all[at]
        height, width = out.shape
        step = 256 if height <= 256 else 128 if height % 256 else 256
        if product.tall:
            columns = pl.ds(pl.multiple_of(half * width, 128), width)

            def strip(index, carry):
                band = pl.ds(pl.multiple_of(index * 176, 16), 176)
                out[band, :] = plain_dot(left[band, :], right[:, columns]).astype(BF16)
                return carry

            lax.fori_loop(0, height // 176, strip, 0)
        else:
            band = pl.ds(pl.multiple_of(half * height, 16), height)

            def strip(index, carry):
                columns = pl.ds(pl.multiple_of(index * 256, 128), 256)
                out[:, columns] = plain_dot(left[band, :], right[:, columns]).astype(BF16)
                return carry

            lax.fori_loop(0, width // 256, strip, 0)
            if width % 256:
                out[:, width - 128 :] = plain_dot(left[band, :], right[:, width - 128 :]).astype(BF16)

    turned = set()

    def product_away(at):
        left = products[at].left
        _, (mine, way) = axes(products[at])
        if left == SUMMED:
            (first_mine, _), _ = axes(products[at])
            arrived(right_all[at], right_recv.at[at, 0])
            height = held[at].shape[0]
            for out, half in ((away[at], 1 - mine), (held[at], mine)):
                own = lanes(rows(rights[at], half, height), first_mine, held[at].shape[1])
                out[...] = (own[...].astype(F32) + rows(right_all[at], half, height)[...].astype(F32)).astype(BF16)
            launch(remote(away[at], came[at], pair_send.at[at], pair_recv.at[at], targets[way], core))
            return
        if left not in turned:
            turned.add(left)
            arrived(slot(left_all[left], 2), left_recv.at[left, 2])
            arrived(slot(left_all[left], 3), left_recv.at[left, 3])
            for each in owns["left", left]:
                each.wait()
            height = left_t[left].shape[0]

            def turn(index, carry):
                band = pl.ds(pl.multiple_of(index * 128, 128), 128)
                left_t[left][band, :] = jnp.transpose(left_all[left][:, band], (1, 0))
                return carry

            lax.fori_loop(0, height // 128, turn, 0)
        arrived(slot(right_all[at], 2), right_recv.at[at, 1])
        arrived(slot(right_all[at], 3), right_recv.at[at, 2])
        for each in owns["right", at]:
            each.wait()
        multiply(at, away[at], 1 - mine)
        launch(remote(away[at], came[at], pair_send.at[at], pair_recv.at[at], targets[way], core))
        multiply(at, held[at], mine)

    def add(into, more):
        into[...] = (into[...].astype(F32) + more[...].astype(F32)).astype(BF16)

    def add_pair(at):
        arrived(came[at], pair_recv.at[at])
        add(held[at], came[at])

    def line_step(at, step):
        height = held[at].shape[0] // 4
        for side, behind, chunk, way in (
            (0, z, lax.rem(z + 3 - step, 4), UP),
            (1, 3 - z, lax.rem(z + step + 1, 4), DOWN),
        ):
            recv_sem = line_recv.at[at, side, chunk]
            landing = rows(line_in[at], chunk + 1 - side, height)

            def land(landing=landing, chunk=chunk, recv_sem=recv_sem):
                arrived(landing, recv_sem)
                add(rows(held[at], chunk, height), landing)

            pl.when(jnp.logical_and(behind > 0, behind <= step))(land)
            if step < 3:
                launch(
                    remote(
                        rows(held[at], chunk, height),
                        landing,
                        line_send.at[at, side, chunk],
                        recv_sem,
                        targets[way],
                        core,
                    ),
                    only=behind <= step,
                )

    def own_piece(at):
        return rows(held[at], z, held[at].shape[0] // 4)

    def window(at, where):
        product = products[at]
        height, width = held[at].shape
        height //= 4
        xx, yy, zz = lax.rem(where, 2), lax.rem(where // 2, 2), where // 4
        one, two = (xx, yy) if product.first == BIT_X else (yy, xx)
        row, column = (zz, one * 2 + two) if product.tall else (two * 4 + zz, one)
        return wholes[at].at[
            pl.ds(pl.multiple_of(row * height, 16), height),
            pl.ds(pl.multiple_of(column * width, 128), width),
        ]

    def send(at, where, way, index, only=None, own=False):
        launch(
            remote(
                own_piece(at) if own else window(at, where),
                window(at, where),
                out_send.at[at, way, index],
                out_recv.at[at, where],
                targets[way],
                core,
            ),
            only,
        )

    def arrive(at, where, only=None):
        def act():
            arrived(window(at, where), out_recv.at[at, where])

        if only is None:
            act()
        else:
            pl.when(only)(act)

    def near(way, zz):
        return place(zz, 1 - y, x) if way == ACROSS_Y else place(zz, y, 1 - x)

    def opposite(zz):
        return place(zz, 1 - y, 1 - x)

    def from_line(apart):
        return (
            (z >= apart, lax.rem(z + 4 - apart, 4), UP, jnp.logical_and(z >= apart, z < 3)),
            (z + apart <= 3, lax.rem(z + apart, 4), DOWN, jnp.logical_and(z + apart <= 3, z > 0)),
        )

    def gather_step(at, step):
        z_first, second, third = products[at].route
        if step == 0:
            owns["piece", at] = local(own_piece(at), window(at, me), own_sem.at[at])
            if at != kv_at:
                finish.append(owns["piece", at].wait)
            if not z_first:
                send(at, me, second, 0, own=True)
                send(at, me, third, 0, own=True)
            send(at, me, UP, 0, only=z < 3, own=True)
            send(at, me, DOWN, 0, only=z > 0, own=True)
            if z_first:
                send(at, me, second, 0, own=True)
                send(at, me, third, 0, own=True)
        elif z_first:
            if step <= 3:
                for side, (there, zz, way, on) in enumerate(from_line(step)):
                    where = place(zz, y, x)
                    arrive(at, where, there)
                    send(at, where, way, step, on)
                    send(at, where, second, 2 * step + side, there)
                    send(at, where, third, 2 * step + side, there)
            elif step <= 7:
                where = near(second, z ^ (step - 4))
                arrive(at, where)
                send(at, where, third, 4 + step)
            elif step == 8:
                for turn in range(4):
                    arrive(at, near(third, z ^ turn))
                    arrive(at, opposite(z ^ turn))
        else:
            if step == 1:
                where = near(second, z)
                arrive(at, where)
                send(at, where, third, 1)
                send(at, where, UP, 1, z < 3)
                send(at, where, DOWN, 1, z > 0)
            elif step == 2:
                for index, where in ((2, near(third, z)), (3, opposite(z))):
                    arrive(at, where)
                    send(at, where, UP, index, z < 3)
                    send(at, where, DOWN, index, z > 0)
            elif step <= 5:
                for there, zz, way, on in from_line(step - 2):
                    for index, where in enumerate(
                        (place(zz, y, x), near(second, zz), near(third, zz), opposite(zz))
                    ):
                        arrive(at, where, there)
                        send(at, where, way, 4 * (step - 2) + index, on)

    def reduce_step(at, step):
        if step == 0:
            add_pair(at)
        if step < 4:
            line_step(at, step)
        else:
            gather_step(at, 0)

    def load_weight(index):
        return pltpu.make_async_copy(
            weights[index], weight_buffer.at[index % 2], weight_sem.at[index % 2]
        )

    def input_gradient():
        load_weight(0).start()
        for index in range(6):
            load_weight(index + 1).start()
            load_weight(index).wait()
            columns = lanes(normed_grad, core if index < 3 else 1 - core, normed_grad.shape[1] // 2)
            term = dot_nt(rights[count - 3 + index % 3][...], weight_buffer[index % 2])
            if index % 3:
                columns[...] += term
            else:
                columns[...] = term
        width = resid_in.shape[1]
        cotan, values = normed_grad[...], resid_in[...]
        rate = lax.rsqrt(jnp.mean(values * values, axis=1, keepdims=True) + EPSILON)
        scaled = cotan * gain_one[...]
        slope = jnp.mean(scaled * values, axis=1, keepdims=True)
        back = rate * scaled - values * (rate * rate * rate) * slope
        input_grad[...] = (resid_grad[...] + back).astype(BF16)
        gain_grad = jnp.sum(cotan * values * rate, axis=0, keepdims=True)
        column = jnp.zeros((BUCKETS, 1), F32)
        for apart in range(lines.shape[0]):
            sums = lines[apart : apart + 1, :TILE]
            if apart + 1 < lines.shape[0]:
                sums = sums + lines[apart + 1 : apart + 2, TILE:]
            column = column + jnp.sum(in_bucket[apart] * sums, axis=1, keepdims=True)
        place_at = lax.broadcasted_iota(jnp.int32, (BUCKETS, 128), 1)
        table = jnp.where(place_at == me, column, 0.0)
        for half in range(2):
            for index in range(4):
                start = (4 * half + index) * 128
                vec_in[half, index : index + 1, :] = gain_grad[:, start : start + 128]
            vec_in[half, 4:16, :] = gains[half]
            vec_in[half, 16:, :] = table[half * (BUCKETS // 2) : (half + 1) * (BUCKETS // 2)]
        vector_step(0)

    def encoder_gradient():
        own = kv_both[0, pl.ds(pl.multiple_of(me * encoder_grad.shape[0], 16), encoder_grad.shape[0]), :]
        width = own.shape[1] // 2
        for side in (0, 1):
            terms = []
            for index in (6 + 2 * side, 7 + 2 * side):
                if index < 9:
                    load_weight(index + 1).start()
                load_weight(index).wait()
                part = slice((index % 2) * width, (index % 2 + 1) * width)
                terms.append(dot_nt(own[:, part], weight_buffer[index % 2]))
            columns = lanes(encoder_grad, core if side == 0 else 1 - core, width // 2)
            columns[...] = (terms[0] + terms[1]).astype(BF16)

    early, late = range(count - 3), range(count - 3, count)
    near_by = [at for at in early if at in far_rights]
    others = [at for at in early if at not in far_rights]

    def wave(some):
        for time in range(len(some) + 4):
            for step in range(5):
                if 0 <= time - step < len(some):
                    reduce_step(some[time - step], step)
            yield

    grad_arrival = to_all(0, lambda peer: grad_packed.at[peer], lambda mine: grad_landed.at[mine])
    send_operands(near_by)
    send_operands(others)
    for at in near_by:
        product_away(at)
    grad_arrival()
    attend_back(
        order, held_at, landed, grad_landed, attn_sum, log_norm, bias_lines, back_packed, lines,
        *attention_scratch,
    )
    back_arrival = to_all(1, lambda peer: back_packed.at[peer], lambda mine: back_landed.at[mine])
    early_wave = wave(near_by + others)
    for index, at in enumerate(others):
        pass_on(at)
        if index:
            product_away(others[index - 1])
    product_away(others[-1])
    next(early_wave)
    next(early_wave)
    back_arrival()
    dq_ref, dk_ref, dv_ref = rights[count - 3 :]
    for pair in range(peers // 2):
        cols = slice(pair * 2 * HEAD_DIM, (pair + 1) * 2 * HEAD_DIM)
        dq_ref[:, cols], dk_ref[:, cols] = unpack_pair(back_landed, pair, slice(0, 2 * BLOCK))
        first, second = unpack_pair(back_landed, pair, slice(2 * BLOCK, 3 * BLOCK))
        dv_ref[:BLOCK, cols] = first
        dv_ref[BLOCK:, cols] = second
    send_operands(late)
    input_gradient()
    for _ in early_wave:
        pass
    for at in late:
        pass_on(at)
    vector_add(0)
    for at in late:
        product_away(at)
    for at in early:
        gather_step(at, 1)
    for time, _ in enumerate(wave(list(late))):
        if time in (1, 3, 5):
            for at in early:
                gather_step(at, 2 + time // 2)
            vector_add(1 + time // 2)
    vector_add(4)
    for step in range(1, 9):
        for at in late:
            gather_step(at, step)
        if step >= 5:
            for at in early:
                gather_step(at, step)
        if step == 5:
            owns["piece", kv_at].wait()
            launch(
                remote(kv_both.at[0], kv_both.at[1], all_send.at[0, 0], all_recv.at[0, 0], me, 1 - core)
            )
            encoder_gradient()
    arrived(kv_both.at[1], all_recv.at[0, 0])
    for each in finish:
        each()


def weight_grads(products, lefts, rights, left_far, right_far, others, weights):
    count, peers = len(products), lax.axis_size("ctx")
    tokens = lefts[0].shape[0]
    length = others[4].shape[1]
    kv_at = [product.left for product in products].index(SUMMED)
    kv_rows, kv_width = rights[kv_at].shape
    spans = length // TILE
    dma = pltpu.SemaphoreType.DMA
    vmem = pltpu.VMEM
    width = HEADS * HEAD_DIM
    halves = [left.shape[1] // 2 for left in lefts]
    widths = [right.shape[1] for right in rights] + [width] * 3
    helds = []
    for product, right in zip(products, widths):
        height = kv_rows if product.left == SUMMED else halves[product.left]
        helds.append((height, right // 4) if product.tall else (height // 2, right // 2))
    lands = [vmem(shape, BF16) for shape in helds]
    chunk = (peers, BLOCK, 2 * HEAD_DIM)
    chunks = (peers, 3 * BLOCK, 2 * HEAD_DIM)
    smem_spec = pl.BlockSpec(memory_space=pltpu.SMEM)
    return pl.pallas_call(
        functools.partial(weight_grad_kernel, products, len(lefts)),
        out_shape=[
            jax.ShapeDtypeStruct((halves[product.left], right), BF16)
            for product, right in zip(products, widths)
            if product.left != SUMMED
        ]
        + [
            jax.ShapeDtypeStruct((32, 128), F32),
            jax.ShapeDtypeStruct((tokens, width), BF16),
            jax.ShapeDtypeStruct((kv_rows // peers, width), BF16),
            jax.ShapeDtypeStruct((2, kv_rows, kv_width), BF16),
        ],
        in_specs=[vmem_spec()] * (len(lefts) + len(rights) + len(left_far) + len(right_far))
        + [smem_spec] * 2
        + [vmem_spec()] * (len(others) - 2)
        + [any_spec()] * len(weights),
        out_specs=[any_spec()] * (count - 1) + [vmem_spec()] * 4,
        scratch_shapes=[vmem((4 * tokens, half), BF16) for half in halves]
        + [vmem((tokens, half), BF16) for half in halves]
        + [vmem((half, 4 * tokens), BF16) for half in halves]
        + [
            vmem((kv_rows if product.left == SUMMED else 4 * tokens, right // 2), BF16)
            for product, right in zip(products, widths)
        ]
        + lands * 3
        + [vmem((5 * height // 4, width_held), BF16) for height, width_held in helds]
        + [vmem((tokens, width), BF16)] * 3
        + [vmem(chunk, BF16), vmem(chunk, BF16), vmem(chunks, BF16), vmem(chunks, BF16)]
        + [vmem((spans, 2 * TILE), F32)]
        + [vmem((length, HEAD_DIM), BF16)] * 4
        + [vmem((HEAD_DIM, length), BF16)]
        + [vmem((spans, TILE, TILE), F32)] * 2
        + [vmem((length, HEAD_DIM), F32)] * 3
        + [vmem((1, length), F32), vmem((HEAD_DIM, length), F32)]
        + [
            vmem((2, 32, 128), F32),
            vmem((4, 32, 128), F32),
            vmem((5, 32, 128), F32),
            vmem((2,) + weights[0].shape, BF16),
            vmem((tokens, width), F32),
        ]
        + [
            dma((len(lefts), 6)),
            dma((len(lefts), 4)),
            dma((count, 5)),
            dma((count, 3)),
            dma((count,)),
            dma((count,)),
            dma((count, 2, 4)),
            dma((count, 2, 4)),
            dma((count, 4, 16)),
            dma((count, peers)),
            dma((count,)),
            dma((5,)),
            dma((5,)),
            dma((2, peers)),
            dma((2, peers)),
            dma((2,)),
            dma((2,)),
        ],
        compiler_params=pltpu.CompilerParams(
            collective_id=5, has_side_effects=True, vmem_limit_bytes=60 * MIB
        ),
        name="weight_grads",
    )(*lefts, *rights, *left_far, *right_far, *others, *weights)


def on_device_by_heads(
    inputs,
    encoder,
    cotangent,
    block_order,
    bucket_of,
    self_gain,
    query_weight,
    key_weight,
    value_weight,
    out_weight,
    bias_table,
    cross_gain,
    cross_query,
    cross_key,
    cross_value,
    cross_out,
    mlp_gain,
    gate_weight,
    up_weight,
    down_weight,
):
    core, me = lax.axis_index("wsh"), lax.axis_index("ctx")

    def swap(values):
        return lax.ppermute(values, "wsh", [(0, 1), (1, 0)])

    def along_x(values):
        return lax.ppermute(values, "ctx", [(at, at ^ 1) for at in range(HEADS)])

    def along_y(values):
        return lax.ppermute(values, "ctx", [(at, at ^ 2) for at in range(HEADS)])

    def other_column(values, bit):
        half = values.shape[1] // 2
        return pick(bit & 1, values[:, :half], values[:, half:])

    def own_half(values):
        half = values.shape[-1] // 2
        return pick(core, values[..., half:], values[..., :half])

    def other_half(values):
        half = values.shape[-1] // 2
        return pick(core, values[..., :half], values[..., half:])

    def join(own, other, axis):
        return pick(
            core,
            jnp.concatenate([other, own], axis=axis),
            jnp.concatenate([own, other], axis=axis),
        )

    def times(values, pair):
        return plain_dot(own_half(values), pair[0]) + plain_dot(other_half(values), pair[1])

    def times_back(values, pair):
        return join(right_contract(values, pair[0]), right_contract(values, pair[1]), 1)

    def both_cores(values):
        return jnp.concatenate([own_half(values), swap(other_half(values))], axis=0)

    small = jnp.concatenate([self_gain, cross_gain, mlp_gain, bias_table.reshape(-1)])
    small_other = swap(small)
    width = self_gain.shape[0]
    gain_one, gain_two, gain_three = (
        join(small[at * width : (at + 1) * width], small_other[at * width : (at + 1) * width], 0).astype(F32)
        for at in range(3)
    )
    bias_rows = join(bias_table, small_other[3 * width :].reshape(bias_table.shape), 0).astype(F32)
    query_pair, key_pair, value_pair = (
        (member, swap(member)) for member in (query_weight, key_weight, value_weight)
    )
    out_pair, cross_query_pair, cross_key_pair, cross_value_pair, cross_out_pair = (
        (member, swap(member))
        for member in (out_weight, cross_query, cross_key, cross_value, cross_out)
    )
    gate_pair, up_pair, down_pair = (
        (member, swap(member)) for member in (gate_weight, up_weight, down_weight)
    )

    resid_in = inputs[0].astype(F32)
    tokens = resid_in.shape[0]
    head_width = HEADS * HEAD_DIM
    length = bucket_of.shape[0]

    normed_one = rms_norm(resid_in, gain_one).astype(BF16)
    queries = times(normed_one, query_pair).astype(BF16)
    keys = times(normed_one, key_pair).astype(BF16)
    values = times(normed_one, value_pair).astype(BF16)
    landed, encoder_all = to_heads(queries, keys, values, encoder[0])
    encoder_all = encoder_all.reshape(-1, encoder.shape[2])

    own_column = jnp.sum(
        jnp.where(jnp.arange(HEADS)[None, :] == me, bias_rows, 0.0), axis=1, keepdims=True
    )
    in_bucket = bucket_of[None, :] == jnp.arange(BUCKETS, dtype=jnp.int32)[:, None]
    by_offset = jnp.sum(jnp.where(in_bucket, own_column, 0.0), axis=0).reshape(-1, TILE)
    before = jnp.concatenate([jnp.full((1, TILE), NEG_BIG, F32), by_offset[:-1]], axis=0)
    bias_lines = jnp.concatenate([by_offset, before], axis=1)

    mixed_packed, attn_sum, log_norm = attend(block_order, landed, bias_lines)
    attended = from_heads(mixed_packed)

    after_self = resid_in + times(attended, out_pair)
    normed_two = rms_norm(after_self, gain_two).astype(BF16)
    cross_q_heads = times(normed_two, cross_query_pair).astype(BF16).reshape(tokens, HEADS, HEAD_DIM)
    cross_k_heads = times(encoder_all, cross_key_pair).astype(BF16).reshape(-1, HEADS, HEAD_DIM)
    cross_v_heads = times(encoder_all, cross_value_pair).astype(BF16).reshape(-1, HEADS, HEAD_DIM)
    cross_logits = jnp.einsum(
        "qhe,khe->hqk", cross_q_heads, cross_k_heads, preferred_element_type=F32
    )
    cross_exact = jnp.exp(cross_logits - jax.nn.logsumexp(cross_logits, axis=-1, keepdims=True))
    cross_probs = cross_exact.astype(BF16)
    cross_mixed = (
        jnp.einsum("hqk,khe->qhe", cross_probs, cross_v_heads, preferred_element_type=F32)
        .reshape(tokens, head_width)
        .astype(BF16)
    )
    after_cross = after_self + times(cross_mixed, cross_out_pair)
    normed_three = rms_norm(after_cross, gain_three).astype(BF16)
    gate_act = times(normed_three, gate_pair)
    up_act = times(normed_three, up_pair)
    hidden_float, mlp_pull = jax.vjp(gelu_product, gate_act, up_act)
    hidden = hidden_float.astype(BF16)
    result = (after_cross + times(hidden, down_pair)).astype(BF16)

    resid_grad = cotangent[0].astype(F32)
    branch_three = cotangent[0]
    gate_grad, up_grad = mlp_pull(times_back(branch_three, down_pair))
    gate_grad, up_grad = gate_grad.astype(BF16), up_grad.astype(BF16)
    normed_three_grad = times_back(gate_grad, gate_pair) + times_back(up_grad, up_pair)
    part_grad, gain_three_grad = norm_back(after_cross, gain_three, normed_three_grad)
    after_cross_grad = resid_grad + part_grad
    branch_two = after_cross_grad.astype(BF16)
    mix_grad = times_back(branch_two, cross_out_pair).astype(BF16).reshape(tokens, HEADS, HEAD_DIM)
    cross_score_grad = jnp.einsum(
        "qhe,khe->hqk", mix_grad, cross_v_heads, preferred_element_type=F32
    )
    cross_delta = jnp.sum(cross_exact * cross_score_grad, axis=-1, keepdims=True)
    cross_dlogits = (cross_exact * (cross_score_grad - cross_delta)).astype(BF16)
    cross_q_grad = (
        jnp.einsum("hqk,khe->qhe", cross_dlogits, cross_k_heads, preferred_element_type=F32)
        .reshape(tokens, head_width)
        .astype(BF16)
    )
    cross_k_part = jnp.einsum(
        "hqk,qhe->khe", cross_dlogits, cross_q_heads, preferred_element_type=F32
    ).reshape(-1, head_width)
    cross_v_part = jnp.einsum(
        "hqk,qhe->khe", cross_probs, mix_grad, preferred_element_type=F32
    ).reshape(-1, head_width)
    cross_kv_part = jnp.concatenate([cross_k_part, cross_v_part], axis=1).astype(BF16)
    normed_two_grad = times_back(cross_q_grad, cross_query_pair)
    part_grad, gain_two_grad = norm_back(after_self, gain_two, normed_two_grad)
    after_self_grad = after_cross_grad + part_grad
    branch_one = after_self_grad.astype(BF16)
    dattn = times_back(branch_one, out_pair).astype(BF16)
    block_ids = jnp.arange(block_order.shape[0], dtype=jnp.int32)
    held_at = jnp.sum(
        jnp.where(block_order[None, :] == block_ids[:, None], block_ids[None, :], 0), axis=1
    )
    gains = jnp.concatenate(
        [gain_two_grad.reshape(2, 4, 128), gain_three_grad.reshape(2, 4, 128), jnp.zeros((2, 4, 128), F32)],
        axis=1,
    )
    bucket_tiles = in_bucket.astype(F32).reshape(BUCKETS, -1, TILE).transpose(1, 0, 2)

    z_then_yx, z_then_xy, z_last = (
        (True, ACROSS_Y, ACROSS_X),
        (True, ACROSS_X, ACROSS_Y),
        (False, ACROSS_Y, ACROSS_X),
    )
    lefts = (normed_three, hidden, cross_mixed, normed_two, attended, normed_one)
    products = (
        Product(0, gate_grad, BIT_Y, False, z_then_yx),
        Product(1, branch_three, BIT_X, True, z_then_yx),
        Product(0, up_grad, BIT_Y, False, z_then_xy),
        Product(SUMMED, cross_kv_part, BIT_X, False, z_last),
        Product(2, branch_two, BIT_X, False, z_last),
        Product(3, cross_q_grad, BIT_Y, False, z_last),
        Product(4, branch_one, BIT_Y, False, z_last),
        Product(5, None, BIT_X, False, z_then_xy),
        Product(5, None, BIT_X, False, z_then_xy),
        Product(5, None, BIT_X, False, z_then_xy),
    )
    *wholes, totals, input_grad, encoder_grad, cross_kv_both = weight_grads(
        products,
        lefts,
        [product.right for product in products[:7]],
        (along_y(normed_three), along_x(hidden)),
        (along_y(other_column(gate_grad, me >> 1)), along_x(other_column(branch_three, me)), along_y(other_column(up_grad, me >> 1))),
        (
            block_order,
            held_at,
            dattn,
            landed,
            attn_sum,
            log_norm,
            bias_lines,
            bucket_tiles,
            resid_in,
            gain_one[None, :],
            after_self_grad,
            gains,
        ),
        [pair[0] for pair in (query_pair, key_pair, value_pair)]
        + [pair[1] for pair in (query_pair, key_pair, value_pair)]
        + [cross_key_pair[0], cross_value_pair[0], cross_key_pair[1], cross_value_pair[1]],
    )
    cross_kv_w_grad = left_contract(
        both_cores(encoder_all), cross_kv_both.reshape(-1, 2 * head_width)
    )
    (
        sum_gate,
        sum_down,
        sum_up,
        sum_cross_out,
        sum_cross_query,
        sum_out,
        sum_query,
        sum_key,
        sum_value,
    ) = (member.astype(F32) for member in wholes)
    sum_gain_one, sum_gain_two, sum_gain_three = (
        totals[4 * at : 4 * at + 4].reshape(-1) for at in range(3)
    )
    sum_table = totals[16:, :HEADS]
    return (
        result[None],
        input_grad[None],
        encoder_grad[None],
        sum_gain_one,
        sum_query,
        sum_key,
        sum_value,
        sum_out,
        sum_table,
        sum_gain_two,
        sum_cross_query,
        cross_kv_w_grad[:, :head_width],
        cross_kv_w_grad[:, head_width:],
        sum_cross_out,
        sum_gain_three,
        sum_gate,
        sum_up,
        sum_down,
    )


def solution(mesh):
    by_heads = mesh.shape["ctx"] == HEADS and mesh.shape["wsh"] == 2
    return jax.shard_map(
        on_device_by_heads if by_heads else on_device,
        mesh=mesh,
        in_specs=(
            P("wsh", "ctx", None),
            P("wsh", "ctx", None),
            P("wsh", "ctx", None),
            P(),
            P(),
            P("wsh"),
            P("wsh", None),
            P("wsh", None),
            P("wsh", None),
            P("wsh", None),
            P("wsh", None),
            P("wsh"),
            P("wsh", None),
            P("wsh", None),
            P("wsh", None),
            P("wsh", None),
            P("wsh"),
            P("wsh", None),
            P("wsh", None),
            P("wsh", None),
        ),
        out_specs=(
            P("wsh", "ctx", None),
            P("wsh", "ctx", None),
            P("wsh", "ctx", None),
            P("wsh"),
            P("wsh", None),
            P("wsh", None),
            P("wsh", None),
            P("wsh", None),
            P("wsh", None),
            P("wsh"),
            P("wsh", None),
            P("wsh", None),
            P("wsh", None),
            P("wsh", None),
            P("wsh"),
            P("wsh", None),
            P("wsh", None),
            P("wsh", None),
        ),
        check_vma=False,
    )
```

```python
import functools

import jax
import jax.numpy as jnp
from jax import lax
from jax.experimental import pallas as pl
from jax.experimental.pallas import tpu as pltpu
from jax.sharding import PartitionSpec as P

HEADS = 16
HEAD_DIM = 64
BUCKETS = 32


EPSILON = 1e-06
NEG_BIG = -1e30


def rms_norm(values, gain):
    return values * lax.rsqrt(jnp.mean(values * values, axis=-1, keepdims=True) + EPSILON) * gain


def plain_dot(left, right):
    return jnp.dot(left, right, preferred_element_type=jnp.float32)


def left_contract(left, right):
    return lax.dot_general(
        left, right, (((0,), (0,)), ((), ())), preferred_element_type=jnp.float32
    )


def right_contract(left, right):
    return lax.dot_general(
        left, right, (((1,), (1,)), ((), ())), preferred_element_type=jnp.float32
    )


def gelu_product(gate_vals, up_vals):
    return jax.nn.gelu(gate_vals, approximate=True) * up_vals


def norm_back(values, gain, cotan):
    normed, pullback = jax.vjp(rms_norm, values, gain)
    return pullback(cotan)


def lookup_positions(block_order, first_row, row_count, block_len):
    token_ids = first_row + jnp.arange(row_count, dtype=jnp.int32)
    block_ids = token_ids // block_len
    matches = block_ids[:, None] == jnp.arange(block_order.shape[0], dtype=jnp.int32)[None, :]
    starts = jnp.sum(jnp.where(matches, block_order[None, :], 0), axis=1)
    return starts * block_len + token_ids % block_len


def fold_groups(step_fn, carried, pieces, shard_rows):
    piece_rows = pieces[0].shape[0]
    shards = max(1, piece_rows // shard_rows)
    group_limit = max(1, 1152 // shard_rows)
    group_size = max(
        (divisor for divisor in range(1, min(shards, group_limit) + 1) if shards % divisor == 0)
    )
    group_rows = group_size * shard_rows

    def group_step(group_idx, inner_state):
        sub_pieces = tuple(
            (
                lax.dynamic_slice_in_dim(member, group_idx * group_rows, group_rows, 0)
                for member in pieces
            )
        )
        return step_fn(inner_state, sub_pieces, group_idx * group_rows)

    return lax.fori_loop(0, shards // group_size, group_step, carried)


def on_device(
    inputs,
    encoder,
    cotangent,
    block_order,
    bucket_of,
    self_gain,
    query_weight,
    key_weight,
    value_weight,
    out_weight,
    bias_table,
    cross_gain,
    cross_query,
    cross_key,
    cross_value,
    cross_out,
    mlp_gain,
    gate_weight,
    up_weight,
    down_weight,
):
    (
        gain_one,
        query_full,
        key_full,
        value_full,
        out_full,
        bias_rows,
        gain_two,
        cross_query_full,
        cross_key_full,
        cross_value_full,
        cross_out_full,
        gain_three,
        gate_full,
        up_full,
        down_full,
    ) = (
        lax.all_gather(self_gain, "wsh", axis=0, tiled=True),
        lax.all_gather(query_weight, "wsh", axis=0, tiled=True),
        lax.all_gather(key_weight, "wsh", axis=0, tiled=True),
        lax.all_gather(value_weight, "wsh", axis=0, tiled=True),
        lax.all_gather(out_weight, "wsh", axis=0, tiled=True),
        lax.all_gather(bias_table, "wsh", axis=0, tiled=True),
        lax.all_gather(cross_gain, "wsh", axis=0, tiled=True),
        lax.all_gather(cross_query, "wsh", axis=0, tiled=True),
        lax.all_gather(cross_key, "wsh", axis=0, tiled=True),
        lax.all_gather(cross_value, "wsh", axis=0, tiled=True),
        lax.all_gather(cross_out, "wsh", axis=0, tiled=True),
        lax.all_gather(mlp_gain, "wsh", axis=0, tiled=True),
        lax.all_gather(gate_weight, "wsh", axis=0, tiled=True),
        lax.all_gather(up_weight, "wsh", axis=0, tiled=True),
        lax.all_gather(down_weight, "wsh", axis=0, tiled=True),
    )
    gain_one = gain_one.astype(jnp.float32)
    gain_two = gain_two.astype(jnp.float32)
    gain_three = gain_three.astype(jnp.float32)
    resid_in = inputs[0].astype(jnp.float32)
    tokens = resid_in.shape[0]
    block_len = tokens // 2
    head_width = HEADS * HEAD_DIM
    total_rows = tokens * lax.axis_size("ctx")
    own_pos = lookup_positions(block_order, lax.axis_index("ctx") * tokens, tokens, block_len)
    bucket_ids = jnp.arange(BUCKETS, dtype=jnp.int32)
    boundaries = jnp.sum((bucket_of[None, :] < bucket_ids[1:, None]).astype(jnp.int32), axis=1)

    def bucket_indicator_of(clipped):
        bucket = jnp.sum((clipped[None] >= boundaries[:, None, None]).astype(jnp.int32), axis=0)
        return (bucket[None] == bucket_ids[:, None, None]).astype(jnp.bfloat16)

    def query_key_logits(query_heads, key_heads, query_pos, key_pos):
        logits = jnp.einsum(
            "qhe,khe->hqk", query_heads, key_heads, preferred_element_type=jnp.float32
        )
        offset = query_pos[:, None] - key_pos[None, :]
        clipped = jnp.maximum(offset, 0)
        indicator = bucket_indicator_of(clipped)
        rel_bias = jnp.einsum(
            "ouw,om->muw", indicator, bias_rows, preferred_element_type=jnp.float32
        )
        allowed = (offset >= 0)[None]
        return (jnp.where(allowed, logits + rel_bias, NEG_BIG), allowed, indicator)

    normed_one = rms_norm(resid_in, gain_one).astype(jnp.bfloat16)
    query_heads = (
        plain_dot(normed_one, query_full).astype(jnp.bfloat16).reshape(tokens, HEADS, HEAD_DIM)
    )
    key_heads = (
        plain_dot(normed_one, key_full).astype(jnp.bfloat16).reshape(tokens, HEADS, HEAD_DIM)
    )
    value_heads = (
        plain_dot(normed_one, value_full).astype(jnp.bfloat16).reshape(tokens, HEADS, HEAD_DIM)
    )

    def norm_step(carried, pieces, first_row):
        running_max, running_sum = carried
        key_pos = lookup_positions(block_order, first_row, pieces[0].shape[0], block_len)
        logits, allowed, indicator = query_key_logits(query_heads, pieces[0], own_pos, key_pos)
        new_max = jnp.maximum(running_max, jnp.max(logits, axis=-1))
        kept = jnp.where(allowed, jnp.exp(logits - new_max[..., None]), 0.0)
        return (new_max, running_sum * jnp.exp(running_max - new_max) + jnp.sum(kept, axis=-1))

    start_state = (
        jnp.full((HEADS, tokens), NEG_BIG, jnp.float32),
        jnp.zeros((HEADS, tokens), jnp.float32),
    )
    running_max, running_sum = fold_groups(
        norm_step, start_state, (lax.all_gather(key_heads, "ctx", axis=0, tiled=True),), tokens
    )
    log_norm = running_max + jnp.log(running_sum)

    def output_step(carried, pieces, first_row):
        key_pos = lookup_positions(block_order, first_row, pieces[0].shape[0], block_len)
        logits, allowed, indicator = query_key_logits(query_heads, pieces[0], own_pos, key_pos)
        attn_probs = jnp.exp(logits - log_norm[..., None]).astype(jnp.bfloat16)
        return carried + jnp.einsum(
            "hqk,khe->qhe", attn_probs, pieces[1], preferred_element_type=jnp.float32
        )

    zero_heads = jnp.zeros((tokens, HEADS, HEAD_DIM), jnp.float32)
    attn_sum = fold_groups(
        output_step,
        zero_heads,
        (
            lax.all_gather(key_heads, "ctx", axis=0, tiled=True),
            lax.all_gather(value_heads, "ctx", axis=0, tiled=True),
        ),
        tokens,
    )
    attended = attn_sum.reshape(tokens, head_width).astype(jnp.bfloat16)
    after_self = resid_in + plain_dot(attended, out_full)
    normed_two = rms_norm(after_self, gain_two).astype(jnp.bfloat16)
    cross_q_heads = (
        plain_dot(normed_two, cross_query_full)
        .astype(jnp.bfloat16)
        .reshape(tokens, HEADS, HEAD_DIM)
    )
    encoder_rows = encoder[0]
    encoder_key_rows, cross_values = (
        lax.all_gather(
            plain_dot(encoder_rows, cross_key_full).astype(jnp.bfloat16), "ctx", axis=0, tiled=True
        ),
        lax.all_gather(
            plain_dot(encoder_rows, cross_value_full).astype(jnp.bfloat16),
            "ctx",
            axis=0,
            tiled=True,
        ),
    )
    cross_k_heads = encoder_key_rows.reshape(encoder_key_rows.shape[0], HEADS, HEAD_DIM)
    cross_v_heads = cross_values.reshape(cross_values.shape[0], HEADS, HEAD_DIM)
    cross_logits = jnp.einsum(
        "qhe,khe->hqk", cross_q_heads, cross_k_heads, preferred_element_type=jnp.float32
    )
    cross_exact = jnp.exp(cross_logits - jax.nn.logsumexp(cross_logits, axis=-1, keepdims=True))
    cross_probs = cross_exact.astype(jnp.bfloat16)
    cross_mixed = (
        jnp.einsum("hqk,khe->qhe", cross_probs, cross_v_heads, preferred_element_type=jnp.float32)
        .reshape(tokens, head_width)
        .astype(jnp.bfloat16)
    )
    after_cross = after_self + plain_dot(cross_mixed, cross_out_full)
    normed_three = rms_norm(after_cross, gain_three).astype(jnp.bfloat16)
    gate_act = plain_dot(normed_three, gate_full)
    up_act = plain_dot(normed_three, up_full)
    hidden_float, mlp_pull = jax.vjp(gelu_product, gate_act, up_act)
    hidden = hidden_float.astype(jnp.bfloat16)
    result = after_cross + plain_dot(hidden, down_full)
    resid_grad = cotangent[0].astype(jnp.float32)
    branch_three = resid_grad.astype(jnp.bfloat16)
    down_grad = left_contract(hidden, branch_three)
    hidden_state_gradient = right_contract(branch_three, down_full)
    gate_grad, up_grad = mlp_pull(hidden_state_gradient)
    gate_grad = gate_grad.astype(jnp.bfloat16)
    up_grad = up_grad.astype(jnp.bfloat16)
    gate_w_grad = left_contract(normed_three, gate_grad)
    up_w_grad = left_contract(normed_three, up_grad)
    normed_three_grad = right_contract(gate_grad, gate_full) + right_contract(up_grad, up_full)
    part_grad, gain_three_grad = norm_back(after_cross, gain_three, normed_three_grad)
    after_cross_grad = resid_grad + part_grad
    branch_two = after_cross_grad.astype(jnp.bfloat16)
    cross_out_grad = left_contract(cross_mixed, branch_two)
    mix_grad = (
        right_contract(branch_two, cross_out_full)
        .astype(jnp.bfloat16)
        .reshape(tokens, HEADS, HEAD_DIM)
    )
    cross_score_grad = jnp.einsum(
        "qhe,khe->hqk", mix_grad, cross_v_heads, preferred_element_type=jnp.float32
    )
    cross_delta = jnp.sum(cross_exact * cross_score_grad, axis=-1, keepdims=True)
    cross_dlogits = (cross_exact * (cross_score_grad - cross_delta)).astype(jnp.bfloat16)
    cross_q_grad = (
        jnp.einsum("hqk,khe->qhe", cross_dlogits, cross_k_heads, preferred_element_type=jnp.float32)
        .reshape(tokens, head_width)
        .astype(jnp.bfloat16)
    )
    cross_k_part = jnp.einsum(
        "hqk,qhe->khe", cross_dlogits, cross_q_heads, preferred_element_type=jnp.float32
    ).reshape(-1, head_width)
    cross_v_part = jnp.einsum(
        "hqk,qhe->khe", cross_probs, mix_grad, preferred_element_type=jnp.float32
    ).reshape(-1, head_width)
    cross_k_grad, cross_v_grad = (
        lax.psum_scatter(cross_k_part, "ctx", scatter_dimension=0, tiled=True),
        lax.psum_scatter(cross_v_part, "ctx", scatter_dimension=0, tiled=True),
    )
    cross_k_grad = cross_k_grad.astype(jnp.bfloat16)
    cross_v_grad = cross_v_grad.astype(jnp.bfloat16)
    cross_query_grad = left_contract(normed_two, cross_q_grad)
    cross_key_grad = left_contract(encoder_rows, cross_k_grad)
    cross_value_grad = left_contract(encoder_rows, cross_v_grad)
    encoder_grad = (
        right_contract(cross_k_grad, cross_key_full)
        + right_contract(cross_v_grad, cross_value_full)
    ).astype(jnp.bfloat16)
    normed_two_grad = right_contract(cross_q_grad, cross_query_full)
    part_grad, gain_two_grad = norm_back(after_self, gain_two, normed_two_grad)
    after_self_grad = after_cross_grad + part_grad
    branch_one = after_self_grad.astype(jnp.bfloat16)
    out_w_grad = left_contract(attended, branch_one)
    dattn_heads = (
        right_contract(branch_one, out_full).astype(jnp.bfloat16).reshape(tokens, HEADS, HEAD_DIM)
    )
    row_delta = jnp.einsum("qhe,qhe->hq", dattn_heads.astype(jnp.float32), attn_sum)

    def block_grads(
        query_side, grad_side, norm_side, delta_side, query_pos, key_side, value_side, key_pos
    ):
        logits, allowed, indicator = query_key_logits(query_side, key_side, query_pos, key_pos)
        exact = jnp.exp(logits - norm_side[..., None])
        score_grad = jnp.einsum(
            "qhe,khe->hqk", grad_side, value_side, preferred_element_type=jnp.float32
        )
        logits_gradient = (exact * (score_grad - delta_side[..., None])).astype(jnp.bfloat16)
        grad_query = jnp.einsum(
            "hqk,khe->qhe", logits_gradient, key_side, preferred_element_type=jnp.float32
        )
        grad_key = jnp.einsum(
            "hqk,qhe->khe", logits_gradient, query_side, preferred_element_type=jnp.float32
        )
        grad_value = jnp.einsum(
            "hqk,qhe->khe",
            exact.astype(jnp.bfloat16),
            grad_side,
            preferred_element_type=jnp.float32,
        )
        bucket_table_gradient = jnp.einsum(
            "ouw,muw->om", indicator, logits_gradient, preferred_element_type=jnp.float32
        )
        return (grad_query, grad_key, grad_value, bucket_table_gradient)

    zero_table = jnp.zeros((BUCKETS, HEADS), jnp.float32)
    full_zero = jnp.zeros((total_rows, HEADS, HEAD_DIM), jnp.float32)

    def key_grad_step(carried, pieces, first_row):
        query_total, table_total, key_total, value_total = carried
        key_pos = lookup_positions(block_order, first_row, pieces[0].shape[0], block_len)
        grad_query, grad_key, grad_value, bucket_table_gradient = block_grads(
            query_heads, dattn_heads, log_norm, row_delta, own_pos, pieces[0], pieces[1], key_pos
        )
        key_total = lax.dynamic_update_slice_in_dim(key_total, grad_key, first_row, 0)
        value_total = lax.dynamic_update_slice_in_dim(value_total, grad_value, first_row, 0)
        return (
            query_total + grad_query,
            table_total + bucket_table_gradient,
            key_total,
            value_total,
        )

    query_sum, table_grad, key_partial, value_partial = fold_groups(
        key_grad_step,
        (zero_heads, zero_table, full_zero, full_zero),
        (
            lax.all_gather(key_heads, "ctx", axis=0, tiled=True),
            lax.all_gather(value_heads, "ctx", axis=0, tiled=True),
        ),
        tokens,
    )
    key_sum, value_accumulated = (
        lax.psum_scatter(key_partial, "ctx", scatter_dimension=0, tiled=True),
        lax.psum_scatter(value_partial, "ctx", scatter_dimension=0, tiled=True),
    )
    query_grad = query_sum.reshape(tokens, head_width).astype(jnp.bfloat16)
    key_grad = key_sum.reshape(tokens, head_width).astype(jnp.bfloat16)
    value_grad = value_accumulated.reshape(tokens, head_width).astype(jnp.bfloat16)
    query_w_grad = left_contract(normed_one, query_grad)
    key_w_grad = left_contract(normed_one, key_grad)
    value_w_grad = left_contract(normed_one, value_grad)
    normed_one_grad = (
        right_contract(query_grad, query_full)
        + right_contract(key_grad, key_full)
        + right_contract(value_grad, value_full)
    )
    part_grad, gain_one_grad = norm_back(resid_in, gain_one, normed_one_grad)
    input_grad = (after_self_grad + part_grad).astype(jnp.bfloat16)
    (
        sum_gain_one,
        sum_query,
        sum_key,
        sum_value,
        sum_out,
        sum_table,
        sum_gain_two,
        sum_cross_query,
        sum_cross_key,
        sum_cross_value,
        sum_cross_out,
        sum_gain_three,
        sum_gate,
        sum_up,
        sum_down,
    ) = (
        lax.psum_scatter(
            gain_one_grad.astype(jnp.bfloat16), "wsh", scatter_dimension=0, tiled=True
        ).astype(jnp.float32),
        lax.psum_scatter(
            query_w_grad.astype(jnp.bfloat16), "wsh", scatter_dimension=0, tiled=True
        ).astype(jnp.float32),
        lax.psum_scatter(
            key_w_grad.astype(jnp.bfloat16), "wsh", scatter_dimension=0, tiled=True
        ).astype(jnp.float32),
        lax.psum_scatter(
            value_w_grad.astype(jnp.bfloat16), "wsh", scatter_dimension=0, tiled=True
        ).astype(jnp.float32),
        lax.psum_scatter(
            out_w_grad.astype(jnp.bfloat16), "wsh", scatter_dimension=0, tiled=True
        ).astype(jnp.float32),
        lax.psum_scatter(
            table_grad.astype(jnp.bfloat16), "wsh", scatter_dimension=0, tiled=True
        ).astype(jnp.float32),
        lax.psum_scatter(
            gain_two_grad.astype(jnp.bfloat16), "wsh", scatter_dimension=0, tiled=True
        ).astype(jnp.float32),
        lax.psum_scatter(
            cross_query_grad.astype(jnp.bfloat16), "wsh", scatter_dimension=0, tiled=True
        ).astype(jnp.float32),
        lax.psum_scatter(
            cross_key_grad.astype(jnp.bfloat16), "wsh", scatter_dimension=0, tiled=True
        ).astype(jnp.float32),
        lax.psum_scatter(
            cross_value_grad.astype(jnp.bfloat16), "wsh", scatter_dimension=0, tiled=True
        ).astype(jnp.float32),
        lax.psum_scatter(
            cross_out_grad.astype(jnp.bfloat16), "wsh", scatter_dimension=0, tiled=True
        ).astype(jnp.float32),
        lax.psum_scatter(
            gain_three_grad.astype(jnp.bfloat16), "wsh", scatter_dimension=0, tiled=True
        ).astype(jnp.float32),
        lax.psum_scatter(
            gate_w_grad.astype(jnp.bfloat16), "wsh", scatter_dimension=0, tiled=True
        ).astype(jnp.float32),
        lax.psum_scatter(
            up_w_grad.astype(jnp.bfloat16), "wsh", scatter_dimension=0, tiled=True
        ).astype(jnp.float32),
        lax.psum_scatter(
            down_grad.astype(jnp.bfloat16), "wsh", scatter_dimension=0, tiled=True
        ).astype(jnp.float32),
    )
    total_grads = lax.psum(
        (
            sum_gain_one,
            sum_query,
            sum_key,
            sum_value,
            sum_out,
            sum_table,
            sum_gain_two,
            sum_cross_query,
            sum_cross_key,
            sum_cross_value,
            sum_cross_out,
            sum_gain_three,
            sum_gate,
            sum_up,
            sum_down,
        ),
        "ctx",
    )
    return (result.astype(jnp.bfloat16)[None], input_grad[None], encoder_grad[None]) + tuple(
        total_grads
    )


F32 = jnp.float32
BF16 = jnp.bfloat16
MESH = pl.DeviceIdType.MESH
TILE = 256
BLOCK = 64
MIB = 2**20


def dot_nt(left, right):
    return lax.dot_general(left, right, (((1,), (1,)), ((), ())), preferred_element_type=F32)


def vmem_spec():
    return pl.BlockSpec(memory_space=pltpu.VMEM)


def any_spec():
    return pl.BlockSpec(memory_space=pl.ANY)


def greet_all(peers):
    me, core = lax.axis_index("ctx"), lax.axis_index("wsh")
    barrier = pltpu.get_barrier_semaphore()
    for step in range(1, peers):
        pl.semaphore_signal(
            barrier, inc=1, device_id=(lax.rem(me + step, peers), core), device_id_type=MESH
        )
    pl.semaphore_wait(barrier, peers - 1)


def exchange_all(packed, landed, send_sem, recv_sem, own_sem):
    peers = packed.shape[0]
    me, core = lax.axis_index("ctx"), lax.axis_index("wsh")

    def copy(step):
        peer = lax.rem(me + step, peers)
        return pltpu.make_async_remote_copy(
            src_ref=packed.at[peer],
            dst_ref=landed.at[me],
            send_sem=send_sem.at[step],
            recv_sem=recv_sem.at[step],
            device_id=(peer, core),
            device_id_type=MESH,
        )

    copies = [copy(step) for step in range(1, peers)]
    for each in copies:
        each.start()
    own = pltpu.make_async_copy(packed.at[me], landed.at[me], own_sem)
    own.start()
    own.wait()
    for each in copies:
        each.wait()


def exchange_scratch(peers):
    return [
        pltpu.SemaphoreType.DMA((peers,)),
        pltpu.SemaphoreType.DMA((peers,)),
        pltpu.SemaphoreType.DMA,
    ]


def to_heads_kernel(q_ref, k_ref, v_ref, rows_ref, landed, rows_out, packed, rows_send, rows_recv, rows_own, *sems):
    peers = packed.shape[0]
    me, core = lax.axis_index("ctx"), lax.axis_index("wsh")
    greet_all(peers)
    copies = []
    for step in range(1, peers):
        copies.append(
            pltpu.make_async_remote_copy(
                src_ref=rows_ref,
                dst_ref=rows_out.at[me],
                send_sem=rows_send.at[step],
                recv_sem=rows_recv.at[step],
                device_id=(lax.rem(me + step, peers), core),
                device_id_type=MESH,
            )
        )
    copies.append(pltpu.make_async_copy(rows_ref, rows_out.at[me], rows_own))
    for head in range(peers):
        cols = slice(head * HEAD_DIM, (head + 1) * HEAD_DIM)
        packed[head, : 2 * BLOCK, :] = jnp.concatenate([q_ref[:, cols], k_ref[:, cols]], axis=1)
        packed[head, 2 * BLOCK :, :] = jnp.concatenate(
            [v_ref[:BLOCK, cols], v_ref[BLOCK:, cols]], axis=1
        )
    for each in copies:
        each.start()
    exchange_all(packed, landed, *sems)
    for each in copies:
        each.wait()


def to_heads(queries, keys, values, rows):
    shape = (HEADS, 3 * BLOCK, 2 * HEAD_DIM)
    return pl.pallas_call(
        to_heads_kernel,
        out_shape=[
            jax.ShapeDtypeStruct(shape, BF16),
            jax.ShapeDtypeStruct((HEADS,) + rows.shape, BF16),
        ],
        in_specs=[vmem_spec()] * 4,
        out_specs=[vmem_spec()] * 2,
        scratch_shapes=[pltpu.VMEM(shape, BF16)] + exchange_scratch(HEADS) * 2,
        compiler_params=pltpu.CompilerParams(
            collective_id=1, has_side_effects=True, vmem_limit_bytes=16 * MIB
        ),
        name="to_heads",
    )(queries, keys, values, rows)


def unpack_pair(landed, pair, rows):
    left, right = landed[2 * pair, rows, :], landed[2 * pair + 1, rows, :]
    return (
        jnp.concatenate([left[:, :HEAD_DIM], right[:, :HEAD_DIM]], axis=1),
        jnp.concatenate([left[:, HEAD_DIM:], right[:, HEAD_DIM:]], axis=1),
    )


def from_heads_kernel(packed, out_ref, landed, *sems):
    peers = packed.shape[0]
    greet_all(peers)
    exchange_all(packed, landed, *sems)
    for pair in range(peers // 2):
        cols = slice(pair * 2 * HEAD_DIM, (pair + 1) * 2 * HEAD_DIM)
        first, second = unpack_pair(landed, pair, slice(0, BLOCK))
        out_ref[:BLOCK, cols] = first
        out_ref[BLOCK:, cols] = second


def from_heads(packed):
    return pl.pallas_call(
        from_heads_kernel,
        out_shape=jax.ShapeDtypeStruct((2 * BLOCK, HEADS * HEAD_DIM), BF16),
        in_specs=[vmem_spec()],
        out_specs=vmem_spec(),
        scratch_shapes=[pltpu.VMEM(packed.shape, BF16)] + exchange_scratch(HEADS),
        compiler_params=pltpu.CompilerParams(
            collective_id=3, has_side_effects=True, vmem_limit_bytes=16 * MIB
        ),
        name="from_heads",
    )(packed)


def place_tiles(bias_lines, tiles):
    for apart in range(tiles.shape[0]):
        line = jnp.broadcast_to(bias_lines[apart : apart + 1, :], (TILE, 2 * TILE))
        tiles[apart] = pltpu.roll(line, 0, 1, stride=1, stride_axis=0)[:, :TILE]


def attend_kernel(order, landed, bias_lines, out_ref, sum_ref, norm_ref, q_s, k_s, vt_s, tiles, ot_s, o_s):
    blocks = order.shape[0]
    spans = blocks * BLOCK // TILE
    for stored in range(blocks):
        device, half = stored // 2, stored % 2
        at = pl.ds(pl.multiple_of(order[stored] * BLOCK, BLOCK), BLOCK)
        pair = landed[device, half * BLOCK : (half + 1) * BLOCK, :]
        q_s[at, :] = pair[:, :HEAD_DIM]
        k_s[at, :] = pair[:, HEAD_DIM:]
        values = landed[device, 2 * BLOCK :, half * HEAD_DIM : (half + 1) * HEAD_DIM]
        o_s[at, :] = values.astype(F32)
    vt_s[...] = jnp.transpose(o_s[...], (1, 0)).astype(BF16)
    place_tiles(bias_lines, tiles)
    for i in range(spans):
        at_i = slice(i * TILE, (i + 1) * TILE)
        queries = q_s[at_i, :]
        scores = [
            dot_nt(k_s[j * TILE : (j + 1) * TILE, :], queries) + tiles[i - j] for j in range(i + 1)
        ]
        top = functools.reduce(
            jnp.maximum, [jnp.max(each, axis=0, keepdims=True) for each in scores]
        )
        total = jnp.zeros((1, TILE), F32)
        mixed = jnp.zeros((HEAD_DIM, TILE), F32)
        for j in range(i + 1):
            weights = jnp.exp(scores[j] - top)
            total = total + jnp.sum(weights, axis=0, keepdims=True)
            mixed = mixed + plain_dot(
                vt_s[:, j * TILE : (j + 1) * TILE], weights.astype(BF16)
            )
        norm_ref[0:1, at_i] = top + jnp.log(total)
        ot_s[:, at_i] = mixed / total
    sum_ref[...] = ot_s[...]
    o_s[...] = jnp.transpose(ot_s[...], (1, 0))
    for stored in range(blocks):
        device, half = stored // 2, stored % 2
        at = pl.ds(pl.multiple_of(order[stored] * BLOCK, BLOCK), BLOCK)
        out_ref[device, :, half * HEAD_DIM : (half + 1) * HEAD_DIM] = o_s[at, :].astype(BF16)


def attend(order, landed, bias_lines):
    blocks = order.shape[0]
    length = blocks * BLOCK
    vmem = pltpu.VMEM
    return pl.pallas_call(
        attend_kernel,
        grid_spec=pltpu.PrefetchScalarGridSpec(
            num_scalar_prefetch=1,
            grid=(),
            in_specs=[vmem_spec()] * 2,
            out_specs=[vmem_spec()] * 3,
            scratch_shapes=[
                vmem((length, HEAD_DIM), BF16),
                vmem((length, HEAD_DIM), BF16),
                vmem((HEAD_DIM, length), BF16),
                vmem((length // TILE, TILE, TILE), F32),
                vmem((HEAD_DIM, length), F32),
                vmem((length, HEAD_DIM), F32),
            ],
        ),
        out_shape=[
            jax.ShapeDtypeStruct((blocks // 2, BLOCK, 2 * HEAD_DIM), BF16),
            jax.ShapeDtypeStruct((HEAD_DIM, length), F32),
            jax.ShapeDtypeStruct((1, length), F32),
        ],
        compiler_params=pltpu.CompilerParams(vmem_limit_bytes=32 * MIB),
        cost_estimate=pl.CostEstimate(
            flops=4 * length * length * HEAD_DIM, bytes_accessed=4 * MIB, transcendentals=length * length // 2
        ),
        name="attend",
    )(order, landed, bias_lines)


def attend_back(
    order, held_at, landed, grad_landed, sums, norm, bias_lines, out_ref, lines_ref,
    q_s, k_s, v_s, do_s, kt_s, tiles, by_offset, dq_s, dk_s, dv_s, delta_s, dqt_s,
):
    blocks = order.shape[0]
    spans = blocks * BLOCK // TILE
    def stored_rows(stored):
        return slice(stored * BLOCK, (stored + 1) * BLOCK), stored // 2, slice(
            stored % 2 * HEAD_DIM, (stored % 2 + 1) * HEAD_DIM
        )

    def in_order(into, staged):
        for block in range(blocks):
            at = slice(block * BLOCK, (block + 1) * BLOCK)
            into[at, :] = staged[pl.ds(held_at[block] * BLOCK, BLOCK), :].astype(BF16)

    for stored in range(blocks):
        at, device, cols = stored_rows(stored)
        pair = landed[device, stored % 2 * BLOCK : (stored % 2 + 1) * BLOCK, :].astype(F32)
        dq_s[at, :] = pair[:, :HEAD_DIM]
        dk_s[at, :] = pair[:, HEAD_DIM:]
        dv_s[at, :] = landed[device, 2 * BLOCK :, cols].astype(F32)
    in_order(q_s, dq_s)
    in_order(k_s, dk_s)
    in_order(v_s, dv_s)
    for stored in range(blocks):
        at, device, cols = stored_rows(stored)
        dq_s[at, :] = grad_landed[device, :, cols].astype(F32)
    in_order(do_s, dq_s)
    place_tiles(bias_lines, tiles)
    kt_s[...] = jnp.transpose(k_s[...].astype(F32), (1, 0)).astype(BF16)
    grad_t = jnp.transpose(do_s[...].astype(F32), (1, 0))
    delta_s[...] = jnp.sum(grad_t * sums[...], axis=0, keepdims=True)
    by_offset[...] = jnp.zeros_like(by_offset)
    dk_s[...] = jnp.zeros_like(dk_s)
    dv_s[...] = jnp.zeros_like(dv_s)
    for i in range(spans):
        at_i = slice(i * TILE, (i + 1) * TILE)
        queries, grads = q_s[at_i, :], do_s[at_i, :]
        norm_i, delta_i = norm[0:1, at_i], delta_s[0:1, at_i]
        dqt = jnp.zeros((HEAD_DIM, TILE), F32)
        for j in range(i + 1):
            at_j = slice(j * TILE, (j + 1) * TILE)
            exact = jnp.exp(dot_nt(k_s[at_j, :], queries) + tiles[i - j] - norm_i)
            dscore = exact * (dot_nt(v_s[at_j, :], grads) - delta_i)
            by_offset[i - j] += dscore
            rounded = dscore.astype(BF16)
            dv_s[at_j, :] += plain_dot(exact.astype(BF16), grads)
            dk_s[at_j, :] += plain_dot(rounded, queries)
            dqt = dqt + plain_dot(kt_s[:, at_j], rounded)
        dqt_s[:, at_i] = dqt
    dq_s[...] = jnp.transpose(dqt_s[...], (1, 0))
    for stored in range(blocks):
        device, half = stored // 2, stored % 2
        at = pl.ds(order[stored] * BLOCK, BLOCK)
        rows = slice(half * BLOCK, (half + 1) * BLOCK)
        cols = slice(half * HEAD_DIM, (half + 1) * HEAD_DIM)
        out_ref[device, rows, :HEAD_DIM] = dq_s[at, :].astype(BF16)
        out_ref[device, rows, HEAD_DIM:] = dk_s[at, :].astype(BF16)
        out_ref[device, 2 * BLOCK :, cols] = dv_s[at, :].astype(BF16)
    for apart in range(spans):
        folded = jnp.zeros((8, 2 * TILE), F32)
        for group in range(TILE // 8):
            rows = by_offset[apart, 8 * group : 8 * group + 8, :]
            wide = jnp.concatenate([rows, jnp.zeros((8, TILE), F32)], axis=1)
            folded = folded + (pltpu.roll(wide, 2 * TILE - 8 * group, 1) if group else wide)
        line = folded[0:1]
        for row in range(1, 8):
            line = line + pltpu.roll(folded[row : row + 1], 2 * TILE - row, 1)
        lines_ref[apart : apart + 1, :] = line


BIT_X, BIT_Y = 0, 1
FAR_LEFTS, FAR_RIGHTS = 2, 3


def pick(flag, when_set, when_clear):
    return jnp.where(flag == 1, when_set, when_clear)


UP, DOWN, ACROSS_Y, ACROSS_X = 0, 1, 2, 3


class Product:
    def __init__(self, left, right, first, tall, route):
        self.left, self.right, self.first, self.tall, self.route = left, right, first, tall, route


SUMMED = -1


def weight_grad_kernel(products, left_count, *refs):
    count = len(products)
    refs = list(refs)

    def take(number):
        taken = refs[:number]
        del refs[:number]
        return taken

    lefts, rights = take(left_count), take(count - 3)
    left_far, right_far = take(FAR_LEFTS), take(FAR_RIGHTS)
    (
        order,
        held_at,
        grad_rows,
        landed,
        attn_sum,
        log_norm,
        bias_lines,
        in_bucket,
        resid_in,
        gain_one,
        resid_grad,
        gains,
    ) = take(12)
    weights = take(10)
    wholes, (vec_out, input_grad, encoder_grad, kv_both) = take(count - 1), take(4)
    kv_at = [product.left for product in products].index(SUMMED)
    wholes.insert(kv_at, kv_both.at[0])
    left_all, left_pass, left_t = take(left_count), take(left_count), take(left_count)
    right_all, away, came, held, line_in = (take(count) for _ in range(5))
    rights += take(3)
    grad_packed, grad_landed, back_packed, back_landed, lines = take(5)
    attention_scratch = take(12)
    vec_in, vec_sums, vec_landed, weight_buffer, normed_grad = take(5)
    (
        left_send,
        left_own,
        left_recv,
        right_send,
        right_own,
        right_recv,
        pair_send,
        pair_recv,
        line_send,
        line_recv,
        out_send,
        out_recv,
        own_sem,
        vec_send,
        vec_recv,
        all_send,
        all_recv,
        all_own,
        kv_sem,
        weight_sem,
    ) = refs
    me, core = lax.axis_index("ctx"), lax.axis_index("wsh")
    peers = lax.axis_size("ctx")
    tokens = lefts[0].shape[0]
    x, y, z = lax.rem(me, 2), lax.rem(me // 2, 2), me // 4

    barrier = pltpu.get_barrier_semaphore()
    for step in range(1, peers):
        pl.semaphore_signal(
            barrier, inc=1, device_id=(lax.rem(me + step, peers), core), device_id_type=MESH
        )
    pl.semaphore_signal(barrier, inc=1, device_id=(me, 1 - core), device_id_type=MESH)
    for head in range(peers):
        cols = slice(head * HEAD_DIM, (head + 1) * HEAD_DIM)
        grad_packed[head] = jnp.concatenate(
            [grad_rows[:BLOCK, cols], grad_rows[BLOCK:, cols]], axis=1
        )
    pl.semaphore_wait(barrier, peers)

    def place(zz, yy, xx):
        return zz * 4 + yy * 2 + xx

    targets = {
        UP: place(lax.rem(z + 1, 4), y, x),
        DOWN: place(lax.rem(z + 3, 4), y, x),
        ACROSS_Y: place(z, 1 - y, x),
        ACROSS_X: place(z, y, 1 - x),
    }
    finish = []

    def remote(src, dst, send_sem, recv_sem, ctx, side):
        return pltpu.make_async_remote_copy(
            src_ref=src,
            dst_ref=dst,
            send_sem=send_sem,
            recv_sem=recv_sem,
            device_id=(ctx, side),
            device_id_type=MESH,
        )

    def launch(copy, only=None):
        if only is None:
            copy.start()
        else:
            pl.when(only)(copy.start)

    def arrived(ref, sem):
        remote(ref, ref, own_sem.at[0], sem, me, 1 - core).wait_recv()

    def left_here(ref, sem):
        finish.append(lambda: remote(ref, ref, sem, own_sem.at[0], me, 1 - core).wait_send())

    def lanes(ref, at, width):
        return ref.at[:, pl.ds(pl.multiple_of(at * width, 128), width)]

    def rows(ref, at, height):
        return ref.at[pl.ds(pl.multiple_of(at * height, 16), height)]

    def slot(ref, index):
        return ref.at[pl.ds(index * tokens, tokens)]

    def axes(product):
        along_x, along_y = (x, ACROSS_X), (y, ACROSS_Y)
        return (along_x, along_y) if product.first == BIT_X else (along_y, along_x)

    left_axis = {product.left: product for product in products}
    far_rights = [at for at in range(count) if 0 <= products[at].left < FAR_LEFTS]

    def local(src, dst, sem):
        copy = pltpu.make_async_copy(src, dst, sem)
        copy.start()
        return copy

    def send_left(at):
        (_, way), _ = axes(left_axis[at])
        half = left_all[at].shape[1]
        send_sem, recv_sem = left_send.at[at], left_recv.at[at]
        mine, others = lanes(lefts[at], core, half), lanes(lefts[at], 1 - core, half)
        copies = [local(mine, slot(left_all[at], 0), left_own.at[at])]
        launch(remote(others, slot(left_all[at], 2), send_sem, recv_sem.at[2], me, 1 - core))
        if at < FAR_LEFTS:
            far_mine, far_others = lanes(left_far[at], core, half), lanes(left_far[at], 1 - core, half)
            copies.append(local(far_mine, slot(left_all[at], 1), left_own.at[at]))
            launch(remote(far_others, slot(left_all[at], 3), send_sem, recv_sem.at[3], me, 1 - core))
            left_here(left_all[at].at[: 2 * tokens], send_sem)
        else:
            launch(remote(mine, slot(left_all[at], 1), send_sem, recv_sem.at[0], targets[way], core))
            launch(remote(others, left_pass[at], send_sem, recv_sem.at[1], targets[way], core))
            left_here(left_all[at], send_sem)
        return left_all[at].at[: len(copies) * tokens], left_own.at[at]

    def send_right(at):
        (mine, way), _ = axes(products[at])
        half = right_all[at].shape[1]
        send_sem, recv_sem = right_send.at[at], right_recv.at[at]
        own, others = lanes(rights[at], mine, half), lanes(rights[at], 1 - mine, half)
        if products[at].left == SUMMED:
            launch(remote(others, right_all[at], send_sem, recv_sem.at[0], targets[way], core))
            left_here(right_all[at], send_sem)
            return None
        copies = [local(own, slot(right_all[at], 0), right_own.at[at])]
        launch(remote(own, slot(right_all[at], 2), send_sem, recv_sem.at[1], me, 1 - core))
        if at in far_rights:
            far = right_far[far_rights.index(at)]
            copies.append(local(far, slot(right_all[at], 1), right_own.at[at]))
            launch(remote(far, slot(right_all[at], 3), send_sem, recv_sem.at[2], me, 1 - core))
            left_here(right_all[at].at[: 2 * tokens], send_sem)
        else:
            launch(remote(others, slot(right_all[at], 1), send_sem, recv_sem.at[0], targets[way], core))
            left_here(right_all[at].at[: 3 * tokens], send_sem)
        return right_all[at].at[: len(copies) * tokens], right_own.at[at]

    def to_all(which, source, target):
        for step in range(1, peers):
            peer = lax.rem(me + step, peers)
            launch(remote(source.at[peer], target.at[me], all_send.at[which], all_recv.at[which], peer, core))
        own = local(source.at[me], target.at[me], all_own.at[which])
        left_here(source.at[1:], all_send.at[which])

        def wait():
            own.wait()
            arrived(target.at[1:], all_recv.at[which])

        return wait

    seen = set()
    owns = {}

    def send_operands(some):
        for at in some:
            left = products[at].left
            if left not in seen and left != SUMMED:
                seen.add(left)
                owns["left", left] = send_left(left)
            owns["right", at] = send_right(at)

    def own_slots(key):
        ref, sem = owns[key]
        pltpu.make_async_copy(ref, ref, sem).wait()

    def vector_step(step):
        if step == 0:
            source, ctx, side = vec_in.at[1 - core], me, 1 - core
        else:
            source, ctx, side = vec_sums.at[step - 1], me ^ (1 << (step - 1)), core
        launch(remote(source, vec_landed.at[step], vec_send.at[step], vec_recv.at[step], ctx, side))
        left_here(source, vec_send.at[step])

    def vector_add(step):
        arrived(vec_landed.at[step], vec_recv.at[step])
        total = (vec_sums[step - 1] if step else vec_in[core]) + vec_landed[step]
        if step < 4:
            vec_sums[step] = total
            vector_step(step + 1)
        else:
            vec_out[...] = total

    passed = set()

    def pass_on(at):
        left = products[at].left
        if left == SUMMED or at in far_rights:
            return
        if left not in passed:
            passed.add(left)
            arrived(slot(left_all[left], 1), left_recv.at[left, 0])
            arrived(left_pass[left], left_recv.at[left, 1])
            launch(remote(left_pass[left], slot(left_all[left], 3), left_send.at[left], left_recv.at[left, 3], me, 1 - core))
        arrived(slot(right_all[at], 1), right_recv.at[at, 0])
        launch(remote(slot(right_all[at], 1), slot(right_all[at], 3), right_send.at[at], right_recv.at[at, 2], me, 1 - core))

    def multiply(at, out, half):
        product = products[at]
        left, right = left_t[product.left], right_all[at]
        height, width = out.shape
        step = 256 if height <= 256 else 128 if height % 256 else 256
        if product.tall:
            columns = pl.ds(pl.multiple_of(half * width, 128), width)

            def strip(index, carry):
                band = pl.ds(pl.multiple_of(index * 176, 16), 176)
                out[band, :] = plain_dot(left[band, :], right[:, columns]).astype(BF16)
                return carry

            lax.fori_loop(0, height // 176, strip, 0)
        else:
            band = pl.ds(pl.multiple_of(half * height, 16), height)

            def strip(index, carry):
                columns = pl.ds(pl.multiple_of(index * 256, 128), 256)
                out[:, columns] = plain_dot(left[band, :], right[:, columns]).astype(BF16)
                return carry

            lax.fori_loop(0, width // 256, strip, 0)
            if width % 256:
                out[:, width - 128 :] = plain_dot(left[band, :], right[:, width - 128 :]).astype(BF16)

    turned = set()

    def product_away(at):
        left = products[at].left
        _, (mine, way) = axes(products[at])
        if left == SUMMED:
            (first_mine, _), _ = axes(products[at])
            arrived(right_all[at], right_recv.at[at, 0])
            height = held[at].shape[0]
            for out, half in ((away[at], 1 - mine), (held[at], mine)):
                own = lanes(rows(rights[at], half, height), first_mine, held[at].shape[1])
                out[...] = (own[...].astype(F32) + rows(right_all[at], half, height)[...].astype(F32)).astype(BF16)
            launch(remote(away[at], came[at], pair_send.at[at], pair_recv.at[at], targets[way], core))
            left_here(away[at], pair_send.at[at])
            return
        if left not in turned:
            turned.add(left)
            arrived(slot(left_all[left], 2), left_recv.at[left, 2])
            arrived(slot(left_all[left], 3), left_recv.at[left, 3])
            own_slots(("left", left))
            height = left_t[left].shape[0]

            def turn(index, carry):
                band = pl.ds(pl.multiple_of(index * 128, 128), 128)
                left_t[left][band, :] = jnp.transpose(left_all[left][:, band], (1, 0))
                return carry

            lax.fori_loop(0, height // 128, turn, 0)
        arrived(slot(right_all[at], 2), right_recv.at[at, 1])
        arrived(slot(right_all[at], 3), right_recv.at[at, 2])
        own_slots(("right", at))
        multiply(at, away[at], 1 - mine)
        launch(remote(away[at], came[at], pair_send.at[at], pair_recv.at[at], targets[way], core))
        left_here(away[at], pair_send.at[at])
        multiply(at, held[at], mine)

    def add(into, more):
        into[...] = (into[...].astype(F32) + more[...].astype(F32)).astype(BF16)

    def add_pair(at):
        arrived(came[at], pair_recv.at[at])
        add(held[at], came[at])

    def line_step(at, step):
        height = held[at].shape[0] // 4
        for side, behind, chunk, way in (
            (0, z, lax.rem(z + 3 - step, 4), UP),
            (1, 3 - z, lax.rem(z + step + 1, 4), DOWN),
        ):
            recv_sem = line_recv.at[at, side, lax.rem(chunk + 2, 3) if side == 0 else lax.rem(chunk, 3)]
            landing = rows(line_in[at], chunk + 1 - side, height)

            def land(landing=landing, chunk=chunk, recv_sem=recv_sem):
                arrived(landing, recv_sem)
                add(rows(held[at], chunk, height), landing)

            pl.when(jnp.logical_and(behind > 0, behind <= step))(land)
            if step < 3:
                launch(
                    remote(
                        rows(held[at], chunk, height),
                        landing,
                        line_send.at[at],
                        recv_sem,
                        targets[way],
                        core,
                    ),
                    only=behind <= step,
                )
        if step == 3:
            left_here(held[at].at[: 3 * height], line_send.at[at])

    def own_piece(at):
        return rows(held[at], z, held[at].shape[0] // 4)

    def window(at, where):
        product = products[at]
        height, width = held[at].shape
        height //= 4
        xx, yy, zz = lax.rem(where, 2), lax.rem(where // 2, 2), where // 4
        one, two = (xx, yy) if product.first == BIT_X else (yy, xx)
        row, column = (zz, one * 2 + two) if product.tall else (two * 4 + zz, one)
        return wholes[at].at[
            pl.ds(pl.multiple_of(row * height, 16), height),
            pl.ds(pl.multiple_of(column * width, 128), width),
        ]

    def send(at, where, way, arrival, only=None, own=False):
        launch(
            remote(
                own_piece(at) if own else window(at, where),
                window(at, where),
                out_send.at[at, min(way, ACROSS_Y)],
                out_recv.at[at, arrival],
                targets[way],
                core,
            ),
            only,
        )

    def arrive(at, where, arrival, only=None):
        def act():
            arrived(window(at, where), out_recv.at[at, arrival])

        if only is None:
            act()
        else:
            pl.when(only)(act)

    def quarters(at, number):
        return wholes[at].at[: wholes[at].shape[0] // 4 * number]

    def near(way, zz):
        return place(zz, 1 - y, x) if way == ACROSS_Y else place(zz, y, 1 - x)

    def opposite(zz):
        return place(zz, 1 - y, 1 - x)

    def from_line(apart):
        return (
            (z >= apart, lax.rem(z + 4 - apart, 4), UP, jnp.logical_and(z >= apart, z < 3)),
            (z + apart <= 3, lax.rem(z + apart, 4), DOWN, jnp.logical_and(z + apart <= 3, z > 0)),
        )

    def line_sent(at, piece_groups):
        for number in (1, 2, 3):
            for way, here in ((UP, z == number - 1), (DOWN, z == 4 - number)):
                ref, sem = piece_groups(number), out_send.at[at, way]
                finish.append(
                    functools.partial(
                        pl.when(here),
                        lambda ref=ref, sem=sem: remote(ref, ref, sem, own_sem.at[0], me, 1 - core).wait_send(),
                    )
                )

    def gather_step(at, step):
        z_first, second, third = products[at].route
        if step == 0:
            owns["piece", at] = local(own_piece(at), window(at, me), own_sem.at[at])
            if at != kv_at:
                finish.append(owns["piece", at].wait)
            if z_first:
                send(at, me, UP, z, z < 3, own=True)
                send(at, me, DOWN, z, z > 0, own=True)
                send(at, me, second, 4 + z, own=True)
                send(at, me, third, 8, own=True)
                left_here(quarters(at, 3), out_send.at[at, ACROSS_Y])
                line_sent(at, lambda number: held[at].at[: held[at].shape[0] // 4 * number])
            else:
                send(at, me, second, 0, own=True)
                send(at, me, third, 1, own=True)
                send(at, me, UP, 4 + z, z < 3, own=True)
                send(at, me, DOWN, 4 + z, z > 0, own=True)
                left_here(held[at].at[: held[at].shape[0] // 4 * 3], out_send.at[at, ACROSS_Y])
                line_sent(at, lambda number: quarters(at, number))
        elif z_first:
            if step <= 3:
                for there, zz, way, on in from_line(step):
                    where = place(zz, y, x)
                    arrive(at, where, zz, there)
                    send(at, where, way, zz, on)
                    send(at, where, second, 4 + zz, there)
                    send(at, where, third, 8, there)
            elif step <= 7:
                zz = z ^ (step - 4)
                where = near(second, zz)
                arrive(at, where, 4 + zz)
                send(at, where, third, 8)
            elif step == 8:
                arrived(quarters(at, 2), out_recv.at[at, 8])
        else:
            if step == 1:
                where = near(second, z)
                arrive(at, where, 0)
                send(at, where, third, 2)
                send(at, where, UP, 4 + z, z < 3)
                send(at, where, DOWN, 4 + z, z > 0)
            elif step == 2:
                for arrival, where in ((1, near(third, z)), (2, opposite(z))):
                    arrive(at, where, arrival)
                    send(at, where, UP, 4 + z, z < 3)
                    send(at, where, DOWN, 4 + z, z > 0)
            elif step <= 5:
                for there, zz, way, on in from_line(step - 2):
                    pl.when(there)(
                        functools.partial(arrived, quarters(at, 1), out_recv.at[at, 4 + zz])
                    )
                    for where in (place(zz, y, x), near(second, zz), near(third, zz), opposite(zz)):
                        send(at, where, way, 4 + zz, on)

    def reduce_step(at, step):
        if step == 0:
            add_pair(at)
        if step < 4:
            line_step(at, step)
        else:
            gather_step(at, 0)

    def load_weight(index):
        return pltpu.make_async_copy(
            weights[index], weight_buffer.at[index % 2], weight_sem.at[index % 2]
        )

    def input_gradient():
        load_weight(0).start()
        for index in range(6):
            load_weight(index + 1).start()
            load_weight(index).wait()
            columns = lanes(normed_grad, core if index < 3 else 1 - core, normed_grad.shape[1] // 2)
            term = dot_nt(rights[count - 3 + index % 3][...], weight_buffer[index % 2])
            if index % 3:
                columns[...] += term
            else:
                columns[...] = term
        width = resid_in.shape[1]
        cotan, values = normed_grad[...], resid_in[...]
        rate = lax.rsqrt(jnp.mean(values * values, axis=1, keepdims=True) + EPSILON)
        scaled = cotan * gain_one[...]
        slope = jnp.mean(scaled * values, axis=1, keepdims=True)
        back = rate * scaled - values * (rate * rate * rate) * slope
        input_grad[...] = (resid_grad[...] + back).astype(BF16)
        gain_grad = jnp.sum(cotan * values * rate, axis=0, keepdims=True)
        column = jnp.zeros((BUCKETS, 1), F32)
        for apart in range(lines.shape[0]):
            sums = lines[apart : apart + 1, :TILE]
            if apart + 1 < lines.shape[0]:
                sums = sums + lines[apart + 1 : apart + 2, TILE:]
            column = column + jnp.sum(in_bucket[apart] * sums, axis=1, keepdims=True)
        place_at = lax.broadcasted_iota(jnp.int32, (BUCKETS, 128), 1)
        table = jnp.where(place_at == me, column, 0.0)
        for half in range(2):
            for index in range(4):
                start = (4 * half + index) * 128
                vec_in[half, index : index + 1, :] = gain_grad[:, start : start + 128]
            vec_in[half, 4:16, :] = gains[half]
            vec_in[half, 16:, :] = table[half * (BUCKETS // 2) : (half + 1) * (BUCKETS // 2)]
        vector_step(0)

    def encoder_gradient():
        own = kv_both[0, pl.ds(pl.multiple_of(me * encoder_grad.shape[0], 16), encoder_grad.shape[0]), :]
        width = own.shape[1] // 2
        for side in (0, 1):
            terms = []
            for index in (6 + 2 * side, 7 + 2 * side):
                if index < 9:
                    load_weight(index + 1).start()
                load_weight(index).wait()
                part = slice((index % 2) * width, (index % 2 + 1) * width)
                terms.append(dot_nt(own[:, part], weight_buffer[index % 2]))
            columns = lanes(encoder_grad, core if side == 0 else 1 - core, width // 2)
            columns[...] = (terms[0] + terms[1]).astype(BF16)

    early, late = range(count - 3), range(count - 3, count)
    near_by = [at for at in early if at in far_rights]
    others = [at for at in early if at not in far_rights]

    def wave(some):
        for time in range(len(some) + 4):
            for step in range(5):
                if 0 <= time - step < len(some):
                    reduce_step(some[time - step], step)
            yield

    def gather_all(some, step):
        for at in some:
            gather_step(at, step)

    def slots(of, number):
        for _ in range(number):
            next(of, None)

    grad_arrival = to_all(0, grad_packed, grad_landed)
    send_operands(near_by)
    for at in near_by:
        product_away(at)
    grad_arrival()
    attend_back(
        order, held_at, landed, grad_landed, attn_sum, log_norm, bias_lines, back_packed, lines,
        *attention_scratch,
    )
    back_arrival = to_all(1, back_packed, back_landed)
    send_operands(others)
    near_wave, other_wave, late_wave = wave(near_by), wave(others), wave(list(late))
    slots(near_wave, 4)
    back_arrival()
    dq_ref, dk_ref, dv_ref = rights[count - 3 :]
    for pair in range(peers // 2):
        cols = slice(pair * 2 * HEAD_DIM, (pair + 1) * 2 * HEAD_DIM)
        dq_ref[:, cols], dk_ref[:, cols] = unpack_pair(back_landed, pair, slice(0, 2 * BLOCK))
        first, second = unpack_pair(back_landed, pair, slice(2 * BLOCK, 3 * BLOCK))
        dv_ref[:BLOCK, cols] = first
        dv_ref[BLOCK:, cols] = second
    send_operands(late)
    slots(near_wave, 4)
    for index, at in enumerate(others):
        pass_on(at)
        if index:
            product_away(others[index - 1])
    product_away(others[-1])
    gather_all(near_by, 1)
    input_gradient()
    gather_all(near_by, 2)
    slots(other_wave, 2)
    for at in late:
        pass_on(at)
    for at in late:
        product_away(at)
    vector_add(0)
    gather_all(near_by, 3)
    slots(other_wave, 3)
    gather_all(near_by, 4)
    vector_add(1)
    slots(late_wave, 1)
    slots(other_wave, 3)
    slots(late_wave, 1)
    gather_all(near_by, 5)
    gather_all(others, 1)
    slots(late_wave, 1)
    vector_add(2)
    gather_all(near_by, 6)
    gather_all(others, 2)
    slots(late_wave, 1)
    vector_add(3)
    slots(late_wave, 1)
    gather_all(near_by, 7)
    gather_all(others, 3)
    slots(late_wave, 1)
    slots(late_wave, 1)
    vector_add(4)
    gather_all(late, 1)
    gather_all(others, 4)
    gather_all(late, 2)
    gather_all(others, 5)
    gather_all(late, 3)
    owns["piece", kv_at].wait()
    launch(remote(kv_both.at[0], kv_both.at[1], kv_sem.at[0], kv_sem.at[1], me, 1 - core))
    left_here(kv_both.at[0], kv_sem.at[0])
    encoder_gradient()
    for step in range(4, 9):
        gather_all(late, step)
    gather_all(near_by, 8)
    arrived(kv_both.at[1], kv_sem.at[1])
    for each in finish:
        each()


def weight_grads(products, lefts, rights, left_far, right_far, others, weights):
    count, peers = len(products), lax.axis_size("ctx")
    tokens = lefts[0].shape[0]
    length = others[4].shape[1]
    kv_at = [product.left for product in products].index(SUMMED)
    kv_rows, kv_width = rights[kv_at].shape
    spans = length // TILE
    dma = pltpu.SemaphoreType.DMA
    vmem = pltpu.VMEM
    width = HEADS * HEAD_DIM
    halves = [left.shape[1] // 2 for left in lefts]
    widths = [right.shape[1] for right in rights] + [width] * 3
    helds = []
    for product, right in zip(products, widths):
        height = kv_rows if product.left == SUMMED else halves[product.left]
        helds.append((height, right // 4) if product.tall else (height // 2, right // 2))
    lands = [vmem(shape, BF16) for shape in helds]
    chunk = (peers, BLOCK, 2 * HEAD_DIM)
    chunks = (peers, 3 * BLOCK, 2 * HEAD_DIM)
    smem_spec = pl.BlockSpec(memory_space=pltpu.SMEM)
    return pl.pallas_call(
        functools.partial(weight_grad_kernel, products, len(lefts)),
        out_shape=[
            jax.ShapeDtypeStruct((halves[product.left], right), BF16)
            for product, right in zip(products, widths)
            if product.left != SUMMED
        ]
        + [
            jax.ShapeDtypeStruct((32, 128), F32),
            jax.ShapeDtypeStruct((tokens, width), BF16),
            jax.ShapeDtypeStruct((kv_rows // peers, width), BF16),
            jax.ShapeDtypeStruct((2, kv_rows, kv_width), BF16),
        ],
        in_specs=[any_spec()] * len(lefts)
        + [vmem_spec() if product.left == SUMMED else any_spec() for product in products[: len(rights)]]
        + [any_spec()] * (len(left_far) + len(right_far))
        + [smem_spec] * 2
        + [vmem_spec()] * (len(others) - 2)
        + [any_spec()] * len(weights),
        out_specs=[any_spec()] * (count - 1) + [vmem_spec()] * 4,
        scratch_shapes=[vmem((4 * tokens, half), BF16) for half in halves]
        + [vmem((tokens, half), BF16) for half in halves]
        + [vmem((half, 4 * tokens), BF16) for half in halves]
        + [
            vmem((kv_rows if product.left == SUMMED else 4 * tokens, right // 2), BF16)
            for product, right in zip(products, widths)
        ]
        + lands * 3
        + [vmem((5 * height // 4, width_held), BF16) for height, width_held in helds]
        + [vmem((tokens, width), BF16)] * 3
        + [vmem(chunk, BF16), vmem(chunk, BF16), vmem(chunks, BF16), vmem(chunks, BF16)]
        + [vmem((spans, 2 * TILE), F32)]
        + [vmem((length, HEAD_DIM), BF16)] * 4
        + [vmem((HEAD_DIM, length), BF16)]
        + [vmem((spans, TILE, TILE), F32)] * 2
        + [vmem((length, HEAD_DIM), F32)] * 3
        + [vmem((1, length), F32), vmem((HEAD_DIM, length), F32)]
        + [
            vmem((2, 32, 128), F32),
            vmem((4, 32, 128), F32),
            vmem((5, 32, 128), F32),
            vmem((2,) + weights[0].shape, BF16),
            vmem((tokens, width), F32),
        ]
        + [
            dma((len(lefts),)),
            dma((len(lefts),)),
            dma((len(lefts), 4)),
            dma((count,)),
            dma((count,)),
            dma((count, 3)),
            dma((count,)),
            dma((count,)),
            dma((count,)),
            dma((count, 2, 3)),
            dma((count, 3)),
            dma((count, 9)),
            dma((count,)),
            dma((5,)),
            dma((5,)),
            dma((2,)),
            dma((2,)),
            dma((2,)),
            dma((2,)),
            dma((2,)),
        ],
        compiler_params=pltpu.CompilerParams(
            collective_id=5, has_side_effects=True, vmem_limit_bytes=60 * MIB
        ),
        name="weight_grads",
    )(*lefts, *rights, *left_far, *right_far, *others, *weights)


def on_device_by_heads(
    inputs,
    encoder,
    cotangent,
    block_order,
    bucket_of,
    self_gain,
    query_weight,
    key_weight,
    value_weight,
    out_weight,
    bias_table,
    cross_gain,
    cross_query,
    cross_key,
    cross_value,
    cross_out,
    mlp_gain,
    gate_weight,
    up_weight,
    down_weight,
):
    core, me = lax.axis_index("wsh"), lax.axis_index("ctx")

    def swap(values):
        return lax.ppermute(values, "wsh", [(0, 1), (1, 0)])

    def along_x(values):
        return lax.ppermute(values, "ctx", [(at, at ^ 1) for at in range(HEADS)])

    def along_y(values):
        return lax.ppermute(values, "ctx", [(at, at ^ 2) for at in range(HEADS)])

    def other_column(values, bit):
        half = values.shape[1] // 2
        return pick(bit & 1, values[:, :half], values[:, half:])

    def own_half(values):
        half = values.shape[-1] // 2
        return pick(core, values[..., half:], values[..., :half])

    def other_half(values):
        half = values.shape[-1] // 2
        return pick(core, values[..., :half], values[..., half:])

    def join(own, other, axis):
        return pick(
            core,
            jnp.concatenate([other, own], axis=axis),
            jnp.concatenate([own, other], axis=axis),
        )

    def times(values, pair):
        return plain_dot(own_half(values), pair[0]) + plain_dot(other_half(values), pair[1])

    def times_back(values, pair):
        return join(right_contract(values, pair[0]), right_contract(values, pair[1]), 1)

    def both_cores(values):
        return jnp.concatenate([own_half(values), swap(other_half(values))], axis=0)

    small = jnp.concatenate([self_gain, cross_gain, mlp_gain, bias_table.reshape(-1)])
    small_other = swap(small)
    width = self_gain.shape[0]
    gain_one, gain_two, gain_three = (
        join(small[at * width : (at + 1) * width], small_other[at * width : (at + 1) * width], 0).astype(F32)
        for at in range(3)
    )
    bias_rows = join(bias_table, small_other[3 * width :].reshape(bias_table.shape), 0).astype(F32)
    query_pair, key_pair, value_pair = (
        (member, swap(member)) for member in (query_weight, key_weight, value_weight)
    )
    out_pair, cross_query_pair, cross_key_pair, cross_value_pair, cross_out_pair = (
        (member, swap(member))
        for member in (out_weight, cross_query, cross_key, cross_value, cross_out)
    )
    gate_pair, up_pair, down_pair = (
        (member, swap(member)) for member in (gate_weight, up_weight, down_weight)
    )

    resid_in = inputs[0].astype(F32)
    tokens = resid_in.shape[0]
    head_width = HEADS * HEAD_DIM
    length = bucket_of.shape[0]

    normed_one = rms_norm(resid_in, gain_one).astype(BF16)
    queries = times(normed_one, query_pair).astype(BF16)
    keys = times(normed_one, key_pair).astype(BF16)
    values = times(normed_one, value_pair).astype(BF16)
    landed, encoder_all = to_heads(queries, keys, values, encoder[0])
    encoder_all = encoder_all.reshape(-1, encoder.shape[2])

    own_column = jnp.sum(
        jnp.where(jnp.arange(HEADS)[None, :] == me, bias_rows, 0.0), axis=1, keepdims=True
    )
    in_bucket = bucket_of[None, :] == jnp.arange(BUCKETS, dtype=jnp.int32)[:, None]
    by_offset = jnp.sum(jnp.where(in_bucket, own_column, 0.0), axis=0).reshape(-1, TILE)
    before = jnp.concatenate([jnp.full((1, TILE), NEG_BIG, F32), by_offset[:-1]], axis=0)
    bias_lines = jnp.concatenate([by_offset, before], axis=1)

    mixed_packed, attn_sum, log_norm = attend(block_order, landed, bias_lines)
    attended = from_heads(mixed_packed)

    after_self = resid_in + times(attended, out_pair)
    normed_two = rms_norm(after_self, gain_two).astype(BF16)
    cross_q_heads = times(normed_two, cross_query_pair).astype(BF16).reshape(tokens, HEADS, HEAD_DIM)
    cross_k_heads = times(encoder_all, cross_key_pair).astype(BF16).reshape(-1, HEADS, HEAD_DIM)
    cross_v_heads = times(encoder_all, cross_value_pair).astype(BF16).reshape(-1, HEADS, HEAD_DIM)
    cross_logits = jnp.einsum(
        "qhe,khe->hqk", cross_q_heads, cross_k_heads, preferred_element_type=F32
    )
    cross_exact = jnp.exp(cross_logits - jax.nn.logsumexp(cross_logits, axis=-1, keepdims=True))
    cross_probs = cross_exact.astype(BF16)
    cross_mixed = (
        jnp.einsum("hqk,khe->qhe", cross_probs, cross_v_heads, preferred_element_type=F32)
        .reshape(tokens, head_width)
        .astype(BF16)
    )
    after_cross = after_self + times(cross_mixed, cross_out_pair)
    normed_three = rms_norm(after_cross, gain_three).astype(BF16)
    gate_act = times(normed_three, gate_pair)
    up_act = times(normed_three, up_pair)
    hidden_float, mlp_pull = jax.vjp(gelu_product, gate_act, up_act)
    hidden = hidden_float.astype(BF16)
    result = (after_cross + times(hidden, down_pair)).astype(BF16)

    resid_grad = cotangent[0].astype(F32)
    branch_three = cotangent[0]
    gate_grad, up_grad = mlp_pull(times_back(branch_three, down_pair))
    gate_grad, up_grad = gate_grad.astype(BF16), up_grad.astype(BF16)
    normed_three_grad = times_back(gate_grad, gate_pair) + times_back(up_grad, up_pair)
    part_grad, gain_three_grad = norm_back(after_cross, gain_three, normed_three_grad)
    after_cross_grad = resid_grad + part_grad
    branch_two = after_cross_grad.astype(BF16)
    mix_grad = times_back(branch_two, cross_out_pair).astype(BF16).reshape(tokens, HEADS, HEAD_DIM)
    cross_score_grad = jnp.einsum(
        "qhe,khe->hqk", mix_grad, cross_v_heads, preferred_element_type=F32
    )
    cross_delta = jnp.sum(cross_exact * cross_score_grad, axis=-1, keepdims=True)
    cross_dlogits = (cross_exact * (cross_score_grad - cross_delta)).astype(BF16)
    cross_q_grad = (
        jnp.einsum("hqk,khe->qhe", cross_dlogits, cross_k_heads, preferred_element_type=F32)
        .reshape(tokens, head_width)
        .astype(BF16)
    )
    cross_k_part = jnp.einsum(
        "hqk,qhe->khe", cross_dlogits, cross_q_heads, preferred_element_type=F32
    ).reshape(-1, head_width)
    cross_v_part = jnp.einsum(
        "hqk,qhe->khe", cross_probs, mix_grad, preferred_element_type=F32
    ).reshape(-1, head_width)
    cross_kv_part = jnp.concatenate([cross_k_part, cross_v_part], axis=1).astype(BF16)
    normed_two_grad = times_back(cross_q_grad, cross_query_pair)
    part_grad, gain_two_grad = norm_back(after_self, gain_two, normed_two_grad)
    after_self_grad = after_cross_grad + part_grad
    branch_one = after_self_grad.astype(BF16)
    dattn = times_back(branch_one, out_pair).astype(BF16)
    block_ids = jnp.arange(block_order.shape[0], dtype=jnp.int32)
    held_at = jnp.sum(
        jnp.where(block_order[None, :] == block_ids[:, None], block_ids[None, :], 0), axis=1
    )
    gains = jnp.concatenate(
        [gain_two_grad.reshape(2, 4, 128), gain_three_grad.reshape(2, 4, 128), jnp.zeros((2, 4, 128), F32)],
        axis=1,
    )
    bucket_tiles = in_bucket.astype(F32).reshape(BUCKETS, -1, TILE).transpose(1, 0, 2)

    z_then_yx, z_then_xy, z_last = (
        (True, ACROSS_Y, ACROSS_X),
        (True, ACROSS_X, ACROSS_Y),
        (False, ACROSS_Y, ACROSS_X),
    )
    lefts = (normed_three, hidden, cross_mixed, normed_two, attended, normed_one)
    products = (
        Product(0, gate_grad, BIT_Y, False, z_then_yx),
        Product(1, branch_three, BIT_X, True, z_then_yx),
        Product(0, up_grad, BIT_Y, False, z_then_xy),
        Product(SUMMED, cross_kv_part, BIT_X, False, z_last),
        Product(2, branch_two, BIT_X, False, z_last),
        Product(3, cross_q_grad, BIT_Y, False, z_last),
        Product(4, branch_one, BIT_Y, False, z_last),
        Product(5, None, BIT_X, False, z_then_xy),
        Product(5, None, BIT_X, False, z_then_xy),
        Product(5, None, BIT_X, False, z_then_xy),
    )
    *wholes, totals, input_grad, encoder_grad, cross_kv_both = weight_grads(
        products,
        lefts,
        [product.right for product in products[:7]],
        (along_y(normed_three), along_x(hidden)),
        (along_y(other_column(gate_grad, me >> 1)), along_x(other_column(branch_three, me)), along_y(other_column(up_grad, me >> 1))),
        (
            block_order,
            held_at,
            dattn,
            landed,
            attn_sum,
            log_norm,
            bias_lines,
            bucket_tiles,
            resid_in,
            gain_one[None, :],
            after_self_grad,
            gains,
        ),
        [pair[0] for pair in (query_pair, key_pair, value_pair)]
        + [pair[1] for pair in (query_pair, key_pair, value_pair)]
        + [cross_key_pair[0], cross_value_pair[0], cross_key_pair[1], cross_value_pair[1]],
    )
    cross_kv_w_grad = left_contract(
        both_cores(encoder_all), cross_kv_both.reshape(-1, 2 * head_width)
    )
    (
        sum_gate,
        sum_down,
        sum_up,
        sum_cross_out,
        sum_cross_query,
        sum_out,
        sum_query,
        sum_key,
        sum_value,
    ) = (member.astype(F32) for member in wholes)
    sum_gain_one, sum_gain_two, sum_gain_three = (
        totals[4 * at : 4 * at + 4].reshape(-1) for at in range(3)
    )
    sum_table = totals[16:, :HEADS]
    return (
        result[None],
        input_grad[None],
        encoder_grad[None],
        sum_gain_one,
        sum_query,
        sum_key,
        sum_value,
        sum_out,
        sum_table,
        sum_gain_two,
        sum_cross_query,
        cross_kv_w_grad[:, :head_width],
        cross_kv_w_grad[:, head_width:],
        sum_cross_out,
        sum_gain_three,
        sum_gate,
        sum_up,
        sum_down,
    )


def solution(mesh):
    by_heads = mesh.shape["ctx"] == HEADS and mesh.shape["wsh"] == 2
    return jax.shard_map(
        on_device_by_heads if by_heads else on_device,
        mesh=mesh,
        in_specs=(
            P("wsh", "ctx", None),
            P("wsh", "ctx", None),
            P("wsh", "ctx", None),
            P(),
            P(),
            P("wsh"),
            P("wsh", None),
            P("wsh", None),
            P("wsh", None),
            P("wsh", None),
            P("wsh", None),
            P("wsh"),
            P("wsh", None),
            P("wsh", None),
            P("wsh", None),
            P("wsh", None),
            P("wsh"),
            P("wsh", None),
            P("wsh", None),
            P("wsh", None),
        ),
        out_specs=(
            P("wsh", "ctx", None),
            P("wsh", "ctx", None),
            P("wsh", "ctx", None),
            P("wsh"),
            P("wsh", None),
            P("wsh", None),
            P("wsh", None),
            P("wsh", None),
            P("wsh", None),
            P("wsh"),
            P("wsh", None),
            P("wsh", None),
            P("wsh", None),
            P("wsh", None),
            P("wsh"),
            P("wsh", None),
            P("wsh", None),
            P("wsh", None),
        ),
        check_vma=False,
    )
```

```python
import functools
from typing import Any, NamedTuple

import jax
import jax.numpy as jnp
from jax import lax
from jax.experimental import pallas as pl
from jax.experimental.pallas import tpu as pltpu
from jax.sharding import PartitionSpec as P

HEADS = 16
HEAD_DIM = 64
BUCKETS = 32


EPSILON = 1e-06
NEG_BIG = -1e30


def rms_norm(values, gain):
    return values * lax.rsqrt(jnp.mean(values * values, axis=-1, keepdims=True) + EPSILON) * gain


def plain_dot(left, right):
    return jnp.dot(left, right, preferred_element_type=jnp.float32)


def left_contract(left, right):
    return lax.dot_general(
        left, right, (((0,), (0,)), ((), ())), preferred_element_type=jnp.float32
    )


def right_contract(left, right):
    return lax.dot_general(
        left, right, (((1,), (1,)), ((), ())), preferred_element_type=jnp.float32
    )


def gelu_product(gate_vals, up_vals):
    return jax.nn.gelu(gate_vals, approximate=True) * up_vals


def norm_back(values, gain, cotan):
    normed, pullback = jax.vjp(rms_norm, values, gain)
    return pullback(cotan)


def lookup_positions(block_order, first_row, row_count, block_len):
    token_ids = first_row + jnp.arange(row_count, dtype=jnp.int32)
    block_ids = token_ids // block_len
    matches = block_ids[:, None] == jnp.arange(block_order.shape[0], dtype=jnp.int32)[None, :]
    starts = jnp.sum(jnp.where(matches, block_order[None, :], 0), axis=1)
    return starts * block_len + token_ids % block_len


def fold_groups(step_fn, carried, pieces, shard_rows):
    piece_rows = pieces[0].shape[0]
    shards = max(1, piece_rows // shard_rows)
    group_limit = max(1, 1152 // shard_rows)
    group_size = max(
        (divisor for divisor in range(1, min(shards, group_limit) + 1) if shards % divisor == 0)
    )
    group_rows = group_size * shard_rows

    def group_step(group_idx, inner_state):
        sub_pieces = tuple(
            (
                lax.dynamic_slice_in_dim(member, group_idx * group_rows, group_rows, 0)
                for member in pieces
            )
        )
        return step_fn(inner_state, sub_pieces, group_idx * group_rows)

    return lax.fori_loop(0, shards // group_size, group_step, carried)


def on_device(
    inputs,
    encoder,
    cotangent,
    block_order,
    bucket_of,
    self_gain,
    query_weight,
    key_weight,
    value_weight,
    out_weight,
    bias_table,
    cross_gain,
    cross_query,
    cross_key,
    cross_value,
    cross_out,
    mlp_gain,
    gate_weight,
    up_weight,
    down_weight,
):
    (
        gain_one,
        query_full,
        key_full,
        value_full,
        out_full,
        bias_rows,
        gain_two,
        cross_query_full,
        cross_key_full,
        cross_value_full,
        cross_out_full,
        gain_three,
        gate_full,
        up_full,
        down_full,
    ) = (
        lax.all_gather(self_gain, "wsh", axis=0, tiled=True),
        lax.all_gather(query_weight, "wsh", axis=0, tiled=True),
        lax.all_gather(key_weight, "wsh", axis=0, tiled=True),
        lax.all_gather(value_weight, "wsh", axis=0, tiled=True),
        lax.all_gather(out_weight, "wsh", axis=0, tiled=True),
        lax.all_gather(bias_table, "wsh", axis=0, tiled=True),
        lax.all_gather(cross_gain, "wsh", axis=0, tiled=True),
        lax.all_gather(cross_query, "wsh", axis=0, tiled=True),
        lax.all_gather(cross_key, "wsh", axis=0, tiled=True),
        lax.all_gather(cross_value, "wsh", axis=0, tiled=True),
        lax.all_gather(cross_out, "wsh", axis=0, tiled=True),
        lax.all_gather(mlp_gain, "wsh", axis=0, tiled=True),
        lax.all_gather(gate_weight, "wsh", axis=0, tiled=True),
        lax.all_gather(up_weight, "wsh", axis=0, tiled=True),
        lax.all_gather(down_weight, "wsh", axis=0, tiled=True),
    )
    gain_one = gain_one.astype(jnp.float32)
    gain_two = gain_two.astype(jnp.float32)
    gain_three = gain_three.astype(jnp.float32)
    resid_in = inputs[0].astype(jnp.float32)
    tokens = resid_in.shape[0]
    block_len = tokens // 2
    head_width = HEADS * HEAD_DIM
    total_rows = tokens * lax.axis_size("ctx")
    own_pos = lookup_positions(block_order, lax.axis_index("ctx") * tokens, tokens, block_len)
    bucket_ids = jnp.arange(BUCKETS, dtype=jnp.int32)
    boundaries = jnp.sum((bucket_of[None, :] < bucket_ids[1:, None]).astype(jnp.int32), axis=1)

    def bucket_indicator_of(clipped):
        bucket = jnp.sum((clipped[None] >= boundaries[:, None, None]).astype(jnp.int32), axis=0)
        return (bucket[None] == bucket_ids[:, None, None]).astype(jnp.bfloat16)

    def query_key_logits(query_heads, key_heads, query_pos, key_pos):
        logits = jnp.einsum(
            "qhe,khe->hqk", query_heads, key_heads, preferred_element_type=jnp.float32
        )
        offset = query_pos[:, None] - key_pos[None, :]
        clipped = jnp.maximum(offset, 0)
        indicator = bucket_indicator_of(clipped)
        rel_bias = jnp.einsum(
            "ouw,om->muw", indicator, bias_rows, preferred_element_type=jnp.float32
        )
        allowed = (offset >= 0)[None]
        return (jnp.where(allowed, logits + rel_bias, NEG_BIG), allowed, indicator)

    normed_one = rms_norm(resid_in, gain_one).astype(jnp.bfloat16)
    query_heads = (
        plain_dot(normed_one, query_full).astype(jnp.bfloat16).reshape(tokens, HEADS, HEAD_DIM)
    )
    key_heads = (
        plain_dot(normed_one, key_full).astype(jnp.bfloat16).reshape(tokens, HEADS, HEAD_DIM)
    )
    value_heads = (
        plain_dot(normed_one, value_full).astype(jnp.bfloat16).reshape(tokens, HEADS, HEAD_DIM)
    )

    def norm_step(carried, pieces, first_row):
        running_max, running_sum = carried
        key_pos = lookup_positions(block_order, first_row, pieces[0].shape[0], block_len)
        logits, allowed, indicator = query_key_logits(query_heads, pieces[0], own_pos, key_pos)
        new_max = jnp.maximum(running_max, jnp.max(logits, axis=-1))
        kept = jnp.where(allowed, jnp.exp(logits - new_max[..., None]), 0.0)
        return (new_max, running_sum * jnp.exp(running_max - new_max) + jnp.sum(kept, axis=-1))

    start_state = (
        jnp.full((HEADS, tokens), NEG_BIG, jnp.float32),
        jnp.zeros((HEADS, tokens), jnp.float32),
    )
    running_max, running_sum = fold_groups(
        norm_step, start_state, (lax.all_gather(key_heads, "ctx", axis=0, tiled=True),), tokens
    )
    log_norm = running_max + jnp.log(running_sum)

    def output_step(carried, pieces, first_row):
        key_pos = lookup_positions(block_order, first_row, pieces[0].shape[0], block_len)
        logits, allowed, indicator = query_key_logits(query_heads, pieces[0], own_pos, key_pos)
        attn_probs = jnp.exp(logits - log_norm[..., None]).astype(jnp.bfloat16)
        return carried + jnp.einsum(
            "hqk,khe->qhe", attn_probs, pieces[1], preferred_element_type=jnp.float32
        )

    zero_heads = jnp.zeros((tokens, HEADS, HEAD_DIM), jnp.float32)
    attn_sum = fold_groups(
        output_step,
        zero_heads,
        (
            lax.all_gather(key_heads, "ctx", axis=0, tiled=True),
            lax.all_gather(value_heads, "ctx", axis=0, tiled=True),
        ),
        tokens,
    )
    attended = attn_sum.reshape(tokens, head_width).astype(jnp.bfloat16)
    after_self = resid_in + plain_dot(attended, out_full)
    normed_two = rms_norm(after_self, gain_two).astype(jnp.bfloat16)
    cross_q_heads = (
        plain_dot(normed_two, cross_query_full)
        .astype(jnp.bfloat16)
        .reshape(tokens, HEADS, HEAD_DIM)
    )
    encoder_rows = encoder[0]
    encoder_key_rows, cross_values = (
        lax.all_gather(
            plain_dot(encoder_rows, cross_key_full).astype(jnp.bfloat16), "ctx", axis=0, tiled=True
        ),
        lax.all_gather(
            plain_dot(encoder_rows, cross_value_full).astype(jnp.bfloat16),
            "ctx",
            axis=0,
            tiled=True,
        ),
    )
    cross_k_heads = encoder_key_rows.reshape(encoder_key_rows.shape[0], HEADS, HEAD_DIM)
    cross_v_heads = cross_values.reshape(cross_values.shape[0], HEADS, HEAD_DIM)
    cross_logits = jnp.einsum(
        "qhe,khe->hqk", cross_q_heads, cross_k_heads, preferred_element_type=jnp.float32
    )
    cross_exact = jnp.exp(cross_logits - jax.nn.logsumexp(cross_logits, axis=-1, keepdims=True))
    cross_probs = cross_exact.astype(jnp.bfloat16)
    cross_mixed = (
        jnp.einsum("hqk,khe->qhe", cross_probs, cross_v_heads, preferred_element_type=jnp.float32)
        .reshape(tokens, head_width)
        .astype(jnp.bfloat16)
    )
    after_cross = after_self + plain_dot(cross_mixed, cross_out_full)
    normed_three = rms_norm(after_cross, gain_three).astype(jnp.bfloat16)
    gate_act = plain_dot(normed_three, gate_full)
    up_act = plain_dot(normed_three, up_full)
    hidden_float, mlp_pull = jax.vjp(gelu_product, gate_act, up_act)
    hidden = hidden_float.astype(jnp.bfloat16)
    result = after_cross + plain_dot(hidden, down_full)
    resid_grad = cotangent[0].astype(jnp.float32)
    branch_three = resid_grad.astype(jnp.bfloat16)
    down_grad = left_contract(hidden, branch_three)
    hidden_state_gradient = right_contract(branch_three, down_full)
    gate_grad, up_grad = mlp_pull(hidden_state_gradient)
    gate_grad = gate_grad.astype(jnp.bfloat16)
    up_grad = up_grad.astype(jnp.bfloat16)
    gate_w_grad = left_contract(normed_three, gate_grad)
    up_w_grad = left_contract(normed_three, up_grad)
    normed_three_grad = right_contract(gate_grad, gate_full) + right_contract(up_grad, up_full)
    part_grad, gain_three_grad = norm_back(after_cross, gain_three, normed_three_grad)
    after_cross_grad = resid_grad + part_grad
    branch_two = after_cross_grad.astype(jnp.bfloat16)
    cross_out_grad = left_contract(cross_mixed, branch_two)
    mix_grad = (
        right_contract(branch_two, cross_out_full)
        .astype(jnp.bfloat16)
        .reshape(tokens, HEADS, HEAD_DIM)
    )
    cross_score_grad = jnp.einsum(
        "qhe,khe->hqk", mix_grad, cross_v_heads, preferred_element_type=jnp.float32
    )
    cross_delta = jnp.sum(cross_exact * cross_score_grad, axis=-1, keepdims=True)
    cross_dlogits = (cross_exact * (cross_score_grad - cross_delta)).astype(jnp.bfloat16)
    cross_q_grad = (
        jnp.einsum("hqk,khe->qhe", cross_dlogits, cross_k_heads, preferred_element_type=jnp.float32)
        .reshape(tokens, head_width)
        .astype(jnp.bfloat16)
    )
    cross_k_part = jnp.einsum(
        "hqk,qhe->khe", cross_dlogits, cross_q_heads, preferred_element_type=jnp.float32
    ).reshape(-1, head_width)
    cross_v_part = jnp.einsum(
        "hqk,qhe->khe", cross_probs, mix_grad, preferred_element_type=jnp.float32
    ).reshape(-1, head_width)
    cross_k_grad, cross_v_grad = (
        lax.psum_scatter(cross_k_part, "ctx", scatter_dimension=0, tiled=True),
        lax.psum_scatter(cross_v_part, "ctx", scatter_dimension=0, tiled=True),
    )
    cross_k_grad = cross_k_grad.astype(jnp.bfloat16)
    cross_v_grad = cross_v_grad.astype(jnp.bfloat16)
    cross_query_grad = left_contract(normed_two, cross_q_grad)
    cross_key_grad = left_contract(encoder_rows, cross_k_grad)
    cross_value_grad = left_contract(encoder_rows, cross_v_grad)
    encoder_grad = (
        right_contract(cross_k_grad, cross_key_full)
        + right_contract(cross_v_grad, cross_value_full)
    ).astype(jnp.bfloat16)
    normed_two_grad = right_contract(cross_q_grad, cross_query_full)
    part_grad, gain_two_grad = norm_back(after_self, gain_two, normed_two_grad)
    after_self_grad = after_cross_grad + part_grad
    branch_one = after_self_grad.astype(jnp.bfloat16)
    out_w_grad = left_contract(attended, branch_one)
    dattn_heads = (
        right_contract(branch_one, out_full).astype(jnp.bfloat16).reshape(tokens, HEADS, HEAD_DIM)
    )
    row_delta = jnp.einsum("qhe,qhe->hq", dattn_heads.astype(jnp.float32), attn_sum)

    def block_grads(
        query_side, grad_side, norm_side, delta_side, query_pos, key_side, value_side, key_pos
    ):
        logits, allowed, indicator = query_key_logits(query_side, key_side, query_pos, key_pos)
        exact = jnp.exp(logits - norm_side[..., None])
        score_grad = jnp.einsum(
            "qhe,khe->hqk", grad_side, value_side, preferred_element_type=jnp.float32
        )
        logits_gradient = (exact * (score_grad - delta_side[..., None])).astype(jnp.bfloat16)
        grad_query = jnp.einsum(
            "hqk,khe->qhe", logits_gradient, key_side, preferred_element_type=jnp.float32
        )
        grad_key = jnp.einsum(
            "hqk,qhe->khe", logits_gradient, query_side, preferred_element_type=jnp.float32
        )
        grad_value = jnp.einsum(
            "hqk,qhe->khe",
            exact.astype(jnp.bfloat16),
            grad_side,
            preferred_element_type=jnp.float32,
        )
        bucket_table_gradient = jnp.einsum(
            "ouw,muw->om", indicator, logits_gradient, preferred_element_type=jnp.float32
        )
        return (grad_query, grad_key, grad_value, bucket_table_gradient)

    zero_table = jnp.zeros((BUCKETS, HEADS), jnp.float32)
    full_zero = jnp.zeros((total_rows, HEADS, HEAD_DIM), jnp.float32)

    def key_grad_step(carried, pieces, first_row):
        query_total, table_total, key_total, value_total = carried
        key_pos = lookup_positions(block_order, first_row, pieces[0].shape[0], block_len)
        grad_query, grad_key, grad_value, bucket_table_gradient = block_grads(
            query_heads, dattn_heads, log_norm, row_delta, own_pos, pieces[0], pieces[1], key_pos
        )
        key_total = lax.dynamic_update_slice_in_dim(key_total, grad_key, first_row, 0)
        value_total = lax.dynamic_update_slice_in_dim(value_total, grad_value, first_row, 0)
        return (
            query_total + grad_query,
            table_total + bucket_table_gradient,
            key_total,
            value_total,
        )

    query_sum, table_grad, key_partial, value_partial = fold_groups(
        key_grad_step,
        (zero_heads, zero_table, full_zero, full_zero),
        (
            lax.all_gather(key_heads, "ctx", axis=0, tiled=True),
            lax.all_gather(value_heads, "ctx", axis=0, tiled=True),
        ),
        tokens,
    )
    key_sum, value_accumulated = (
        lax.psum_scatter(key_partial, "ctx", scatter_dimension=0, tiled=True),
        lax.psum_scatter(value_partial, "ctx", scatter_dimension=0, tiled=True),
    )
    query_grad = query_sum.reshape(tokens, head_width).astype(jnp.bfloat16)
    key_grad = key_sum.reshape(tokens, head_width).astype(jnp.bfloat16)
    value_grad = value_accumulated.reshape(tokens, head_width).astype(jnp.bfloat16)
    query_w_grad = left_contract(normed_one, query_grad)
    key_w_grad = left_contract(normed_one, key_grad)
    value_w_grad = left_contract(normed_one, value_grad)
    normed_one_grad = (
        right_contract(query_grad, query_full)
        + right_contract(key_grad, key_full)
        + right_contract(value_grad, value_full)
    )
    part_grad, gain_one_grad = norm_back(resid_in, gain_one, normed_one_grad)
    input_grad = (after_self_grad + part_grad).astype(jnp.bfloat16)
    (
        sum_gain_one,
        sum_query,
        sum_key,
        sum_value,
        sum_out,
        sum_table,
        sum_gain_two,
        sum_cross_query,
        sum_cross_key,
        sum_cross_value,
        sum_cross_out,
        sum_gain_three,
        sum_gate,
        sum_up,
        sum_down,
    ) = (
        lax.psum_scatter(
            gain_one_grad.astype(jnp.bfloat16), "wsh", scatter_dimension=0, tiled=True
        ).astype(jnp.float32),
        lax.psum_scatter(
            query_w_grad.astype(jnp.bfloat16), "wsh", scatter_dimension=0, tiled=True
        ).astype(jnp.float32),
        lax.psum_scatter(
            key_w_grad.astype(jnp.bfloat16), "wsh", scatter_dimension=0, tiled=True
        ).astype(jnp.float32),
        lax.psum_scatter(
            value_w_grad.astype(jnp.bfloat16), "wsh", scatter_dimension=0, tiled=True
        ).astype(jnp.float32),
        lax.psum_scatter(
            out_w_grad.astype(jnp.bfloat16), "wsh", scatter_dimension=0, tiled=True
        ).astype(jnp.float32),
        lax.psum_scatter(
            table_grad.astype(jnp.bfloat16), "wsh", scatter_dimension=0, tiled=True
        ).astype(jnp.float32),
        lax.psum_scatter(
            gain_two_grad.astype(jnp.bfloat16), "wsh", scatter_dimension=0, tiled=True
        ).astype(jnp.float32),
        lax.psum_scatter(
            cross_query_grad.astype(jnp.bfloat16), "wsh", scatter_dimension=0, tiled=True
        ).astype(jnp.float32),
        lax.psum_scatter(
            cross_key_grad.astype(jnp.bfloat16), "wsh", scatter_dimension=0, tiled=True
        ).astype(jnp.float32),
        lax.psum_scatter(
            cross_value_grad.astype(jnp.bfloat16), "wsh", scatter_dimension=0, tiled=True
        ).astype(jnp.float32),
        lax.psum_scatter(
            cross_out_grad.astype(jnp.bfloat16), "wsh", scatter_dimension=0, tiled=True
        ).astype(jnp.float32),
        lax.psum_scatter(
            gain_three_grad.astype(jnp.bfloat16), "wsh", scatter_dimension=0, tiled=True
        ).astype(jnp.float32),
        lax.psum_scatter(
            gate_w_grad.astype(jnp.bfloat16), "wsh", scatter_dimension=0, tiled=True
        ).astype(jnp.float32),
        lax.psum_scatter(
            up_w_grad.astype(jnp.bfloat16), "wsh", scatter_dimension=0, tiled=True
        ).astype(jnp.float32),
        lax.psum_scatter(
            down_grad.astype(jnp.bfloat16), "wsh", scatter_dimension=0, tiled=True
        ).astype(jnp.float32),
    )
    total_grads = lax.psum(
        (
            sum_gain_one,
            sum_query,
            sum_key,
            sum_value,
            sum_out,
            sum_table,
            sum_gain_two,
            sum_cross_query,
            sum_cross_key,
            sum_cross_value,
            sum_cross_out,
            sum_gain_three,
            sum_gate,
            sum_up,
            sum_down,
        ),
        "ctx",
    )
    return (result.astype(jnp.bfloat16)[None], input_grad[None], encoder_grad[None]) + tuple(
        total_grads
    )


F32 = jnp.float32
BF16 = jnp.bfloat16
MESH = pl.DeviceIdType.MESH
TILE = 256
BLOCK = 64
MIB = 2**20
GELU_RATE, GELU_CUBE = 0.7978845608, 0.044715


def dot_nt(left, right):
    return lax.dot_general(left, right, (((1,), (1,)), ((), ())), preferred_element_type=F32)


def vmem_spec():
    return pl.BlockSpec(memory_space=pltpu.VMEM)


def any_spec():
    return pl.BlockSpec(memory_space=pl.ANY)


def unpack_pair(landed, pair, rows):
    left, right = landed[2 * pair, rows, :], landed[2 * pair + 1, rows, :]
    return (
        jnp.concatenate([left[:, :HEAD_DIM], right[:, :HEAD_DIM]], axis=1),
        jnp.concatenate([left[:, HEAD_DIM:], right[:, HEAD_DIM:]], axis=1),
    )


def place_tiles(bias_lines, tiles):
    for apart in range(tiles.shape[0]):
        line = jnp.broadcast_to(bias_lines[apart : apart + 1, :], (TILE, 2 * TILE))
        tiles[apart] = pltpu.roll(line, 0, 1, stride=1, stride_axis=0)[:, :TILE]


def attend_scratch(blocks):
    length = blocks * BLOCK
    vmem = pltpu.VMEM
    return [
        vmem((length, HEAD_DIM), BF16),
        vmem((length, HEAD_DIM), BF16),
        vmem((HEAD_DIM, length), BF16),
        vmem((length // TILE, TILE, TILE), F32),
        vmem((length, HEAD_DIM), F32),
        vmem((length, HEAD_DIM), F32),
    ]


def attend(order, held_at, pairs, lone, bias_lines, out_ref, sum_ref, norm_ref, q_s, k_s, vt_s, tiles, staged, o_s):
    blocks = held_at.shape[0]
    spans = blocks * BLOCK // TILE

    def in_order(into):
        for block in range(blocks):
            at = slice(block * BLOCK, (block + 1) * BLOCK)
            into[at, :] = staged[pl.ds(held_at[block] * BLOCK, BLOCK), :].astype(into.dtype)

    for side, into in ((0, q_s), (1, k_s)):
        for device in range(blocks // 2):
            at = slice(2 * device * BLOCK, 2 * (device + 1) * BLOCK)
            staged[at, :] = pairs[device, :, side * HEAD_DIM : (side + 1) * HEAD_DIM].astype(F32)
        in_order(into)
    for stored in range(blocks):
        at = slice(stored * BLOCK, (stored + 1) * BLOCK)
        cols = slice(stored % 2 * HEAD_DIM, (stored % 2 + 1) * HEAD_DIM)
        staged[at, :] = lone[stored // 2, :, cols].astype(F32)
    in_order(o_s)
    vt_s[...] = jnp.transpose(o_s[...], (1, 0)).astype(BF16)
    place_tiles(bias_lines, tiles)
    for i in range(spans):
        at_i = slice(i * TILE, (i + 1) * TILE)
        queries = q_s[at_i, :]
        scores = [
            dot_nt(k_s[j * TILE : (j + 1) * TILE, :], queries) + tiles[i - j] for j in range(i + 1)
        ]
        top = functools.reduce(
            jnp.maximum, [jnp.max(each, axis=0, keepdims=True) for each in scores]
        )
        total = jnp.zeros((1, TILE), F32)
        mixed = jnp.zeros((HEAD_DIM, TILE), F32)
        for j in range(i + 1):
            weights = jnp.exp(scores[j] - top)
            total = total + jnp.sum(weights, axis=0, keepdims=True)
            mixed = mixed + plain_dot(
                vt_s[:, j * TILE : (j + 1) * TILE], weights.astype(BF16)
            )
        norm_ref[0:1, at_i] = top + jnp.log(total)
        sum_ref[:, at_i] = mixed / total
    o_s[...] = jnp.transpose(sum_ref[...], (1, 0))
    for stored in range(blocks):
        cols = slice(stored % 2 * HEAD_DIM, (stored % 2 + 1) * HEAD_DIM)
        out_ref[stored // 2, :, cols] = o_s[pl.ds(order[stored] * BLOCK, BLOCK), :].astype(BF16)


def attend_back(
    order, held_at, pairs, lone, grad_landed, sums, norm, bias_lines, out_ref, lines_ref,
    q_s, k_s, v_s, do_s, kt_s, tiles, by_offset, dq_s, dk_s, dv_s, delta_s, dqt_s,
):
    blocks = order.shape[0]
    spans = blocks * BLOCK // TILE
    def stored_rows(stored):
        return slice(stored * BLOCK, (stored + 1) * BLOCK), stored // 2, slice(
            stored % 2 * HEAD_DIM, (stored % 2 + 1) * HEAD_DIM
        )

    def in_order(into, staged):
        for block in range(blocks):
            at = slice(block * BLOCK, (block + 1) * BLOCK)
            into[at, :] = staged[pl.ds(held_at[block] * BLOCK, BLOCK), :].astype(BF16)

    for stored in range(blocks):
        at, device, cols = stored_rows(stored)
        pair = pairs[device, stored % 2 * BLOCK : (stored % 2 + 1) * BLOCK, :].astype(F32)
        dq_s[at, :] = pair[:, :HEAD_DIM]
        dk_s[at, :] = pair[:, HEAD_DIM:]
        dv_s[at, :] = lone[device, :, cols].astype(F32)
    in_order(q_s, dq_s)
    in_order(k_s, dk_s)
    in_order(v_s, dv_s)
    for stored in range(blocks):
        at, device, cols = stored_rows(stored)
        dq_s[at, :] = grad_landed[device, :, cols].astype(F32)
    in_order(do_s, dq_s)
    place_tiles(bias_lines, tiles)
    kt_s[...] = jnp.transpose(k_s[...].astype(F32), (1, 0)).astype(BF16)
    grad_t = jnp.transpose(do_s[...].astype(F32), (1, 0))
    delta_s[...] = jnp.sum(grad_t * sums[...], axis=0, keepdims=True)
    by_offset[...] = jnp.zeros_like(by_offset)
    dk_s[...] = jnp.zeros_like(dk_s)
    dv_s[...] = jnp.zeros_like(dv_s)
    for i in range(spans):
        at_i = slice(i * TILE, (i + 1) * TILE)
        queries, grads = q_s[at_i, :], do_s[at_i, :]
        norm_i, delta_i = norm[0:1, at_i], delta_s[0:1, at_i]
        dqt = jnp.zeros((HEAD_DIM, TILE), F32)
        for j in range(i + 1):
            at_j = slice(j * TILE, (j + 1) * TILE)
            exact = jnp.exp(dot_nt(k_s[at_j, :], queries) + tiles[i - j] - norm_i)
            dscore = exact * (dot_nt(v_s[at_j, :], grads) - delta_i)
            by_offset[i - j] += dscore
            rounded = dscore.astype(BF16)
            dv_s[at_j, :] += plain_dot(exact.astype(BF16), grads)
            dk_s[at_j, :] += plain_dot(rounded, queries)
            dqt = dqt + plain_dot(kt_s[:, at_j], rounded)
        dqt_s[:, at_i] = dqt
    dq_s[...] = jnp.transpose(dqt_s[...], (1, 0))
    for stored in range(blocks):
        device, half = stored // 2, stored % 2
        at = pl.ds(order[stored] * BLOCK, BLOCK)
        rows = slice(half * BLOCK, (half + 1) * BLOCK)
        cols = slice(half * HEAD_DIM, (half + 1) * HEAD_DIM)
        out_ref[device, rows, :HEAD_DIM] = dq_s[at, :].astype(BF16)
        out_ref[device, rows, HEAD_DIM:] = dk_s[at, :].astype(BF16)
        out_ref[device, 2 * BLOCK :, cols] = dv_s[at, :].astype(BF16)
    for apart in range(spans):
        folded = jnp.zeros((8, 2 * TILE), F32)
        for group in range(TILE // 8):
            rows = by_offset[apart, 8 * group : 8 * group + 8, :]
            wide = jnp.concatenate([rows, jnp.zeros((8, TILE), F32)], axis=1)
            folded = folded + (pltpu.roll(wide, 2 * TILE - 8 * group, 1) if group else wide)
        line = folded[0:1]
        for row in range(1, 8):
            line = line + pltpu.roll(folded[row : row + 1], 2 * TILE - row, 1)
        lines_ref[apart : apart + 1, :] = line


class Weights(NamedTuple):
    query: Any
    key: Any
    value: Any
    out: Any
    cross_key: Any
    cross_value: Any
    cross_query: Any
    cross_out: Any
    gate: Any
    up: Any
    down: Any


W = Weights(*range(11))
LENT = (W.query, W.key, W.value, W.cross_key, W.cross_value)


class Made(NamedTuple):
    normed_one: Any
    pairs: Any
    lone: Any
    attn_sum: Any
    log_norm: Any
    attended: Any
    normed_two: Any
    cross_mixed: Any
    normed_three: Any
    hidden: Any
    gate_grad: Any
    up_grad: Any
    branch_two: Any
    cross_q_grad: Any
    branch_one: Any
    dattn: Any
    kv_part: Any
    resid_grad: Any
    result: Any
    gain_grads: Any
    gain_one: Any
    bias_lines: Any
    encoder_both: Any


class Far(NamedTuple):
    normed_three: Any
    hidden: Any
    gate: Any
    up: Any
    branch_three: Any


class Scratch(NamedTuple):
    small_far: Any
    table_far: Any
    pairs_out: Any
    lone_out: Any
    encoder_all: Any
    mixed_out: Any
    mixed_in: Any
    cross_keys: Any
    cross_values: Any
    cross_queries: Any
    cross_exact: Any
    after_self: Any
    after_cross: Any
    gate_act: Any
    up_act: Any
    mix_grad: Any


def norm_parts(values):
    return lax.rsqrt(jnp.mean(values * values, axis=1, keepdims=True) + EPSILON)


def norm_backward(values, gain, cotan):
    rate = norm_parts(values)
    scaled = cotan * gain
    slope = jnp.mean(scaled * values, axis=1, keepdims=True)
    return (
        rate * scaled - values * (rate * rate * rate) * slope,
        jnp.sum(cotan * values * rate, axis=0, keepdims=True),
    )


def layer_kernel(tokens_in, cotangent, encoder, small, table, in_bucket, held_at, order, *refs):
    refs = list(refs)

    def take(number):
        taken = refs[:number]
        del refs[:number]
        return taken

    sources = take(len(W))
    out = Made(*take(len(Made._fields)))
    far = Far(*take(len(Far._fields)))
    lent = take(len(LENT))
    weights = take(len(W))
    own = Scratch(*take(len(Scratch._fields)))
    (own_sem, weight_own, weight_send, weight_recv, lent_send, lent_recv, far_send, far_recv, all_own, all_send, all_recv) = refs
    me, core = lax.axis_index("ctx"), lax.axis_index("wsh")
    peers = lax.axis_size("ctx")
    x, y = lax.rem(me, 2), lax.rem(me // 2, 2)
    tokens, width = tokens_in.shape
    finish = []

    barrier = pltpu.get_barrier_semaphore()
    for step in range(1, peers):
        pl.semaphore_signal(
            barrier, inc=1, device_id=(lax.rem(me + step, peers), core), device_id_type=MESH
        )
    pl.semaphore_signal(barrier, inc=1, device_id=(me, 1 - core), device_id_type=MESH)

    def half_rows(ref, side):
        half = ref.shape[0] // 2
        return ref.at[pl.ds(pl.multiple_of(side * half, 16), half)]

    def remote(src, dst, send_sem, recv_sem, ctx, side):
        return pltpu.make_async_remote_copy(
            src_ref=src,
            dst_ref=dst,
            send_sem=send_sem,
            recv_sem=recv_sem,
            device_id=(ctx, side),
            device_id_type=MESH,
        )

    def arrived(ref, sem):
        remote(ref, ref, own_sem, sem, me, 1 - core).wait_recv()

    def launch(src, dst, send_sem, recv_sem, ctx, side):
        remote(src, dst, send_sem, recv_sem, ctx, side).start()
        finish.append(lambda: remote(src, src, send_sem, own_sem, me, 1 - core).wait_send())

    local = {}
    for at in W:
        local[at] = pltpu.make_async_copy(sources[at], half_rows(weights[at], core), weight_own.at[at])
        local[at].start()
    pl.semaphore_wait(barrier, peers)

    launch(small, own.small_far, far_send.at[5], far_recv.at[5], me, 1 - core)
    launch(table, own.table_far, far_send.at[6], far_recv.at[6], me, 1 - core)
    for at in W:
        launch(sources[at], half_rows(weights[at], core), weight_send.at[at], weight_recv.at[at], me, 1 - core)
    for at, source in enumerate(LENT):
        launch(sources[source], lent[at], lent_send.at[at], lent_recv.at[at], me, 1 - core)

    def weight(at):
        if at in local:
            local.pop(at).wait()
            arrived(half_rows(weights[at], 1 - core), weight_recv.at[at])
        return weights[at]

    def to_all(which, source, target, spread=True):
        for step in range(1, peers):
            peer = lax.rem(me + step, peers)
            remote(
                source.at[peer] if spread else source, target.at[me], all_send.at[which], all_recv.at[which], peer, core
            ).start()
        kept = pltpu.make_async_copy(source.at[me] if spread else source, target.at[me], all_own.at[which])
        kept.start()
        finish.append(lambda: remote(target.at[1:], target.at[1:], all_send.at[which], own_sem, me, 1 - core).wait_send())

        def wait():
            kept.wait()
            arrived(target.at[1:], all_recv.at[which])

        return wait

    def tiles_of(total):
        return [slice(at, at + 256) for at in range(0, total, 256)]

    def times(values, name):
        ref = weight(name)
        return jnp.concatenate([plain_dot(values, ref[:, cols]) for cols in tiles_of(ref.shape[1])], axis=1)

    def times_back(values, name):
        ref = weight(name)
        return jnp.concatenate([dot_nt(values, ref[cols, :]) for cols in tiles_of(ref.shape[0])], axis=1)

    def head(at):
        return slice(at * HEAD_DIM, (at + 1) * HEAD_DIM)

    def head_pair(at):
        return slice(2 * at * HEAD_DIM, 2 * (at + 1) * HEAD_DIM)

    arrived(own.small_far, far_recv.at[5])
    arrived(own.table_far, far_recv.at[6])

    def both(mine, others, axis):
        first = jnp.where(core == 0, mine, others)
        second = jnp.where(core == 0, others, mine)
        return jnp.concatenate([first, second], axis=axis)

    gain_one, gain_two, gain_three = (
        both(small[at : at + 1, :], own.small_far[at : at + 1, :], 1) for at in range(3)
    )
    out.gain_one[...] = gain_one
    whole_table = both(table[...], own.table_far[...], 0)
    lane = lax.broadcasted_iota(jnp.int32, whole_table.shape, 1)
    column = jnp.sum(jnp.where(lane == me, whole_table, 0.0), axis=1, keepdims=True)
    spans = in_bucket.shape[0]
    for apart in range(spans):
        line = jnp.sum(in_bucket[apart] * column, axis=0, keepdims=True)
        out.bias_lines[apart : apart + 1, :TILE] = line
        if apart + 1 < spans:
            out.bias_lines[apart + 1 : apart + 2, TILE:] = line
    out.bias_lines[0:1, TILE:] = jnp.full((1, TILE), NEG_BIG, F32)

    resid = tokens_in[...].astype(F32)
    out.normed_one[...] = (resid * norm_parts(resid) * gain_one).astype(BF16)
    normed_one = out.normed_one[...]
    queries = times(normed_one, W.query).astype(BF16)
    keys = times(normed_one, W.key).astype(BF16)
    for at in range(peers):
        own.pairs_out[at] = jnp.concatenate([queries[:, head(at)], keys[:, head(at)]], axis=1)
    pairs_arrival = to_all(0, own.pairs_out, out.pairs)
    values = times(normed_one, W.value).astype(BF16)
    for at in range(peers):
        own.lone_out[at] = jnp.concatenate(
            [values[:BLOCK, head(at)], values[BLOCK:, head(at)]], axis=1
        )
    lone_arrival = to_all(1, own.lone_out, out.lone)
    encoder_arrival = to_all(2, encoder, own.encoder_all, spread=False)
    launch(
        cotangent.at[:, pl.ds(pl.multiple_of((1 - x) * (width // 2), 128), width // 2)],
        far.branch_three, far_send.at[4], far_recv.at[4], me ^ 1, core,
    )
    place_bias = out.bias_lines
    pairs_arrival()
    lone_arrival()
    pl.run_scoped(
        functools.partial(
            attend, order, held_at, out.pairs, out.lone, place_bias, own.mixed_out, out.attn_sum, out.log_norm
        ),
        *attend_scratch(held_at.shape[0]),
    )
    mixed_arrival = to_all(3, own.mixed_out, own.mixed_in)

    encoder_arrival()
    encoder_rows = jnp.concatenate([own.encoder_all[at] for at in range(peers)], axis=0)
    half = width // 2
    count = encoder_rows.shape[0]
    out.encoder_both[:count, :] = jnp.where(core == 0, encoder_rows[:, :half], encoder_rows[:, half:])
    own.cross_keys[...] = times(encoder_rows, W.cross_key).astype(BF16)
    own.cross_values[...] = times(encoder_rows, W.cross_value).astype(BF16)

    mixed_arrival()
    for pair in range(peers // 2):
        first, second = unpack_pair(own.mixed_in, pair, slice(0, BLOCK))
        out.attended[:BLOCK, head_pair(pair)] = first
        out.attended[BLOCK:, head_pair(pair)] = second
    own.after_self[...] = tokens_in[...].astype(F32) + times(out.attended[...], W.out)
    after_self = own.after_self[...]
    out.normed_two[...] = (after_self * norm_parts(after_self) * gain_two).astype(BF16)
    own.cross_queries[...] = times(out.normed_two[...], W.cross_query).astype(BF16)

    for pair in range(peers // 2):
        mixed = []
        for at in (2 * pair, 2 * pair + 1):
            scores = dot_nt(own.cross_keys[:, head(at)], own.cross_queries[:, head(at)])
            weight_t = jnp.exp(scores - jnp.max(scores, axis=0, keepdims=True))
            exact = weight_t / jnp.sum(weight_t, axis=0, keepdims=True)
            own.cross_exact[at] = exact
            mixed.append(left_contract(exact.astype(BF16), own.cross_values[:, head(at)]))
        out.cross_mixed[:, head_pair(pair)] = jnp.concatenate(mixed, axis=1).astype(BF16)
    own.after_cross[...] = own.after_self[...] + times(out.cross_mixed[...], W.cross_out)
    after_cross = own.after_cross[...]
    out.normed_three[...] = (after_cross * norm_parts(after_cross) * gain_three).astype(BF16)
    launch(out.normed_three, far.normed_three, far_send.at[0], far_recv.at[0], me ^ 2, core)

    normed_three = out.normed_three[...]
    gate, up, down = weight(W.gate), weight(W.up), weight(W.down)
    for cols in tiles_of(gate.shape[1]):
        gate_act = plain_dot(normed_three, gate[:, cols])
        up_act = plain_dot(normed_three, up[:, cols])
        own.gate_act[:, cols] = gate_act
        own.up_act[:, cols] = up_act
        curve = jnp.tanh(GELU_RATE * (gate_act + GELU_CUBE * gate_act * gate_act * gate_act))
        out.hidden[:, cols] = (0.5 * gate_act * (1.0 + curve) * up_act).astype(BF16)
    launch(out.hidden, far.hidden, far_send.at[1], far_recv.at[1], me ^ 1, core)
    out.result[...] = (own.after_cross[...] + times(out.hidden[...], W.down)).astype(BF16)

    branch_three = cotangent[...]
    for cols in tiles_of(down.shape[0]):
        hidden_grad = dot_nt(branch_three, down[cols, :])
        gate_act, up_act = own.gate_act[:, cols], own.up_act[:, cols]
        square = gate_act * gate_act
        curve = jnp.tanh(GELU_RATE * (gate_act + GELU_CUBE * gate_act * square))
        rise = 0.5 * (1.0 + curve) + 0.5 * gate_act * (1.0 - curve * curve) * (
            GELU_RATE * (1.0 + 3.0 * GELU_CUBE * square)
        )
        out.gate_grad[:, cols] = (hidden_grad * up_act * rise).astype(BF16)
        out.up_grad[:, cols] = (hidden_grad * (0.5 * gate_act * (1.0 + curve))).astype(BF16)
    for at, mine in ((2, out.gate_grad), (3, out.up_grad)):
        half = mine.shape[1] // 2
        launch(
            mine.at[:, pl.ds(pl.multiple_of((1 - y) * half, 128), half)],
            far[at], far_send.at[at], far_recv.at[at], me ^ 2, core,
        )
    normed_grad = times_back(out.gate_grad[...], W.gate) + times_back(out.up_grad[...], W.up)
    back, gain_three_grad = norm_backward(own.after_cross[...], gain_three, normed_grad)
    out.resid_grad[...] = cotangent[...].astype(F32) + back
    out.branch_two[...] = out.resid_grad[...].astype(BF16)

    own.mix_grad[...] = times_back(out.branch_two[...], W.cross_out).astype(BF16)
    for pair in range(peers // 2):
        terms = []
        for at in (2 * pair, 2 * pair + 1):
            exact = own.cross_exact[at]
            grads = own.mix_grad[:, head(at)]
            score_grad = dot_nt(own.cross_values[:, head(at)], grads)
            slope = jnp.sum(exact * score_grad, axis=0, keepdims=True)
            rounded = (exact * (score_grad - slope)).astype(BF16)
            terms.append(
                (
                    left_contract(rounded, own.cross_keys[:, head(at)]),
                    plain_dot(rounded, own.cross_queries[:, head(at)]),
                    plain_dot(exact.astype(BF16), grads),
                )
            )
        cols = head_pair(pair)
        values_cols = slice(width + cols.start, width + cols.stop)
        for ref, into, at in ((out.cross_q_grad, cols, 0), (out.kv_part, cols, 1), (out.kv_part, values_cols, 2)):
            ref[:, into] = jnp.concatenate([terms[0][at], terms[1][at]], axis=1).astype(BF16)
    normed_grad = times_back(out.cross_q_grad[...], W.cross_query)
    back, gain_two_grad = norm_backward(own.after_self[...], gain_two, normed_grad)
    out.resid_grad[...] += back
    out.branch_one[...] = out.resid_grad[...].astype(BF16)
    out.dattn[...] = times_back(out.branch_one[...], W.out).astype(BF16)

    for half in range(2):
        for index in range(4):
            cols = slice((4 * half + index) * 128, (4 * half + index + 1) * 128)
            out.gain_grads[half, index : index + 1, :] = gain_two_grad[:, cols]
            out.gain_grads[half, 4 + index : 5 + index, :] = gain_three_grad[:, cols]
        out.gain_grads[half, 8:, :] = jnp.zeros((4, 128), F32)

    other_half = pl.ds(pl.multiple_of((1 - core) * (width // 2), 128), width // 2)
    for at in range(peers):
        rows_at = own.encoder_all.shape[1]
        remote(
            own.encoder_all.at[at, :, other_half],
            out.encoder_both.at[count + at * rows_at : count + (at + 1) * rows_at],
            far_send.at[7], far_recv.at[7], me, 1 - core,
        ).start()
    arrived(out.encoder_both.at[count:], far_recv.at[7])
    finish.append(
        lambda: remote(
            out.encoder_both.at[count:], out.encoder_both.at[count:], far_send.at[7], own_sem, me, 1 - core
        ).wait_send()
    )
    for at, ref in enumerate(far):
        arrived(ref, far_recv.at[at])
    for at, ref in enumerate(lent):
        arrived(ref, lent_recv.at[at])
    for each in finish:
        each()


def layer(tokens_in, cotangent, encoder, small, table, in_bucket, held_at, order, sources):
    peers = lax.axis_size("ctx")
    tokens, width = tokens_in.shape
    hidden = sources.gate.shape[1]
    blocks = held_at.shape[0]
    length = blocks * BLOCK
    rows = encoder.shape[0] * peers
    dma, vmem = pltpu.SemaphoreType.DMA, pltpu.VMEM

    def shaped(*shape):
        return jax.ShapeDtypeStruct(shape, BF16)

    def exact(*shape):
        return jax.ShapeDtypeStruct(shape, F32)

    square, wide, half_wide = shaped(tokens, width), shaped(tokens, hidden), shaped(tokens, hidden // 2)
    pairs, lone = (peers, 2 * BLOCK, 2 * HEAD_DIM), (peers, BLOCK, 2 * HEAD_DIM)
    outputs = Made(
        normed_one=square,
        pairs=shaped(*pairs),
        lone=shaped(*lone),
        attn_sum=exact(HEAD_DIM, length),
        log_norm=exact(1, length),
        attended=square,
        normed_two=square,
        cross_mixed=square,
        normed_three=square,
        hidden=wide,
        gate_grad=wide,
        up_grad=wide,
        branch_two=square,
        cross_q_grad=square,
        branch_one=square,
        dattn=square,
        kv_part=shaped(rows, 2 * width),
        resid_grad=exact(tokens, width),
        result=square,
        gain_grads=exact(2, 12, 128),
        gain_one=exact(1, width),
        bias_lines=exact(length // TILE, 2 * TILE),
        encoder_both=shaped(2 * rows, width // 2),
    )
    fars = Far(
        normed_three=square, hidden=wide, gate=half_wide, up=half_wide, branch_three=shaped(tokens, width // 2)
    )
    buffers = Scratch(
        small_far=vmem(small.shape, F32),
        table_far=vmem(table.shape, F32),
        pairs_out=vmem(pairs, BF16),
        lone_out=vmem(lone, BF16),
        encoder_all=vmem((peers,) + encoder.shape, BF16),
        mixed_out=vmem(lone, BF16),
        mixed_in=vmem(lone, BF16),
        cross_keys=vmem((rows, width), BF16),
        cross_values=vmem((rows, width), BF16),
        cross_queries=vmem((tokens, width), BF16),
        cross_exact=vmem((HEADS, rows, tokens), F32),
        after_self=vmem((tokens, width), F32),
        after_cross=vmem((tokens, width), F32),
        gate_act=vmem((tokens, hidden), F32),
        up_act=vmem((tokens, hidden), F32),
        mix_grad=vmem((tokens, width), BF16),
    )
    smem_spec = pl.BlockSpec(memory_space=pltpu.SMEM)
    results = pl.pallas_call(
        layer_kernel,
        out_shape=[*outputs, *fars, *(shaped(*sources[at].shape) for at in LENT)],
        in_specs=[vmem_spec()] * 6 + [smem_spec] * 2 + [any_spec()] * len(W),
        out_specs=[vmem_spec()] * len(outputs) + [any_spec()] * (len(fars) + len(LENT)),
        scratch_shapes=[vmem((2 * each.shape[0], each.shape[1]), BF16) for each in sources]
        + list(buffers)
        + [
            dma,
            dma((len(W),)),
            dma((len(W),)),
            dma((len(W),)),
            dma((len(LENT),)),
            dma((len(LENT),)),
            dma((8,)),
            dma((8,)),
            dma((4,)),
            dma((4,)),
            dma((4,)),
        ],
        compiler_params=pltpu.CompilerParams(
            collective_id=1, has_side_effects=True, vmem_limit_bytes=62 * MIB
        ),
        name="layer",
    )(tokens_in, cotangent, encoder, small, table, in_bucket, held_at, order, *sources)
    made, results = results[: len(outputs)], results[len(outputs) :]
    return Made(*made), Far(*results[: len(fars)]), results[len(fars) :]


BIT_X, BIT_Y = 0, 1
FAR_LEFTS, FAR_RIGHTS = 2, 3
SCHEDULE = (
    1, 256, 17, 0, 4, 5, 16, 32, 33, 2, 257, 18, 21, 49, 34, 48, 65, 64, 3, 20,
    50, 6, 36, 81, 258, 7, 37, 8, 22, 19, 35, 9, 80, 38, 23, 96, 39, 112, 51, 66,
    24, 53, 25, 97, 67, 128, 40, 52, 82, 259, 54, 144, 98, 69, 68, 114, 55, 83, 56, 113,
    130, 85, 41, 84, 146, 72, 71, 70, 101, 99, 160, 100, 115, 117, 86, 162, 102, 133, 116, 88,
    178, 87, 194, 104, 129, 260, 118, 176, 57, 103, 120, 132, 119, 131, 73, 136, 147, 89, 135, 148,
    134, 105, 150, 192, 166, 121, 182, 149, 145, 210, 137, 163, 198, 152, 151, 168, 179, 153, 167, 184,
    161, 183, 164, 199, 208, 215, 195, 214, 180, 261, 200, 211, 231, 226, 165, 196, 181, 262, 212, 216,
    224, 169, 232, 177, 185, 227, 228, 197, 201, 217, 240, 213, 229, 230, 233, 242, 243, 265, 263, 247,
    193, 264, 209, 246, 225, 248, 244, 245, 241, 249,
)


UP, DOWN, ACROSS_Y, ACROSS_X = 0, 1, 2, 3
LEFT, RIGHT, PIECE = 0, 1, 2


class Product:
    def __init__(self, left, right, first, tall, route):
        self.left, self.right, self.first, self.tall, self.route = left, right, first, tall, route


SUMMED = -1


def weight_grad_kernel(products, left_count, *refs):
    count = len(products)
    refs = list(refs)

    def take(number):
        taken = refs[:number]
        del refs[:number]
        return taken

    lefts, rights = take(left_count), take(count - 3)
    left_far, right_far = take(FAR_LEFTS), take(FAR_RIGHTS)
    (
        order,
        held_at,
        grad_rows,
        pairs,
        lone,
        attn_sum,
        log_norm,
        bias_lines,
        in_bucket,
        resid_in,
        gain_one,
        resid_grad,
        gains,
    ) = take(13)
    weights = take(10)
    wholes, (vec_out, input_grad, encoder_grad, kv_both) = take(count - 1), take(4)
    kv_at = [product.left for product in products].index(SUMMED)
    wholes.insert(kv_at, kv_both.at[0])
    left_all, left_pass, left_t = take(left_count), take(left_count), take(left_count)
    right_all, away, came, held, line_in = (take(count) for _ in range(5))
    rights += take(3)
    grad_packed, grad_landed, back_packed, back_landed, lines = take(5)
    attention_scratch = take(12)
    vec_in, vec_sums, vec_landed, weight_buffer, normed_grad = take(5)
    (
        left_send,
        left_own,
        left_recv,
        right_send,
        right_own,
        right_recv,
        pair_send,
        pair_recv,
        line_send,
        line_recv,
        out_send,
        out_recv,
        own_sem,
        vec_send,
        vec_recv,
        all_send,
        all_recv,
        all_own,
        kv_sem,
        weight_sem,
    ) = refs
    me, core = lax.axis_index("ctx"), lax.axis_index("wsh")
    peers = lax.axis_size("ctx")
    tokens = lefts[0].shape[0]
    x, y, z = lax.rem(me, 2), lax.rem(me // 2, 2), me // 4

    barrier = pltpu.get_barrier_semaphore()
    for step in range(1, peers):
        pl.semaphore_signal(
            barrier, inc=1, device_id=(lax.rem(me + step, peers), core), device_id_type=MESH
        )
    pl.semaphore_signal(barrier, inc=1, device_id=(me, 1 - core), device_id_type=MESH)
    for head in range(peers):
        cols = slice(head * HEAD_DIM, (head + 1) * HEAD_DIM)
        grad_packed[head] = jnp.concatenate(
            [grad_rows[:BLOCK, cols], grad_rows[BLOCK:, cols]], axis=1
        )
    pl.semaphore_wait(barrier, peers)

    def place(zz, yy, xx):
        return zz * 4 + yy * 2 + xx

    targets = {
        UP: place(lax.rem(z + 1, 4), y, x),
        DOWN: place(lax.rem(z + 3, 4), y, x),
        ACROSS_Y: place(z, 1 - y, x),
        ACROSS_X: place(z, y, 1 - x),
    }
    finish = []

    def remote(src, dst, send_sem, recv_sem, ctx, side):
        return pltpu.make_async_remote_copy(
            src_ref=src,
            dst_ref=dst,
            send_sem=send_sem,
            recv_sem=recv_sem,
            device_id=(ctx, side),
            device_id_type=MESH,
        )

    def launch(copy, only=None):
        if only is None:
            copy.start()
        else:
            pl.when(only)(copy.start)

    def arrived(ref, sem):
        remote(ref, ref, own_sem.at[0], sem, me, 1 - core).wait_recv()

    def left_here(ref, sem):
        finish.append(lambda: remote(ref, ref, sem, own_sem.at[0], me, 1 - core).wait_send())

    def lanes(ref, at, width):
        return ref.at[:, pl.ds(pl.multiple_of(at * width, 128), width)]

    def rows(ref, at, height):
        return ref.at[pl.ds(pl.multiple_of(at * height, 16), height)]

    def slot(ref, index):
        return ref.at[pl.ds(index * tokens, tokens)]

    def axes(product):
        along_x, along_y = (x, ACROSS_X), (y, ACROSS_Y)
        return (along_x, along_y) if product.first == BIT_X else (along_y, along_x)

    left_axis = {product.left: product for product in products}
    far_rights = [at for at in range(count) if 0 <= products[at].left < FAR_LEFTS]

    def local(src, dst, sem):
        copy = pltpu.make_async_copy(src, dst, sem)
        copy.start()
        return copy

    def send_left(at):
        (_, way), _ = axes(left_axis[at])
        half = left_all[at].shape[1]
        send_sem, recv_sem = left_send.at[at], left_recv.at[at]
        mine, others = lanes(lefts[at], core, half), lanes(lefts[at], 1 - core, half)
        copies = [local(mine, slot(left_all[at], 0), left_own.at[at])]
        launch(remote(others, slot(left_all[at], 2), send_sem, recv_sem.at[2], me, 1 - core))
        if at < FAR_LEFTS:
            far_mine, far_others = lanes(left_far[at], core, half), lanes(left_far[at], 1 - core, half)
            copies.append(local(far_mine, slot(left_all[at], 1), left_own.at[at]))
            launch(remote(far_others, slot(left_all[at], 3), send_sem, recv_sem.at[3], me, 1 - core))
            left_here(left_all[at].at[: 2 * tokens], send_sem)
        else:
            launch(remote(mine, slot(left_all[at], 1), send_sem, recv_sem.at[0], targets[way], core))
            launch(remote(others, left_pass[at], send_sem, recv_sem.at[1], targets[way], core))
            left_here(left_all[at], send_sem)
        return left_all[at].at[: len(copies) * tokens], left_own.at[at]

    def send_right(at):
        (mine, way), _ = axes(products[at])
        half = right_all[at].shape[1]
        send_sem, recv_sem = right_send.at[at], right_recv.at[at]
        own, others = lanes(rights[at], mine, half), lanes(rights[at], 1 - mine, half)
        if products[at].left == SUMMED:
            launch(remote(others, right_all[at], send_sem, recv_sem.at[0], targets[way], core))
            left_here(right_all[at], send_sem)
            return None
        copies = [local(own, slot(right_all[at], 0), right_own.at[at])]
        launch(remote(own, slot(right_all[at], 2), send_sem, recv_sem.at[1], me, 1 - core))
        if at in far_rights:
            far = right_far[far_rights.index(at)]
            copies.append(local(far, slot(right_all[at], 1), right_own.at[at]))
            launch(remote(far, slot(right_all[at], 3), send_sem, recv_sem.at[2], me, 1 - core))
            left_here(right_all[at].at[: 2 * tokens], send_sem)
        else:
            launch(remote(others, slot(right_all[at], 1), send_sem, recv_sem.at[0], targets[way], core))
            left_here(right_all[at].at[: 3 * tokens], send_sem)
        return right_all[at].at[: len(copies) * tokens], right_own.at[at]

    def to_all(which, source, target):
        for step in range(1, peers):
            peer = lax.rem(me + step, peers)
            launch(remote(source.at[peer], target.at[me], all_send.at[which], all_recv.at[which], peer, core))
        own = local(source.at[me], target.at[me], all_own.at[which])
        left_here(source.at[1:], all_send.at[which])

        def wait():
            own.wait()
            arrived(target.at[1:], all_recv.at[which])

        return wait

    seen = set()
    owns = {}

    def send_operands(some):
        for at in some:
            left = products[at].left
            if left not in seen and left != SUMMED:
                seen.add(left)
                owns[LEFT, left] = send_left(left)
            owns[RIGHT, at] = send_right(at)

    def own_slots(key):
        ref, sem = owns[key]
        pltpu.make_async_copy(ref, ref, sem).wait()

    def vector_step(step):
        if step == 0:
            source, ctx, side = vec_in.at[1 - core], me, 1 - core
        else:
            source, ctx, side = vec_sums.at[step - 1], me ^ (1 << (step - 1)), core
        launch(remote(source, vec_landed.at[step], vec_send.at[step], vec_recv.at[step], ctx, side))
        left_here(source, vec_send.at[step])

    def vector_add(step):
        arrived(vec_landed.at[step], vec_recv.at[step])
        total = (vec_sums[step - 1] if step else vec_in[core]) + vec_landed[step]
        if step < 4:
            vec_sums[step] = total
            vector_step(step + 1)
        else:
            vec_out[...] = total

    passed = set()

    def pass_on(at):
        left = products[at].left
        if left == SUMMED or at in far_rights:
            return
        if left not in passed:
            passed.add(left)
            arrived(slot(left_all[left], 1), left_recv.at[left, 0])
            arrived(left_pass[left], left_recv.at[left, 1])
            launch(remote(left_pass[left], slot(left_all[left], 3), left_send.at[left], left_recv.at[left, 3], me, 1 - core))
        arrived(slot(right_all[at], 1), right_recv.at[at, 0])
        launch(remote(slot(right_all[at], 1), slot(right_all[at], 3), right_send.at[at], right_recv.at[at, 2], me, 1 - core))

    def multiply(at, out, half):
        product = products[at]
        left, right = left_t[product.left], right_all[at]
        height, width = out.shape
        step = 256 if height <= 256 else 128 if height % 256 else 256
        if product.tall:
            columns = pl.ds(pl.multiple_of(half * width, 128), width)

            def strip(index, carry):
                band = pl.ds(pl.multiple_of(index * 176, 16), 176)
                out[band, :] = plain_dot(left[band, :], right[:, columns]).astype(BF16)
                return carry

            lax.fori_loop(0, height // 176, strip, 0)
        else:
            band = pl.ds(pl.multiple_of(half * height, 16), height)

            def strip(index, carry):
                columns = pl.ds(pl.multiple_of(index * 256, 128), 256)
                out[:, columns] = plain_dot(left[band, :], right[:, columns]).astype(BF16)
                return carry

            lax.fori_loop(0, width // 256, strip, 0)
            if width % 256:
                out[:, width - 128 :] = plain_dot(left[band, :], right[:, width - 128 :]).astype(BF16)

    turned = set()

    def product_away(at):
        left = products[at].left
        _, (mine, way) = axes(products[at])
        if left == SUMMED:
            (first_mine, _), _ = axes(products[at])
            arrived(right_all[at], right_recv.at[at, 0])
            height = held[at].shape[0]
            for out, half in ((away[at], 1 - mine), (held[at], mine)):
                own = lanes(rows(rights[at], half, height), first_mine, held[at].shape[1])
                out[...] = (own[...].astype(F32) + rows(right_all[at], half, height)[...].astype(F32)).astype(BF16)
            launch(remote(away[at], came[at], pair_send.at[at], pair_recv.at[at], targets[way], core))
            left_here(away[at], pair_send.at[at])
            return
        if left not in turned:
            turned.add(left)
            arrived(slot(left_all[left], 2), left_recv.at[left, 2])
            arrived(slot(left_all[left], 3), left_recv.at[left, 3])
            own_slots((LEFT, left))
            height = left_t[left].shape[0]

            def turn(index, carry):
                band = pl.ds(pl.multiple_of(index * 128, 128), 128)
                left_t[left][band, :] = jnp.transpose(left_all[left][:, band], (1, 0))
                return carry

            lax.fori_loop(0, height // 128, turn, 0)
        arrived(slot(right_all[at], 2), right_recv.at[at, 1])
        arrived(slot(right_all[at], 3), right_recv.at[at, 2])
        own_slots((RIGHT, at))
        multiply(at, away[at], 1 - mine)
        launch(remote(away[at], came[at], pair_send.at[at], pair_recv.at[at], targets[way], core))
        left_here(away[at], pair_send.at[at])
        multiply(at, held[at], mine)

    def add(into, more):
        into[...] = (into[...].astype(F32) + more[...].astype(F32)).astype(BF16)

    def add_pair(at):
        arrived(came[at], pair_recv.at[at])
        add(held[at], came[at])

    def line_step(at, step):
        height = held[at].shape[0] // 4
        for side, behind, chunk, way in (
            (0, z, lax.rem(z + 3 - step, 4), UP),
            (1, 3 - z, lax.rem(z + step + 1, 4), DOWN),
        ):
            recv_sem = line_recv.at[at, side, lax.rem(chunk + 2, 3) if side == 0 else lax.rem(chunk, 3)]
            landing = rows(line_in[at], chunk + 1 - side, height)

            def land(landing=landing, chunk=chunk, recv_sem=recv_sem):
                arrived(landing, recv_sem)
                add(rows(held[at], chunk, height), landing)

            pl.when(jnp.logical_and(behind > 0, behind <= step))(land)
            if step < 3:
                launch(
                    remote(
                        rows(held[at], chunk, height),
                        landing,
                        line_send.at[at],
                        recv_sem,
                        targets[way],
                        core,
                    ),
                    only=behind <= step,
                )
        if step == 3:
            left_here(held[at].at[: 3 * height], line_send.at[at])

    def own_piece(at):
        return rows(held[at], z, held[at].shape[0] // 4)

    def window(at, where):
        product = products[at]
        height, width = held[at].shape
        height //= 4
        xx, yy, zz = lax.rem(where, 2), lax.rem(where // 2, 2), where // 4
        one, two = (xx, yy) if product.first == BIT_X else (yy, xx)
        row, column = (zz, one * 2 + two) if product.tall else (two * 4 + zz, one)
        return wholes[at].at[
            pl.ds(pl.multiple_of(row * height, 16), height),
            pl.ds(pl.multiple_of(column * width, 128), width),
        ]

    def send(at, where, way, arrival, only=None, own=False):
        launch(
            remote(
                own_piece(at) if own else window(at, where),
                window(at, where),
                out_send.at[at, min(way, ACROSS_Y)],
                out_recv.at[at, arrival],
                targets[way],
                core,
            ),
            only,
        )

    def arrive(at, where, arrival, only=None):
        def act():
            arrived(window(at, where), out_recv.at[at, arrival])

        if only is None:
            act()
        else:
            pl.when(only)(act)

    def quarters(at, number):
        return wholes[at].at[: wholes[at].shape[0] // 4 * number]

    def near(way, zz):
        return place(zz, 1 - y, x) if way == ACROSS_Y else place(zz, y, 1 - x)

    def opposite(zz):
        return place(zz, 1 - y, 1 - x)

    def from_line(apart):
        return (
            (z >= apart, lax.rem(z + 4 - apart, 4), UP, jnp.logical_and(z >= apart, z < 3)),
            (z + apart <= 3, lax.rem(z + apart, 4), DOWN, jnp.logical_and(z + apart <= 3, z > 0)),
        )

    def line_sent(at, piece_groups):
        for number in (1, 2, 3):
            for way, here in ((UP, z == number - 1), (DOWN, z == 4 - number)):
                ref, sem = piece_groups(number), out_send.at[at, way]
                finish.append(
                    functools.partial(
                        pl.when(here),
                        lambda ref=ref, sem=sem: remote(ref, ref, sem, own_sem.at[0], me, 1 - core).wait_send(),
                    )
                )

    def gather_step(at, step):
        z_first, second, third = products[at].route
        if step == 0:
            owns[PIECE, at] = local(own_piece(at), window(at, me), own_sem.at[at])
            if at != kv_at:
                finish.append(owns[PIECE, at].wait)
            if z_first:
                send(at, me, UP, z, z < 3, own=True)
                send(at, me, DOWN, z, z > 0, own=True)
                send(at, me, second, 4 + z, own=True)
                send(at, me, third, 8, own=True)
                left_here(quarters(at, 3), out_send.at[at, ACROSS_Y])
                line_sent(at, lambda number: held[at].at[: held[at].shape[0] // 4 * number])
            else:
                send(at, me, second, 0, own=True)
                send(at, me, third, 1, own=True)
                send(at, me, UP, 4 + z, z < 3, own=True)
                send(at, me, DOWN, 4 + z, z > 0, own=True)
                left_here(held[at].at[: held[at].shape[0] // 4 * 3], out_send.at[at, ACROSS_Y])
                line_sent(at, lambda number: quarters(at, number))
        elif z_first:
            if step <= 3:
                for there, zz, way, on in from_line(step):
                    where = place(zz, y, x)
                    arrive(at, where, zz, there)
                    send(at, where, way, zz, on)
                    send(at, where, second, 4 + zz, there)
                    send(at, where, third, 8, there)
            elif step <= 7:
                zz = z ^ (step - 4)
                where = near(second, zz)
                arrive(at, where, 4 + zz)
                send(at, where, third, 8)
            elif step == 8:
                arrived(quarters(at, 2), out_recv.at[at, 8])
        else:
            if step == 1:
                where = near(second, z)
                arrive(at, where, 0)
                send(at, where, third, 2)
                send(at, where, UP, 4 + z, z < 3)
                send(at, where, DOWN, 4 + z, z > 0)
            elif step == 2:
                for arrival, where in ((1, near(third, z)), (2, opposite(z))):
                    arrive(at, where, arrival)
                    send(at, where, UP, 4 + z, z < 3)
                    send(at, where, DOWN, 4 + z, z > 0)
            elif step <= 5:
                for there, zz, way, on in from_line(step - 2):
                    pl.when(there)(
                        functools.partial(arrived, quarters(at, 1), out_recv.at[at, 4 + zz])
                    )
                    for where in (place(zz, y, x), near(second, zz), near(third, zz), opposite(zz)):
                        send(at, where, way, 4 + zz, on)

    def load_weight(index):
        return pltpu.make_async_copy(
            weights[index], weight_buffer.at[index % 2], weight_sem.at[index % 2]
        )

    def input_gradient():
        load_weight(0).start()
        for index in range(6):
            load_weight(index + 1).start()
            load_weight(index).wait()
            columns = lanes(normed_grad, core if index < 3 else 1 - core, normed_grad.shape[1] // 2)
            term = dot_nt(rights[count - 3 + index % 3][...], weight_buffer[index % 2])
            if index % 3:
                columns[...] += term
            else:
                columns[...] = term
        width = resid_in.shape[1]
        cotan, values = normed_grad[...], resid_in[...].astype(F32)
        rate = lax.rsqrt(jnp.mean(values * values, axis=1, keepdims=True) + EPSILON)
        scaled = cotan * gain_one[...]
        slope = jnp.mean(scaled * values, axis=1, keepdims=True)
        back = rate * scaled - values * (rate * rate * rate) * slope
        input_grad[...] = (resid_grad[...] + back).astype(BF16)
        gain_grad = jnp.sum(cotan * values * rate, axis=0, keepdims=True)
        column = jnp.zeros((BUCKETS, 1), F32)
        for apart in range(lines.shape[0]):
            sums = lines[apart : apart + 1, :TILE]
            if apart + 1 < lines.shape[0]:
                sums = sums + lines[apart + 1 : apart + 2, TILE:]
            column = column + jnp.sum(in_bucket[apart] * sums, axis=1, keepdims=True)
        place_at = lax.broadcasted_iota(jnp.int32, (BUCKETS, 128), 1)
        table = jnp.where(place_at == me, column, 0.0)
        for half in range(2):
            for index in range(4):
                start = (4 * half + index) * 128
                vec_in[half, index : index + 1, :] = gain_grad[:, start : start + 128]
            vec_in[half, 4:16, :] = gains[half]
            vec_in[half, 16:, :] = table[half * (BUCKETS // 2) : (half + 1) * (BUCKETS // 2)]
        vector_step(0)

    def encoder_gradient():
        own = kv_both[0, pl.ds(pl.multiple_of(me * encoder_grad.shape[0], 16), encoder_grad.shape[0]), :]
        width = own.shape[1] // 2
        for side in (0, 1):
            terms = []
            for index in (6 + 2 * side, 7 + 2 * side):
                if index < 9:
                    load_weight(index + 1).start()
                load_weight(index).wait()
                part = slice((index % 2) * width, (index % 2 + 1) * width)
                terms.append(dot_nt(own[:, part], weight_buffer[index % 2]))
            columns = lanes(encoder_grad, core if side == 0 else 1 - core, width // 2)
            columns[...] = (terms[0] + terms[1]).astype(BF16)

    later = {}

    def grads_leave():
        later[0] = to_all(0, grad_packed, grad_landed)

    def attention():
        later[0]()
        attend_back(
            order, held_at, pairs, lone, grad_landed, attn_sum, log_norm, bias_lines, back_packed, lines,
            *attention_scratch,
        )
        later[1] = to_all(1, back_packed, back_landed)

    def grads_return():
        later[1]()
        dq_ref, dk_ref, dv_ref = rights[count - 3 :]
        for pair in range(peers // 2):
            cols = slice(pair * 2 * HEAD_DIM, (pair + 1) * 2 * HEAD_DIM)
            dq_ref[:, cols], dk_ref[:, cols] = unpack_pair(back_landed, pair, slice(0, 2 * BLOCK))
            first, second = unpack_pair(back_landed, pair, slice(2 * BLOCK, 3 * BLOCK))
            dv_ref[:BLOCK, cols] = first
            dv_ref[BLOCK:, cols] = second

    def kv_gathered():
        owns[PIECE, kv_at].wait()
        launch(remote(kv_both.at[0], kv_both.at[1], kv_sem.at[0], kv_sem.at[1], me, 1 - core))
        left_here(kv_both.at[0], kv_sem.at[0])
        encoder_gradient()

    single = [grads_leave, attention, grads_return, input_gradient]
    single += [functools.partial(vector_add, step) for step in range(5)] + [kv_gathered]
    for code in SCHEDULE:
        stage, at = divmod(code, 16)
        if stage == 0:
            send_operands([at])
        elif stage == 1:
            pass_on(at)
        elif stage == 2:
            product_away(at)
        elif stage == 3:
            add_pair(at)
            line_step(at, 0)
        elif stage < 7:
            line_step(at, stage - 3)
        elif stage < 16:
            gather_step(at, stage - 7)
        else:
            single[at]()

    arrived(kv_both.at[1], kv_sem.at[1])
    for each in finish:
        each()


def weight_grads(products, lefts, rights, left_far, right_far, others, weights):
    count, peers = len(products), lax.axis_size("ctx")
    tokens = lefts[0].shape[0]
    length = others[5].shape[1]
    kv_at = [product.left for product in products].index(SUMMED)
    kv_rows, kv_width = rights[kv_at].shape
    spans = length // TILE
    dma = pltpu.SemaphoreType.DMA
    vmem = pltpu.VMEM
    width = HEADS * HEAD_DIM
    halves = [left.shape[1] // 2 for left in lefts]
    widths = [right.shape[1] for right in rights] + [width] * 3
    helds = []
    for product, right in zip(products, widths):
        height = kv_rows if product.left == SUMMED else halves[product.left]
        helds.append((height, right // 4) if product.tall else (height // 2, right // 2))
    lands = [vmem(shape, BF16) for shape in helds]
    chunk = (peers, BLOCK, 2 * HEAD_DIM)
    chunks = (peers, 3 * BLOCK, 2 * HEAD_DIM)
    smem_spec = pl.BlockSpec(memory_space=pltpu.SMEM)
    return pl.pallas_call(
        functools.partial(weight_grad_kernel, products, len(lefts)),
        out_shape=[
            jax.ShapeDtypeStruct((halves[product.left], right), BF16)
            for product, right in zip(products, widths)
            if product.left != SUMMED
        ]
        + [
            jax.ShapeDtypeStruct((32, 128), F32),
            jax.ShapeDtypeStruct((tokens, width), BF16),
            jax.ShapeDtypeStruct((kv_rows // peers, width), BF16),
            jax.ShapeDtypeStruct((2, kv_rows, kv_width), BF16),
        ],
        in_specs=[any_spec()] * len(lefts)
        + [vmem_spec() if product.left == SUMMED else any_spec() for product in products[: len(rights)]]
        + [any_spec()] * (len(left_far) + len(right_far))
        + [smem_spec] * 2
        + [vmem_spec()] * (len(others) - 2)
        + [any_spec()] * len(weights),
        out_specs=[any_spec()] * (count - 1) + [vmem_spec()] * 4,
        scratch_shapes=[vmem((4 * tokens, half), BF16) for half in halves]
        + [vmem((tokens, half), BF16) for half in halves]
        + [vmem((half, 4 * tokens), BF16) for half in halves]
        + [
            vmem((kv_rows if product.left == SUMMED else 4 * tokens, right // 2), BF16)
            for product, right in zip(products, widths)
        ]
        + lands * 3
        + [vmem((5 * height // 4, width_held), BF16) for height, width_held in helds]
        + [vmem((tokens, width), BF16)] * 3
        + [vmem(chunk, BF16), vmem(chunk, BF16), vmem(chunks, BF16), vmem(chunks, BF16)]
        + [vmem((spans, 2 * TILE), F32)]
        + [vmem((length, HEAD_DIM), BF16)] * 4
        + [vmem((HEAD_DIM, length), BF16)]
        + [vmem((spans, TILE, TILE), F32)] * 2
        + [vmem((length, HEAD_DIM), F32)] * 3
        + [vmem((1, length), F32), vmem((HEAD_DIM, length), F32)]
        + [
            vmem((2, 32, 128), F32),
            vmem((4, 32, 128), F32),
            vmem((5, 32, 128), F32),
            vmem((2,) + weights[0].shape, BF16),
            vmem((tokens, width), F32),
        ]
        + [
            dma((len(lefts),)),
            dma((len(lefts),)),
            dma((len(lefts), 4)),
            dma((count,)),
            dma((count,)),
            dma((count, 3)),
            dma((count,)),
            dma((count,)),
            dma((count,)),
            dma((count, 2, 3)),
            dma((count, 3)),
            dma((count, 9)),
            dma((count,)),
            dma((5,)),
            dma((5,)),
            dma((2,)),
            dma((2,)),
            dma((2,)),
            dma((2,)),
            dma((2,)),
        ],
        compiler_params=pltpu.CompilerParams(
            collective_id=5, has_side_effects=True, vmem_limit_bytes=60 * MIB
        ),
        name="weight_grads",
    )(*lefts, *rights, *left_far, *right_far, *others, *weights)


def on_device_by_heads(
    inputs,
    encoder,
    cotangent,
    block_order,
    bucket_of,
    self_gain,
    query_weight,
    key_weight,
    value_weight,
    out_weight,
    bias_table,
    cross_gain,
    cross_query,
    cross_key,
    cross_value,
    cross_out,
    mlp_gain,
    gate_weight,
    up_weight,
    down_weight,
):
    blocks = block_order.shape[0]
    block_ids = jnp.arange(blocks, dtype=jnp.int32)
    held_at = jnp.sum(
        jnp.where(block_order[None, :] == block_ids[:, None], block_ids[None, :], 0), axis=1
    )
    bucket_ids = jnp.arange(BUCKETS, dtype=jnp.int32)[None, :, None]
    bucket_tiles = (bucket_of.reshape(-1, 1, TILE) == bucket_ids).astype(F32)
    small = jnp.concatenate(
        [jnp.stack([self_gain, cross_gain, mlp_gain]).astype(F32), jnp.zeros((5,) + self_gain.shape, F32)]
    )
    table = jnp.pad(bias_table.astype(F32), ((0, 0), (0, 128 - HEADS)))
    sources = Weights(
        query=query_weight,
        key=key_weight,
        value=value_weight,
        out=out_weight,
        cross_key=cross_key,
        cross_value=cross_value,
        cross_query=cross_query,
        cross_out=cross_out,
        gate=gate_weight,
        up=up_weight,
        down=down_weight,
    )
    made, far, lent = layer(
        inputs[0], cotangent[0], encoder[0], small, table, bucket_tiles, held_at, block_order, sources
    )

    z_then_yx, z_then_xy, yx_then_z, xy_then_z = (
        (True, ACROSS_Y, ACROSS_X),
        (True, ACROSS_X, ACROSS_Y),
        (False, ACROSS_Y, ACROSS_X),
        (False, ACROSS_X, ACROSS_Y),
    )
    lefts = (
        made.normed_three, made.hidden, made.cross_mixed, made.normed_two, made.attended, made.normed_one
    )
    products = (
        Product(0, made.gate_grad, BIT_Y, False, z_then_xy),
        Product(1, cotangent[0], BIT_X, True, xy_then_z),
        Product(0, made.up_grad, BIT_Y, False, z_then_yx),
        Product(SUMMED, made.kv_part, BIT_X, False, z_then_yx),
        Product(2, made.branch_two, BIT_X, False, z_then_xy),
        Product(3, made.cross_q_grad, BIT_Y, False, z_then_xy),
        Product(4, made.branch_one, BIT_Y, False, z_then_yx),
        Product(5, None, BIT_X, False, z_then_yx),
        Product(5, None, BIT_X, False, z_then_xy),
        Product(5, None, BIT_X, False, z_then_yx),
    )
    *wholes, totals, input_grad, encoder_grad, cross_kv_both = weight_grads(
        products,
        lefts,
        [product.right for product in products[:7]],
        [far.normed_three, far.hidden],
        [far.gate, far.branch_three, far.up],
        [
            block_order,
            held_at,
            made.dattn,
            made.pairs,
            made.lone,
            made.attn_sum,
            made.log_norm,
            made.bias_lines,
            bucket_tiles,
            inputs[0],
            made.gain_one,
            made.resid_grad,
            made.gain_grads,
        ],
        [query_weight, key_weight, value_weight, *lent[:3], cross_key, cross_value, *lent[3:]],
    )
    head_width = HEADS * HEAD_DIM
    cross_kv_w_grad = left_contract(
        made.encoder_both, cross_kv_both.reshape(-1, 2 * head_width)
    )
    (
        sum_gate,
        sum_down,
        sum_up,
        sum_cross_out,
        sum_cross_query,
        sum_out,
        sum_query,
        sum_key,
        sum_value,
    ) = (member.astype(F32) for member in wholes)
    sum_gain_one, sum_gain_two, sum_gain_three = (
        totals[4 * at : 4 * at + 4].reshape(-1) for at in range(3)
    )
    sum_table = totals[16:, :HEADS]
    return (
        made.result[None],
        input_grad[None],
        encoder_grad[None],
        sum_gain_one,
        sum_query,
        sum_key,
        sum_value,
        sum_out,
        sum_table,
        sum_gain_two,
        sum_cross_query,
        cross_kv_w_grad[:, :head_width],
        cross_kv_w_grad[:, head_width:],
        sum_cross_out,
        sum_gain_three,
        sum_gate,
        sum_up,
        sum_down,
    )


def solution(mesh):
    by_heads = mesh.shape["ctx"] == HEADS and mesh.shape["wsh"] == 2
    return jax.shard_map(
        on_device_by_heads if by_heads else on_device,
        mesh=mesh,
        in_specs=(
            P("wsh", "ctx", None),
            P("wsh", "ctx", None),
            P("wsh", "ctx", None),
            P(),
            P(),
            P("wsh"),
            P("wsh", None),
            P("wsh", None),
            P("wsh", None),
            P("wsh", None),
            P("wsh", None),
            P("wsh"),
            P("wsh", None),
            P("wsh", None),
            P("wsh", None),
            P("wsh", None),
            P("wsh"),
            P("wsh", None),
            P("wsh", None),
            P("wsh", None),
        ),
        out_specs=(
            P("wsh", "ctx", None),
            P("wsh", "ctx", None),
            P("wsh", "ctx", None),
            P("wsh"),
            P("wsh", None),
            P("wsh", None),
            P("wsh", None),
            P("wsh", None),
            P("wsh", None),
            P("wsh"),
            P("wsh", None),
            P("wsh", None),
            P("wsh", None),
            P("wsh", None),
            P("wsh"),
            P("wsh", None),
            P("wsh", None),
            P("wsh", None),
        ),
        check_vma=False,
    )
```

```python
import functools
from typing import Any, NamedTuple

import jax
import jax.numpy as jnp
from jax import lax
from jax.experimental import pallas as pl
from jax.experimental.pallas import tpu as pltpu
from jax.sharding import PartitionSpec as P

HEADS = 16
HEAD_DIM = 64
BUCKETS = 32


EPSILON = 1e-06
NEG_BIG = -1e30


def rms_norm(values, gain):
    return values * lax.rsqrt(jnp.mean(values * values, axis=-1, keepdims=True) + EPSILON) * gain


def plain_dot(left, right):
    return jnp.dot(left, right, preferred_element_type=jnp.float32)


def left_contract(left, right):
    return lax.dot_general(
        left, right, (((0,), (0,)), ((), ())), preferred_element_type=jnp.float32
    )


def right_contract(left, right):
    return lax.dot_general(
        left, right, (((1,), (1,)), ((), ())), preferred_element_type=jnp.float32
    )


def gelu_product(gate_vals, up_vals):
    return jax.nn.gelu(gate_vals, approximate=True) * up_vals


def norm_back(values, gain, cotan):
    normed, pullback = jax.vjp(rms_norm, values, gain)
    return pullback(cotan)


def lookup_positions(block_order, first_row, row_count, block_len):
    token_ids = first_row + jnp.arange(row_count, dtype=jnp.int32)
    block_ids = token_ids // block_len
    matches = block_ids[:, None] == jnp.arange(block_order.shape[0], dtype=jnp.int32)[None, :]
    starts = jnp.sum(jnp.where(matches, block_order[None, :], 0), axis=1)
    return starts * block_len + token_ids % block_len


def fold_groups(step_fn, carried, pieces, shard_rows):
    piece_rows = pieces[0].shape[0]
    shards = max(1, piece_rows // shard_rows)
    group_limit = max(1, 1152 // shard_rows)
    group_size = max(
        (divisor for divisor in range(1, min(shards, group_limit) + 1) if shards % divisor == 0)
    )
    group_rows = group_size * shard_rows

    def group_step(group_idx, inner_state):
        sub_pieces = tuple(
            (
                lax.dynamic_slice_in_dim(member, group_idx * group_rows, group_rows, 0)
                for member in pieces
            )
        )
        return step_fn(inner_state, sub_pieces, group_idx * group_rows)

    return lax.fori_loop(0, shards // group_size, group_step, carried)


def on_device(
    inputs,
    encoder,
    cotangent,
    block_order,
    bucket_of,
    self_gain,
    query_weight,
    key_weight,
    value_weight,
    out_weight,
    bias_table,
    cross_gain,
    cross_query,
    cross_key,
    cross_value,
    cross_out,
    mlp_gain,
    gate_weight,
    up_weight,
    down_weight,
):
    (
        gain_one,
        query_full,
        key_full,
        value_full,
        out_full,
        bias_rows,
        gain_two,
        cross_query_full,
        cross_key_full,
        cross_value_full,
        cross_out_full,
        gain_three,
        gate_full,
        up_full,
        down_full,
    ) = (
        lax.all_gather(self_gain, "wsh", axis=0, tiled=True),
        lax.all_gather(query_weight, "wsh", axis=0, tiled=True),
        lax.all_gather(key_weight, "wsh", axis=0, tiled=True),
        lax.all_gather(value_weight, "wsh", axis=0, tiled=True),
        lax.all_gather(out_weight, "wsh", axis=0, tiled=True),
        lax.all_gather(bias_table, "wsh", axis=0, tiled=True),
        lax.all_gather(cross_gain, "wsh", axis=0, tiled=True),
        lax.all_gather(cross_query, "wsh", axis=0, tiled=True),
        lax.all_gather(cross_key, "wsh", axis=0, tiled=True),
        lax.all_gather(cross_value, "wsh", axis=0, tiled=True),
        lax.all_gather(cross_out, "wsh", axis=0, tiled=True),
        lax.all_gather(mlp_gain, "wsh", axis=0, tiled=True),
        lax.all_gather(gate_weight, "wsh", axis=0, tiled=True),
        lax.all_gather(up_weight, "wsh", axis=0, tiled=True),
        lax.all_gather(down_weight, "wsh", axis=0, tiled=True),
    )
    gain_one = gain_one.astype(jnp.float32)
    gain_two = gain_two.astype(jnp.float32)
    gain_three = gain_three.astype(jnp.float32)
    resid_in = inputs[0].astype(jnp.float32)
    tokens = resid_in.shape[0]
    block_len = tokens // 2
    head_width = HEADS * HEAD_DIM
    total_rows = tokens * lax.axis_size("ctx")
    own_pos = lookup_positions(block_order, lax.axis_index("ctx") * tokens, tokens, block_len)
    bucket_ids = jnp.arange(BUCKETS, dtype=jnp.int32)
    boundaries = jnp.sum((bucket_of[None, :] < bucket_ids[1:, None]).astype(jnp.int32), axis=1)

    def bucket_indicator_of(clipped):
        bucket = jnp.sum((clipped[None] >= boundaries[:, None, None]).astype(jnp.int32), axis=0)
        return (bucket[None] == bucket_ids[:, None, None]).astype(jnp.bfloat16)

    def query_key_logits(query_heads, key_heads, query_pos, key_pos):
        logits = jnp.einsum(
            "qhe,khe->hqk", query_heads, key_heads, preferred_element_type=jnp.float32
        )
        offset = query_pos[:, None] - key_pos[None, :]
        clipped = jnp.maximum(offset, 0)
        indicator = bucket_indicator_of(clipped)
        rel_bias = jnp.einsum(
            "ouw,om->muw", indicator, bias_rows, preferred_element_type=jnp.float32
        )
        allowed = (offset >= 0)[None]
        return (jnp.where(allowed, logits + rel_bias, NEG_BIG), allowed, indicator)

    normed_one = rms_norm(resid_in, gain_one).astype(jnp.bfloat16)
    query_heads = (
        plain_dot(normed_one, query_full).astype(jnp.bfloat16).reshape(tokens, HEADS, HEAD_DIM)
    )
    key_heads = (
        plain_dot(normed_one, key_full).astype(jnp.bfloat16).reshape(tokens, HEADS, HEAD_DIM)
    )
    value_heads = (
        plain_dot(normed_one, value_full).astype(jnp.bfloat16).reshape(tokens, HEADS, HEAD_DIM)
    )

    def norm_step(carried, pieces, first_row):
        running_max, running_sum = carried
        key_pos = lookup_positions(block_order, first_row, pieces[0].shape[0], block_len)
        logits, allowed, indicator = query_key_logits(query_heads, pieces[0], own_pos, key_pos)
        new_max = jnp.maximum(running_max, jnp.max(logits, axis=-1))
        kept = jnp.where(allowed, jnp.exp(logits - new_max[..., None]), 0.0)
        return (new_max, running_sum * jnp.exp(running_max - new_max) + jnp.sum(kept, axis=-1))

    start_state = (
        jnp.full((HEADS, tokens), NEG_BIG, jnp.float32),
        jnp.zeros((HEADS, tokens), jnp.float32),
    )
    running_max, running_sum = fold_groups(
        norm_step, start_state, (lax.all_gather(key_heads, "ctx", axis=0, tiled=True),), tokens
    )
    log_norm = running_max + jnp.log(running_sum)

    def output_step(carried, pieces, first_row):
        key_pos = lookup_positions(block_order, first_row, pieces[0].shape[0], block_len)
        logits, allowed, indicator = query_key_logits(query_heads, pieces[0], own_pos, key_pos)
        attn_probs = jnp.exp(logits - log_norm[..., None]).astype(jnp.bfloat16)
        return carried + jnp.einsum(
            "hqk,khe->qhe", attn_probs, pieces[1], preferred_element_type=jnp.float32
        )

    zero_heads = jnp.zeros((tokens, HEADS, HEAD_DIM), jnp.float32)
    attn_sum = fold_groups(
        output_step,
        zero_heads,
        (
            lax.all_gather(key_heads, "ctx", axis=0, tiled=True),
            lax.all_gather(value_heads, "ctx", axis=0, tiled=True),
        ),
        tokens,
    )
    attended = attn_sum.reshape(tokens, head_width).astype(jnp.bfloat16)
    after_self = resid_in + plain_dot(attended, out_full)
    normed_two = rms_norm(after_self, gain_two).astype(jnp.bfloat16)
    cross_q_heads = (
        plain_dot(normed_two, cross_query_full)
        .astype(jnp.bfloat16)
        .reshape(tokens, HEADS, HEAD_DIM)
    )
    encoder_rows = encoder[0]
    encoder_key_rows, cross_values = (
        lax.all_gather(
            plain_dot(encoder_rows, cross_key_full).astype(jnp.bfloat16), "ctx", axis=0, tiled=True
        ),
        lax.all_gather(
            plain_dot(encoder_rows, cross_value_full).astype(jnp.bfloat16),
            "ctx",
            axis=0,
            tiled=True,
        ),
    )
    cross_k_heads = encoder_key_rows.reshape(encoder_key_rows.shape[0], HEADS, HEAD_DIM)
    cross_v_heads = cross_values.reshape(cross_values.shape[0], HEADS, HEAD_DIM)
    cross_logits = jnp.einsum(
        "qhe,khe->hqk", cross_q_heads, cross_k_heads, preferred_element_type=jnp.float32
    )
    cross_exact = jnp.exp(cross_logits - jax.nn.logsumexp(cross_logits, axis=-1, keepdims=True))
    cross_probs = cross_exact.astype(jnp.bfloat16)
    cross_mixed = (
        jnp.einsum("hqk,khe->qhe", cross_probs, cross_v_heads, preferred_element_type=jnp.float32)
        .reshape(tokens, head_width)
        .astype(jnp.bfloat16)
    )
    after_cross = after_self + plain_dot(cross_mixed, cross_out_full)
    normed_three = rms_norm(after_cross, gain_three).astype(jnp.bfloat16)
    gate_act = plain_dot(normed_three, gate_full)
    up_act = plain_dot(normed_three, up_full)
    hidden_float, mlp_pull = jax.vjp(gelu_product, gate_act, up_act)
    hidden = hidden_float.astype(jnp.bfloat16)
    result = after_cross + plain_dot(hidden, down_full)
    resid_grad = cotangent[0].astype(jnp.float32)
    branch_three = resid_grad.astype(jnp.bfloat16)
    down_grad = left_contract(hidden, branch_three)
    hidden_state_gradient = right_contract(branch_three, down_full)
    gate_grad, up_grad = mlp_pull(hidden_state_gradient)
    gate_grad = gate_grad.astype(jnp.bfloat16)
    up_grad = up_grad.astype(jnp.bfloat16)
    gate_w_grad = left_contract(normed_three, gate_grad)
    up_w_grad = left_contract(normed_three, up_grad)
    normed_three_grad = right_contract(gate_grad, gate_full) + right_contract(up_grad, up_full)
    part_grad, gain_three_grad = norm_back(after_cross, gain_three, normed_three_grad)
    after_cross_grad = resid_grad + part_grad
    branch_two = after_cross_grad.astype(jnp.bfloat16)
    cross_out_grad = left_contract(cross_mixed, branch_two)
    mix_grad = (
        right_contract(branch_two, cross_out_full)
        .astype(jnp.bfloat16)
        .reshape(tokens, HEADS, HEAD_DIM)
    )
    cross_score_grad = jnp.einsum(
        "qhe,khe->hqk", mix_grad, cross_v_heads, preferred_element_type=jnp.float32
    )
    cross_delta = jnp.sum(cross_exact * cross_score_grad, axis=-1, keepdims=True)
    cross_dlogits = (cross_exact * (cross_score_grad - cross_delta)).astype(jnp.bfloat16)
    cross_q_grad = (
        jnp.einsum("hqk,khe->qhe", cross_dlogits, cross_k_heads, preferred_element_type=jnp.float32)
        .reshape(tokens, head_width)
        .astype(jnp.bfloat16)
    )
    cross_k_part = jnp.einsum(
        "hqk,qhe->khe", cross_dlogits, cross_q_heads, preferred_element_type=jnp.float32
    ).reshape(-1, head_width)
    cross_v_part = jnp.einsum(
        "hqk,qhe->khe", cross_probs, mix_grad, preferred_element_type=jnp.float32
    ).reshape(-1, head_width)
    cross_k_grad, cross_v_grad = (
        lax.psum_scatter(cross_k_part, "ctx", scatter_dimension=0, tiled=True),
        lax.psum_scatter(cross_v_part, "ctx", scatter_dimension=0, tiled=True),
    )
    cross_k_grad = cross_k_grad.astype(jnp.bfloat16)
    cross_v_grad = cross_v_grad.astype(jnp.bfloat16)
    cross_query_grad = left_contract(normed_two, cross_q_grad)
    cross_key_grad = left_contract(encoder_rows, cross_k_grad)
    cross_value_grad = left_contract(encoder_rows, cross_v_grad)
    encoder_grad = (
        right_contract(cross_k_grad, cross_key_full)
        + right_contract(cross_v_grad, cross_value_full)
    ).astype(jnp.bfloat16)
    normed_two_grad = right_contract(cross_q_grad, cross_query_full)
    part_grad, gain_two_grad = norm_back(after_self, gain_two, normed_two_grad)
    after_self_grad = after_cross_grad + part_grad
    branch_one = after_self_grad.astype(jnp.bfloat16)
    out_w_grad = left_contract(attended, branch_one)
    dattn_heads = (
        right_contract(branch_one, out_full).astype(jnp.bfloat16).reshape(tokens, HEADS, HEAD_DIM)
    )
    row_delta = jnp.einsum("qhe,qhe->hq", dattn_heads.astype(jnp.float32), attn_sum)

    def block_grads(
        query_side, grad_side, norm_side, delta_side, query_pos, key_side, value_side, key_pos
    ):
        logits, allowed, indicator = query_key_logits(query_side, key_side, query_pos, key_pos)
        exact = jnp.exp(logits - norm_side[..., None])
        score_grad = jnp.einsum(
            "qhe,khe->hqk", grad_side, value_side, preferred_element_type=jnp.float32
        )
        logits_gradient = (exact * (score_grad - delta_side[..., None])).astype(jnp.bfloat16)
        grad_query = jnp.einsum(
            "hqk,khe->qhe", logits_gradient, key_side, preferred_element_type=jnp.float32
        )
        grad_key = jnp.einsum(
            "hqk,qhe->khe", logits_gradient, query_side, preferred_element_type=jnp.float32
        )
        grad_value = jnp.einsum(
            "hqk,qhe->khe",
            exact.astype(jnp.bfloat16),
            grad_side,
            preferred_element_type=jnp.float32,
        )
        bucket_table_gradient = jnp.einsum(
            "ouw,muw->om", indicator, logits_gradient, preferred_element_type=jnp.float32
        )
        return (grad_query, grad_key, grad_value, bucket_table_gradient)

    zero_table = jnp.zeros((BUCKETS, HEADS), jnp.float32)
    full_zero = jnp.zeros((total_rows, HEADS, HEAD_DIM), jnp.float32)

    def key_grad_step(carried, pieces, first_row):
        query_total, table_total, key_total, value_total = carried
        key_pos = lookup_positions(block_order, first_row, pieces[0].shape[0], block_len)
        grad_query, grad_key, grad_value, bucket_table_gradient = block_grads(
            query_heads, dattn_heads, log_norm, row_delta, own_pos, pieces[0], pieces[1], key_pos
        )
        key_total = lax.dynamic_update_slice_in_dim(key_total, grad_key, first_row, 0)
        value_total = lax.dynamic_update_slice_in_dim(value_total, grad_value, first_row, 0)
        return (
            query_total + grad_query,
            table_total + bucket_table_gradient,
            key_total,
            value_total,
        )

    query_sum, table_grad, key_partial, value_partial = fold_groups(
        key_grad_step,
        (zero_heads, zero_table, full_zero, full_zero),
        (
            lax.all_gather(key_heads, "ctx", axis=0, tiled=True),
            lax.all_gather(value_heads, "ctx", axis=0, tiled=True),
        ),
        tokens,
    )
    key_sum, value_accumulated = (
        lax.psum_scatter(key_partial, "ctx", scatter_dimension=0, tiled=True),
        lax.psum_scatter(value_partial, "ctx", scatter_dimension=0, tiled=True),
    )
    query_grad = query_sum.reshape(tokens, head_width).astype(jnp.bfloat16)
    key_grad = key_sum.reshape(tokens, head_width).astype(jnp.bfloat16)
    value_grad = value_accumulated.reshape(tokens, head_width).astype(jnp.bfloat16)
    query_w_grad = left_contract(normed_one, query_grad)
    key_w_grad = left_contract(normed_one, key_grad)
    value_w_grad = left_contract(normed_one, value_grad)
    normed_one_grad = (
        right_contract(query_grad, query_full)
        + right_contract(key_grad, key_full)
        + right_contract(value_grad, value_full)
    )
    part_grad, gain_one_grad = norm_back(resid_in, gain_one, normed_one_grad)
    input_grad = (after_self_grad + part_grad).astype(jnp.bfloat16)
    (
        sum_gain_one,
        sum_query,
        sum_key,
        sum_value,
        sum_out,
        sum_table,
        sum_gain_two,
        sum_cross_query,
        sum_cross_key,
        sum_cross_value,
        sum_cross_out,
        sum_gain_three,
        sum_gate,
        sum_up,
        sum_down,
    ) = (
        lax.psum_scatter(
            gain_one_grad.astype(jnp.bfloat16), "wsh", scatter_dimension=0, tiled=True
        ).astype(jnp.float32),
        lax.psum_scatter(
            query_w_grad.astype(jnp.bfloat16), "wsh", scatter_dimension=0, tiled=True
        ).astype(jnp.float32),
        lax.psum_scatter(
            key_w_grad.astype(jnp.bfloat16), "wsh", scatter_dimension=0, tiled=True
        ).astype(jnp.float32),
        lax.psum_scatter(
            value_w_grad.astype(jnp.bfloat16), "wsh", scatter_dimension=0, tiled=True
        ).astype(jnp.float32),
        lax.psum_scatter(
            out_w_grad.astype(jnp.bfloat16), "wsh", scatter_dimension=0, tiled=True
        ).astype(jnp.float32),
        lax.psum_scatter(
            table_grad.astype(jnp.bfloat16), "wsh", scatter_dimension=0, tiled=True
        ).astype(jnp.float32),
        lax.psum_scatter(
            gain_two_grad.astype(jnp.bfloat16), "wsh", scatter_dimension=0, tiled=True
        ).astype(jnp.float32),
        lax.psum_scatter(
            cross_query_grad.astype(jnp.bfloat16), "wsh", scatter_dimension=0, tiled=True
        ).astype(jnp.float32),
        lax.psum_scatter(
            cross_key_grad.astype(jnp.bfloat16), "wsh", scatter_dimension=0, tiled=True
        ).astype(jnp.float32),
        lax.psum_scatter(
            cross_value_grad.astype(jnp.bfloat16), "wsh", scatter_dimension=0, tiled=True
        ).astype(jnp.float32),
        lax.psum_scatter(
            cross_out_grad.astype(jnp.bfloat16), "wsh", scatter_dimension=0, tiled=True
        ).astype(jnp.float32),
        lax.psum_scatter(
            gain_three_grad.astype(jnp.bfloat16), "wsh", scatter_dimension=0, tiled=True
        ).astype(jnp.float32),
        lax.psum_scatter(
            gate_w_grad.astype(jnp.bfloat16), "wsh", scatter_dimension=0, tiled=True
        ).astype(jnp.float32),
        lax.psum_scatter(
            up_w_grad.astype(jnp.bfloat16), "wsh", scatter_dimension=0, tiled=True
        ).astype(jnp.float32),
        lax.psum_scatter(
            down_grad.astype(jnp.bfloat16), "wsh", scatter_dimension=0, tiled=True
        ).astype(jnp.float32),
    )
    total_grads = lax.psum(
        (
            sum_gain_one,
            sum_query,
            sum_key,
            sum_value,
            sum_out,
            sum_table,
            sum_gain_two,
            sum_cross_query,
            sum_cross_key,
            sum_cross_value,
            sum_cross_out,
            sum_gain_three,
            sum_gate,
            sum_up,
            sum_down,
        ),
        "ctx",
    )
    return (result.astype(jnp.bfloat16)[None], input_grad[None], encoder_grad[None]) + tuple(
        total_grads
    )


F32 = jnp.float32
BF16 = jnp.bfloat16
MESH = pl.DeviceIdType.MESH
TILE = 256
BLOCK = 64
MIB = 2**20
GELU_RATE, GELU_CUBE = 0.7978845608, 0.044715


def dot_nt(left, right):
    return lax.dot_general(left, right, (((1,), (1,)), ((), ())), preferred_element_type=F32)


def vmem_spec():
    return pl.BlockSpec(memory_space=pltpu.VMEM)


def any_spec():
    return pl.BlockSpec(memory_space=pl.ANY)


def unpack_pair(landed, pair, rows):
    left, right = landed[2 * pair, rows, :], landed[2 * pair + 1, rows, :]
    return (
        jnp.concatenate([left[:, :HEAD_DIM], right[:, :HEAD_DIM]], axis=1),
        jnp.concatenate([left[:, HEAD_DIM:], right[:, HEAD_DIM:]], axis=1),
    )


def place_tiles(bias_lines, tiles):
    for apart in range(tiles.shape[0]):
        line = jnp.broadcast_to(bias_lines[apart : apart + 1, :], (TILE, 2 * TILE))
        tiles[apart] = pltpu.roll(line, 0, 1, stride=1, stride_axis=0)[:, :TILE]


def attend_scratch(blocks):
    length = blocks * BLOCK
    vmem = pltpu.VMEM
    return [
        vmem((length, HEAD_DIM), BF16),
        vmem((length, HEAD_DIM), BF16),
        vmem((HEAD_DIM, length), BF16),
        vmem((length // TILE, TILE, TILE), F32),
        vmem((length, HEAD_DIM), F32),
        vmem((length, HEAD_DIM), F32),
    ]


def attend(order, held_at, pairs, lone, bias_lines, out_ref, sum_ref, norm_ref, q_s, k_s, vt_s, tiles, staged, o_s):
    blocks = held_at.shape[0]
    spans = blocks * BLOCK // TILE

    def in_order(into):
        for block in range(blocks):
            at = slice(block * BLOCK, (block + 1) * BLOCK)
            into[at, :] = staged[pl.ds(held_at[block] * BLOCK, BLOCK), :].astype(into.dtype)

    for side, into in ((0, q_s), (1, k_s)):
        for device in range(blocks // 2):
            at = slice(2 * device * BLOCK, 2 * (device + 1) * BLOCK)
            staged[at, :] = pairs[device, :, side * HEAD_DIM : (side + 1) * HEAD_DIM].astype(F32)
        in_order(into)
    for stored in range(blocks):
        at = slice(stored * BLOCK, (stored + 1) * BLOCK)
        cols = slice(stored % 2 * HEAD_DIM, (stored % 2 + 1) * HEAD_DIM)
        staged[at, :] = lone[stored // 2, :, cols].astype(F32)
    in_order(o_s)
    vt_s[...] = jnp.transpose(o_s[...], (1, 0)).astype(BF16)
    place_tiles(bias_lines, tiles)
    for i in range(spans):
        at_i = slice(i * TILE, (i + 1) * TILE)
        queries = q_s[at_i, :]
        scores = [
            dot_nt(k_s[j * TILE : (j + 1) * TILE, :], queries) + tiles[i - j] for j in range(i + 1)
        ]
        top = functools.reduce(
            jnp.maximum, [jnp.max(each, axis=0, keepdims=True) for each in scores]
        )
        total = jnp.zeros((1, TILE), F32)
        mixed = jnp.zeros((HEAD_DIM, TILE), F32)
        for j in range(i + 1):
            weights = jnp.exp(scores[j] - top)
            total = total + jnp.sum(weights, axis=0, keepdims=True)
            mixed = mixed + plain_dot(
                vt_s[:, j * TILE : (j + 1) * TILE], weights.astype(BF16)
            )
        norm_ref[0:1, at_i] = top + jnp.log(total)
        sum_ref[:, at_i] = mixed / total
    o_s[...] = jnp.transpose(sum_ref[...], (1, 0))
    for stored in range(blocks):
        cols = slice(stored % 2 * HEAD_DIM, (stored % 2 + 1) * HEAD_DIM)
        out_ref[stored // 2, :, cols] = o_s[pl.ds(order[stored] * BLOCK, BLOCK), :].astype(BF16)


def attend_back(
    order, held_at, pairs, lone, grad_landed, sums, norm, bias_lines, out_ref, lines_ref,
    q_s, k_s, v_s, do_s, kt_s, tiles, by_offset, dq_s, dk_s, dv_s, delta_s, dqt_s,
):
    blocks = order.shape[0]
    spans = blocks * BLOCK // TILE
    def stored_rows(stored):
        return slice(stored * BLOCK, (stored + 1) * BLOCK), stored // 2, slice(
            stored % 2 * HEAD_DIM, (stored % 2 + 1) * HEAD_DIM
        )

    def in_order(into, staged):
        for block in range(blocks):
            at = slice(block * BLOCK, (block + 1) * BLOCK)
            into[at, :] = staged[pl.ds(held_at[block] * BLOCK, BLOCK), :].astype(BF16)

    for stored in range(blocks):
        at, device, cols = stored_rows(stored)
        pair = pairs[device, stored % 2 * BLOCK : (stored % 2 + 1) * BLOCK, :].astype(F32)
        dq_s[at, :] = pair[:, :HEAD_DIM]
        dk_s[at, :] = pair[:, HEAD_DIM:]
        dv_s[at, :] = lone[device, :, cols].astype(F32)
    in_order(q_s, dq_s)
    in_order(k_s, dk_s)
    in_order(v_s, dv_s)
    for stored in range(blocks):
        at, device, cols = stored_rows(stored)
        dq_s[at, :] = grad_landed[device, :, cols].astype(F32)
    in_order(do_s, dq_s)
    place_tiles(bias_lines, tiles)
    kt_s[...] = jnp.transpose(k_s[...].astype(F32), (1, 0)).astype(BF16)
    grad_t = jnp.transpose(do_s[...].astype(F32), (1, 0))
    delta_s[...] = jnp.sum(grad_t * sums[...], axis=0, keepdims=True)
    by_offset[...] = jnp.zeros_like(by_offset)
    dk_s[...] = jnp.zeros_like(dk_s)
    dv_s[...] = jnp.zeros_like(dv_s)
    for i in range(spans):
        at_i = slice(i * TILE, (i + 1) * TILE)
        queries, grads = q_s[at_i, :], do_s[at_i, :]
        norm_i, delta_i = norm[0:1, at_i], delta_s[0:1, at_i]
        dqt = jnp.zeros((HEAD_DIM, TILE), F32)
        for j in range(i + 1):
            at_j = slice(j * TILE, (j + 1) * TILE)
            exact = jnp.exp(dot_nt(k_s[at_j, :], queries) + tiles[i - j] - norm_i)
            dscore = exact * (dot_nt(v_s[at_j, :], grads) - delta_i)
            by_offset[i - j] += dscore
            rounded = dscore.astype(BF16)
            dv_s[at_j, :] += plain_dot(exact.astype(BF16), grads)
            dk_s[at_j, :] += plain_dot(rounded, queries)
            dqt = dqt + plain_dot(kt_s[:, at_j], rounded)
        dqt_s[:, at_i] = dqt
    dq_s[...] = jnp.transpose(dqt_s[...], (1, 0))
    for stored in range(blocks):
        device, half = stored // 2, stored % 2
        at = pl.ds(order[stored] * BLOCK, BLOCK)
        rows = slice(half * BLOCK, (half + 1) * BLOCK)
        cols = slice(half * HEAD_DIM, (half + 1) * HEAD_DIM)
        out_ref[device, rows, :HEAD_DIM] = dq_s[at, :].astype(BF16)
        out_ref[device, rows, HEAD_DIM:] = dk_s[at, :].astype(BF16)
        out_ref[device, 2 * BLOCK :, cols] = dv_s[at, :].astype(BF16)
    for apart in range(spans):
        folded = jnp.zeros((8, 2 * TILE), F32)
        for group in range(TILE // 8):
            rows = by_offset[apart, 8 * group : 8 * group + 8, :]
            wide = jnp.concatenate([rows, jnp.zeros((8, TILE), F32)], axis=1)
            folded = folded + (pltpu.roll(wide, 2 * TILE - 8 * group, 1) if group else wide)
        line = folded[0:1]
        for row in range(1, 8):
            line = line + pltpu.roll(folded[row : row + 1], 2 * TILE - row, 1)
        lines_ref[apart : apart + 1, :] = line


class Weights(NamedTuple):
    query: Any
    key: Any
    value: Any
    out: Any
    cross_key: Any
    cross_value: Any
    cross_query: Any
    cross_out: Any
    gate: Any
    up: Any
    down: Any


W = Weights(*range(11))
LENT = (W.query, W.key, W.value, W.cross_key, W.cross_value)


class Made(NamedTuple):
    normed_one: Any
    pairs: Any
    lone: Any
    attn_sum: Any
    log_norm: Any
    attended: Any
    normed_two: Any
    cross_mixed: Any
    normed_three: Any
    hidden: Any
    gate_grad: Any
    up_grad: Any
    branch_two: Any
    cross_q_grad: Any
    branch_one: Any
    dattn: Any
    kv_part: Any
    resid_grad: Any
    result: Any
    gain_grads: Any
    gain_one: Any
    bias_lines: Any
    encoder_both: Any


class Far(NamedTuple):
    normed_three: Any
    hidden: Any
    cross_mixed: Any
    normed_two: Any
    attended: Any
    normed_one: Any
    gate: Any
    branch_three: Any
    up: Any
    branch_two: Any


BIT_X, BIT_Y = 0, 1
FAR = Far(*range(10))
FAR_AXIS = Far(
    normed_three=BIT_Y,
    hidden=BIT_X,
    cross_mixed=BIT_X,
    normed_two=BIT_X,
    attended=BIT_Y,
    normed_one=BIT_X,
    gate=BIT_Y,
    branch_three=BIT_X,
    up=BIT_Y,
    branch_two=BIT_X,
)


class Scratch(NamedTuple):
    small_far: Any
    table_far: Any
    pairs_out: Any
    lone_out: Any
    encoder_all: Any
    mixed_out: Any
    mixed_in: Any
    cross_keys: Any
    cross_values: Any
    cross_queries: Any
    cross_exact: Any
    after_self: Any
    after_cross: Any
    gate_act: Any
    up_act: Any
    mix_grad: Any


def norm_parts(values):
    return lax.rsqrt(jnp.mean(values * values, axis=1, keepdims=True) + EPSILON)


def norm_backward(values, gain, cotan):
    rate = norm_parts(values)
    scaled = cotan * gain
    slope = jnp.mean(scaled * values, axis=1, keepdims=True)
    return (
        rate * scaled - values * (rate * rate * rate) * slope,
        jnp.sum(cotan * values * rate, axis=0, keepdims=True),
    )


def layer_kernel(tokens_in, cotangent, encoder, small, table, in_bucket, held_at, order, *refs):
    refs = list(refs)

    def take(number):
        taken = refs[:number]
        del refs[:number]
        return taken

    sources = take(len(W))
    out = Made(*take(len(Made._fields)))
    far = Far(*take(len(Far._fields)))
    lent = take(len(LENT))
    weights = take(len(W))
    own = Scratch(*take(len(Scratch._fields)))
    (own_sem, weight_own, weight_send, weight_recv, lent_send, lent_recv, far_send, far_recv, all_own, all_send, all_recv) = refs
    me, core = lax.axis_index("ctx"), lax.axis_index("wsh")
    peers = lax.axis_size("ctx")
    x, y = lax.rem(me, 2), lax.rem(me // 2, 2)
    tokens, width = tokens_in.shape
    finish = []

    barrier = pltpu.get_barrier_semaphore()
    for step in range(1, peers):
        pl.semaphore_signal(
            barrier, inc=1, device_id=(lax.rem(me + step, peers), core), device_id_type=MESH
        )
    pl.semaphore_signal(barrier, inc=1, device_id=(me, 1 - core), device_id_type=MESH)

    def half_rows(ref, side):
        half = ref.shape[0] // 2
        return ref.at[pl.ds(pl.multiple_of(side * half, 16), half)]

    def remote(src, dst, send_sem, recv_sem, ctx, side):
        return pltpu.make_async_remote_copy(
            src_ref=src,
            dst_ref=dst,
            send_sem=send_sem,
            recv_sem=recv_sem,
            device_id=(ctx, side),
            device_id_type=MESH,
        )

    def arrived(ref, sem):
        remote(ref, ref, own_sem, sem, me, 1 - core).wait_recv()

    def launch(src, dst, send_sem, recv_sem, ctx, side):
        remote(src, dst, send_sem, recv_sem, ctx, side).start()
        finish.append(lambda: remote(src, src, send_sem, own_sem, me, 1 - core).wait_send())

    def to_pair(at, source, halves=False):
        bit = FAR_AXIS[at]
        if halves:
            half = source.shape[1] // 2
            source = source.at[:, pl.ds(pl.multiple_of((1 - (x, y)[bit]) * half, 128), half)]
        launch(source, far[at], far_send.at[at], far_recv.at[at], me ^ (1 << bit), core)

    small_sem, table_sem, encoder_sem = (len(Far._fields) + at for at in range(3))
    local = {}
    for at in W:
        local[at] = pltpu.make_async_copy(sources[at], half_rows(weights[at], core), weight_own.at[at])
        local[at].start()
    pl.semaphore_wait(barrier, peers)

    launch(small, own.small_far, far_send.at[small_sem], far_recv.at[small_sem], me, 1 - core)
    launch(table, own.table_far, far_send.at[table_sem], far_recv.at[table_sem], me, 1 - core)
    for at in W:
        launch(sources[at], half_rows(weights[at], core), weight_send.at[at], weight_recv.at[at], me, 1 - core)
    for at, source in enumerate(LENT):
        launch(sources[source], lent[at], lent_send.at[at], lent_recv.at[at], me, 1 - core)

    def weight(at):
        if at in local:
            local.pop(at).wait()
            arrived(half_rows(weights[at], 1 - core), weight_recv.at[at])
        return weights[at]

    def to_all(which, source, target, spread=True):
        for step in range(1, peers):
            peer = lax.rem(me + step, peers)
            remote(
                source.at[peer] if spread else source, target.at[me], all_send.at[which], all_recv.at[which], peer, core
            ).start()
        kept = pltpu.make_async_copy(source.at[me] if spread else source, target.at[me], all_own.at[which])
        kept.start()
        finish.append(lambda: remote(target.at[1:], target.at[1:], all_send.at[which], own_sem, me, 1 - core).wait_send())

        def wait():
            kept.wait()
            arrived(target.at[1:], all_recv.at[which])

        return wait

    def tiles_of(total):
        return [slice(at, at + 256) for at in range(0, total, 256)]

    def times(values, name):
        ref = weight(name)
        return jnp.concatenate([plain_dot(values, ref[:, cols]) for cols in tiles_of(ref.shape[1])], axis=1)

    def times_back(values, name):
        ref = weight(name)
        return jnp.concatenate([dot_nt(values, ref[cols, :]) for cols in tiles_of(ref.shape[0])], axis=1)

    def head(at):
        return slice(at * HEAD_DIM, (at + 1) * HEAD_DIM)

    def head_pair(at):
        return slice(2 * at * HEAD_DIM, 2 * (at + 1) * HEAD_DIM)

    arrived(own.small_far, far_recv.at[small_sem])
    arrived(own.table_far, far_recv.at[table_sem])

    def both(mine, others, axis):
        first = jnp.where(core == 0, mine, others)
        second = jnp.where(core == 0, others, mine)
        return jnp.concatenate([first, second], axis=axis)

    gain_one, gain_two, gain_three = (
        both(small[at : at + 1, :], own.small_far[at : at + 1, :], 1) for at in range(3)
    )
    out.gain_one[...] = gain_one
    whole_table = both(table[...], own.table_far[...], 0)
    lane = lax.broadcasted_iota(jnp.int32, whole_table.shape, 1)
    column = jnp.sum(jnp.where(lane == me, whole_table, 0.0), axis=1, keepdims=True)
    spans = in_bucket.shape[0]
    for apart in range(spans):
        line = jnp.sum(in_bucket[apart] * column, axis=0, keepdims=True)
        out.bias_lines[apart : apart + 1, :TILE] = line
        if apart + 1 < spans:
            out.bias_lines[apart + 1 : apart + 2, TILE:] = line
    out.bias_lines[0:1, TILE:] = jnp.full((1, TILE), NEG_BIG, F32)

    resid = tokens_in[...].astype(F32)
    out.normed_one[...] = (resid * norm_parts(resid) * gain_one).astype(BF16)
    normed_one = out.normed_one[...]
    queries = times(normed_one, W.query).astype(BF16)
    keys = times(normed_one, W.key).astype(BF16)
    for at in range(peers):
        own.pairs_out[at] = jnp.concatenate([queries[:, head(at)], keys[:, head(at)]], axis=1)
    pairs_arrival = to_all(0, own.pairs_out, out.pairs)
    values = times(normed_one, W.value).astype(BF16)
    for at in range(peers):
        own.lone_out[at] = jnp.concatenate(
            [values[:BLOCK, head(at)], values[BLOCK:, head(at)]], axis=1
        )
    lone_arrival = to_all(1, own.lone_out, out.lone)
    encoder_arrival = to_all(2, encoder, own.encoder_all, spread=False)
    to_pair(FAR.branch_three, cotangent, halves=True)
    to_pair(FAR.normed_one, out.normed_one)
    place_bias = out.bias_lines
    pairs_arrival()
    lone_arrival()
    pl.run_scoped(
        functools.partial(
            attend, order, held_at, out.pairs, out.lone, place_bias, own.mixed_out, out.attn_sum, out.log_norm
        ),
        *attend_scratch(held_at.shape[0]),
    )
    mixed_arrival = to_all(3, own.mixed_out, own.mixed_in)

    encoder_arrival()
    encoder_rows = jnp.concatenate([own.encoder_all[at] for at in range(peers)], axis=0)
    half = width // 2
    count = encoder_rows.shape[0]
    out.encoder_both[:count, :] = jnp.where(core == 0, encoder_rows[:, :half], encoder_rows[:, half:])
    own.cross_keys[...] = times(encoder_rows, W.cross_key).astype(BF16)
    own.cross_values[...] = times(encoder_rows, W.cross_value).astype(BF16)

    mixed_arrival()
    for pair in range(peers // 2):
        first, second = unpack_pair(own.mixed_in, pair, slice(0, BLOCK))
        out.attended[:BLOCK, head_pair(pair)] = first
        out.attended[BLOCK:, head_pair(pair)] = second
    to_pair(FAR.attended, out.attended)
    own.after_self[...] = tokens_in[...].astype(F32) + times(out.attended[...], W.out)
    after_self = own.after_self[...]
    out.normed_two[...] = (after_self * norm_parts(after_self) * gain_two).astype(BF16)
    to_pair(FAR.normed_two, out.normed_two)
    own.cross_queries[...] = times(out.normed_two[...], W.cross_query).astype(BF16)

    for pair in range(peers // 2):
        mixed = []
        for at in (2 * pair, 2 * pair + 1):
            scores = dot_nt(own.cross_keys[:, head(at)], own.cross_queries[:, head(at)])
            weight_t = jnp.exp(scores - jnp.max(scores, axis=0, keepdims=True))
            exact = weight_t / jnp.sum(weight_t, axis=0, keepdims=True)
            own.cross_exact[at] = exact
            mixed.append(left_contract(exact.astype(BF16), own.cross_values[:, head(at)]))
        out.cross_mixed[:, head_pair(pair)] = jnp.concatenate(mixed, axis=1).astype(BF16)
    to_pair(FAR.cross_mixed, out.cross_mixed)
    own.after_cross[...] = own.after_self[...] + times(out.cross_mixed[...], W.cross_out)
    after_cross = own.after_cross[...]
    out.normed_three[...] = (after_cross * norm_parts(after_cross) * gain_three).astype(BF16)
    to_pair(FAR.normed_three, out.normed_three)

    normed_three = out.normed_three[...]
    gate, up, down = weight(W.gate), weight(W.up), weight(W.down)
    for cols in tiles_of(gate.shape[1]):
        gate_act = plain_dot(normed_three, gate[:, cols])
        up_act = plain_dot(normed_three, up[:, cols])
        own.gate_act[:, cols] = gate_act
        own.up_act[:, cols] = up_act
        curve = jnp.tanh(GELU_RATE * (gate_act + GELU_CUBE * gate_act * gate_act * gate_act))
        out.hidden[:, cols] = (0.5 * gate_act * (1.0 + curve) * up_act).astype(BF16)
    to_pair(FAR.hidden, out.hidden)
    out.result[...] = (own.after_cross[...] + times(out.hidden[...], W.down)).astype(BF16)

    branch_three = cotangent[...]
    half = down.shape[0] // 2
    for side in (1 - y, y):
        for start in range(0, half, 256):
            size = min(256, half - start)
            cols = pl.ds(pl.multiple_of(side * half + start, 128), size)
            hidden_grad = dot_nt(branch_three, down[pl.ds(pl.multiple_of(side * half + start, 128), size), :])
            gate_act, up_act = own.gate_act[:, cols], own.up_act[:, cols]
            square = gate_act * gate_act
            curve = jnp.tanh(GELU_RATE * (gate_act + GELU_CUBE * gate_act * square))
            rise = 0.5 * (1.0 + curve) + 0.5 * gate_act * (1.0 - curve * curve) * (
                GELU_RATE * (1.0 + 3.0 * GELU_CUBE * square)
            )
            out.gate_grad[:, cols] = (hidden_grad * up_act * rise).astype(BF16)
            out.up_grad[:, cols] = (hidden_grad * (0.5 * gate_act * (1.0 + curve))).astype(BF16)
        if side is not y:
            to_pair(FAR.gate, out.gate_grad, halves=True)
            to_pair(FAR.up, out.up_grad, halves=True)
    normed_grad = times_back(out.gate_grad[...], W.gate) + times_back(out.up_grad[...], W.up)
    back, gain_three_grad = norm_backward(own.after_cross[...], gain_three, normed_grad)
    out.resid_grad[...] = cotangent[...].astype(F32) + back
    out.branch_two[...] = out.resid_grad[...].astype(BF16)

    to_pair(FAR.branch_two, out.branch_two, halves=True)
    own.mix_grad[...] = times_back(out.branch_two[...], W.cross_out).astype(BF16)
    for pair in range(peers // 2):
        terms = []
        for at in (2 * pair, 2 * pair + 1):
            exact = own.cross_exact[at]
            grads = own.mix_grad[:, head(at)]
            score_grad = dot_nt(own.cross_values[:, head(at)], grads)
            slope = jnp.sum(exact * score_grad, axis=0, keepdims=True)
            rounded = (exact * (score_grad - slope)).astype(BF16)
            terms.append(
                (
                    left_contract(rounded, own.cross_keys[:, head(at)]),
                    plain_dot(rounded, own.cross_queries[:, head(at)]),
                    plain_dot(exact.astype(BF16), grads),
                )
            )
        cols = head_pair(pair)
        values_cols = slice(width + cols.start, width + cols.stop)
        for ref, into, at in ((out.cross_q_grad, cols, 0), (out.kv_part, cols, 1), (out.kv_part, values_cols, 2)):
            ref[:, into] = jnp.concatenate([terms[0][at], terms[1][at]], axis=1).astype(BF16)
    normed_grad = times_back(out.cross_q_grad[...], W.cross_query)
    back, gain_two_grad = norm_backward(own.after_self[...], gain_two, normed_grad)
    out.resid_grad[...] += back
    out.branch_one[...] = out.resid_grad[...].astype(BF16)
    out.dattn[...] = times_back(out.branch_one[...], W.out).astype(BF16)

    for half in range(2):
        for index in range(4):
            cols = slice((4 * half + index) * 128, (4 * half + index + 1) * 128)
            out.gain_grads[half, index : index + 1, :] = gain_two_grad[:, cols]
            out.gain_grads[half, 4 + index : 5 + index, :] = gain_three_grad[:, cols]
        out.gain_grads[half, 8:, :] = jnp.zeros((4, 128), F32)

    other_half = pl.ds(pl.multiple_of((1 - core) * (width // 2), 128), width // 2)
    for at in range(peers):
        rows_at = own.encoder_all.shape[1]
        remote(
            own.encoder_all.at[at, :, other_half],
            out.encoder_both.at[count + at * rows_at : count + (at + 1) * rows_at],
            far_send.at[encoder_sem], far_recv.at[encoder_sem], me, 1 - core,
        ).start()
    arrived(out.encoder_both.at[count:], far_recv.at[encoder_sem])
    finish.append(
        lambda: remote(
            out.encoder_both.at[count:], out.encoder_both.at[count:], far_send.at[encoder_sem], own_sem, me, 1 - core
        ).wait_send()
    )
    for at, ref in enumerate(far):
        arrived(ref, far_recv.at[at])
    for at, ref in enumerate(lent):
        arrived(ref, lent_recv.at[at])
    for each in finish:
        each()


def layer(tokens_in, cotangent, encoder, small, table, in_bucket, held_at, order, sources):
    peers = lax.axis_size("ctx")
    tokens, width = tokens_in.shape
    hidden = sources.gate.shape[1]
    blocks = held_at.shape[0]
    length = blocks * BLOCK
    rows = encoder.shape[0] * peers
    dma, vmem = pltpu.SemaphoreType.DMA, pltpu.VMEM

    def shaped(*shape):
        return jax.ShapeDtypeStruct(shape, BF16)

    def exact(*shape):
        return jax.ShapeDtypeStruct(shape, F32)

    square, wide, half_wide = shaped(tokens, width), shaped(tokens, hidden), shaped(tokens, hidden // 2)
    pairs, lone = (peers, 2 * BLOCK, 2 * HEAD_DIM), (peers, BLOCK, 2 * HEAD_DIM)
    outputs = Made(
        normed_one=square,
        pairs=shaped(*pairs),
        lone=shaped(*lone),
        attn_sum=exact(HEAD_DIM, length),
        log_norm=exact(1, length),
        attended=square,
        normed_two=square,
        cross_mixed=square,
        normed_three=square,
        hidden=wide,
        gate_grad=wide,
        up_grad=wide,
        branch_two=square,
        cross_q_grad=square,
        branch_one=square,
        dattn=square,
        kv_part=shaped(rows, 2 * width),
        resid_grad=exact(tokens, width),
        result=square,
        gain_grads=exact(2, 12, 128),
        gain_one=exact(1, width),
        bias_lines=exact(length // TILE, 2 * TILE),
        encoder_both=shaped(2 * rows, width // 2),
    )
    half_square = shaped(tokens, width // 2)
    fars = Far(
        normed_three=square,
        hidden=wide,
        cross_mixed=square,
        normed_two=square,
        attended=square,
        normed_one=square,
        gate=half_wide,
        branch_three=half_square,
        up=half_wide,
        branch_two=half_square,
    )
    buffers = Scratch(
        small_far=vmem(small.shape, F32),
        table_far=vmem(table.shape, F32),
        pairs_out=vmem(pairs, BF16),
        lone_out=vmem(lone, BF16),
        encoder_all=vmem((peers,) + encoder.shape, BF16),
        mixed_out=vmem(lone, BF16),
        mixed_in=vmem(lone, BF16),
        cross_keys=vmem((rows, width), BF16),
        cross_values=vmem((rows, width), BF16),
        cross_queries=vmem((tokens, width), BF16),
        cross_exact=vmem((HEADS, rows, tokens), F32),
        after_self=vmem((tokens, width), F32),
        after_cross=vmem((tokens, width), F32),
        gate_act=vmem((tokens, hidden), F32),
        up_act=vmem((tokens, hidden), F32),
        mix_grad=vmem((tokens, width), BF16),
    )
    smem_spec = pl.BlockSpec(memory_space=pltpu.SMEM)
    results = pl.pallas_call(
        layer_kernel,
        out_shape=[*outputs, *fars, *(shaped(*sources[at].shape) for at in LENT)],
        in_specs=[vmem_spec()] * 6 + [smem_spec] * 2 + [any_spec()] * len(W),
        out_specs=[vmem_spec()] * len(outputs) + [any_spec()] * (len(fars) + len(LENT)),
        scratch_shapes=[vmem((2 * each.shape[0], each.shape[1]), BF16) for each in sources]
        + list(buffers)
        + [
            dma,
            dma((len(W),)),
            dma((len(W),)),
            dma((len(W),)),
            dma((len(LENT),)),
            dma((len(LENT),)),
            dma((len(fars) + 3,)),
            dma((len(fars) + 3,)),
            dma((4,)),
            dma((4,)),
            dma((4,)),
        ],
        compiler_params=pltpu.CompilerParams(
            collective_id=1, has_side_effects=True, vmem_limit_bytes=62 * MIB
        ),
        name="layer",
    )(tokens_in, cotangent, encoder, small, table, in_bucket, held_at, order, *sources)
    made, results = results[: len(outputs)], results[len(outputs) :]
    return Made(*made), Far(*results[: len(fars)]), results[len(fars) :]


FAR_LEFTS, FAR_RIGHTS = 6, (0, 1, 2, 4)
SCHEDULE = (
    0, 256, 5, 16, 32, 3, 2, 257, 1, 6, 18, 4, 48, 34, 21, 17, 19, 37, 22, 33,
    20, 64, 38, 53, 35, 80, 69, 50, 96, 112, 258, 66, 7, 36, 49, 8, 128, 51, 65, 144,
    23, 67, 82, 52, 160, 39, 81, 24, 259, 98, 68, 97, 113, 54, 40, 84, 9, 83, 55, 85,
    114, 70, 129, 71, 99, 101, 117, 115, 176, 25, 145, 87, 133, 56, 260, 86, 100, 161, 192, 72,
    103, 116, 131, 102, 118, 41, 119, 130, 134, 146, 147, 57, 88, 73, 149, 104, 163, 150, 165, 162,
    89, 179, 132, 135, 178, 194, 105, 177, 195, 166, 193, 121, 120, 148, 151, 137, 210, 136, 211, 153,
    261, 169, 185, 167, 209, 226, 164, 208, 182, 224, 152, 181, 180, 201, 227, 262, 197, 183, 198, 217,
    196, 225, 212, 168, 199, 233, 263, 243, 214, 228, 265, 213, 229, 230, 184, 240, 200, 264, 249, 215,
    241, 245, 216, 231, 247, 242, 244, 232, 248, 246,
)


UP, DOWN, ACROSS_Y, ACROSS_X = 0, 1, 2, 3
LEFT, RIGHT, PIECE = 0, 1, 2


class Product:
    def __init__(self, left, right, first, tall, route):
        self.left, self.right, self.first, self.tall, self.route = left, right, first, tall, route


SUMMED = -1


def weight_grad_kernel(products, left_count, *refs):
    count = len(products)
    refs = list(refs)

    def take(number):
        taken = refs[:number]
        del refs[:number]
        return taken

    lefts, rights = take(left_count), take(count - 3)
    left_far, right_far = take(FAR_LEFTS), take(len(FAR_RIGHTS))
    (
        order,
        held_at,
        grad_rows,
        pairs,
        lone,
        attn_sum,
        log_norm,
        bias_lines,
        in_bucket,
        resid_in,
        gain_one,
        resid_grad,
        gains,
    ) = take(13)
    weights = take(10)
    wholes, (vec_out, input_grad, encoder_grad, kv_both) = take(count - 1), take(4)
    kv_at = [product.left for product in products].index(SUMMED)
    wholes.insert(kv_at, kv_both.at[0])
    left_all, left_t = take(left_count), take(left_count)
    right_all, away, came, held, line_in = (take(count) for _ in range(5))
    rights += take(3)
    grad_packed, grad_landed, back_packed, back_landed, lines = take(5)
    attention_scratch = take(12)
    vec_in, vec_sums, vec_landed, weight_buffer, normed_grad = take(5)
    (
        left_send,
        left_own,
        left_recv,
        right_send,
        right_own,
        right_recv,
        pair_send,
        pair_recv,
        line_send,
        line_recv,
        out_send,
        out_recv,
        own_sem,
        vec_send,
        vec_recv,
        all_send,
        all_recv,
        all_own,
        kv_sem,
        weight_sem,
    ) = refs
    me, core = lax.axis_index("ctx"), lax.axis_index("wsh")
    peers = lax.axis_size("ctx")
    tokens = lefts[0].shape[0]
    x, y, z = lax.rem(me, 2), lax.rem(me // 2, 2), me // 4

    barrier = pltpu.get_barrier_semaphore()
    for step in range(1, peers):
        pl.semaphore_signal(
            barrier, inc=1, device_id=(lax.rem(me + step, peers), core), device_id_type=MESH
        )
    pl.semaphore_signal(barrier, inc=1, device_id=(me, 1 - core), device_id_type=MESH)
    for head in range(peers):
        cols = slice(head * HEAD_DIM, (head + 1) * HEAD_DIM)
        grad_packed[head] = jnp.concatenate(
            [grad_rows[:BLOCK, cols], grad_rows[BLOCK:, cols]], axis=1
        )
    pl.semaphore_wait(barrier, peers)

    def place(zz, yy, xx):
        return zz * 4 + yy * 2 + xx

    targets = {
        UP: place(lax.rem(z + 1, 4), y, x),
        DOWN: place(lax.rem(z + 3, 4), y, x),
        ACROSS_Y: place(z, 1 - y, x),
        ACROSS_X: place(z, y, 1 - x),
    }
    finish = []

    def remote(src, dst, send_sem, recv_sem, ctx, side):
        return pltpu.make_async_remote_copy(
            src_ref=src,
            dst_ref=dst,
            send_sem=send_sem,
            recv_sem=recv_sem,
            device_id=(ctx, side),
            device_id_type=MESH,
        )

    def launch(copy, only=None):
        if only is None:
            copy.start()
        else:
            pl.when(only)(copy.start)

    def arrived(ref, sem):
        remote(ref, ref, own_sem.at[0], sem, me, 1 - core).wait_recv()

    def left_here(ref, sem):
        finish.append(lambda: remote(ref, ref, sem, own_sem.at[0], me, 1 - core).wait_send())

    def lanes(ref, at, width):
        return ref.at[:, pl.ds(pl.multiple_of(at * width, 128), width)]

    def rows(ref, at, height):
        return ref.at[pl.ds(pl.multiple_of(at * height, 16), height)]

    def slot(ref, index):
        return ref.at[pl.ds(index * tokens, tokens)]

    def axes(product):
        along_x, along_y = (x, ACROSS_X), (y, ACROSS_Y)
        return (along_x, along_y) if product.first == BIT_X else (along_y, along_x)

    left_axis = {product.left: product for product in products}

    def local(src, dst, sem):
        copy = pltpu.make_async_copy(src, dst, sem)
        copy.start()
        return copy

    def send_left(at):
        half = left_all[at].shape[1]
        for index, ref in enumerate((lefts[at], left_far[at])):
            local(lanes(ref, core, half), slot(left_all[at], index), left_own.at[at])
            launch(remote(lanes(ref, 1 - core, half), slot(left_all[at], 2 + index), left_send.at[at], left_recv.at[at], me, 1 - core))
        left_here(left_all[at].at[: 2 * tokens], left_send.at[at])
        return left_all[at].at[: 2 * tokens], left_own.at[at]

    def send_right(at):
        (mine, way), _ = axes(products[at])
        half = right_all[at].shape[1]
        send_sem, recv_sem = right_send.at[at], right_recv.at[at]
        own, others = lanes(rights[at], mine, half), lanes(rights[at], 1 - mine, half)
        if products[at].left == SUMMED:
            launch(remote(others, right_all[at], send_sem, recv_sem.at[0], targets[way], core))
            left_here(right_all[at], send_sem)
            return None
        copies = [local(own, slot(right_all[at], 0), right_own.at[at])]
        launch(remote(own, slot(right_all[at], 2), send_sem, recv_sem.at[1], me, 1 - core))
        if at in FAR_RIGHTS:
            far = right_far[FAR_RIGHTS.index(at)]
            copies.append(local(far, slot(right_all[at], 1), right_own.at[at]))
            launch(remote(far, slot(right_all[at], 3), send_sem, recv_sem.at[2], me, 1 - core))
            left_here(right_all[at].at[: 2 * tokens], send_sem)
        else:
            launch(remote(others, slot(right_all[at], 1), send_sem, recv_sem.at[0], targets[way], core))
            left_here(right_all[at].at[: 3 * tokens], send_sem)
        return right_all[at].at[: len(copies) * tokens], right_own.at[at]

    def to_all(which, source, target):
        for step in range(1, peers):
            peer = lax.rem(me + step, peers)
            launch(remote(source.at[peer], target.at[me], all_send.at[which], all_recv.at[which], peer, core))
        own = local(source.at[me], target.at[me], all_own.at[which])
        left_here(source.at[1:], all_send.at[which])

        def wait():
            own.wait()
            arrived(target.at[1:], all_recv.at[which])

        return wait

    seen = set()
    owns = {}

    def send_operands(some):
        for at in some:
            left = products[at].left
            if left not in seen and left != SUMMED:
                seen.add(left)
                owns[LEFT, left] = send_left(left)
            owns[RIGHT, at] = send_right(at)

    def own_slots(key):
        ref, sem = owns[key]
        pltpu.make_async_copy(ref, ref, sem).wait()

    def vector_step(step):
        if step == 0:
            source, ctx, side = vec_in.at[1 - core], me, 1 - core
        else:
            source, ctx, side = vec_sums.at[step - 1], me ^ (1 << (step - 1)), core
        launch(remote(source, vec_landed.at[step], vec_send.at[step], vec_recv.at[step], ctx, side))
        left_here(source, vec_send.at[step])

    def vector_add(step):
        arrived(vec_landed.at[step], vec_recv.at[step])
        total = (vec_sums[step - 1] if step else vec_in[core]) + vec_landed[step]
        if step < 4:
            vec_sums[step] = total
            vector_step(step + 1)
        else:
            vec_out[...] = total

    def pass_on(at):
        if products[at].left == SUMMED or at in FAR_RIGHTS:
            return
        arrived(slot(right_all[at], 1), right_recv.at[at, 0])
        launch(remote(slot(right_all[at], 1), slot(right_all[at], 3), right_send.at[at], right_recv.at[at, 2], me, 1 - core))

    def multiply(at, out, half):
        product = products[at]
        left, right = left_t[product.left], right_all[at]
        height, width = out.shape
        step = 256 if height <= 256 else 128 if height % 256 else 256
        if product.tall:
            columns = pl.ds(pl.multiple_of(half * width, 128), width)

            def strip(index, carry):
                band = pl.ds(pl.multiple_of(index * 176, 16), 176)
                out[band, :] = plain_dot(left[band, :], right[:, columns]).astype(BF16)
                return carry

            lax.fori_loop(0, height // 176, strip, 0)
        else:
            band = pl.ds(pl.multiple_of(half * height, 16), height)

            def strip(index, carry):
                columns = pl.ds(pl.multiple_of(index * 256, 128), 256)
                out[:, columns] = plain_dot(left[band, :], right[:, columns]).astype(BF16)
                return carry

            lax.fori_loop(0, width // 256, strip, 0)
            if width % 256:
                out[:, width - 128 :] = plain_dot(left[band, :], right[:, width - 128 :]).astype(BF16)

    turned = set()

    def product_away(at):
        left = products[at].left
        _, (mine, way) = axes(products[at])
        if left == SUMMED:
            (first_mine, _), _ = axes(products[at])
            arrived(right_all[at], right_recv.at[at, 0])
            height = held[at].shape[0]
            for out, half in ((away[at], 1 - mine), (held[at], mine)):
                own = lanes(rows(rights[at], half, height), first_mine, held[at].shape[1])
                out[...] = (own[...].astype(F32) + rows(right_all[at], half, height)[...].astype(F32)).astype(BF16)
            launch(remote(away[at], came[at], pair_send.at[at], pair_recv.at[at], targets[way], core))
            left_here(away[at], pair_send.at[at])
            return
        if left not in turned:
            turned.add(left)
            arrived(left_all[left].at[2 * tokens :], left_recv.at[left])
            own_slots((LEFT, left))
            height = left_t[left].shape[0]

            def turn(index, carry):
                band = pl.ds(pl.multiple_of(index * 128, 128), 128)
                left_t[left][band, :] = jnp.transpose(left_all[left][:, band], (1, 0))
                return carry

            lax.fori_loop(0, height // 128, turn, 0)
        arrived(slot(right_all[at], 2), right_recv.at[at, 1])
        arrived(slot(right_all[at], 3), right_recv.at[at, 2])
        own_slots((RIGHT, at))
        multiply(at, away[at], 1 - mine)
        launch(remote(away[at], came[at], pair_send.at[at], pair_recv.at[at], targets[way], core))
        left_here(away[at], pair_send.at[at])
        multiply(at, held[at], mine)

    def add(into, more):
        into[...] = (into[...].astype(F32) + more[...].astype(F32)).astype(BF16)

    def add_pair(at):
        arrived(came[at], pair_recv.at[at])
        add(held[at], came[at])

    def line_step(at, step):
        height = held[at].shape[0] // 4
        for side, behind, chunk, way in (
            (0, z, lax.rem(z + 3 - step, 4), UP),
            (1, 3 - z, lax.rem(z + step + 1, 4), DOWN),
        ):
            recv_sem = line_recv.at[at, side, lax.rem(chunk + 2, 3) if side == 0 else lax.rem(chunk, 3)]
            landing = rows(line_in[at], chunk + 1 - side, height)

            def land(landing=landing, chunk=chunk, recv_sem=recv_sem):
                arrived(landing, recv_sem)
                add(rows(held[at], chunk, height), landing)

            pl.when(jnp.logical_and(behind > 0, behind <= step))(land)
            if step < 3:
                launch(
                    remote(
                        rows(held[at], chunk, height),
                        landing,
                        line_send.at[at],
                        recv_sem,
                        targets[way],
                        core,
                    ),
                    only=behind <= step,
                )
        if step == 3:
            left_here(held[at].at[: 3 * height], line_send.at[at])

    def own_piece(at):
        return rows(held[at], z, held[at].shape[0] // 4)

    def window(at, where):
        product = products[at]
        height, width = held[at].shape
        height //= 4
        xx, yy, zz = lax.rem(where, 2), lax.rem(where // 2, 2), where // 4
        one, two = (xx, yy) if product.first == BIT_X else (yy, xx)
        row, column = (zz, one * 2 + two) if product.tall else (two * 4 + zz, one)
        return wholes[at].at[
            pl.ds(pl.multiple_of(row * height, 16), height),
            pl.ds(pl.multiple_of(column * width, 128), width),
        ]

    def send(at, where, way, arrival, only=None, own=False):
        launch(
            remote(
                own_piece(at) if own else window(at, where),
                window(at, where),
                out_send.at[at, min(way, ACROSS_Y)],
                out_recv.at[at, arrival],
                targets[way],
                core,
            ),
            only,
        )

    def arrive(at, where, arrival, only=None):
        def act():
            arrived(window(at, where), out_recv.at[at, arrival])

        if only is None:
            act()
        else:
            pl.when(only)(act)

    def quarters(at, number):
        return wholes[at].at[: wholes[at].shape[0] // 4 * number]

    def near(way, zz):
        return place(zz, 1 - y, x) if way == ACROSS_Y else place(zz, y, 1 - x)

    def opposite(zz):
        return place(zz, 1 - y, 1 - x)

    def from_line(apart):
        return (
            (z >= apart, lax.rem(z + 4 - apart, 4), UP, jnp.logical_and(z >= apart, z < 3)),
            (z + apart <= 3, lax.rem(z + apart, 4), DOWN, jnp.logical_and(z + apart <= 3, z > 0)),
        )

    def line_sent(at, piece_groups):
        for number in (1, 2, 3):
            for way, here in ((UP, z == number - 1), (DOWN, z == 4 - number)):
                ref, sem = piece_groups(number), out_send.at[at, way]
                finish.append(
                    functools.partial(
                        pl.when(here),
                        lambda ref=ref, sem=sem: remote(ref, ref, sem, own_sem.at[0], me, 1 - core).wait_send(),
                    )
                )

    def gather_step(at, step):
        z_first, second, third = products[at].route
        if step == 0:
            owns[PIECE, at] = local(own_piece(at), window(at, me), own_sem.at[at])
            if at != kv_at:
                finish.append(owns[PIECE, at].wait)
            if z_first:
                send(at, me, UP, z, z < 3, own=True)
                send(at, me, DOWN, z, z > 0, own=True)
                send(at, me, second, 4 + z, own=True)
                send(at, me, third, 8, own=True)
                left_here(quarters(at, 3), out_send.at[at, ACROSS_Y])
                line_sent(at, lambda number: held[at].at[: held[at].shape[0] // 4 * number])
            else:
                send(at, me, second, 0, own=True)
                send(at, me, third, 1, own=True)
                send(at, me, UP, 4 + z, z < 3, own=True)
                send(at, me, DOWN, 4 + z, z > 0, own=True)
                left_here(held[at].at[: held[at].shape[0] // 4 * 3], out_send.at[at, ACROSS_Y])
                line_sent(at, lambda number: quarters(at, number))
        elif z_first:
            if step <= 3:
                for there, zz, way, on in from_line(step):
                    where = place(zz, y, x)
                    arrive(at, where, zz, there)
                    send(at, where, way, zz, on)
                    send(at, where, second, 4 + zz, there)
                    send(at, where, third, 8, there)
            elif step <= 7:
                zz = z ^ (step - 4)
                where = near(second, zz)
                arrive(at, where, 4 + zz)
                send(at, where, third, 8)
            elif step == 8:
                arrived(quarters(at, 2), out_recv.at[at, 8])
        else:
            if step == 1:
                where = near(second, z)
                arrive(at, where, 0)
                send(at, where, third, 2)
                send(at, where, UP, 4 + z, z < 3)
                send(at, where, DOWN, 4 + z, z > 0)
            elif step == 2:
                for arrival, where in ((1, near(third, z)), (2, opposite(z))):
                    arrive(at, where, arrival)
                    send(at, where, UP, 4 + z, z < 3)
                    send(at, where, DOWN, 4 + z, z > 0)
            elif step <= 5:
                for there, zz, way, on in from_line(step - 2):
                    pl.when(there)(
                        functools.partial(arrived, quarters(at, 1), out_recv.at[at, 4 + zz])
                    )
                    for where in (place(zz, y, x), near(second, zz), near(third, zz), opposite(zz)):
                        send(at, where, way, 4 + zz, on)

    def load_weight(index):
        return pltpu.make_async_copy(
            weights[index], weight_buffer.at[index % 2], weight_sem.at[index % 2]
        )

    def input_gradient():
        load_weight(0).start()
        for index in range(6):
            load_weight(index + 1).start()
            load_weight(index).wait()
            columns = lanes(normed_grad, core if index < 3 else 1 - core, normed_grad.shape[1] // 2)
            term = dot_nt(rights[count - 3 + index % 3][...], weight_buffer[index % 2])
            if index % 3:
                columns[...] += term
            else:
                columns[...] = term
        width = resid_in.shape[1]
        cotan, values = normed_grad[...], resid_in[...].astype(F32)
        rate = lax.rsqrt(jnp.mean(values * values, axis=1, keepdims=True) + EPSILON)
        scaled = cotan * gain_one[...]
        slope = jnp.mean(scaled * values, axis=1, keepdims=True)
        back = rate * scaled - values * (rate * rate * rate) * slope
        input_grad[...] = (resid_grad[...] + back).astype(BF16)
        gain_grad = jnp.sum(cotan * values * rate, axis=0, keepdims=True)
        column = jnp.zeros((BUCKETS, 1), F32)
        for apart in range(lines.shape[0]):
            sums = lines[apart : apart + 1, :TILE]
            if apart + 1 < lines.shape[0]:
                sums = sums + lines[apart + 1 : apart + 2, TILE:]
            column = column + jnp.sum(in_bucket[apart] * sums, axis=1, keepdims=True)
        place_at = lax.broadcasted_iota(jnp.int32, (BUCKETS, 128), 1)
        table = jnp.where(place_at == me, column, 0.0)
        for half in range(2):
            for index in range(4):
                start = (4 * half + index) * 128
                vec_in[half, index : index + 1, :] = gain_grad[:, start : start + 128]
            vec_in[half, 4:16, :] = gains[half]
            vec_in[half, 16:, :] = table[half * (BUCKETS // 2) : (half + 1) * (BUCKETS // 2)]
        vector_step(0)

    def encoder_gradient():
        own = kv_both[0, pl.ds(pl.multiple_of(me * encoder_grad.shape[0], 16), encoder_grad.shape[0]), :]
        width = own.shape[1] // 2
        for side in (0, 1):
            terms = []
            for index in (6 + 2 * side, 7 + 2 * side):
                if index < 9:
                    load_weight(index + 1).start()
                load_weight(index).wait()
                part = slice((index % 2) * width, (index % 2 + 1) * width)
                terms.append(dot_nt(own[:, part], weight_buffer[index % 2]))
            columns = lanes(encoder_grad, core if side == 0 else 1 - core, width // 2)
            columns[...] = (terms[0] + terms[1]).astype(BF16)

    later = {}

    def grads_leave():
        later[0] = to_all(0, grad_packed, grad_landed)

    def attention():
        later[0]()
        attend_back(
            order, held_at, pairs, lone, grad_landed, attn_sum, log_norm, bias_lines, back_packed, lines,
            *attention_scratch,
        )
        later[1] = to_all(1, back_packed, back_landed)

    def grads_return():
        later[1]()
        dq_ref, dk_ref, dv_ref = rights[count - 3 :]
        for pair in range(peers // 2):
            cols = slice(pair * 2 * HEAD_DIM, (pair + 1) * 2 * HEAD_DIM)
            dq_ref[:, cols], dk_ref[:, cols] = unpack_pair(back_landed, pair, slice(0, 2 * BLOCK))
            first, second = unpack_pair(back_landed, pair, slice(2 * BLOCK, 3 * BLOCK))
            dv_ref[:BLOCK, cols] = first
            dv_ref[BLOCK:, cols] = second

    def kv_gathered():
        owns[PIECE, kv_at].wait()
        launch(remote(kv_both.at[0], kv_both.at[1], kv_sem.at[0], kv_sem.at[1], me, 1 - core))
        left_here(kv_both.at[0], kv_sem.at[0])
        encoder_gradient()

    single = [grads_leave, attention, grads_return, input_gradient]
    single += [functools.partial(vector_add, step) for step in range(5)] + [kv_gathered]
    for code in SCHEDULE:
        stage, at = divmod(code, 16)
        if stage == 0:
            send_operands([at])
        elif stage == 1:
            pass_on(at)
        elif stage == 2:
            product_away(at)
        elif stage == 3:
            add_pair(at)
            line_step(at, 0)
        elif stage < 7:
            line_step(at, stage - 3)
        elif stage < 16:
            gather_step(at, stage - 7)
        else:
            single[at]()

    arrived(kv_both.at[1], kv_sem.at[1])
    for each in finish:
        each()


def weight_grads(products, lefts, rights, left_far, right_far, others, weights):
    count, peers = len(products), lax.axis_size("ctx")
    tokens = lefts[0].shape[0]
    length = others[5].shape[1]
    kv_at = [product.left for product in products].index(SUMMED)
    kv_rows, kv_width = rights[kv_at].shape
    spans = length // TILE
    dma = pltpu.SemaphoreType.DMA
    vmem = pltpu.VMEM
    width = HEADS * HEAD_DIM
    halves = [left.shape[1] // 2 for left in lefts]
    widths = [right.shape[1] for right in rights] + [width] * 3
    helds = []
    for product, right in zip(products, widths):
        height = kv_rows if product.left == SUMMED else halves[product.left]
        helds.append((height, right // 4) if product.tall else (height // 2, right // 2))
    lands = [vmem(shape, BF16) for shape in helds]
    chunk = (peers, BLOCK, 2 * HEAD_DIM)
    chunks = (peers, 3 * BLOCK, 2 * HEAD_DIM)
    smem_spec = pl.BlockSpec(memory_space=pltpu.SMEM)
    return pl.pallas_call(
        functools.partial(weight_grad_kernel, products, len(lefts)),
        out_shape=[
            jax.ShapeDtypeStruct((halves[product.left], right), BF16)
            for product, right in zip(products, widths)
            if product.left != SUMMED
        ]
        + [
            jax.ShapeDtypeStruct((32, 128), F32),
            jax.ShapeDtypeStruct((tokens, width), BF16),
            jax.ShapeDtypeStruct((kv_rows // peers, width), BF16),
            jax.ShapeDtypeStruct((2, kv_rows, kv_width), BF16),
        ],
        in_specs=[any_spec()] * len(lefts)
        + [vmem_spec() if product.left == SUMMED else any_spec() for product in products[: len(rights)]]
        + [any_spec()] * (len(left_far) + len(right_far))
        + [smem_spec] * 2
        + [vmem_spec()] * (len(others) - 2)
        + [any_spec()] * len(weights),
        out_specs=[any_spec()] * (count - 1) + [vmem_spec()] * 4,
        scratch_shapes=[vmem((4 * tokens, half), BF16) for half in halves]
        + [vmem((half, 4 * tokens), BF16) for half in halves]
        + [
            vmem((kv_rows if product.left == SUMMED else 4 * tokens, right // 2), BF16)
            for product, right in zip(products, widths)
        ]
        + lands * 3
        + [vmem((5 * height // 4, width_held), BF16) for height, width_held in helds]
        + [vmem((tokens, width), BF16)] * 3
        + [vmem(chunk, BF16), vmem(chunk, BF16), vmem(chunks, BF16), vmem(chunks, BF16)]
        + [vmem((spans, 2 * TILE), F32)]
        + [vmem((length, HEAD_DIM), BF16)] * 4
        + [vmem((HEAD_DIM, length), BF16)]
        + [vmem((spans, TILE, TILE), F32)] * 2
        + [vmem((length, HEAD_DIM), F32)] * 3
        + [vmem((1, length), F32), vmem((HEAD_DIM, length), F32)]
        + [
            vmem((2, 32, 128), F32),
            vmem((4, 32, 128), F32),
            vmem((5, 32, 128), F32),
            vmem((2,) + weights[0].shape, BF16),
            vmem((tokens, width), F32),
        ]
        + [
            dma((len(lefts),)),
            dma((len(lefts),)),
            dma((len(lefts),)),
            dma((count,)),
            dma((count,)),
            dma((count, 3)),
            dma((count,)),
            dma((count,)),
            dma((count,)),
            dma((count, 2, 3)),
            dma((count, 3)),
            dma((count, 9)),
            dma((count,)),
            dma((5,)),
            dma((5,)),
            dma((2,)),
            dma((2,)),
            dma((2,)),
            dma((2,)),
            dma((2,)),
        ],
        compiler_params=pltpu.CompilerParams(
            collective_id=5, has_side_effects=True, vmem_limit_bytes=60 * MIB
        ),
        name="weight_grads",
    )(*lefts, *rights, *left_far, *right_far, *others, *weights)


def on_device_by_heads(
    inputs,
    encoder,
    cotangent,
    block_order,
    bucket_of,
    self_gain,
    query_weight,
    key_weight,
    value_weight,
    out_weight,
    bias_table,
    cross_gain,
    cross_query,
    cross_key,
    cross_value,
    cross_out,
    mlp_gain,
    gate_weight,
    up_weight,
    down_weight,
):
    blocks = block_order.shape[0]
    block_ids = jnp.arange(blocks, dtype=jnp.int32)
    held_at = jnp.sum(
        jnp.where(block_order[None, :] == block_ids[:, None], block_ids[None, :], 0), axis=1
    )
    bucket_ids = jnp.arange(BUCKETS, dtype=jnp.int32)[None, :, None]
    bucket_tiles = (bucket_of.reshape(-1, 1, TILE) == bucket_ids).astype(F32)
    row = jnp.arange(8, dtype=jnp.int32)[:, None]
    small = jnp.where(
        row == 0, self_gain[None], jnp.where(row == 1, cross_gain[None], mlp_gain[None])
    ).astype(F32)
    table = jnp.pad(bias_table.astype(F32), ((0, 0), (0, 128 - HEADS)))
    sources = Weights(
        query=query_weight,
        key=key_weight,
        value=value_weight,
        out=out_weight,
        cross_key=cross_key,
        cross_value=cross_value,
        cross_query=cross_query,
        cross_out=cross_out,
        gate=gate_weight,
        up=up_weight,
        down=down_weight,
    )
    made, far, lent = layer(
        inputs[0], cotangent[0], encoder[0], small, table, bucket_tiles, held_at, block_order, sources
    )

    z_then_yx, z_then_xy, yx_then_z, xy_then_z = (
        (True, ACROSS_Y, ACROSS_X),
        (True, ACROSS_X, ACROSS_Y),
        (False, ACROSS_Y, ACROSS_X),
        (False, ACROSS_X, ACROSS_Y),
    )
    lefts = (
        made.normed_three, made.hidden, made.cross_mixed, made.normed_two, made.attended, made.normed_one
    )
    products = (
        Product(0, made.gate_grad, BIT_Y, False, z_then_yx),
        Product(1, cotangent[0], BIT_X, True, z_then_yx),
        Product(0, made.up_grad, BIT_Y, False, z_then_xy),
        Product(SUMMED, made.kv_part, BIT_Y, False, yx_then_z),
        Product(2, made.branch_two, BIT_X, False, z_then_xy),
        Product(3, made.cross_q_grad, BIT_X, False, z_then_xy),
        Product(4, made.branch_one, BIT_Y, False, z_then_xy),
        Product(5, None, BIT_X, False, yx_then_z),
        Product(5, None, BIT_X, False, yx_then_z),
        Product(5, None, BIT_X, False, z_then_yx),
    )
    *wholes, totals, input_grad, encoder_grad, cross_kv_both = weight_grads(
        products,
        lefts,
        [product.right for product in products[:7]],
        far[:FAR_LEFTS],
        far[FAR_LEFTS:],
        [
            block_order,
            held_at,
            made.dattn,
            made.pairs,
            made.lone,
            made.attn_sum,
            made.log_norm,
            made.bias_lines,
            bucket_tiles,
            inputs[0],
            made.gain_one,
            made.resid_grad,
            made.gain_grads,
        ],
        [query_weight, key_weight, value_weight, *lent[:3], cross_key, cross_value, *lent[3:]],
    )
    head_width = HEADS * HEAD_DIM
    cross_kv_rows = cross_kv_both.reshape(-1, 2 * head_width)
    sum_cross_key = left_contract(made.encoder_both, cross_kv_rows[:, :head_width])
    sum_cross_value = left_contract(made.encoder_both, cross_kv_rows[:, head_width:])
    (
        sum_gate,
        sum_down,
        sum_up,
        sum_cross_out,
        sum_cross_query,
        sum_out,
        sum_query,
        sum_key,
        sum_value,
    ) = (member.astype(F32) for member in wholes)
    sum_gain_one, sum_gain_two, sum_gain_three = (
        totals[4 * at : 4 * at + 4].reshape(-1) for at in range(3)
    )
    sum_table = totals[16:, :HEADS]
    return (
        made.result[None],
        input_grad[None],
        encoder_grad[None],
        sum_gain_one,
        sum_query,
        sum_key,
        sum_value,
        sum_out,
        sum_table,
        sum_gain_two,
        sum_cross_query,
        sum_cross_key,
        sum_cross_value,
        sum_cross_out,
        sum_gain_three,
        sum_gate,
        sum_up,
        sum_down,
    )


def solution(mesh):
    by_heads = mesh.shape["ctx"] == HEADS and mesh.shape["wsh"] == 2
    return jax.shard_map(
        on_device_by_heads if by_heads else on_device,
        mesh=mesh,
        in_specs=(
            P("wsh", "ctx", None),
            P("wsh", "ctx", None),
            P("wsh", "ctx", None),
            P(),
            P(),
            P("wsh"),
            P("wsh", None),
            P("wsh", None),
            P("wsh", None),
            P("wsh", None),
            P("wsh", None),
            P("wsh"),
            P("wsh", None),
            P("wsh", None),
            P("wsh", None),
            P("wsh", None),
            P("wsh"),
            P("wsh", None),
            P("wsh", None),
            P("wsh", None),
        ),
        out_specs=(
            P("wsh", "ctx", None),
            P("wsh", "ctx", None),
            P("wsh", "ctx", None),
            P("wsh"),
            P("wsh", None),
            P("wsh", None),
            P("wsh", None),
            P("wsh", None),
            P("wsh", None),
            P("wsh"),
            P("wsh", None),
            P("wsh", None),
            P("wsh", None),
            P("wsh", None),
            P("wsh"),
            P("wsh", None),
            P("wsh", None),
            P("wsh", None),
        ),
        check_vma=False,
    )
```

```python
import functools
from typing import Any, NamedTuple

import jax
import jax.numpy as jnp
from jax import lax
from jax.experimental import pallas as pl
from jax.experimental.pallas import tpu as pltpu
from jax.sharding import PartitionSpec as P

HEADS = 16
HEAD_DIM = 64
BUCKETS = 32


EPSILON = 1e-06
NEG_BIG = -1e30


def rms_norm(values, gain):
    return values * lax.rsqrt(jnp.mean(values * values, axis=-1, keepdims=True) + EPSILON) * gain


def plain_dot(left, right):
    return jnp.dot(left, right, preferred_element_type=jnp.float32)


def left_contract(left, right):
    return lax.dot_general(
        left, right, (((0,), (0,)), ((), ())), preferred_element_type=jnp.float32
    )


def right_contract(left, right):
    return lax.dot_general(
        left, right, (((1,), (1,)), ((), ())), preferred_element_type=jnp.float32
    )


def gelu_product(gate_vals, up_vals):
    return jax.nn.gelu(gate_vals, approximate=True) * up_vals


def norm_back(values, gain, cotan):
    normed, pullback = jax.vjp(rms_norm, values, gain)
    return pullback(cotan)


def lookup_positions(block_order, first_row, row_count, block_len):
    token_ids = first_row + jnp.arange(row_count, dtype=jnp.int32)
    block_ids = token_ids // block_len
    matches = block_ids[:, None] == jnp.arange(block_order.shape[0], dtype=jnp.int32)[None, :]
    starts = jnp.sum(jnp.where(matches, block_order[None, :], 0), axis=1)
    return starts * block_len + token_ids % block_len


def fold_groups(step_fn, carried, pieces, shard_rows):
    piece_rows = pieces[0].shape[0]
    shards = max(1, piece_rows // shard_rows)
    group_limit = max(1, 1152 // shard_rows)
    group_size = max(
        (divisor for divisor in range(1, min(shards, group_limit) + 1) if shards % divisor == 0)
    )
    group_rows = group_size * shard_rows

    def group_step(group_idx, inner_state):
        sub_pieces = tuple(
            (
                lax.dynamic_slice_in_dim(member, group_idx * group_rows, group_rows, 0)
                for member in pieces
            )
        )
        return step_fn(inner_state, sub_pieces, group_idx * group_rows)

    return lax.fori_loop(0, shards // group_size, group_step, carried)


def on_device(
    inputs,
    encoder,
    cotangent,
    block_order,
    bucket_of,
    self_gain,
    query_weight,
    key_weight,
    value_weight,
    out_weight,
    bias_table,
    cross_gain,
    cross_query,
    cross_key,
    cross_value,
    cross_out,
    mlp_gain,
    gate_weight,
    up_weight,
    down_weight,
):
    (
        gain_one,
        query_full,
        key_full,
        value_full,
        out_full,
        bias_rows,
        gain_two,
        cross_query_full,
        cross_key_full,
        cross_value_full,
        cross_out_full,
        gain_three,
        gate_full,
        up_full,
        down_full,
    ) = (
        lax.all_gather(self_gain, "wsh", axis=0, tiled=True),
        lax.all_gather(query_weight, "wsh", axis=0, tiled=True),
        lax.all_gather(key_weight, "wsh", axis=0, tiled=True),
        lax.all_gather(value_weight, "wsh", axis=0, tiled=True),
        lax.all_gather(out_weight, "wsh", axis=0, tiled=True),
        lax.all_gather(bias_table, "wsh", axis=0, tiled=True),
        lax.all_gather(cross_gain, "wsh", axis=0, tiled=True),
        lax.all_gather(cross_query, "wsh", axis=0, tiled=True),
        lax.all_gather(cross_key, "wsh", axis=0, tiled=True),
        lax.all_gather(cross_value, "wsh", axis=0, tiled=True),
        lax.all_gather(cross_out, "wsh", axis=0, tiled=True),
        lax.all_gather(mlp_gain, "wsh", axis=0, tiled=True),
        lax.all_gather(gate_weight, "wsh", axis=0, tiled=True),
        lax.all_gather(up_weight, "wsh", axis=0, tiled=True),
        lax.all_gather(down_weight, "wsh", axis=0, tiled=True),
    )
    gain_one = gain_one.astype(jnp.float32)
    gain_two = gain_two.astype(jnp.float32)
    gain_three = gain_three.astype(jnp.float32)
    resid_in = inputs[0].astype(jnp.float32)
    tokens = resid_in.shape[0]
    block_len = tokens // 2
    head_width = HEADS * HEAD_DIM
    total_rows = tokens * lax.axis_size("ctx")
    own_pos = lookup_positions(block_order, lax.axis_index("ctx") * tokens, tokens, block_len)
    bucket_ids = jnp.arange(BUCKETS, dtype=jnp.int32)
    boundaries = jnp.sum((bucket_of[None, :] < bucket_ids[1:, None]).astype(jnp.int32), axis=1)

    def bucket_indicator_of(clipped):
        bucket = jnp.sum((clipped[None] >= boundaries[:, None, None]).astype(jnp.int32), axis=0)
        return (bucket[None] == bucket_ids[:, None, None]).astype(jnp.bfloat16)

    def query_key_logits(query_heads, key_heads, query_pos, key_pos):
        logits = jnp.einsum(
            "qhe,khe->hqk", query_heads, key_heads, preferred_element_type=jnp.float32
        )
        offset = query_pos[:, None] - key_pos[None, :]
        clipped = jnp.maximum(offset, 0)
        indicator = bucket_indicator_of(clipped)
        rel_bias = jnp.einsum(
            "ouw,om->muw", indicator, bias_rows, preferred_element_type=jnp.float32
        )
        allowed = (offset >= 0)[None]
        return (jnp.where(allowed, logits + rel_bias, NEG_BIG), allowed, indicator)

    normed_one = rms_norm(resid_in, gain_one).astype(jnp.bfloat16)
    query_heads = (
        plain_dot(normed_one, query_full).astype(jnp.bfloat16).reshape(tokens, HEADS, HEAD_DIM)
    )
    key_heads = (
        plain_dot(normed_one, key_full).astype(jnp.bfloat16).reshape(tokens, HEADS, HEAD_DIM)
    )
    value_heads = (
        plain_dot(normed_one, value_full).astype(jnp.bfloat16).reshape(tokens, HEADS, HEAD_DIM)
    )

    def norm_step(carried, pieces, first_row):
        running_max, running_sum = carried
        key_pos = lookup_positions(block_order, first_row, pieces[0].shape[0], block_len)
        logits, allowed, indicator = query_key_logits(query_heads, pieces[0], own_pos, key_pos)
        new_max = jnp.maximum(running_max, jnp.max(logits, axis=-1))
        kept = jnp.where(allowed, jnp.exp(logits - new_max[..., None]), 0.0)
        return (new_max, running_sum * jnp.exp(running_max - new_max) + jnp.sum(kept, axis=-1))

    start_state = (
        jnp.full((HEADS, tokens), NEG_BIG, jnp.float32),
        jnp.zeros((HEADS, tokens), jnp.float32),
    )
    running_max, running_sum = fold_groups(
        norm_step, start_state, (lax.all_gather(key_heads, "ctx", axis=0, tiled=True),), tokens
    )
    log_norm = running_max + jnp.log(running_sum)

    def output_step(carried, pieces, first_row):
        key_pos = lookup_positions(block_order, first_row, pieces[0].shape[0], block_len)
        logits, allowed, indicator = query_key_logits(query_heads, pieces[0], own_pos, key_pos)
        attn_probs = jnp.exp(logits - log_norm[..., None]).astype(jnp.bfloat16)
        return carried + jnp.einsum(
            "hqk,khe->qhe", attn_probs, pieces[1], preferred_element_type=jnp.float32
        )

    zero_heads = jnp.zeros((tokens, HEADS, HEAD_DIM), jnp.float32)
    attn_sum = fold_groups(
        output_step,
        zero_heads,
        (
            lax.all_gather(key_heads, "ctx", axis=0, tiled=True),
            lax.all_gather(value_heads, "ctx", axis=0, tiled=True),
        ),
        tokens,
    )
    attended = attn_sum.reshape(tokens, head_width).astype(jnp.bfloat16)
    after_self = resid_in + plain_dot(attended, out_full)
    normed_two = rms_norm(after_self, gain_two).astype(jnp.bfloat16)
    cross_q_heads = (
        plain_dot(normed_two, cross_query_full)
        .astype(jnp.bfloat16)
        .reshape(tokens, HEADS, HEAD_DIM)
    )
    encoder_rows = encoder[0]
    encoder_key_rows, cross_values = (
        lax.all_gather(
            plain_dot(encoder_rows, cross_key_full).astype(jnp.bfloat16), "ctx", axis=0, tiled=True
        ),
        lax.all_gather(
            plain_dot(encoder_rows, cross_value_full).astype(jnp.bfloat16),
            "ctx",
            axis=0,
            tiled=True,
        ),
    )
    cross_k_heads = encoder_key_rows.reshape(encoder_key_rows.shape[0], HEADS, HEAD_DIM)
    cross_v_heads = cross_values.reshape(cross_values.shape[0], HEADS, HEAD_DIM)
    cross_logits = jnp.einsum(
        "qhe,khe->hqk", cross_q_heads, cross_k_heads, preferred_element_type=jnp.float32
    )
    cross_exact = jnp.exp(cross_logits - jax.nn.logsumexp(cross_logits, axis=-1, keepdims=True))
    cross_probs = cross_exact.astype(jnp.bfloat16)
    cross_mixed = (
        jnp.einsum("hqk,khe->qhe", cross_probs, cross_v_heads, preferred_element_type=jnp.float32)
        .reshape(tokens, head_width)
        .astype(jnp.bfloat16)
    )
    after_cross = after_self + plain_dot(cross_mixed, cross_out_full)
    normed_three = rms_norm(after_cross, gain_three).astype(jnp.bfloat16)
    gate_act = plain_dot(normed_three, gate_full)
    up_act = plain_dot(normed_three, up_full)
    hidden_float, mlp_pull = jax.vjp(gelu_product, gate_act, up_act)
    hidden = hidden_float.astype(jnp.bfloat16)
    result = after_cross + plain_dot(hidden, down_full)
    resid_grad = cotangent[0].astype(jnp.float32)
    branch_three = resid_grad.astype(jnp.bfloat16)
    down_grad = left_contract(hidden, branch_three)
    hidden_state_gradient = right_contract(branch_three, down_full)
    gate_grad, up_grad = mlp_pull(hidden_state_gradient)
    gate_grad = gate_grad.astype(jnp.bfloat16)
    up_grad = up_grad.astype(jnp.bfloat16)
    gate_w_grad = left_contract(normed_three, gate_grad)
    up_w_grad = left_contract(normed_three, up_grad)
    normed_three_grad = right_contract(gate_grad, gate_full) + right_contract(up_grad, up_full)
    part_grad, gain_three_grad = norm_back(after_cross, gain_three, normed_three_grad)
    after_cross_grad = resid_grad + part_grad
    branch_two = after_cross_grad.astype(jnp.bfloat16)
    cross_out_grad = left_contract(cross_mixed, branch_two)
    mix_grad = (
        right_contract(branch_two, cross_out_full)
        .astype(jnp.bfloat16)
        .reshape(tokens, HEADS, HEAD_DIM)
    )
    cross_score_grad = jnp.einsum(
        "qhe,khe->hqk", mix_grad, cross_v_heads, preferred_element_type=jnp.float32
    )
    cross_delta = jnp.sum(cross_exact * cross_score_grad, axis=-1, keepdims=True)
    cross_dlogits = (cross_exact * (cross_score_grad - cross_delta)).astype(jnp.bfloat16)
    cross_q_grad = (
        jnp.einsum("hqk,khe->qhe", cross_dlogits, cross_k_heads, preferred_element_type=jnp.float32)
        .reshape(tokens, head_width)
        .astype(jnp.bfloat16)
    )
    cross_k_part = jnp.einsum(
        "hqk,qhe->khe", cross_dlogits, cross_q_heads, preferred_element_type=jnp.float32
    ).reshape(-1, head_width)
    cross_v_part = jnp.einsum(
        "hqk,qhe->khe", cross_probs, mix_grad, preferred_element_type=jnp.float32
    ).reshape(-1, head_width)
    cross_k_grad, cross_v_grad = (
        lax.psum_scatter(cross_k_part, "ctx", scatter_dimension=0, tiled=True),
        lax.psum_scatter(cross_v_part, "ctx", scatter_dimension=0, tiled=True),
    )
    cross_k_grad = cross_k_grad.astype(jnp.bfloat16)
    cross_v_grad = cross_v_grad.astype(jnp.bfloat16)
    cross_query_grad = left_contract(normed_two, cross_q_grad)
    cross_key_grad = left_contract(encoder_rows, cross_k_grad)
    cross_value_grad = left_contract(encoder_rows, cross_v_grad)
    encoder_grad = (
        right_contract(cross_k_grad, cross_key_full)
        + right_contract(cross_v_grad, cross_value_full)
    ).astype(jnp.bfloat16)
    normed_two_grad = right_contract(cross_q_grad, cross_query_full)
    part_grad, gain_two_grad = norm_back(after_self, gain_two, normed_two_grad)
    after_self_grad = after_cross_grad + part_grad
    branch_one = after_self_grad.astype(jnp.bfloat16)
    out_w_grad = left_contract(attended, branch_one)
    dattn_heads = (
        right_contract(branch_one, out_full).astype(jnp.bfloat16).reshape(tokens, HEADS, HEAD_DIM)
    )
    row_delta = jnp.einsum("qhe,qhe->hq", dattn_heads.astype(jnp.float32), attn_sum)

    def block_grads(
        query_side, grad_side, norm_side, delta_side, query_pos, key_side, value_side, key_pos
    ):
        logits, allowed, indicator = query_key_logits(query_side, key_side, query_pos, key_pos)
        exact = jnp.exp(logits - norm_side[..., None])
        score_grad = jnp.einsum(
            "qhe,khe->hqk", grad_side, value_side, preferred_element_type=jnp.float32
        )
        logits_gradient = (exact * (score_grad - delta_side[..., None])).astype(jnp.bfloat16)
        grad_query = jnp.einsum(
            "hqk,khe->qhe", logits_gradient, key_side, preferred_element_type=jnp.float32
        )
        grad_key = jnp.einsum(
            "hqk,qhe->khe", logits_gradient, query_side, preferred_element_type=jnp.float32
        )
        grad_value = jnp.einsum(
            "hqk,qhe->khe",
            exact.astype(jnp.bfloat16),
            grad_side,
            preferred_element_type=jnp.float32,
        )
        bucket_table_gradient = jnp.einsum(
            "ouw,muw->om", indicator, logits_gradient, preferred_element_type=jnp.float32
        )
        return (grad_query, grad_key, grad_value, bucket_table_gradient)

    zero_table = jnp.zeros((BUCKETS, HEADS), jnp.float32)
    full_zero = jnp.zeros((total_rows, HEADS, HEAD_DIM), jnp.float32)

    def key_grad_step(carried, pieces, first_row):
        query_total, table_total, key_total, value_total = carried
        key_pos = lookup_positions(block_order, first_row, pieces[0].shape[0], block_len)
        grad_query, grad_key, grad_value, bucket_table_gradient = block_grads(
            query_heads, dattn_heads, log_norm, row_delta, own_pos, pieces[0], pieces[1], key_pos
        )
        key_total = lax.dynamic_update_slice_in_dim(key_total, grad_key, first_row, 0)
        value_total = lax.dynamic_update_slice_in_dim(value_total, grad_value, first_row, 0)
        return (
            query_total + grad_query,
            table_total + bucket_table_gradient,
            key_total,
            value_total,
        )

    query_sum, table_grad, key_partial, value_partial = fold_groups(
        key_grad_step,
        (zero_heads, zero_table, full_zero, full_zero),
        (
            lax.all_gather(key_heads, "ctx", axis=0, tiled=True),
            lax.all_gather(value_heads, "ctx", axis=0, tiled=True),
        ),
        tokens,
    )
    key_sum, value_accumulated = (
        lax.psum_scatter(key_partial, "ctx", scatter_dimension=0, tiled=True),
        lax.psum_scatter(value_partial, "ctx", scatter_dimension=0, tiled=True),
    )
    query_grad = query_sum.reshape(tokens, head_width).astype(jnp.bfloat16)
    key_grad = key_sum.reshape(tokens, head_width).astype(jnp.bfloat16)
    value_grad = value_accumulated.reshape(tokens, head_width).astype(jnp.bfloat16)
    query_w_grad = left_contract(normed_one, query_grad)
    key_w_grad = left_contract(normed_one, key_grad)
    value_w_grad = left_contract(normed_one, value_grad)
    normed_one_grad = (
        right_contract(query_grad, query_full)
        + right_contract(key_grad, key_full)
        + right_contract(value_grad, value_full)
    )
    part_grad, gain_one_grad = norm_back(resid_in, gain_one, normed_one_grad)
    input_grad = (after_self_grad + part_grad).astype(jnp.bfloat16)
    (
        sum_gain_one,
        sum_query,
        sum_key,
        sum_value,
        sum_out,
        sum_table,
        sum_gain_two,
        sum_cross_query,
        sum_cross_key,
        sum_cross_value,
        sum_cross_out,
        sum_gain_three,
        sum_gate,
        sum_up,
        sum_down,
    ) = (
        lax.psum_scatter(
            gain_one_grad.astype(jnp.bfloat16), "wsh", scatter_dimension=0, tiled=True
        ).astype(jnp.float32),
        lax.psum_scatter(
            query_w_grad.astype(jnp.bfloat16), "wsh", scatter_dimension=0, tiled=True
        ).astype(jnp.float32),
        lax.psum_scatter(
            key_w_grad.astype(jnp.bfloat16), "wsh", scatter_dimension=0, tiled=True
        ).astype(jnp.float32),
        lax.psum_scatter(
            value_w_grad.astype(jnp.bfloat16), "wsh", scatter_dimension=0, tiled=True
        ).astype(jnp.float32),
        lax.psum_scatter(
            out_w_grad.astype(jnp.bfloat16), "wsh", scatter_dimension=0, tiled=True
        ).astype(jnp.float32),
        lax.psum_scatter(
            table_grad.astype(jnp.bfloat16), "wsh", scatter_dimension=0, tiled=True
        ).astype(jnp.float32),
        lax.psum_scatter(
            gain_two_grad.astype(jnp.bfloat16), "wsh", scatter_dimension=0, tiled=True
        ).astype(jnp.float32),
        lax.psum_scatter(
            cross_query_grad.astype(jnp.bfloat16), "wsh", scatter_dimension=0, tiled=True
        ).astype(jnp.float32),
        lax.psum_scatter(
            cross_key_grad.astype(jnp.bfloat16), "wsh", scatter_dimension=0, tiled=True
        ).astype(jnp.float32),
        lax.psum_scatter(
            cross_value_grad.astype(jnp.bfloat16), "wsh", scatter_dimension=0, tiled=True
        ).astype(jnp.float32),
        lax.psum_scatter(
            cross_out_grad.astype(jnp.bfloat16), "wsh", scatter_dimension=0, tiled=True
        ).astype(jnp.float32),
        lax.psum_scatter(
            gain_three_grad.astype(jnp.bfloat16), "wsh", scatter_dimension=0, tiled=True
        ).astype(jnp.float32),
        lax.psum_scatter(
            gate_w_grad.astype(jnp.bfloat16), "wsh", scatter_dimension=0, tiled=True
        ).astype(jnp.float32),
        lax.psum_scatter(
            up_w_grad.astype(jnp.bfloat16), "wsh", scatter_dimension=0, tiled=True
        ).astype(jnp.float32),
        lax.psum_scatter(
            down_grad.astype(jnp.bfloat16), "wsh", scatter_dimension=0, tiled=True
        ).astype(jnp.float32),
    )
    total_grads = lax.psum(
        (
            sum_gain_one,
            sum_query,
            sum_key,
            sum_value,
            sum_out,
            sum_table,
            sum_gain_two,
            sum_cross_query,
            sum_cross_key,
            sum_cross_value,
            sum_cross_out,
            sum_gain_three,
            sum_gate,
            sum_up,
            sum_down,
        ),
        "ctx",
    )
    return (result.astype(jnp.bfloat16)[None], input_grad[None], encoder_grad[None]) + tuple(
        total_grads
    )


F32 = jnp.float32
BF16 = jnp.bfloat16
MESH = pl.DeviceIdType.MESH
TILE = 256
BLOCK = 64
MIB = 2**20
GELU_RATE, GELU_CUBE = 0.7978845608, 0.044715


def dot_nt(left, right):
    return lax.dot_general(left, right, (((1,), (1,)), ((), ())), preferred_element_type=F32)


def vmem_spec():
    return pl.BlockSpec(memory_space=pltpu.VMEM)


def any_spec():
    return pl.BlockSpec(memory_space=pl.ANY)


def unpack_pair(landed, pair, rows):
    left, right = landed[2 * pair, rows, :], landed[2 * pair + 1, rows, :]
    return (
        jnp.concatenate([left[:, :HEAD_DIM], right[:, :HEAD_DIM]], axis=1),
        jnp.concatenate([left[:, HEAD_DIM:], right[:, HEAD_DIM:]], axis=1),
    )


def place_tiles(bias_lines, tiles):
    for apart in range(tiles.shape[0]):
        line = jnp.broadcast_to(bias_lines[apart : apart + 1, :], (TILE, 2 * TILE))
        tiles[apart] = pltpu.roll(line, 0, 1, stride=1, stride_axis=0)[:, :TILE]


def attend_scratch(blocks):
    length = blocks * BLOCK
    vmem = pltpu.VMEM
    return [
        vmem((length, HEAD_DIM), BF16),
        vmem((length, HEAD_DIM), BF16),
        vmem((HEAD_DIM, length), BF16),
        vmem((length // TILE, TILE, TILE), F32),
        vmem((length, HEAD_DIM), F32),
        vmem((length, HEAD_DIM), F32),
    ]


def attend(order, held_at, pairs, lone, bias_lines, out_ref, sum_ref, norm_ref, q_s, k_s, vt_s, tiles, staged, o_s):
    blocks = held_at.shape[0]
    spans = blocks * BLOCK // TILE

    def in_order(into):
        for block in range(blocks):
            at = slice(block * BLOCK, (block + 1) * BLOCK)
            into[at, :] = staged[pl.ds(held_at[block] * BLOCK, BLOCK), :].astype(into.dtype)

    for side, into in ((0, q_s), (1, k_s)):
        for device in range(blocks // 2):
            at = slice(2 * device * BLOCK, 2 * (device + 1) * BLOCK)
            staged[at, :] = pairs[device, :, side * HEAD_DIM : (side + 1) * HEAD_DIM].astype(F32)
        in_order(into)
    for stored in range(blocks):
        at = slice(stored * BLOCK, (stored + 1) * BLOCK)
        cols = slice(stored % 2 * HEAD_DIM, (stored % 2 + 1) * HEAD_DIM)
        staged[at, :] = lone[stored // 2, :, cols].astype(F32)
    in_order(o_s)
    vt_s[...] = jnp.transpose(o_s[...], (1, 0)).astype(BF16)
    place_tiles(bias_lines, tiles)
    for i in range(spans):
        at_i = slice(i * TILE, (i + 1) * TILE)
        queries = q_s[at_i, :]
        scores = [
            dot_nt(k_s[j * TILE : (j + 1) * TILE, :], queries) + tiles[i - j] for j in range(i + 1)
        ]
        top = functools.reduce(
            jnp.maximum, [jnp.max(each, axis=0, keepdims=True) for each in scores]
        )
        total = jnp.zeros((1, TILE), F32)
        mixed = jnp.zeros((HEAD_DIM, TILE), F32)
        for j in range(i + 1):
            weights = jnp.exp(scores[j] - top)
            total = total + jnp.sum(weights, axis=0, keepdims=True)
            mixed = mixed + plain_dot(
                vt_s[:, j * TILE : (j + 1) * TILE], weights.astype(BF16)
            )
        norm_ref[0:1, at_i] = top + jnp.log(total)
        sum_ref[:, at_i] = mixed / total
    o_s[...] = jnp.transpose(sum_ref[...], (1, 0))
    for stored in range(blocks):
        cols = slice(stored % 2 * HEAD_DIM, (stored % 2 + 1) * HEAD_DIM)
        out_ref[stored // 2, :, cols] = o_s[pl.ds(order[stored] * BLOCK, BLOCK), :].astype(BF16)


def attend_back(
    order, held_at, pairs, lone, grad_landed, sums, norm, bias_lines, out_ref, lines_ref,
    q_s, k_s, v_s, do_s, kt_s, tiles, by_offset, dq_s, dk_s, dv_s, delta_s, dqt_s,
):
    blocks = order.shape[0]
    spans = blocks * BLOCK // TILE
    def stored_rows(stored):
        return slice(stored * BLOCK, (stored + 1) * BLOCK), stored // 2, slice(
            stored % 2 * HEAD_DIM, (stored % 2 + 1) * HEAD_DIM
        )

    def in_order(into, staged):
        for block in range(blocks):
            at = slice(block * BLOCK, (block + 1) * BLOCK)
            into[at, :] = staged[pl.ds(held_at[block] * BLOCK, BLOCK), :].astype(BF16)

    for stored in range(blocks):
        at, device, cols = stored_rows(stored)
        pair = pairs[device, stored % 2 * BLOCK : (stored % 2 + 1) * BLOCK, :].astype(F32)
        dq_s[at, :] = pair[:, :HEAD_DIM]
        dk_s[at, :] = pair[:, HEAD_DIM:]
        dv_s[at, :] = lone[device, :, cols].astype(F32)
    in_order(q_s, dq_s)
    in_order(k_s, dk_s)
    in_order(v_s, dv_s)
    for stored in range(blocks):
        at, device, cols = stored_rows(stored)
        dq_s[at, :] = grad_landed[device, :, cols].astype(F32)
    in_order(do_s, dq_s)
    place_tiles(bias_lines, tiles)
    kt_s[...] = jnp.transpose(k_s[...].astype(F32), (1, 0)).astype(BF16)
    grad_t = jnp.transpose(do_s[...].astype(F32), (1, 0))
    delta_s[...] = jnp.sum(grad_t * sums[...], axis=0, keepdims=True)
    by_offset[...] = jnp.zeros_like(by_offset)
    dk_s[...] = jnp.zeros_like(dk_s)
    dv_s[...] = jnp.zeros_like(dv_s)
    for i in range(spans):
        at_i = slice(i * TILE, (i + 1) * TILE)
        queries, grads = q_s[at_i, :], do_s[at_i, :]
        norm_i, delta_i = norm[0:1, at_i], delta_s[0:1, at_i]
        dqt = jnp.zeros((HEAD_DIM, TILE), F32)
        for j in range(i + 1):
            at_j = slice(j * TILE, (j + 1) * TILE)
            exact = jnp.exp(dot_nt(k_s[at_j, :], queries) + tiles[i - j] - norm_i)
            dscore = exact * (dot_nt(v_s[at_j, :], grads) - delta_i)
            by_offset[i - j] += dscore
            rounded = dscore.astype(BF16)
            dv_s[at_j, :] += plain_dot(exact.astype(BF16), grads)
            dk_s[at_j, :] += plain_dot(rounded, queries)
            dqt = dqt + plain_dot(kt_s[:, at_j], rounded)
        dqt_s[:, at_i] = dqt
    dq_s[...] = jnp.transpose(dqt_s[...], (1, 0))
    for stored in range(blocks):
        device, half = stored // 2, stored % 2
        at = pl.ds(order[stored] * BLOCK, BLOCK)
        rows = slice(half * BLOCK, (half + 1) * BLOCK)
        cols = slice(half * HEAD_DIM, (half + 1) * HEAD_DIM)
        out_ref[device, rows, :HEAD_DIM] = dq_s[at, :].astype(BF16)
        out_ref[device, rows, HEAD_DIM:] = dk_s[at, :].astype(BF16)
        out_ref[device, 2 * BLOCK :, cols] = dv_s[at, :].astype(BF16)
    for apart in range(spans):
        folded = jnp.zeros((8, 2 * TILE), F32)
        for group in range(TILE // 8):
            rows = by_offset[apart, 8 * group : 8 * group + 8, :]
            wide = jnp.concatenate([rows, jnp.zeros((8, TILE), F32)], axis=1)
            folded = folded + (pltpu.roll(wide, 2 * TILE - 8 * group, 1) if group else wide)
        line = folded[0:1]
        for row in range(1, 8):
            line = line + pltpu.roll(folded[row : row + 1], 2 * TILE - row, 1)
        lines_ref[apart : apart + 1, :] = line


class Weights(NamedTuple):
    query: Any
    key: Any
    value: Any
    out: Any
    cross_key: Any
    cross_value: Any
    cross_query: Any
    cross_out: Any
    gate: Any
    up: Any
    down: Any


W = Weights(*range(11))
LENT = (W.query, W.key, W.value, W.cross_key, W.cross_value)


class Made(NamedTuple):
    normed_one: Any
    pairs: Any
    lone: Any
    attn_sum: Any
    log_norm: Any
    attended: Any
    normed_two: Any
    cross_mixed: Any
    normed_three: Any
    hidden: Any
    gate_grad: Any
    up_grad: Any
    branch_two: Any
    cross_q_grad: Any
    branch_one: Any
    dattn: Any
    kv_part: Any
    resid_grad: Any
    result: Any
    gain_grads: Any
    gain_one: Any
    bias_lines: Any
    encoder_both: Any


M = Made(*range(23))


class Far(NamedTuple):
    normed_three: Any
    hidden: Any
    cross_mixed: Any
    normed_two: Any
    attended: Any
    normed_one: Any
    gate: Any
    branch_three: Any
    up: Any
    branch_two: Any


BIT_X, BIT_Y = 0, 1
FAR = Far(*range(10))
FAR_AXIS = Far(
    normed_three=BIT_Y,
    hidden=BIT_X,
    cross_mixed=BIT_X,
    normed_two=BIT_X,
    attended=BIT_Y,
    normed_one=BIT_X,
    gate=BIT_Y,
    branch_three=BIT_X,
    up=BIT_Y,
    branch_two=BIT_X,
)


class Scratch(NamedTuple):
    small_far: Any
    table_far: Any
    pairs_out: Any
    lone_out: Any
    encoder_all: Any
    mixed_out: Any
    mixed_in: Any
    cross_keys: Any
    cross_values: Any
    cross_queries: Any
    cross_exact: Any
    after_self: Any
    after_cross: Any
    gate_act: Any
    up_act: Any
    mix_grad: Any


def norm_parts(values):
    return lax.rsqrt(jnp.mean(values * values, axis=1, keepdims=True) + EPSILON)


def norm_backward(values, gain, cotan):
    rate = norm_parts(values)
    scaled = cotan * gain
    slope = jnp.mean(scaled * values, axis=1, keepdims=True)
    return (
        rate * scaled - values * (rate * rate * rate) * slope,
        jnp.sum(cotan * values * rate, axis=0, keepdims=True),
    )


def layer_kernel(tokens_in, cotangent, encoder, small, table, in_bucket, held_at, order, *refs):
    refs = list(refs)

    def take(number):
        taken = refs[:number]
        del refs[:number]
        return taken

    sources = take(len(W))
    saved = Made(*take(len(Made._fields)))
    far = Far(*take(len(Far._fields)))
    lent = take(len(LENT))
    weights = take(len(W))
    own = Scratch(*take(len(Scratch._fields)))
    out = Made(*take(len(Made._fields)))
    (save_sem, own_sem, weight_own, weight_send, weight_recv, lent_send, lent_recv, far_send, far_recv, all_own, all_send, all_recv) = refs
    me, core = lax.axis_index("ctx"), lax.axis_index("wsh")
    peers = lax.axis_size("ctx")
    x, y = lax.rem(me, 2), lax.rem(me // 2, 2)
    tokens, width = tokens_in.shape
    finish = []

    barrier = pltpu.get_barrier_semaphore()
    for step in range(1, peers):
        pl.semaphore_signal(
            barrier, inc=1, device_id=(lax.rem(me + step, peers), core), device_id_type=MESH
        )
    pl.semaphore_signal(barrier, inc=1, device_id=(me, 1 - core), device_id_type=MESH)

    def half_rows(ref, side):
        half = ref.shape[0] // 2
        return ref.at[pl.ds(pl.multiple_of(side * half, 16), half)]

    def remote(src, dst, send_sem, recv_sem, ctx, side):
        return pltpu.make_async_remote_copy(
            src_ref=src,
            dst_ref=dst,
            send_sem=send_sem,
            recv_sem=recv_sem,
            device_id=(ctx, side),
            device_id_type=MESH,
        )

    def arrived(ref, sem):
        remote(ref, ref, own_sem, sem, me, 1 - core).wait_recv()

    def launch(src, dst, send_sem, recv_sem, ctx, side):
        remote(src, dst, send_sem, recv_sem, ctx, side).start()
        finish.append(lambda: remote(src, src, send_sem, own_sem, me, 1 - core).wait_send())

    def to_pair(at, source, halves=False):
        bit = FAR_AXIS[at]
        if halves:
            half = source.shape[1] // 2
            source = source.at[:, pl.ds(pl.multiple_of((1 - (x, y)[bit]) * half, 128), half)]
        launch(source, far[at], far_send.at[at], far_recv.at[at], me ^ (1 << bit), core)

    def save(*made):
        for at in made:
            copy = pltpu.make_async_copy(out[at], saved[at], save_sem.at[at])
            copy.start()
            finish.append(copy.wait)

    small_sem, table_sem, encoder_sem = (len(Far._fields) + at for at in range(3))
    local = {}
    for at in W:
        local[at] = pltpu.make_async_copy(sources[at], half_rows(weights[at], core), weight_own.at[at])
        local[at].start()
    pl.semaphore_wait(barrier, peers)

    launch(small, own.small_far, far_send.at[small_sem], far_recv.at[small_sem], me, 1 - core)
    launch(table, own.table_far, far_send.at[table_sem], far_recv.at[table_sem], me, 1 - core)
    for at in W:
        launch(sources[at], half_rows(weights[at], core), weight_send.at[at], weight_recv.at[at], me, 1 - core)
    for at, source in enumerate(LENT):
        launch(sources[source], lent[at], lent_send.at[at], lent_recv.at[at], me, 1 - core)

    def weight(at):
        if at in local:
            local.pop(at).wait()
            arrived(half_rows(weights[at], 1 - core), weight_recv.at[at])
        return weights[at]

    def to_all(which, source, target, spread=True):
        for step in range(1, peers):
            peer = lax.rem(me + step, peers)
            remote(
                source.at[peer] if spread else source, target.at[me], all_send.at[which], all_recv.at[which], peer, core
            ).start()
        kept = pltpu.make_async_copy(source.at[me] if spread else source, target.at[me], all_own.at[which])
        kept.start()
        finish.append(lambda: remote(target.at[1:], target.at[1:], all_send.at[which], own_sem, me, 1 - core).wait_send())

        def wait():
            kept.wait()
            arrived(target.at[1:], all_recv.at[which])

        return wait

    def tiles_of(total):
        return [slice(at, at + 256) for at in range(0, total, 256)]

    def times(values, name):
        ref = weight(name)
        return jnp.concatenate([plain_dot(values, ref[:, cols]) for cols in tiles_of(ref.shape[1])], axis=1)

    def times_back(values, name):
        ref = weight(name)
        return jnp.concatenate([dot_nt(values, ref[cols, :]) for cols in tiles_of(ref.shape[0])], axis=1)

    def head(at):
        return slice(at * HEAD_DIM, (at + 1) * HEAD_DIM)

    def head_pair(at):
        return slice(2 * at * HEAD_DIM, 2 * (at + 1) * HEAD_DIM)

    arrived(own.small_far, far_recv.at[small_sem])
    arrived(own.table_far, far_recv.at[table_sem])

    def both(mine, others, axis):
        first = jnp.where(core == 0, mine, others)
        second = jnp.where(core == 0, others, mine)
        return jnp.concatenate([first, second], axis=axis)

    gain_one, gain_two, gain_three = (
        both(small[at : at + 1, :], own.small_far[at : at + 1, :], 1) for at in range(3)
    )
    out.gain_one[...] = gain_one
    whole_table = both(table[...], own.table_far[...], 0)
    lane = lax.broadcasted_iota(jnp.int32, whole_table.shape, 1)
    column = jnp.sum(jnp.where(lane == me, whole_table, 0.0), axis=1, keepdims=True)
    spans = in_bucket.shape[0]
    for apart in range(spans):
        line = jnp.sum(in_bucket[apart] * column, axis=0, keepdims=True)
        out.bias_lines[apart : apart + 1, :TILE] = line
        if apart + 1 < spans:
            out.bias_lines[apart + 1 : apart + 2, TILE:] = line
    out.bias_lines[0:1, TILE:] = jnp.full((1, TILE), NEG_BIG, F32)

    resid = tokens_in[...].astype(F32)
    out.normed_one[...] = (resid * norm_parts(resid) * gain_one).astype(BF16)
    normed_one = out.normed_one[...]
    queries = times(normed_one, W.query).astype(BF16)
    keys = times(normed_one, W.key).astype(BF16)
    for at in range(peers):
        own.pairs_out[at] = jnp.concatenate([queries[:, head(at)], keys[:, head(at)]], axis=1)
    pairs_arrival = to_all(0, own.pairs_out, out.pairs)
    values = times(normed_one, W.value).astype(BF16)
    for at in range(peers):
        own.lone_out[at] = jnp.concatenate(
            [values[:BLOCK, head(at)], values[BLOCK:, head(at)]], axis=1
        )
    lone_arrival = to_all(1, own.lone_out, out.lone)
    encoder_arrival = to_all(2, encoder, own.encoder_all, spread=False)
    to_pair(FAR.branch_three, cotangent, halves=True)
    to_pair(FAR.normed_one, out.normed_one)
    save(M.normed_one, M.gain_one, M.bias_lines)
    place_bias = out.bias_lines
    pairs_arrival()
    lone_arrival()
    pl.run_scoped(
        functools.partial(
            attend, order, held_at, out.pairs, out.lone, place_bias, own.mixed_out, out.attn_sum, out.log_norm
        ),
        *attend_scratch(held_at.shape[0]),
    )
    mixed_arrival = to_all(3, own.mixed_out, own.mixed_in)
    save(M.pairs, M.lone, M.attn_sum, M.log_norm)

    encoder_arrival()
    encoder_rows = jnp.concatenate([own.encoder_all[at] for at in range(peers)], axis=0)
    half = width // 2
    count = encoder_rows.shape[0]
    out.encoder_both[:count, :] = jnp.where(core == 0, encoder_rows[:, :half], encoder_rows[:, half:])
    own.cross_keys[...] = times(encoder_rows, W.cross_key).astype(BF16)
    own.cross_values[...] = times(encoder_rows, W.cross_value).astype(BF16)

    mixed_arrival()
    for pair in range(peers // 2):
        first, second = unpack_pair(own.mixed_in, pair, slice(0, BLOCK))
        out.attended[:BLOCK, head_pair(pair)] = first
        out.attended[BLOCK:, head_pair(pair)] = second
    to_pair(FAR.attended, out.attended)
    save(M.attended)
    own.after_self[...] = tokens_in[...].astype(F32) + times(out.attended[...], W.out)
    after_self = own.after_self[...]
    out.normed_two[...] = (after_self * norm_parts(after_self) * gain_two).astype(BF16)
    to_pair(FAR.normed_two, out.normed_two)
    save(M.normed_two)
    own.cross_queries[...] = times(out.normed_two[...], W.cross_query).astype(BF16)

    for pair in range(peers // 2):
        mixed = []
        for at in (2 * pair, 2 * pair + 1):
            scores = dot_nt(own.cross_keys[:, head(at)], own.cross_queries[:, head(at)])
            weight_t = jnp.exp(scores - jnp.max(scores, axis=0, keepdims=True))
            exact = weight_t / jnp.sum(weight_t, axis=0, keepdims=True)
            own.cross_exact[at] = exact
            mixed.append(left_contract(exact.astype(BF16), own.cross_values[:, head(at)]))
        out.cross_mixed[:, head_pair(pair)] = jnp.concatenate(mixed, axis=1).astype(BF16)
    to_pair(FAR.cross_mixed, out.cross_mixed)
    save(M.cross_mixed)
    own.after_cross[...] = own.after_self[...] + times(out.cross_mixed[...], W.cross_out)
    after_cross = own.after_cross[...]
    out.normed_three[...] = (after_cross * norm_parts(after_cross) * gain_three).astype(BF16)
    to_pair(FAR.normed_three, out.normed_three)
    save(M.normed_three)

    normed_three = out.normed_three[...]
    gate, up, down = weight(W.gate), weight(W.up), weight(W.down)
    for cols in tiles_of(gate.shape[1]):
        gate_act = plain_dot(normed_three, gate[:, cols])
        up_act = plain_dot(normed_three, up[:, cols])
        own.gate_act[:, cols] = gate_act
        own.up_act[:, cols] = up_act
        curve = jnp.tanh(GELU_RATE * (gate_act + GELU_CUBE * gate_act * gate_act * gate_act))
        out.hidden[:, cols] = (0.5 * gate_act * (1.0 + curve) * up_act).astype(BF16)
    to_pair(FAR.hidden, out.hidden)
    save(M.hidden)
    out.result[...] = (own.after_cross[...] + times(out.hidden[...], W.down)).astype(BF16)

    branch_three = cotangent[...]
    half = down.shape[0] // 2
    for side in (1 - y, y):
        for start in range(0, half, 256):
            size = min(256, half - start)
            cols = pl.ds(pl.multiple_of(side * half + start, 128), size)
            hidden_grad = dot_nt(branch_three, down[pl.ds(pl.multiple_of(side * half + start, 128), size), :])
            gate_act, up_act = own.gate_act[:, cols], own.up_act[:, cols]
            square = gate_act * gate_act
            curve = jnp.tanh(GELU_RATE * (gate_act + GELU_CUBE * gate_act * square))
            rise = 0.5 * (1.0 + curve) + 0.5 * gate_act * (1.0 - curve * curve) * (
                GELU_RATE * (1.0 + 3.0 * GELU_CUBE * square)
            )
            out.gate_grad[:, cols] = (hidden_grad * up_act * rise).astype(BF16)
            out.up_grad[:, cols] = (hidden_grad * (0.5 * gate_act * (1.0 + curve))).astype(BF16)
        if side is not y:
            to_pair(FAR.gate, out.gate_grad, halves=True)
            to_pair(FAR.up, out.up_grad, halves=True)
    save(M.result, M.gate_grad, M.up_grad)
    normed_grad = times_back(out.gate_grad[...], W.gate) + times_back(out.up_grad[...], W.up)
    back, gain_three_grad = norm_backward(own.after_cross[...], gain_three, normed_grad)
    out.resid_grad[...] = cotangent[...].astype(F32) + back
    out.branch_two[...] = out.resid_grad[...].astype(BF16)

    to_pair(FAR.branch_two, out.branch_two, halves=True)
    save(M.branch_two)
    own.mix_grad[...] = times_back(out.branch_two[...], W.cross_out).astype(BF16)
    for pair in range(peers // 2):
        terms = []
        for at in (2 * pair, 2 * pair + 1):
            exact = own.cross_exact[at]
            grads = own.mix_grad[:, head(at)]
            score_grad = dot_nt(own.cross_values[:, head(at)], grads)
            slope = jnp.sum(exact * score_grad, axis=0, keepdims=True)
            rounded = (exact * (score_grad - slope)).astype(BF16)
            terms.append(
                (
                    left_contract(rounded, own.cross_keys[:, head(at)]),
                    plain_dot(rounded, own.cross_queries[:, head(at)]),
                    plain_dot(exact.astype(BF16), grads),
                )
            )
        cols = head_pair(pair)
        values_cols = slice(width + cols.start, width + cols.stop)
        for ref, into, at in ((out.cross_q_grad, cols, 0), (out.kv_part, cols, 1), (out.kv_part, values_cols, 2)):
            ref[:, into] = jnp.concatenate([terms[0][at], terms[1][at]], axis=1).astype(BF16)
    save(M.cross_q_grad, M.kv_part)
    normed_grad = times_back(out.cross_q_grad[...], W.cross_query)
    back, gain_two_grad = norm_backward(own.after_self[...], gain_two, normed_grad)
    out.resid_grad[...] += back
    out.branch_one[...] = out.resid_grad[...].astype(BF16)
    save(M.resid_grad, M.branch_one)
    out.dattn[...] = times_back(out.branch_one[...], W.out).astype(BF16)
    save(M.dattn)

    for half in range(2):
        for index in range(4):
            cols = slice((4 * half + index) * 128, (4 * half + index + 1) * 128)
            out.gain_grads[half, index : index + 1, :] = gain_two_grad[:, cols]
            out.gain_grads[half, 4 + index : 5 + index, :] = gain_three_grad[:, cols]
        out.gain_grads[half, 8:, :] = jnp.zeros((4, 128), F32)
    save(M.gain_grads)

    other_half = pl.ds(pl.multiple_of((1 - core) * (width // 2), 128), width // 2)
    for at in range(peers):
        rows_at = own.encoder_all.shape[1]
        remote(
            own.encoder_all.at[at, :, other_half],
            out.encoder_both.at[count + at * rows_at : count + (at + 1) * rows_at],
            far_send.at[encoder_sem], far_recv.at[encoder_sem], me, 1 - core,
        ).start()
    arrived(out.encoder_both.at[count:], far_recv.at[encoder_sem])
    save(M.encoder_both)
    finish.append(
        lambda: remote(
            out.encoder_both.at[count:], out.encoder_both.at[count:], far_send.at[encoder_sem], own_sem, me, 1 - core
        ).wait_send()
    )
    for at, ref in enumerate(far):
        arrived(ref, far_recv.at[at])
    for at, ref in enumerate(lent):
        arrived(ref, lent_recv.at[at])
    for each in finish:
        each()


def layer(tokens_in, cotangent, encoder, small, table, in_bucket, held_at, order, sources):
    peers = lax.axis_size("ctx")
    tokens, width = tokens_in.shape
    hidden = sources.gate.shape[1]
    blocks = held_at.shape[0]
    length = blocks * BLOCK
    rows = encoder.shape[0] * peers
    dma, vmem = pltpu.SemaphoreType.DMA, pltpu.VMEM

    def shaped(*shape):
        return jax.ShapeDtypeStruct(shape, BF16)

    def exact(*shape):
        return jax.ShapeDtypeStruct(shape, F32)

    square, wide, half_wide = shaped(tokens, width), shaped(tokens, hidden), shaped(tokens, hidden // 2)
    pairs, lone = (peers, 2 * BLOCK, 2 * HEAD_DIM), (peers, BLOCK, 2 * HEAD_DIM)
    outputs = Made(
        normed_one=square,
        pairs=shaped(*pairs),
        lone=shaped(*lone),
        attn_sum=exact(HEAD_DIM, length),
        log_norm=exact(1, length),
        attended=square,
        normed_two=square,
        cross_mixed=square,
        normed_three=square,
        hidden=wide,
        gate_grad=wide,
        up_grad=wide,
        branch_two=square,
        cross_q_grad=square,
        branch_one=square,
        dattn=square,
        kv_part=shaped(rows, 2 * width),
        resid_grad=exact(tokens, width),
        result=square,
        gain_grads=exact(2, 12, 128),
        gain_one=exact(1, width),
        bias_lines=exact(length // TILE, 2 * TILE),
        encoder_both=shaped(2 * rows, width // 2),
    )
    half_square = shaped(tokens, width // 2)
    fars = Far(
        normed_three=square,
        hidden=wide,
        cross_mixed=square,
        normed_two=square,
        attended=square,
        normed_one=square,
        gate=half_wide,
        branch_three=half_square,
        up=half_wide,
        branch_two=half_square,
    )
    buffers = Scratch(
        small_far=vmem(small.shape, F32),
        table_far=vmem(table.shape, F32),
        pairs_out=vmem(pairs, BF16),
        lone_out=vmem(lone, BF16),
        encoder_all=vmem((peers,) + encoder.shape, BF16),
        mixed_out=vmem(lone, BF16),
        mixed_in=vmem(lone, BF16),
        cross_keys=vmem((rows, width), BF16),
        cross_values=vmem((rows, width), BF16),
        cross_queries=vmem((tokens, width), BF16),
        cross_exact=vmem((HEADS, rows, tokens), F32),
        after_self=vmem((tokens, width), F32),
        after_cross=vmem((tokens, width), F32),
        gate_act=vmem((tokens, hidden), F32),
        up_act=vmem((tokens, hidden), F32),
        mix_grad=vmem((tokens, width), BF16),
    )
    smem_spec = pl.BlockSpec(memory_space=pltpu.SMEM)
    results = pl.pallas_call(
        layer_kernel,
        out_shape=[*outputs, *fars, *(shaped(*sources[at].shape) for at in LENT)],
        in_specs=[vmem_spec()] * 6 + [smem_spec] * 2 + [any_spec()] * len(W),
        out_specs=[any_spec()] * (len(outputs) + len(fars) + len(LENT)),
        scratch_shapes=[vmem((2 * each.shape[0], each.shape[1]), BF16) for each in sources]
        + list(buffers)
        + [vmem(each.shape, each.dtype) for each in outputs]
        + [
            dma((len(outputs),)),
            dma,
            dma((len(W),)),
            dma((len(W),)),
            dma((len(W),)),
            dma((len(LENT),)),
            dma((len(LENT),)),
            dma((len(fars) + 3,)),
            dma((len(fars) + 3,)),
            dma((4,)),
            dma((4,)),
            dma((4,)),
        ],
        compiler_params=pltpu.CompilerParams(
            collective_id=1, has_side_effects=True, vmem_limit_bytes=62 * MIB
        ),
        name="layer",
    )(tokens_in, cotangent, encoder, small, table, in_bucket, held_at, order, *sources)
    made, results = results[: len(outputs)], results[len(outputs) :]
    return Made(*made), Far(*results[: len(fars)]), results[len(fars) :]


FAR_LEFTS, FAR_RIGHTS = 6, (0, 1, 2, 4)
SCHEDULE = (
    0, 256, 5, 16, 32, 3, 2, 257, 1, 6, 18, 4, 48, 34, 21, 17, 19, 37, 22, 33,
    20, 64, 38, 53, 35, 80, 69, 50, 96, 112, 258, 66, 7, 36, 49, 8, 128, 51, 65, 144,
    23, 67, 82, 52, 160, 39, 81, 24, 259, 98, 68, 97, 113, 54, 40, 84, 9, 83, 55, 85,
    114, 70, 129, 71, 99, 101, 117, 115, 176, 25, 145, 87, 133, 56, 260, 86, 100, 161, 192, 72,
    103, 116, 131, 102, 118, 41, 119, 130, 134, 146, 147, 57, 88, 73, 149, 104, 163, 150, 165, 162,
    89, 179, 132, 135, 178, 194, 105, 177, 195, 166, 193, 121, 120, 148, 151, 137, 210, 136, 211, 153,
    261, 169, 185, 167, 209, 226, 164, 208, 182, 224, 152, 181, 180, 201, 227, 262, 197, 183, 198, 217,
    196, 225, 212, 168, 199, 233, 263, 243, 214, 228, 265, 213, 229, 230, 184, 240, 200, 264, 249, 215,
    241, 245, 216, 231, 247, 242, 244, 232, 248, 246,
)


UP, DOWN, ACROSS_Y, ACROSS_X = 0, 1, 2, 3
LEFT, RIGHT, PIECE = 0, 1, 2


class Product:
    def __init__(self, left, right, first, tall, route):
        self.left, self.right, self.first, self.tall, self.route = left, right, first, tall, route


SUMMED = -1


def weight_grad_kernel(products, left_count, *refs):
    count = len(products)
    refs = list(refs)

    def take(number):
        taken = refs[:number]
        del refs[:number]
        return taken

    lefts, rights = take(left_count), take(count - 3)
    left_far, right_far = take(FAR_LEFTS), take(len(FAR_RIGHTS))
    (
        order,
        held_at,
        grad_rows,
        pairs,
        lone,
        attn_sum,
        log_norm,
        bias_lines,
        in_bucket,
        resid_in,
        gain_one,
        resid_grad,
        gains,
    ) = take(13)
    weights = take(10)
    wholes, (vec_out, input_grad, encoder_grad, kv_both) = take(count - 1), take(4)
    kv_at = [product.left for product in products].index(SUMMED)
    wholes.insert(kv_at, kv_both.at[0])
    left_all, left_t = take(left_count), take(left_count)
    right_all, away, came, held, line_in = (take(count) for _ in range(5))
    rights += take(3)
    grad_packed, grad_landed, back_packed, back_landed, lines = take(5)
    attention_scratch = take(12)
    vec_in, vec_sums, vec_landed, weight_buffer, normed_grad = take(5)
    (
        left_send,
        left_own,
        left_recv,
        right_send,
        right_own,
        right_recv,
        pair_send,
        pair_recv,
        line_send,
        line_recv,
        out_send,
        out_recv,
        own_sem,
        vec_send,
        vec_recv,
        all_send,
        all_recv,
        all_own,
        kv_sem,
        weight_sem,
    ) = refs
    me, core = lax.axis_index("ctx"), lax.axis_index("wsh")
    peers = lax.axis_size("ctx")
    tokens = lefts[0].shape[0]
    x, y, z = lax.rem(me, 2), lax.rem(me // 2, 2), me // 4

    barrier = pltpu.get_barrier_semaphore()
    for step in range(1, peers):
        pl.semaphore_signal(
            barrier, inc=1, device_id=(lax.rem(me + step, peers), core), device_id_type=MESH
        )
    pl.semaphore_signal(barrier, inc=1, device_id=(me, 1 - core), device_id_type=MESH)
    for head in range(peers):
        cols = slice(head * HEAD_DIM, (head + 1) * HEAD_DIM)
        grad_packed[head] = jnp.concatenate(
            [grad_rows[:BLOCK, cols], grad_rows[BLOCK:, cols]], axis=1
        )
    pl.semaphore_wait(barrier, peers)

    def place(zz, yy, xx):
        return zz * 4 + yy * 2 + xx

    targets = {
        UP: place(lax.rem(z + 1, 4), y, x),
        DOWN: place(lax.rem(z + 3, 4), y, x),
        ACROSS_Y: place(z, 1 - y, x),
        ACROSS_X: place(z, y, 1 - x),
    }
    finish = []

    def remote(src, dst, send_sem, recv_sem, ctx, side):
        return pltpu.make_async_remote_copy(
            src_ref=src,
            dst_ref=dst,
            send_sem=send_sem,
            recv_sem=recv_sem,
            device_id=(ctx, side),
            device_id_type=MESH,
        )

    def launch(copy, only=None):
        if only is None:
            copy.start()
        else:
            pl.when(only)(copy.start)

    def arrived(ref, sem):
        remote(ref, ref, own_sem.at[0], sem, me, 1 - core).wait_recv()

    def left_here(ref, sem):
        finish.append(lambda: remote(ref, ref, sem, own_sem.at[0], me, 1 - core).wait_send())

    def lanes(ref, at, width):
        return ref.at[:, pl.ds(pl.multiple_of(at * width, 128), width)]

    def rows(ref, at, height):
        return ref.at[pl.ds(pl.multiple_of(at * height, 16), height)]

    def slot(ref, index):
        return ref.at[pl.ds(index * tokens, tokens)]

    def axes(product):
        along_x, along_y = (x, ACROSS_X), (y, ACROSS_Y)
        return (along_x, along_y) if product.first == BIT_X else (along_y, along_x)

    left_axis = {product.left: product for product in products}

    def local(src, dst, sem):
        copy = pltpu.make_async_copy(src, dst, sem)
        copy.start()
        return copy

    def send_left(at):
        half = left_all[at].shape[1]
        for index, ref in enumerate((lefts[at], left_far[at])):
            local(lanes(ref, core, half), slot(left_all[at], index), left_own.at[at])
            launch(remote(lanes(ref, 1 - core, half), slot(left_all[at], 2 + index), left_send.at[at], left_recv.at[at], me, 1 - core))
        left_here(left_all[at].at[: 2 * tokens], left_send.at[at])
        return left_all[at].at[: 2 * tokens], left_own.at[at]

    def send_right(at):
        (mine, way), _ = axes(products[at])
        half = right_all[at].shape[1]
        send_sem, recv_sem = right_send.at[at], right_recv.at[at]
        own, others = lanes(rights[at], mine, half), lanes(rights[at], 1 - mine, half)
        if products[at].left == SUMMED:
            launch(remote(others, right_all[at], send_sem, recv_sem.at[0], targets[way], core))
            left_here(right_all[at], send_sem)
            return None
        copies = [local(own, slot(right_all[at], 0), right_own.at[at])]
        launch(remote(own, slot(right_all[at], 2), send_sem, recv_sem.at[1], me, 1 - core))
        if at in FAR_RIGHTS:
            far = right_far[FAR_RIGHTS.index(at)]
            copies.append(local(far, slot(right_all[at], 1), right_own.at[at]))
            launch(remote(far, slot(right_all[at], 3), send_sem, recv_sem.at[2], me, 1 - core))
            left_here(right_all[at].at[: 2 * tokens], send_sem)
        else:
            launch(remote(others, slot(right_all[at], 1), send_sem, recv_sem.at[0], targets[way], core))
            left_here(right_all[at].at[: 3 * tokens], send_sem)
        return right_all[at].at[: len(copies) * tokens], right_own.at[at]

    def to_all(which, source, target):
        for step in range(1, peers):
            peer = lax.rem(me + step, peers)
            launch(remote(source.at[peer], target.at[me], all_send.at[which], all_recv.at[which], peer, core))
        own = local(source.at[me], target.at[me], all_own.at[which])
        left_here(source.at[1:], all_send.at[which])

        def wait():
            own.wait()
            arrived(target.at[1:], all_recv.at[which])

        return wait

    seen = set()
    owns = {}

    def send_operands(some):
        for at in some:
            left = products[at].left
            if left not in seen and left != SUMMED:
                seen.add(left)
                owns[LEFT, left] = send_left(left)
            owns[RIGHT, at] = send_right(at)

    def own_slots(key):
        ref, sem = owns[key]
        pltpu.make_async_copy(ref, ref, sem).wait()

    def vector_step(step):
        if step == 0:
            source, ctx, side = vec_in.at[1 - core], me, 1 - core
        else:
            source, ctx, side = vec_sums.at[step - 1], me ^ (1 << (step - 1)), core
        launch(remote(source, vec_landed.at[step], vec_send.at[step], vec_recv.at[step], ctx, side))
        left_here(source, vec_send.at[step])

    def vector_add(step):
        arrived(vec_landed.at[step], vec_recv.at[step])
        total = (vec_sums[step - 1] if step else vec_in[core]) + vec_landed[step]
        if step < 4:
            vec_sums[step] = total
            vector_step(step + 1)
        else:
            vec_out[...] = total

    def pass_on(at):
        if products[at].left == SUMMED or at in FAR_RIGHTS:
            return
        arrived(slot(right_all[at], 1), right_recv.at[at, 0])
        launch(remote(slot(right_all[at], 1), slot(right_all[at], 3), right_send.at[at], right_recv.at[at, 2], me, 1 - core))

    def multiply(at, out, half):
        product = products[at]
        left, right = left_t[product.left], right_all[at]
        height, width = out.shape
        step = 256 if height <= 256 else 128 if height % 256 else 256
        if product.tall:
            columns = pl.ds(pl.multiple_of(half * width, 128), width)

            def strip(index, carry):
                band = pl.ds(pl.multiple_of(index * 176, 16), 176)
                out[band, :] = plain_dot(left[band, :], right[:, columns]).astype(BF16)
                return carry

            lax.fori_loop(0, height // 176, strip, 0)
        else:
            band = pl.ds(pl.multiple_of(half * height, 16), height)

            def strip(index, carry):
                columns = pl.ds(pl.multiple_of(index * 256, 128), 256)
                out[:, columns] = plain_dot(left[band, :], right[:, columns]).astype(BF16)
                return carry

            lax.fori_loop(0, width // 256, strip, 0)
            if width % 256:
                out[:, width - 128 :] = plain_dot(left[band, :], right[:, width - 128 :]).astype(BF16)

    turned = set()

    def product_away(at):
        left = products[at].left
        _, (mine, way) = axes(products[at])
        if left == SUMMED:
            (first_mine, _), _ = axes(products[at])
            arrived(right_all[at], right_recv.at[at, 0])
            height = held[at].shape[0]
            for out, half in ((away[at], 1 - mine), (held[at], mine)):
                own = lanes(rows(rights[at], half, height), first_mine, held[at].shape[1])
                out[...] = (own[...].astype(F32) + rows(right_all[at], half, height)[...].astype(F32)).astype(BF16)
            launch(remote(away[at], came[at], pair_send.at[at], pair_recv.at[at], targets[way], core))
            left_here(away[at], pair_send.at[at])
            return
        if left not in turned:
            turned.add(left)
            arrived(left_all[left].at[2 * tokens :], left_recv.at[left])
            own_slots((LEFT, left))
            height = left_t[left].shape[0]

            def turn(index, carry):
                band = pl.ds(pl.multiple_of(index * 128, 128), 128)
                left_t[left][band, :] = jnp.transpose(left_all[left][:, band], (1, 0))
                return carry

            lax.fori_loop(0, height // 128, turn, 0)
        arrived(slot(right_all[at], 2), right_recv.at[at, 1])
        arrived(slot(right_all[at], 3), right_recv.at[at, 2])
        own_slots((RIGHT, at))
        multiply(at, away[at], 1 - mine)
        launch(remote(away[at], came[at], pair_send.at[at], pair_recv.at[at], targets[way], core))
        left_here(away[at], pair_send.at[at])
        multiply(at, held[at], mine)

    def add(into, more):
        into[...] = (into[...].astype(F32) + more[...].astype(F32)).astype(BF16)

    def add_pair(at):
        arrived(came[at], pair_recv.at[at])
        add(held[at], came[at])

    def line_step(at, step):
        height = held[at].shape[0] // 4
        for side, behind, chunk, way in (
            (0, z, lax.rem(z + 3 - step, 4), UP),
            (1, 3 - z, lax.rem(z + step + 1, 4), DOWN),
        ):
            recv_sem = line_recv.at[at, side, lax.rem(chunk + 2, 3) if side == 0 else lax.rem(chunk, 3)]
            landing = rows(line_in[at], chunk + 1 - side, height)

            def land(landing=landing, chunk=chunk, recv_sem=recv_sem):
                arrived(landing, recv_sem)
                add(rows(held[at], chunk, height), landing)

            pl.when(jnp.logical_and(behind > 0, behind <= step))(land)
            if step < 3:
                launch(
                    remote(
                        rows(held[at], chunk, height),
                        landing,
                        line_send.at[at],
                        recv_sem,
                        targets[way],
                        core,
                    ),
                    only=behind <= step,
                )
        if step == 3:
            left_here(held[at].at[: 3 * height], line_send.at[at])

    def own_piece(at):
        return rows(held[at], z, held[at].shape[0] // 4)

    def window(at, where):
        product = products[at]
        height, width = held[at].shape
        height //= 4
        xx, yy, zz = lax.rem(where, 2), lax.rem(where // 2, 2), where // 4
        one, two = (xx, yy) if product.first == BIT_X else (yy, xx)
        row, column = (zz, one * 2 + two) if product.tall else (two * 4 + zz, one)
        return wholes[at].at[
            pl.ds(pl.multiple_of(row * height, 16), height),
            pl.ds(pl.multiple_of(column * width, 128), width),
        ]

    def send(at, where, way, arrival, only=None, own=False):
        launch(
            remote(
                own_piece(at) if own else window(at, where),
                window(at, where),
                out_send.at[at, min(way, ACROSS_Y)],
                out_recv.at[at, arrival],
                targets[way],
                core,
            ),
            only,
        )

    def arrive(at, where, arrival, only=None):
        def act():
            arrived(window(at, where), out_recv.at[at, arrival])

        if only is None:
            act()
        else:
            pl.when(only)(act)

    def quarters(at, number):
        return wholes[at].at[: wholes[at].shape[0] // 4 * number]

    def near(way, zz):
        return place(zz, 1 - y, x) if way == ACROSS_Y else place(zz, y, 1 - x)

    def opposite(zz):
        return place(zz, 1 - y, 1 - x)

    def from_line(apart):
        return (
            (z >= apart, lax.rem(z + 4 - apart, 4), UP, jnp.logical_and(z >= apart, z < 3)),
            (z + apart <= 3, lax.rem(z + apart, 4), DOWN, jnp.logical_and(z + apart <= 3, z > 0)),
        )

    def line_sent(at, piece_groups):
        for number in (1, 2, 3):
            for way, here in ((UP, z == number - 1), (DOWN, z == 4 - number)):
                ref, sem = piece_groups(number), out_send.at[at, way]
                finish.append(
                    functools.partial(
                        pl.when(here),
                        lambda ref=ref, sem=sem: remote(ref, ref, sem, own_sem.at[0], me, 1 - core).wait_send(),
                    )
                )

    def gather_step(at, step):
        z_first, second, third = products[at].route
        if step == 0:
            owns[PIECE, at] = local(own_piece(at), window(at, me), own_sem.at[at])
            if at != kv_at:
                finish.append(owns[PIECE, at].wait)
            if z_first:
                send(at, me, UP, z, z < 3, own=True)
                send(at, me, DOWN, z, z > 0, own=True)
                send(at, me, second, 4 + z, own=True)
                send(at, me, third, 8, own=True)
                left_here(quarters(at, 3), out_send.at[at, ACROSS_Y])
                line_sent(at, lambda number: held[at].at[: held[at].shape[0] // 4 * number])
            else:
                send(at, me, second, 0, own=True)
                send(at, me, third, 1, own=True)
                send(at, me, UP, 4 + z, z < 3, own=True)
                send(at, me, DOWN, 4 + z, z > 0, own=True)
                left_here(held[at].at[: held[at].shape[0] // 4 * 3], out_send.at[at, ACROSS_Y])
                line_sent(at, lambda number: quarters(at, number))
        elif z_first:
            if step <= 3:
                for there, zz, way, on in from_line(step):
                    where = place(zz, y, x)
                    arrive(at, where, zz, there)
                    send(at, where, way, zz, on)
                    send(at, where, second, 4 + zz, there)
                    send(at, where, third, 8, there)
            elif step <= 7:
                zz = z ^ (step - 4)
                where = near(second, zz)
                arrive(at, where, 4 + zz)
                send(at, where, third, 8)
            elif step == 8:
                arrived(quarters(at, 2), out_recv.at[at, 8])
        else:
            if step == 1:
                where = near(second, z)
                arrive(at, where, 0)
                send(at, where, third, 2)
                send(at, where, UP, 4 + z, z < 3)
                send(at, where, DOWN, 4 + z, z > 0)
            elif step == 2:
                for arrival, where in ((1, near(third, z)), (2, opposite(z))):
                    arrive(at, where, arrival)
                    send(at, where, UP, 4 + z, z < 3)
                    send(at, where, DOWN, 4 + z, z > 0)
            elif step <= 5:
                for there, zz, way, on in from_line(step - 2):
                    pl.when(there)(
                        functools.partial(arrived, quarters(at, 1), out_recv.at[at, 4 + zz])
                    )
                    for where in (place(zz, y, x), near(second, zz), near(third, zz), opposite(zz)):
                        send(at, where, way, 4 + zz, on)

    def load_weight(index):
        return pltpu.make_async_copy(
            weights[index], weight_buffer.at[index % 2], weight_sem.at[index % 2]
        )

    def input_gradient():
        load_weight(0).start()
        for index in range(6):
            load_weight(index + 1).start()
            load_weight(index).wait()
            columns = lanes(normed_grad, core if index < 3 else 1 - core, normed_grad.shape[1] // 2)
            term = dot_nt(rights[count - 3 + index % 3][...], weight_buffer[index % 2])
            if index % 3:
                columns[...] += term
            else:
                columns[...] = term
        width = resid_in.shape[1]
        cotan, values = normed_grad[...], resid_in[...].astype(F32)
        rate = lax.rsqrt(jnp.mean(values * values, axis=1, keepdims=True) + EPSILON)
        scaled = cotan * gain_one[...]
        slope = jnp.mean(scaled * values, axis=1, keepdims=True)
        back = rate * scaled - values * (rate * rate * rate) * slope
        input_grad[...] = (resid_grad[...] + back).astype(BF16)
        gain_grad = jnp.sum(cotan * values * rate, axis=0, keepdims=True)
        column = jnp.zeros((BUCKETS, 1), F32)
        for apart in range(lines.shape[0]):
            sums = lines[apart : apart + 1, :TILE]
            if apart + 1 < lines.shape[0]:
                sums = sums + lines[apart + 1 : apart + 2, TILE:]
            column = column + jnp.sum(in_bucket[apart] * sums, axis=1, keepdims=True)
        place_at = lax.broadcasted_iota(jnp.int32, (BUCKETS, 128), 1)
        table = jnp.where(place_at == me, column, 0.0)
        for half in range(2):
            for index in range(4):
                start = (4 * half + index) * 128
                vec_in[half, index : index + 1, :] = gain_grad[:, start : start + 128]
            vec_in[half, 4:16, :] = gains[half]
            vec_in[half, 16:, :] = table[half * (BUCKETS // 2) : (half + 1) * (BUCKETS // 2)]
        vector_step(0)

    def encoder_gradient():
        own = kv_both[0, pl.ds(pl.multiple_of(me * encoder_grad.shape[0], 16), encoder_grad.shape[0]), :]
        width = own.shape[1] // 2
        for side in (0, 1):
            terms = []
            for index in (6 + 2 * side, 7 + 2 * side):
                if index < 9:
                    load_weight(index + 1).start()
                load_weight(index).wait()
                part = slice((index % 2) * width, (index % 2 + 1) * width)
                terms.append(dot_nt(own[:, part], weight_buffer[index % 2]))
            columns = lanes(encoder_grad, core if side == 0 else 1 - core, width // 2)
            columns[...] = (terms[0] + terms[1]).astype(BF16)

    later = {}

    def grads_leave():
        later[0] = to_all(0, grad_packed, grad_landed)

    def attention():
        later[0]()
        attend_back(
            order, held_at, pairs, lone, grad_landed, attn_sum, log_norm, bias_lines, back_packed, lines,
            *attention_scratch,
        )
        later[1] = to_all(1, back_packed, back_landed)

    def grads_return():
        later[1]()
        dq_ref, dk_ref, dv_ref = rights[count - 3 :]
        for pair in range(peers // 2):
            cols = slice(pair * 2 * HEAD_DIM, (pair + 1) * 2 * HEAD_DIM)
            dq_ref[:, cols], dk_ref[:, cols] = unpack_pair(back_landed, pair, slice(0, 2 * BLOCK))
            first, second = unpack_pair(back_landed, pair, slice(2 * BLOCK, 3 * BLOCK))
            dv_ref[:BLOCK, cols] = first
            dv_ref[BLOCK:, cols] = second

    def kv_gathered():
        owns[PIECE, kv_at].wait()
        launch(remote(kv_both.at[0], kv_both.at[1], kv_sem.at[0], kv_sem.at[1], me, 1 - core))
        left_here(kv_both.at[0], kv_sem.at[0])
        encoder_gradient()

    single = [grads_leave, attention, grads_return, input_gradient]
    single += [functools.partial(vector_add, step) for step in range(5)] + [kv_gathered]
    for code in SCHEDULE:
        stage, at = divmod(code, 16)
        if stage == 0:
            send_operands([at])
        elif stage == 1:
            pass_on(at)
        elif stage == 2:
            product_away(at)
        elif stage == 3:
            add_pair(at)
            line_step(at, 0)
        elif stage < 7:
            line_step(at, stage - 3)
        elif stage < 16:
            gather_step(at, stage - 7)
        else:
            single[at]()

    arrived(kv_both.at[1], kv_sem.at[1])
    for each in finish:
        each()


def weight_grads(products, lefts, rights, left_far, right_far, others, weights):
    count, peers = len(products), lax.axis_size("ctx")
    tokens = lefts[0].shape[0]
    length = others[5].shape[1]
    kv_at = [product.left for product in products].index(SUMMED)
    kv_rows, kv_width = rights[kv_at].shape
    spans = length // TILE
    dma = pltpu.SemaphoreType.DMA
    vmem = pltpu.VMEM
    width = HEADS * HEAD_DIM
    halves = [left.shape[1] // 2 for left in lefts]
    widths = [right.shape[1] for right in rights] + [width] * 3
    helds = []
    for product, right in zip(products, widths):
        height = kv_rows if product.left == SUMMED else halves[product.left]
        helds.append((height, right // 4) if product.tall else (height // 2, right // 2))
    lands = [vmem(shape, BF16) for shape in helds]
    chunk = (peers, BLOCK, 2 * HEAD_DIM)
    chunks = (peers, 3 * BLOCK, 2 * HEAD_DIM)
    smem_spec = pl.BlockSpec(memory_space=pltpu.SMEM)
    return pl.pallas_call(
        functools.partial(weight_grad_kernel, products, len(lefts)),
        out_shape=[
            jax.ShapeDtypeStruct((halves[product.left], right), BF16)
            for product, right in zip(products, widths)
            if product.left != SUMMED
        ]
        + [
            jax.ShapeDtypeStruct((32, 128), F32),
            jax.ShapeDtypeStruct((tokens, width), BF16),
            jax.ShapeDtypeStruct((kv_rows // peers, width), BF16),
            jax.ShapeDtypeStruct((2, kv_rows, kv_width), BF16),
        ],
        in_specs=[any_spec()] * len(lefts)
        + [vmem_spec() if product.left == SUMMED else any_spec() for product in products[: len(rights)]]
        + [any_spec()] * (len(left_far) + len(right_far))
        + [smem_spec] * 2
        + [vmem_spec()] * (len(others) - 2)
        + [any_spec()] * len(weights),
        out_specs=[any_spec()] * (count - 1) + [vmem_spec()] * 4,
        scratch_shapes=[vmem((4 * tokens, half), BF16) for half in halves]
        + [vmem((half, 4 * tokens), BF16) for half in halves]
        + [
            vmem((kv_rows if product.left == SUMMED else 4 * tokens, right // 2), BF16)
            for product, right in zip(products, widths)
        ]
        + lands * 3
        + [vmem((5 * height // 4, width_held), BF16) for height, width_held in helds]
        + [vmem((tokens, width), BF16)] * 3
        + [vmem(chunk, BF16), vmem(chunk, BF16), vmem(chunks, BF16), vmem(chunks, BF16)]
        + [vmem((spans, 2 * TILE), F32)]
        + [vmem((length, HEAD_DIM), BF16)] * 4
        + [vmem((HEAD_DIM, length), BF16)]
        + [vmem((spans, TILE, TILE), F32)] * 2
        + [vmem((length, HEAD_DIM), F32)] * 3
        + [vmem((1, length), F32), vmem((HEAD_DIM, length), F32)]
        + [
            vmem((2, 32, 128), F32),
            vmem((4, 32, 128), F32),
            vmem((5, 32, 128), F32),
            vmem((2,) + weights[0].shape, BF16),
            vmem((tokens, width), F32),
        ]
        + [
            dma((len(lefts),)),
            dma((len(lefts),)),
            dma((len(lefts),)),
            dma((count,)),
            dma((count,)),
            dma((count, 3)),
            dma((count,)),
            dma((count,)),
            dma((count,)),
            dma((count, 2, 3)),
            dma((count, 3)),
            dma((count, 9)),
            dma((count,)),
            dma((5,)),
            dma((5,)),
            dma((2,)),
            dma((2,)),
            dma((2,)),
            dma((2,)),
            dma((2,)),
        ],
        compiler_params=pltpu.CompilerParams(
            collective_id=5, has_side_effects=True, vmem_limit_bytes=60 * MIB
        ),
        name="weight_grads",
    )(*lefts, *rights, *left_far, *right_far, *others, *weights)


def on_device_by_heads(
    inputs,
    encoder,
    cotangent,
    block_order,
    bucket_of,
    self_gain,
    query_weight,
    key_weight,
    value_weight,
    out_weight,
    bias_table,
    cross_gain,
    cross_query,
    cross_key,
    cross_value,
    cross_out,
    mlp_gain,
    gate_weight,
    up_weight,
    down_weight,
):
    blocks = block_order.shape[0]
    block_ids = jnp.arange(blocks, dtype=jnp.int32)
    held_at = jnp.sum(
        jnp.where(block_order[None, :] == block_ids[:, None], block_ids[None, :], 0), axis=1
    )
    bucket_ids = jnp.arange(BUCKETS, dtype=jnp.int32)[None, :, None]
    bucket_tiles = (bucket_of.reshape(-1, 1, TILE) == bucket_ids).astype(F32)
    row = jnp.arange(8, dtype=jnp.int32)[:, None]
    small = jnp.where(
        row == 0, self_gain[None], jnp.where(row == 1, cross_gain[None], mlp_gain[None])
    ).astype(F32)
    table = jnp.pad(bias_table.astype(F32), ((0, 0), (0, 128 - HEADS)))
    sources = Weights(
        query=query_weight,
        key=key_weight,
        value=value_weight,
        out=out_weight,
        cross_key=cross_key,
        cross_value=cross_value,
        cross_query=cross_query,
        cross_out=cross_out,
        gate=gate_weight,
        up=up_weight,
        down=down_weight,
    )
    made, far, lent = layer(
        inputs[0], cotangent[0], encoder[0], small, table, bucket_tiles, held_at, block_order, sources
    )

    z_then_yx, z_then_xy, yx_then_z, xy_then_z = (
        (True, ACROSS_Y, ACROSS_X),
        (True, ACROSS_X, ACROSS_Y),
        (False, ACROSS_Y, ACROSS_X),
        (False, ACROSS_X, ACROSS_Y),
    )
    lefts = (
        made.normed_three, made.hidden, made.cross_mixed, made.normed_two, made.attended, made.normed_one
    )
    products = (
        Product(0, made.gate_grad, BIT_Y, False, z_then_yx),
        Product(1, cotangent[0], BIT_X, True, z_then_yx),
        Product(0, made.up_grad, BIT_Y, False, z_then_xy),
        Product(SUMMED, made.kv_part, BIT_Y, False, yx_then_z),
        Product(2, made.branch_two, BIT_X, False, z_then_xy),
        Product(3, made.cross_q_grad, BIT_X, False, z_then_xy),
        Product(4, made.branch_one, BIT_Y, False, z_then_xy),
        Product(5, None, BIT_X, False, yx_then_z),
        Product(5, None, BIT_X, False, yx_then_z),
        Product(5, None, BIT_X, False, z_then_yx),
    )
    *wholes, totals, input_grad, encoder_grad, cross_kv_both = weight_grads(
        products,
        lefts,
        [product.right for product in products[:7]],
        far[:FAR_LEFTS],
        far[FAR_LEFTS:],
        [
            block_order,
            held_at,
            made.dattn,
            made.pairs,
            made.lone,
            made.attn_sum,
            made.log_norm,
            made.bias_lines,
            bucket_tiles,
            inputs[0],
            made.gain_one,
            made.resid_grad,
            made.gain_grads,
        ],
        [query_weight, key_weight, value_weight, *lent[:3], cross_key, cross_value, *lent[3:]],
    )
    head_width = HEADS * HEAD_DIM
    cross_kv_rows = cross_kv_both.reshape(-1, 2 * head_width)
    sum_cross_key = left_contract(made.encoder_both, cross_kv_rows[:, :head_width])
    sum_cross_value = left_contract(made.encoder_both, cross_kv_rows[:, head_width:])
    (
        sum_gate,
        sum_down,
        sum_up,
        sum_cross_out,
        sum_cross_query,
        sum_out,
        sum_query,
        sum_key,
        sum_value,
    ) = (member.astype(F32) for member in wholes)
    sum_gain_one, sum_gain_two, sum_gain_three = (
        totals[4 * at : 4 * at + 4].reshape(-1) for at in range(3)
    )
    sum_table = totals[16:, :HEADS]
    return (
        made.result[None],
        input_grad[None],
        encoder_grad[None],
        sum_gain_one,
        sum_query,
        sum_key,
        sum_value,
        sum_out,
        sum_table,
        sum_gain_two,
        sum_cross_query,
        sum_cross_key,
        sum_cross_value,
        sum_cross_out,
        sum_gain_three,
        sum_gate,
        sum_up,
        sum_down,
    )


def solution(mesh):
    by_heads = mesh.shape["ctx"] == HEADS and mesh.shape["wsh"] == 2
    return jax.shard_map(
        on_device_by_heads if by_heads else on_device,
        mesh=mesh,
        in_specs=(
            P("wsh", "ctx", None),
            P("wsh", "ctx", None),
            P("wsh", "ctx", None),
            P(),
            P(),
            P("wsh"),
            P("wsh", None),
            P("wsh", None),
            P("wsh", None),
            P("wsh", None),
            P("wsh", None),
            P("wsh"),
            P("wsh", None),
            P("wsh", None),
            P("wsh", None),
            P("wsh", None),
            P("wsh"),
            P("wsh", None),
            P("wsh", None),
            P("wsh", None),
        ),
        out_specs=(
            P("wsh", "ctx", None),
            P("wsh", "ctx", None),
            P("wsh", "ctx", None),
            P("wsh"),
            P("wsh", None),
            P("wsh", None),
            P("wsh", None),
            P("wsh", None),
            P("wsh", None),
            P("wsh"),
            P("wsh", None),
            P("wsh", None),
            P("wsh", None),
            P("wsh", None),
            P("wsh"),
            P("wsh", None),
            P("wsh", None),
            P("wsh", None),
        ),
        check_vma=False,
    )
```

```python
import functools
from typing import Any, NamedTuple

import jax
import jax.numpy as jnp
from jax import lax
from jax.experimental import pallas as pl
from jax.experimental.pallas import tpu as pltpu
from jax.sharding import PartitionSpec as P

HEADS = 16
HEAD_DIM = 64
BUCKETS = 32


EPSILON = 1e-06
NEG_BIG = -1e30


def rms_norm(values, gain):
    return values * lax.rsqrt(jnp.mean(values * values, axis=-1, keepdims=True) + EPSILON) * gain


def plain_dot(left, right):
    return jnp.dot(left, right, preferred_element_type=jnp.float32)


def left_contract(left, right):
    return lax.dot_general(
        left, right, (((0,), (0,)), ((), ())), preferred_element_type=jnp.float32
    )


def right_contract(left, right):
    return lax.dot_general(
        left, right, (((1,), (1,)), ((), ())), preferred_element_type=jnp.float32
    )


def gelu_product(gate_vals, up_vals):
    return jax.nn.gelu(gate_vals, approximate=True) * up_vals


def norm_back(values, gain, cotan):
    normed, pullback = jax.vjp(rms_norm, values, gain)
    return pullback(cotan)


def lookup_positions(block_order, first_row, row_count, block_len):
    token_ids = first_row + jnp.arange(row_count, dtype=jnp.int32)
    block_ids = token_ids // block_len
    matches = block_ids[:, None] == jnp.arange(block_order.shape[0], dtype=jnp.int32)[None, :]
    starts = jnp.sum(jnp.where(matches, block_order[None, :], 0), axis=1)
    return starts * block_len + token_ids % block_len


def fold_groups(step_fn, carried, pieces, shard_rows):
    piece_rows = pieces[0].shape[0]
    shards = max(1, piece_rows // shard_rows)
    group_limit = max(1, 1152 // shard_rows)
    group_size = max(
        (divisor for divisor in range(1, min(shards, group_limit) + 1) if shards % divisor == 0)
    )
    group_rows = group_size * shard_rows

    def group_step(group_idx, inner_state):
        sub_pieces = tuple(
            (
                lax.dynamic_slice_in_dim(member, group_idx * group_rows, group_rows, 0)
                for member in pieces
            )
        )
        return step_fn(inner_state, sub_pieces, group_idx * group_rows)

    return lax.fori_loop(0, shards // group_size, group_step, carried)


def on_device(
    inputs,
    encoder,
    cotangent,
    block_order,
    bucket_of,
    self_gain,
    query_weight,
    key_weight,
    value_weight,
    out_weight,
    bias_table,
    cross_gain,
    cross_query,
    cross_key,
    cross_value,
    cross_out,
    mlp_gain,
    gate_weight,
    up_weight,
    down_weight,
):
    (
        gain_one,
        query_full,
        key_full,
        value_full,
        out_full,
        bias_rows,
        gain_two,
        cross_query_full,
        cross_key_full,
        cross_value_full,
        cross_out_full,
        gain_three,
        gate_full,
        up_full,
        down_full,
    ) = (
        lax.all_gather(self_gain, "wsh", axis=0, tiled=True),
        lax.all_gather(query_weight, "wsh", axis=0, tiled=True),
        lax.all_gather(key_weight, "wsh", axis=0, tiled=True),
        lax.all_gather(value_weight, "wsh", axis=0, tiled=True),
        lax.all_gather(out_weight, "wsh", axis=0, tiled=True),
        lax.all_gather(bias_table, "wsh", axis=0, tiled=True),
        lax.all_gather(cross_gain, "wsh", axis=0, tiled=True),
        lax.all_gather(cross_query, "wsh", axis=0, tiled=True),
        lax.all_gather(cross_key, "wsh", axis=0, tiled=True),
        lax.all_gather(cross_value, "wsh", axis=0, tiled=True),
        lax.all_gather(cross_out, "wsh", axis=0, tiled=True),
        lax.all_gather(mlp_gain, "wsh", axis=0, tiled=True),
        lax.all_gather(gate_weight, "wsh", axis=0, tiled=True),
        lax.all_gather(up_weight, "wsh", axis=0, tiled=True),
        lax.all_gather(down_weight, "wsh", axis=0, tiled=True),
    )
    gain_one = gain_one.astype(jnp.float32)
    gain_two = gain_two.astype(jnp.float32)
    gain_three = gain_three.astype(jnp.float32)
    resid_in = inputs[0].astype(jnp.float32)
    tokens = resid_in.shape[0]
    block_len = tokens // 2
    head_width = HEADS * HEAD_DIM
    total_rows = tokens * lax.axis_size("ctx")
    own_pos = lookup_positions(block_order, lax.axis_index("ctx") * tokens, tokens, block_len)
    bucket_ids = jnp.arange(BUCKETS, dtype=jnp.int32)
    boundaries = jnp.sum((bucket_of[None, :] < bucket_ids[1:, None]).astype(jnp.int32), axis=1)

    def bucket_indicator_of(clipped):
        bucket = jnp.sum((clipped[None] >= boundaries[:, None, None]).astype(jnp.int32), axis=0)
        return (bucket[None] == bucket_ids[:, None, None]).astype(jnp.bfloat16)

    def query_key_logits(query_heads, key_heads, query_pos, key_pos):
        logits = jnp.einsum(
            "qhe,khe->hqk", query_heads, key_heads, preferred_element_type=jnp.float32
        )
        offset = query_pos[:, None] - key_pos[None, :]
        clipped = jnp.maximum(offset, 0)
        indicator = bucket_indicator_of(clipped)
        rel_bias = jnp.einsum(
            "ouw,om->muw", indicator, bias_rows, preferred_element_type=jnp.float32
        )
        allowed = (offset >= 0)[None]
        return (jnp.where(allowed, logits + rel_bias, NEG_BIG), allowed, indicator)

    normed_one = rms_norm(resid_in, gain_one).astype(jnp.bfloat16)
    query_heads = (
        plain_dot(normed_one, query_full).astype(jnp.bfloat16).reshape(tokens, HEADS, HEAD_DIM)
    )
    key_heads = (
        plain_dot(normed_one, key_full).astype(jnp.bfloat16).reshape(tokens, HEADS, HEAD_DIM)
    )
    value_heads = (
        plain_dot(normed_one, value_full).astype(jnp.bfloat16).reshape(tokens, HEADS, HEAD_DIM)
    )

    def norm_step(carried, pieces, first_row):
        running_max, running_sum = carried
        key_pos = lookup_positions(block_order, first_row, pieces[0].shape[0], block_len)
        logits, allowed, indicator = query_key_logits(query_heads, pieces[0], own_pos, key_pos)
        new_max = jnp.maximum(running_max, jnp.max(logits, axis=-1))
        kept = jnp.where(allowed, jnp.exp(logits - new_max[..., None]), 0.0)
        return (new_max, running_sum * jnp.exp(running_max - new_max) + jnp.sum(kept, axis=-1))

    start_state = (
        jnp.full((HEADS, tokens), NEG_BIG, jnp.float32),
        jnp.zeros((HEADS, tokens), jnp.float32),
    )
    running_max, running_sum = fold_groups(
        norm_step, start_state, (lax.all_gather(key_heads, "ctx", axis=0, tiled=True),), tokens
    )
    log_norm = running_max + jnp.log(running_sum)

    def output_step(carried, pieces, first_row):
        key_pos = lookup_positions(block_order, first_row, pieces[0].shape[0], block_len)
        logits, allowed, indicator = query_key_logits(query_heads, pieces[0], own_pos, key_pos)
        attn_probs = jnp.exp(logits - log_norm[..., None]).astype(jnp.bfloat16)
        return carried + jnp.einsum(
            "hqk,khe->qhe", attn_probs, pieces[1], preferred_element_type=jnp.float32
        )

    zero_heads = jnp.zeros((tokens, HEADS, HEAD_DIM), jnp.float32)
    attn_sum = fold_groups(
        output_step,
        zero_heads,
        (
            lax.all_gather(key_heads, "ctx", axis=0, tiled=True),
            lax.all_gather(value_heads, "ctx", axis=0, tiled=True),
        ),
        tokens,
    )
    attended = attn_sum.reshape(tokens, head_width).astype(jnp.bfloat16)
    after_self = resid_in + plain_dot(attended, out_full)
    normed_two = rms_norm(after_self, gain_two).astype(jnp.bfloat16)
    cross_q_heads = (
        plain_dot(normed_two, cross_query_full)
        .astype(jnp.bfloat16)
        .reshape(tokens, HEADS, HEAD_DIM)
    )
    encoder_rows = encoder[0]
    encoder_key_rows, cross_values = (
        lax.all_gather(
            plain_dot(encoder_rows, cross_key_full).astype(jnp.bfloat16), "ctx", axis=0, tiled=True
        ),
        lax.all_gather(
            plain_dot(encoder_rows, cross_value_full).astype(jnp.bfloat16),
            "ctx",
            axis=0,
            tiled=True,
        ),
    )
    cross_k_heads = encoder_key_rows.reshape(encoder_key_rows.shape[0], HEADS, HEAD_DIM)
    cross_v_heads = cross_values.reshape(cross_values.shape[0], HEADS, HEAD_DIM)
    cross_logits = jnp.einsum(
        "qhe,khe->hqk", cross_q_heads, cross_k_heads, preferred_element_type=jnp.float32
    )
    cross_exact = jnp.exp(cross_logits - jax.nn.logsumexp(cross_logits, axis=-1, keepdims=True))
    cross_probs = cross_exact.astype(jnp.bfloat16)
    cross_mixed = (
        jnp.einsum("hqk,khe->qhe", cross_probs, cross_v_heads, preferred_element_type=jnp.float32)
        .reshape(tokens, head_width)
        .astype(jnp.bfloat16)
    )
    after_cross = after_self + plain_dot(cross_mixed, cross_out_full)
    normed_three = rms_norm(after_cross, gain_three).astype(jnp.bfloat16)
    gate_act = plain_dot(normed_three, gate_full)
    up_act = plain_dot(normed_three, up_full)
    hidden_float, mlp_pull = jax.vjp(gelu_product, gate_act, up_act)
    hidden = hidden_float.astype(jnp.bfloat16)
    result = after_cross + plain_dot(hidden, down_full)
    resid_grad = cotangent[0].astype(jnp.float32)
    branch_three = resid_grad.astype(jnp.bfloat16)
    down_grad = left_contract(hidden, branch_three)
    hidden_state_gradient = right_contract(branch_three, down_full)
    gate_grad, up_grad = mlp_pull(hidden_state_gradient)
    gate_grad = gate_grad.astype(jnp.bfloat16)
    up_grad = up_grad.astype(jnp.bfloat16)
    gate_w_grad = left_contract(normed_three, gate_grad)
    up_w_grad = left_contract(normed_three, up_grad)
    normed_three_grad = right_contract(gate_grad, gate_full) + right_contract(up_grad, up_full)
    part_grad, gain_three_grad = norm_back(after_cross, gain_three, normed_three_grad)
    after_cross_grad = resid_grad + part_grad
    branch_two = after_cross_grad.astype(jnp.bfloat16)
    cross_out_grad = left_contract(cross_mixed, branch_two)
    mix_grad = (
        right_contract(branch_two, cross_out_full)
        .astype(jnp.bfloat16)
        .reshape(tokens, HEADS, HEAD_DIM)
    )
    cross_score_grad = jnp.einsum(
        "qhe,khe->hqk", mix_grad, cross_v_heads, preferred_element_type=jnp.float32
    )
    cross_delta = jnp.sum(cross_exact * cross_score_grad, axis=-1, keepdims=True)
    cross_dlogits = (cross_exact * (cross_score_grad - cross_delta)).astype(jnp.bfloat16)
    cross_q_grad = (
        jnp.einsum("hqk,khe->qhe", cross_dlogits, cross_k_heads, preferred_element_type=jnp.float32)
        .reshape(tokens, head_width)
        .astype(jnp.bfloat16)
    )
    cross_k_part = jnp.einsum(
        "hqk,qhe->khe", cross_dlogits, cross_q_heads, preferred_element_type=jnp.float32
    ).reshape(-1, head_width)
    cross_v_part = jnp.einsum(
        "hqk,qhe->khe", cross_probs, mix_grad, preferred_element_type=jnp.float32
    ).reshape(-1, head_width)
    cross_k_grad, cross_v_grad = (
        lax.psum_scatter(cross_k_part, "ctx", scatter_dimension=0, tiled=True),
        lax.psum_scatter(cross_v_part, "ctx", scatter_dimension=0, tiled=True),
    )
    cross_k_grad = cross_k_grad.astype(jnp.bfloat16)
    cross_v_grad = cross_v_grad.astype(jnp.bfloat16)
    cross_query_grad = left_contract(normed_two, cross_q_grad)
    cross_key_grad = left_contract(encoder_rows, cross_k_grad)
    cross_value_grad = left_contract(encoder_rows, cross_v_grad)
    encoder_grad = (
        right_contract(cross_k_grad, cross_key_full)
        + right_contract(cross_v_grad, cross_value_full)
    ).astype(jnp.bfloat16)
    normed_two_grad = right_contract(cross_q_grad, cross_query_full)
    part_grad, gain_two_grad = norm_back(after_self, gain_two, normed_two_grad)
    after_self_grad = after_cross_grad + part_grad
    branch_one = after_self_grad.astype(jnp.bfloat16)
    out_w_grad = left_contract(attended, branch_one)
    dattn_heads = (
        right_contract(branch_one, out_full).astype(jnp.bfloat16).reshape(tokens, HEADS, HEAD_DIM)
    )
    row_delta = jnp.einsum("qhe,qhe->hq", dattn_heads.astype(jnp.float32), attn_sum)

    def block_grads(
        query_side, grad_side, norm_side, delta_side, query_pos, key_side, value_side, key_pos
    ):
        logits, allowed, indicator = query_key_logits(query_side, key_side, query_pos, key_pos)
        exact = jnp.exp(logits - norm_side[..., None])
        score_grad = jnp.einsum(
            "qhe,khe->hqk", grad_side, value_side, preferred_element_type=jnp.float32
        )
        logits_gradient = (exact * (score_grad - delta_side[..., None])).astype(jnp.bfloat16)
        grad_query = jnp.einsum(
            "hqk,khe->qhe", logits_gradient, key_side, preferred_element_type=jnp.float32
        )
        grad_key = jnp.einsum(
            "hqk,qhe->khe", logits_gradient, query_side, preferred_element_type=jnp.float32
        )
        grad_value = jnp.einsum(
            "hqk,qhe->khe",
            exact.astype(jnp.bfloat16),
            grad_side,
            preferred_element_type=jnp.float32,
        )
        bucket_table_gradient = jnp.einsum(
            "ouw,muw->om", indicator, logits_gradient, preferred_element_type=jnp.float32
        )
        return (grad_query, grad_key, grad_value, bucket_table_gradient)

    zero_table = jnp.zeros((BUCKETS, HEADS), jnp.float32)
    full_zero = jnp.zeros((total_rows, HEADS, HEAD_DIM), jnp.float32)

    def key_grad_step(carried, pieces, first_row):
        query_total, table_total, key_total, value_total = carried
        key_pos = lookup_positions(block_order, first_row, pieces[0].shape[0], block_len)
        grad_query, grad_key, grad_value, bucket_table_gradient = block_grads(
            query_heads, dattn_heads, log_norm, row_delta, own_pos, pieces[0], pieces[1], key_pos
        )
        key_total = lax.dynamic_update_slice_in_dim(key_total, grad_key, first_row, 0)
        value_total = lax.dynamic_update_slice_in_dim(value_total, grad_value, first_row, 0)
        return (
            query_total + grad_query,
            table_total + bucket_table_gradient,
            key_total,
            value_total,
        )

    query_sum, table_grad, key_partial, value_partial = fold_groups(
        key_grad_step,
        (zero_heads, zero_table, full_zero, full_zero),
        (
            lax.all_gather(key_heads, "ctx", axis=0, tiled=True),
            lax.all_gather(value_heads, "ctx", axis=0, tiled=True),
        ),
        tokens,
    )
    key_sum, value_accumulated = (
        lax.psum_scatter(key_partial, "ctx", scatter_dimension=0, tiled=True),
        lax.psum_scatter(value_partial, "ctx", scatter_dimension=0, tiled=True),
    )
    query_grad = query_sum.reshape(tokens, head_width).astype(jnp.bfloat16)
    key_grad = key_sum.reshape(tokens, head_width).astype(jnp.bfloat16)
    value_grad = value_accumulated.reshape(tokens, head_width).astype(jnp.bfloat16)
    query_w_grad = left_contract(normed_one, query_grad)
    key_w_grad = left_contract(normed_one, key_grad)
    value_w_grad = left_contract(normed_one, value_grad)
    normed_one_grad = (
        right_contract(query_grad, query_full)
        + right_contract(key_grad, key_full)
        + right_contract(value_grad, value_full)
    )
    part_grad, gain_one_grad = norm_back(resid_in, gain_one, normed_one_grad)
    input_grad = (after_self_grad + part_grad).astype(jnp.bfloat16)
    (
        sum_gain_one,
        sum_query,
        sum_key,
        sum_value,
        sum_out,
        sum_table,
        sum_gain_two,
        sum_cross_query,
        sum_cross_key,
        sum_cross_value,
        sum_cross_out,
        sum_gain_three,
        sum_gate,
        sum_up,
        sum_down,
    ) = (
        lax.psum_scatter(
            gain_one_grad.astype(jnp.bfloat16), "wsh", scatter_dimension=0, tiled=True
        ).astype(jnp.float32),
        lax.psum_scatter(
            query_w_grad.astype(jnp.bfloat16), "wsh", scatter_dimension=0, tiled=True
        ).astype(jnp.float32),
        lax.psum_scatter(
            key_w_grad.astype(jnp.bfloat16), "wsh", scatter_dimension=0, tiled=True
        ).astype(jnp.float32),
        lax.psum_scatter(
            value_w_grad.astype(jnp.bfloat16), "wsh", scatter_dimension=0, tiled=True
        ).astype(jnp.float32),
        lax.psum_scatter(
            out_w_grad.astype(jnp.bfloat16), "wsh", scatter_dimension=0, tiled=True
        ).astype(jnp.float32),
        lax.psum_scatter(
            table_grad.astype(jnp.bfloat16), "wsh", scatter_dimension=0, tiled=True
        ).astype(jnp.float32),
        lax.psum_scatter(
            gain_two_grad.astype(jnp.bfloat16), "wsh", scatter_dimension=0, tiled=True
        ).astype(jnp.float32),
        lax.psum_scatter(
            cross_query_grad.astype(jnp.bfloat16), "wsh", scatter_dimension=0, tiled=True
        ).astype(jnp.float32),
        lax.psum_scatter(
            cross_key_grad.astype(jnp.bfloat16), "wsh", scatter_dimension=0, tiled=True
        ).astype(jnp.float32),
        lax.psum_scatter(
            cross_value_grad.astype(jnp.bfloat16), "wsh", scatter_dimension=0, tiled=True
        ).astype(jnp.float32),
        lax.psum_scatter(
            cross_out_grad.astype(jnp.bfloat16), "wsh", scatter_dimension=0, tiled=True
        ).astype(jnp.float32),
        lax.psum_scatter(
            gain_three_grad.astype(jnp.bfloat16), "wsh", scatter_dimension=0, tiled=True
        ).astype(jnp.float32),
        lax.psum_scatter(
            gate_w_grad.astype(jnp.bfloat16), "wsh", scatter_dimension=0, tiled=True
        ).astype(jnp.float32),
        lax.psum_scatter(
            up_w_grad.astype(jnp.bfloat16), "wsh", scatter_dimension=0, tiled=True
        ).astype(jnp.float32),
        lax.psum_scatter(
            down_grad.astype(jnp.bfloat16), "wsh", scatter_dimension=0, tiled=True
        ).astype(jnp.float32),
    )
    total_grads = lax.psum(
        (
            sum_gain_one,
            sum_query,
            sum_key,
            sum_value,
            sum_out,
            sum_table,
            sum_gain_two,
            sum_cross_query,
            sum_cross_key,
            sum_cross_value,
            sum_cross_out,
            sum_gain_three,
            sum_gate,
            sum_up,
            sum_down,
        ),
        "ctx",
    )
    return (result.astype(jnp.bfloat16)[None], input_grad[None], encoder_grad[None]) + tuple(
        total_grads
    )


F32 = jnp.float32
BF16 = jnp.bfloat16
MESH = pl.DeviceIdType.MESH
TILE = 256
BLOCK = 64
MIB = 2**20
GELU_RATE, GELU_CUBE = 0.7978845608, 0.044715


def dot_nt(left, right):
    return lax.dot_general(left, right, (((1,), (1,)), ((), ())), preferred_element_type=F32)


def vmem_spec():
    return pl.BlockSpec(memory_space=pltpu.VMEM)


def any_spec():
    return pl.BlockSpec(memory_space=pl.ANY)


def unpack_pair(landed, pair, rows):
    left, right = landed[2 * pair, rows, :], landed[2 * pair + 1, rows, :]
    return (
        jnp.concatenate([left[:, :HEAD_DIM], right[:, :HEAD_DIM]], axis=1),
        jnp.concatenate([left[:, HEAD_DIM:], right[:, HEAD_DIM:]], axis=1),
    )


def place_tiles(bias_lines, tiles):
    for apart in range(tiles.shape[0]):
        line = jnp.broadcast_to(bias_lines[apart : apart + 1, :], (TILE, 2 * TILE))
        tiles[apart] = pltpu.roll(line, 0, 1, stride=1, stride_axis=0)[:, :TILE]


def attend_scratch(blocks):
    length = blocks * BLOCK
    vmem = pltpu.VMEM
    return [
        vmem((length, HEAD_DIM), BF16),
        vmem((length, HEAD_DIM), BF16),
        vmem((HEAD_DIM, length), BF16),
        vmem((length // TILE, TILE, TILE), F32),
        vmem((length, HEAD_DIM), F32),
        vmem((length, HEAD_DIM), F32),
    ]


def attend(order, held_at, pairs, lone, bias_lines, out_ref, sum_ref, norm_ref, q_s, k_s, vt_s, tiles, staged, o_s):
    blocks = held_at.shape[0]
    spans = blocks * BLOCK // TILE

    def in_order(into):
        for block in range(blocks):
            at = slice(block * BLOCK, (block + 1) * BLOCK)
            into[at, :] = staged[pl.ds(held_at[block] * BLOCK, BLOCK), :].astype(into.dtype)

    for side, into in ((0, q_s), (1, k_s)):
        for device in range(blocks // 2):
            at = slice(2 * device * BLOCK, 2 * (device + 1) * BLOCK)
            staged[at, :] = pairs[device, :, side * HEAD_DIM : (side + 1) * HEAD_DIM].astype(F32)
        in_order(into)
    for stored in range(blocks):
        at = slice(stored * BLOCK, (stored + 1) * BLOCK)
        cols = slice(stored % 2 * HEAD_DIM, (stored % 2 + 1) * HEAD_DIM)
        staged[at, :] = lone[stored // 2, :, cols].astype(F32)
    in_order(o_s)
    vt_s[...] = jnp.transpose(o_s[...], (1, 0)).astype(BF16)
    place_tiles(bias_lines, tiles)
    for i in range(spans):
        at_i = slice(i * TILE, (i + 1) * TILE)
        queries = q_s[at_i, :]
        scores = [
            dot_nt(k_s[j * TILE : (j + 1) * TILE, :], queries) + tiles[i - j] for j in range(i + 1)
        ]
        top = functools.reduce(
            jnp.maximum, [jnp.max(each, axis=0, keepdims=True) for each in scores]
        )
        total = jnp.zeros((1, TILE), F32)
        mixed = jnp.zeros((HEAD_DIM, TILE), F32)
        for j in range(i + 1):
            weights = jnp.exp(scores[j] - top)
            total = total + jnp.sum(weights, axis=0, keepdims=True)
            mixed = mixed + plain_dot(
                vt_s[:, j * TILE : (j + 1) * TILE], weights.astype(BF16)
            )
        norm_ref[0:1, at_i] = top + jnp.log(total)
        sum_ref[:, at_i] = mixed / total
    o_s[...] = jnp.transpose(sum_ref[...], (1, 0))
    for stored in range(blocks):
        cols = slice(stored % 2 * HEAD_DIM, (stored % 2 + 1) * HEAD_DIM)
        out_ref[stored // 2, :, cols] = o_s[pl.ds(order[stored] * BLOCK, BLOCK), :].astype(BF16)


def attend_back(
    order, held_at, pairs, lone, grad_landed, sums, norm, bias_lines, out_ref, lines_ref,
    q_s, k_s, v_s, do_s, kt_s, tiles, by_offset, dq_s, dk_s, dv_s, delta_s, dqt_s,
):
    blocks = order.shape[0]
    spans = blocks * BLOCK // TILE
    def stored_rows(stored):
        return slice(stored * BLOCK, (stored + 1) * BLOCK), stored // 2, slice(
            stored % 2 * HEAD_DIM, (stored % 2 + 1) * HEAD_DIM
        )

    def in_order(into, staged):
        for block in range(blocks):
            at = slice(block * BLOCK, (block + 1) * BLOCK)
            into[at, :] = staged[pl.ds(held_at[block] * BLOCK, BLOCK), :].astype(BF16)

    for stored in range(blocks):
        at, device, cols = stored_rows(stored)
        pair = pairs[device, stored % 2 * BLOCK : (stored % 2 + 1) * BLOCK, :].astype(F32)
        dq_s[at, :] = pair[:, :HEAD_DIM]
        dk_s[at, :] = pair[:, HEAD_DIM:]
        dv_s[at, :] = lone[device, :, cols].astype(F32)
    in_order(q_s, dq_s)
    in_order(k_s, dk_s)
    in_order(v_s, dv_s)
    for stored in range(blocks):
        at, device, cols = stored_rows(stored)
        dq_s[at, :] = grad_landed[device, :, cols].astype(F32)
    in_order(do_s, dq_s)
    place_tiles(bias_lines, tiles)
    kt_s[...] = jnp.transpose(k_s[...].astype(F32), (1, 0)).astype(BF16)
    grad_t = jnp.transpose(do_s[...].astype(F32), (1, 0))
    delta_s[...] = jnp.sum(grad_t * sums[...], axis=0, keepdims=True)
    by_offset[...] = jnp.zeros_like(by_offset)
    dk_s[...] = jnp.zeros_like(dk_s)
    dv_s[...] = jnp.zeros_like(dv_s)
    for i in range(spans):
        at_i = slice(i * TILE, (i + 1) * TILE)
        queries, grads = q_s[at_i, :], do_s[at_i, :]
        norm_i, delta_i = norm[0:1, at_i], delta_s[0:1, at_i]
        dqt = jnp.zeros((HEAD_DIM, TILE), F32)
        for j in range(i + 1):
            at_j = slice(j * TILE, (j + 1) * TILE)
            exact = jnp.exp(dot_nt(k_s[at_j, :], queries) + tiles[i - j] - norm_i)
            dscore = exact * (dot_nt(v_s[at_j, :], grads) - delta_i)
            by_offset[i - j] += dscore
            rounded = dscore.astype(BF16)
            dv_s[at_j, :] += plain_dot(exact.astype(BF16), grads)
            dk_s[at_j, :] += plain_dot(rounded, queries)
            dqt = dqt + plain_dot(kt_s[:, at_j], rounded)
        dqt_s[:, at_i] = dqt
    dq_s[...] = jnp.transpose(dqt_s[...], (1, 0))
    for stored in range(blocks):
        device, half = stored // 2, stored % 2
        at = pl.ds(order[stored] * BLOCK, BLOCK)
        rows = slice(half * BLOCK, (half + 1) * BLOCK)
        cols = slice(half * HEAD_DIM, (half + 1) * HEAD_DIM)
        out_ref[device, rows, :HEAD_DIM] = dq_s[at, :].astype(BF16)
        out_ref[device, rows, HEAD_DIM:] = dk_s[at, :].astype(BF16)
        out_ref[device, 2 * BLOCK :, cols] = dv_s[at, :].astype(BF16)
    for apart in range(spans):
        folded = jnp.zeros((8, 2 * TILE), F32)
        for group in range(TILE // 8):
            rows = by_offset[apart, 8 * group : 8 * group + 8, :]
            wide = jnp.concatenate([rows, jnp.zeros((8, TILE), F32)], axis=1)
            folded = folded + (pltpu.roll(wide, 2 * TILE - 8 * group, 1) if group else wide)
        line = folded[0:1]
        for row in range(1, 8):
            line = line + pltpu.roll(folded[row : row + 1], 2 * TILE - row, 1)
        lines_ref[apart : apart + 1, :] = line


class Weights(NamedTuple):
    query: Any
    key: Any
    value: Any
    out: Any
    cross_key: Any
    cross_value: Any
    cross_query: Any
    cross_out: Any
    gate: Any
    up: Any
    down: Any


W = Weights(*range(11))
LENT = (W.query, W.key, W.value, W.cross_key, W.cross_value)


class Made(NamedTuple):
    normed_one: Any
    pairs: Any
    lone: Any
    attn_sum: Any
    log_norm: Any
    attended: Any
    normed_two: Any
    cross_mixed: Any
    normed_three: Any
    hidden: Any
    gate_grad: Any
    up_grad: Any
    branch_two: Any
    cross_q_grad: Any
    branch_one: Any
    dattn: Any
    kv_part: Any
    resid_grad: Any
    result: Any
    gain_grads: Any
    gain_one: Any
    bias_lines: Any
    encoder_both: Any


M = Made(*range(23))


class Far(NamedTuple):
    normed_three: Any
    hidden: Any
    cross_mixed: Any
    normed_two: Any
    attended: Any
    normed_one: Any
    gate: Any
    branch_three: Any
    up: Any
    branch_two: Any


BIT_X, BIT_Y = 0, 1
FAR = Far(*range(10))
FAR_AXIS = Far(
    normed_three=BIT_Y,
    hidden=BIT_X,
    cross_mixed=BIT_X,
    normed_two=BIT_X,
    attended=BIT_Y,
    normed_one=BIT_X,
    gate=BIT_Y,
    branch_three=BIT_X,
    up=BIT_Y,
    branch_two=BIT_X,
)


class Scratch(NamedTuple):
    small_far: Any
    table_far: Any
    pairs_out: Any
    lone_out: Any
    encoder_all: Any
    mixed_out: Any
    mixed_in: Any
    cross_keys: Any
    cross_values: Any
    cross_queries: Any
    cross_exact: Any
    after_self: Any
    after_cross: Any
    gate_act: Any
    up_act: Any
    mix_grad: Any


def norm_parts(values):
    return lax.rsqrt(jnp.mean(values * values, axis=1, keepdims=True) + EPSILON)


def norm_backward(values, gain, cotan):
    rate = norm_parts(values)
    scaled = cotan * gain
    slope = jnp.mean(scaled * values, axis=1, keepdims=True)
    return (
        rate * scaled - values * (rate * rate * rate) * slope,
        jnp.sum(cotan * values * rate, axis=0, keepdims=True),
    )


def layer_kernel(tokens_in, cotangent, encoder, small, table, in_bucket, held_at, order, *refs):
    refs = list(refs)

    def take(number):
        taken = refs[:number]
        del refs[:number]
        return taken

    sources = take(len(W))
    saved = Made(*take(len(Made._fields)))
    far = Far(*take(len(Far._fields)))
    lent = take(len(LENT))
    weights = take(len(W))
    own = Scratch(*take(len(Scratch._fields)))
    out = Made(*take(len(Made._fields)))
    (save_sem, own_sem, weight_own, weight_send, weight_recv, lent_send, lent_recv, far_send, far_recv, all_own, all_send, all_recv) = refs
    me, core = lax.axis_index("ctx"), lax.axis_index("wsh")
    peers = lax.axis_size("ctx")
    x, y = lax.rem(me, 2), lax.rem(me // 2, 2)
    tokens, width = tokens_in.shape
    finish = []

    barrier = pltpu.get_barrier_semaphore()
    for step in range(1, peers):
        pl.semaphore_signal(
            barrier, inc=1, device_id=(lax.rem(me + step, peers), core), device_id_type=MESH
        )
    pl.semaphore_signal(barrier, inc=1, device_id=(me, 1 - core), device_id_type=MESH)

    def half_rows(ref, side):
        half = ref.shape[0] // 2
        return ref.at[pl.ds(pl.multiple_of(side * half, 16), half)]

    def remote(src, dst, send_sem, recv_sem, ctx, side):
        return pltpu.make_async_remote_copy(
            src_ref=src,
            dst_ref=dst,
            send_sem=send_sem,
            recv_sem=recv_sem,
            device_id=(ctx, side),
            device_id_type=MESH,
        )

    def arrived(ref, sem):
        remote(ref, ref, own_sem, sem, me, 1 - core).wait_recv()

    def launch(src, dst, send_sem, recv_sem, ctx, side):
        remote(src, dst, send_sem, recv_sem, ctx, side).start()
        finish.append(lambda: remote(src, src, send_sem, own_sem, me, 1 - core).wait_send())

    def to_pair(at, source, halves=False):
        bit = FAR_AXIS[at]
        if halves:
            half = source.shape[1] // 2
            source = source.at[:, pl.ds(pl.multiple_of((1 - (x, y)[bit]) * half, 128), half)]
        launch(source, far[at], far_send.at[at], far_recv.at[at], me ^ (1 << bit), core)

    def save(*made):
        for at in made:
            copy = pltpu.make_async_copy(out[at], saved[at], save_sem.at[at])
            copy.start()
            finish.append(copy.wait)

    small_sem, table_sem, encoder_sem = (len(Far._fields) + at for at in range(3))
    local = {}
    for at in W:
        local[at] = pltpu.make_async_copy(sources[at], half_rows(weights[at], core), weight_own.at[at])
        local[at].start()
    pl.semaphore_wait(barrier, peers)

    launch(small, own.small_far, far_send.at[small_sem], far_recv.at[small_sem], me, 1 - core)
    launch(table, own.table_far, far_send.at[table_sem], far_recv.at[table_sem], me, 1 - core)
    for at in W:
        launch(sources[at], half_rows(weights[at], core), weight_send.at[at], weight_recv.at[at], me, 1 - core)
    for at, source in enumerate(LENT):
        launch(sources[source], lent[at], lent_send.at[at], lent_recv.at[at], me, 1 - core)

    def weight(at):
        if at in local:
            local.pop(at).wait()
            arrived(half_rows(weights[at], 1 - core), weight_recv.at[at])
        return weights[at]

    def to_all(which, source, target, spread=True):
        for step in range(1, peers):
            peer = lax.rem(me + step, peers)
            remote(
                source.at[peer] if spread else source, target.at[me], all_send.at[which], all_recv.at[which], peer, core
            ).start()
        kept = pltpu.make_async_copy(source.at[me] if spread else source, target.at[me], all_own.at[which])
        kept.start()
        finish.append(lambda: remote(target.at[1:], target.at[1:], all_send.at[which], own_sem, me, 1 - core).wait_send())

        def wait():
            kept.wait()
            arrived(target.at[1:], all_recv.at[which])

        return wait

    def tiles_of(total):
        return [slice(at, at + 256) for at in range(0, total, 256)]

    def times(values, name):
        ref = weight(name)
        return jnp.concatenate([plain_dot(values, ref[:, cols]) for cols in tiles_of(ref.shape[1])], axis=1)

    def times_back(values, name):
        ref = weight(name)
        return jnp.concatenate([dot_nt(values, ref[cols, :]) for cols in tiles_of(ref.shape[0])], axis=1)

    def head(at):
        return slice(at * HEAD_DIM, (at + 1) * HEAD_DIM)

    def head_pair(at):
        return slice(2 * at * HEAD_DIM, 2 * (at + 1) * HEAD_DIM)

    arrived(own.small_far, far_recv.at[small_sem])
    arrived(own.table_far, far_recv.at[table_sem])

    def both(mine, others, axis):
        first = jnp.where(core == 0, mine, others)
        second = jnp.where(core == 0, others, mine)
        return jnp.concatenate([first, second], axis=axis)

    gain_one, gain_two, gain_three = (
        both(small[at : at + 1, :], own.small_far[at : at + 1, :], 1) for at in range(3)
    )
    out.gain_one[...] = gain_one
    whole_table = both(table[...], own.table_far[...], 0)
    lane = lax.broadcasted_iota(jnp.int32, whole_table.shape, 1)
    column = jnp.sum(jnp.where(lane == me, whole_table, 0.0), axis=1, keepdims=True)
    spans = in_bucket.shape[0]
    for apart in range(spans):
        line = jnp.sum(in_bucket[apart] * column, axis=0, keepdims=True)
        out.bias_lines[apart : apart + 1, :TILE] = line
        if apart + 1 < spans:
            out.bias_lines[apart + 1 : apart + 2, TILE:] = line
    out.bias_lines[0:1, TILE:] = jnp.full((1, TILE), NEG_BIG, F32)

    resid = tokens_in[...].astype(F32)
    out.normed_one[...] = (resid * norm_parts(resid) * gain_one).astype(BF16)
    normed_one = out.normed_one[...]
    queries = times(normed_one, W.query).astype(BF16)
    keys = times(normed_one, W.key).astype(BF16)
    for at in range(peers):
        own.pairs_out[at] = jnp.concatenate([queries[:, head(at)], keys[:, head(at)]], axis=1)
    pairs_arrival = to_all(0, own.pairs_out, out.pairs)
    values = times(normed_one, W.value).astype(BF16)
    for at in range(peers):
        own.lone_out[at] = jnp.concatenate(
            [values[:BLOCK, head(at)], values[BLOCK:, head(at)]], axis=1
        )
    lone_arrival = to_all(1, own.lone_out, out.lone)
    encoder_arrival = to_all(2, encoder, own.encoder_all, spread=False)
    save(M.normed_one, M.gain_one, M.bias_lines)
    place_bias = out.bias_lines
    pairs_arrival()
    lone_arrival()
    to_pair(FAR.branch_three, cotangent, halves=True)
    to_pair(FAR.normed_one, out.normed_one)
    pl.run_scoped(
        functools.partial(
            attend, order, held_at, out.pairs, out.lone, place_bias, own.mixed_out, out.attn_sum, out.log_norm
        ),
        *attend_scratch(held_at.shape[0]),
    )
    mixed_arrival = to_all(3, own.mixed_out, own.mixed_in)
    save(M.pairs, M.lone, M.attn_sum, M.log_norm)

    encoder_arrival()
    encoder_rows = jnp.concatenate([own.encoder_all[at] for at in range(peers)], axis=0)
    half = width // 2
    count = encoder_rows.shape[0]
    out.encoder_both[:count, :] = jnp.where(core == 0, encoder_rows[:, :half], encoder_rows[:, half:])
    own.cross_keys[...] = times(encoder_rows, W.cross_key).astype(BF16)
    own.cross_values[...] = times(encoder_rows, W.cross_value).astype(BF16)

    mixed_arrival()
    for pair in range(peers // 2):
        first, second = unpack_pair(own.mixed_in, pair, slice(0, BLOCK))
        out.attended[:BLOCK, head_pair(pair)] = first
        out.attended[BLOCK:, head_pair(pair)] = second
    to_pair(FAR.attended, out.attended)
    save(M.attended)
    own.after_self[...] = tokens_in[...].astype(F32) + times(out.attended[...], W.out)
    after_self = own.after_self[...]
    out.normed_two[...] = (after_self * norm_parts(after_self) * gain_two).astype(BF16)
    to_pair(FAR.normed_two, out.normed_two)
    save(M.normed_two)
    own.cross_queries[...] = times(out.normed_two[...], W.cross_query).astype(BF16)

    for pair in range(peers // 2):
        mixed = []
        for at in (2 * pair, 2 * pair + 1):
            scores = dot_nt(own.cross_keys[:, head(at)], own.cross_queries[:, head(at)])
            weight_t = jnp.exp(scores - jnp.max(scores, axis=0, keepdims=True))
            exact = weight_t / jnp.sum(weight_t, axis=0, keepdims=True)
            own.cross_exact[at] = exact
            mixed.append(left_contract(exact.astype(BF16), own.cross_values[:, head(at)]))
        out.cross_mixed[:, head_pair(pair)] = jnp.concatenate(mixed, axis=1).astype(BF16)
    to_pair(FAR.cross_mixed, out.cross_mixed)
    save(M.cross_mixed)
    own.after_cross[...] = own.after_self[...] + times(out.cross_mixed[...], W.cross_out)
    after_cross = own.after_cross[...]
    out.normed_three[...] = (after_cross * norm_parts(after_cross) * gain_three).astype(BF16)
    to_pair(FAR.normed_three, out.normed_three)
    save(M.normed_three)

    normed_three = out.normed_three[...]
    gate, up, down = weight(W.gate), weight(W.up), weight(W.down)
    for cols in tiles_of(gate.shape[1]):
        gate_act = plain_dot(normed_three, gate[:, cols])
        up_act = plain_dot(normed_three, up[:, cols])
        own.gate_act[:, cols] = gate_act
        own.up_act[:, cols] = up_act
        curve = jnp.tanh(GELU_RATE * (gate_act + GELU_CUBE * gate_act * gate_act * gate_act))
        out.hidden[:, cols] = (0.5 * gate_act * (1.0 + curve) * up_act).astype(BF16)
    to_pair(FAR.hidden, out.hidden)
    save(M.hidden)
    out.result[...] = (own.after_cross[...] + times(out.hidden[...], W.down)).astype(BF16)

    branch_three = cotangent[...]
    half = down.shape[0] // 2
    for side in (1 - y, y):
        for start in range(0, half, 256):
            size = min(256, half - start)
            cols = pl.ds(pl.multiple_of(side * half + start, 128), size)
            hidden_grad = dot_nt(branch_three, down[pl.ds(pl.multiple_of(side * half + start, 128), size), :])
            gate_act, up_act = own.gate_act[:, cols], own.up_act[:, cols]
            square = gate_act * gate_act
            curve = jnp.tanh(GELU_RATE * (gate_act + GELU_CUBE * gate_act * square))
            rise = 0.5 * (1.0 + curve) + 0.5 * gate_act * (1.0 - curve * curve) * (
                GELU_RATE * (1.0 + 3.0 * GELU_CUBE * square)
            )
            out.gate_grad[:, cols] = (hidden_grad * up_act * rise).astype(BF16)
            out.up_grad[:, cols] = (hidden_grad * (0.5 * gate_act * (1.0 + curve))).astype(BF16)
        if side is not y:
            to_pair(FAR.gate, out.gate_grad, halves=True)
            to_pair(FAR.up, out.up_grad, halves=True)
    save(M.result, M.gate_grad, M.up_grad)
    normed_grad = times_back(out.gate_grad[...], W.gate) + times_back(out.up_grad[...], W.up)
    back, gain_three_grad = norm_backward(own.after_cross[...], gain_three, normed_grad)
    out.resid_grad[...] = cotangent[...].astype(F32) + back
    out.branch_two[...] = out.resid_grad[...].astype(BF16)

    to_pair(FAR.branch_two, out.branch_two, halves=True)
    save(M.branch_two)
    own.mix_grad[...] = times_back(out.branch_two[...], W.cross_out).astype(BF16)
    for pair in range(peers // 2):
        terms = []
        for at in (2 * pair, 2 * pair + 1):
            exact = own.cross_exact[at]
            grads = own.mix_grad[:, head(at)]
            score_grad = dot_nt(own.cross_values[:, head(at)], grads)
            slope = jnp.sum(exact * score_grad, axis=0, keepdims=True)
            rounded = (exact * (score_grad - slope)).astype(BF16)
            terms.append(
                (
                    left_contract(rounded, own.cross_keys[:, head(at)]),
                    plain_dot(rounded, own.cross_queries[:, head(at)]),
                    plain_dot(exact.astype(BF16), grads),
                )
            )
        cols = head_pair(pair)
        values_cols = slice(width + cols.start, width + cols.stop)
        for ref, into, at in ((out.cross_q_grad, cols, 0), (out.kv_part, cols, 1), (out.kv_part, values_cols, 2)):
            ref[:, into] = jnp.concatenate([terms[0][at], terms[1][at]], axis=1).astype(BF16)
    save(M.cross_q_grad, M.kv_part)
    normed_grad = times_back(out.cross_q_grad[...], W.cross_query)
    back, gain_two_grad = norm_backward(own.after_self[...], gain_two, normed_grad)
    out.resid_grad[...] += back
    out.branch_one[...] = out.resid_grad[...].astype(BF16)
    save(M.resid_grad, M.branch_one)
    out.dattn[...] = times_back(out.branch_one[...], W.out).astype(BF16)
    save(M.dattn)

    for half in range(2):
        for index in range(4):
            cols = slice((4 * half + index) * 128, (4 * half + index + 1) * 128)
            out.gain_grads[half, index : index + 1, :] = gain_two_grad[:, cols]
            out.gain_grads[half, 4 + index : 5 + index, :] = gain_three_grad[:, cols]
        out.gain_grads[half, 8:, :] = jnp.zeros((4, 128), F32)
    save(M.gain_grads)

    other_half = pl.ds(pl.multiple_of((1 - core) * (width // 2), 128), width // 2)
    for at in range(peers):
        rows_at = own.encoder_all.shape[1]
        remote(
            own.encoder_all.at[at, :, other_half],
            out.encoder_both.at[count + at * rows_at : count + (at + 1) * rows_at],
            far_send.at[encoder_sem], far_recv.at[encoder_sem], me, 1 - core,
        ).start()
    arrived(out.encoder_both.at[count:], far_recv.at[encoder_sem])
    save(M.encoder_both)
    finish.append(
        lambda: remote(
            out.encoder_both.at[count:], out.encoder_both.at[count:], far_send.at[encoder_sem], own_sem, me, 1 - core
        ).wait_send()
    )
    for at, ref in enumerate(far):
        arrived(ref, far_recv.at[at])
    for at, ref in enumerate(lent):
        arrived(ref, lent_recv.at[at])
    for each in finish:
        each()


def layer(tokens_in, cotangent, encoder, small, table, in_bucket, held_at, order, sources):
    peers = lax.axis_size("ctx")
    tokens, width = tokens_in.shape
    hidden = sources.gate.shape[1]
    blocks = held_at.shape[0]
    length = blocks * BLOCK
    rows = encoder.shape[0] * peers
    dma, vmem = pltpu.SemaphoreType.DMA, pltpu.VMEM

    def shaped(*shape):
        return jax.ShapeDtypeStruct(shape, BF16)

    def exact(*shape):
        return jax.ShapeDtypeStruct(shape, F32)

    square, wide, half_wide = shaped(tokens, width), shaped(tokens, hidden), shaped(tokens, hidden // 2)
    pairs, lone = (peers, 2 * BLOCK, 2 * HEAD_DIM), (peers, BLOCK, 2 * HEAD_DIM)
    outputs = Made(
        normed_one=square,
        pairs=shaped(*pairs),
        lone=shaped(*lone),
        attn_sum=exact(HEAD_DIM, length),
        log_norm=exact(1, length),
        attended=square,
        normed_two=square,
        cross_mixed=square,
        normed_three=square,
        hidden=wide,
        gate_grad=wide,
        up_grad=wide,
        branch_two=square,
        cross_q_grad=square,
        branch_one=square,
        dattn=square,
        kv_part=shaped(rows, 2 * width),
        resid_grad=exact(tokens, width),
        result=square,
        gain_grads=exact(2, 12, 128),
        gain_one=exact(1, width),
        bias_lines=exact(length // TILE, 2 * TILE),
        encoder_both=shaped(2 * rows, width // 2),
    )
    half_square = shaped(tokens, width // 2)
    fars = Far(
        normed_three=square,
        hidden=wide,
        cross_mixed=square,
        normed_two=square,
        attended=square,
        normed_one=square,
        gate=half_wide,
        branch_three=half_square,
        up=half_wide,
        branch_two=half_square,
    )
    buffers = Scratch(
        small_far=vmem(small.shape, F32),
        table_far=vmem(table.shape, F32),
        pairs_out=vmem(pairs, BF16),
        lone_out=vmem(lone, BF16),
        encoder_all=vmem((peers,) + encoder.shape, BF16),
        mixed_out=vmem(lone, BF16),
        mixed_in=vmem(lone, BF16),
        cross_keys=vmem((rows, width), BF16),
        cross_values=vmem((rows, width), BF16),
        cross_queries=vmem((tokens, width), BF16),
        cross_exact=vmem((HEADS, rows, tokens), F32),
        after_self=vmem((tokens, width), F32),
        after_cross=vmem((tokens, width), F32),
        gate_act=vmem((tokens, hidden), F32),
        up_act=vmem((tokens, hidden), F32),
        mix_grad=vmem((tokens, width), BF16),
    )
    smem_spec = pl.BlockSpec(memory_space=pltpu.SMEM)
    results = pl.pallas_call(
        layer_kernel,
        out_shape=[*outputs, *fars, *(shaped(*sources[at].shape) for at in LENT)],
        in_specs=[vmem_spec()] * 6 + [smem_spec] * 2 + [any_spec()] * len(W),
        out_specs=[any_spec()] * (len(outputs) + len(fars) + len(LENT)),
        scratch_shapes=[vmem((2 * each.shape[0], each.shape[1]), BF16) for each in sources]
        + list(buffers)
        + [vmem(each.shape, each.dtype) for each in outputs]
        + [
            dma((len(outputs),)),
            dma,
            dma((len(W),)),
            dma((len(W),)),
            dma((len(W),)),
            dma((len(LENT),)),
            dma((len(LENT),)),
            dma((len(fars) + 3,)),
            dma((len(fars) + 3,)),
            dma((4,)),
            dma((4,)),
            dma((4,)),
        ],
        compiler_params=pltpu.CompilerParams(
            collective_id=1, has_side_effects=True, vmem_limit_bytes=62 * MIB
        ),
        name="layer",
    )(tokens_in, cotangent, encoder, small, table, in_bucket, held_at, order, *sources)
    made, results = results[: len(outputs)], results[len(outputs) :]
    return Made(*made), Far(*results[: len(fars)]), results[len(fars) :]


FAR_LEFTS, FAR_RIGHTS = 6, (0, 1, 2, 4)
SCHEDULE = (
    0, 256, 5, 16, 32, 3, 2, 257, 1, 6, 18, 4, 48, 34, 21, 17, 19, 37, 22, 33,
    20, 64, 38, 53, 35, 80, 69, 50, 96, 112, 258, 66, 7, 36, 49, 8, 128, 51, 65, 144,
    23, 67, 82, 52, 160, 39, 81, 24, 259, 98, 68, 97, 113, 54, 40, 84, 9, 83, 55, 85,
    114, 70, 129, 71, 99, 101, 117, 115, 176, 25, 145, 87, 133, 56, 260, 86, 100, 161, 192, 72,
    103, 116, 131, 102, 118, 41, 119, 130, 134, 146, 147, 57, 88, 73, 149, 104, 163, 150, 165, 162,
    89, 179, 132, 135, 178, 194, 105, 177, 195, 166, 193, 121, 120, 148, 151, 137, 210, 136, 211, 153,
    261, 169, 185, 167, 209, 226, 164, 208, 182, 224, 152, 181, 180, 201, 227, 262, 197, 183, 198, 217,
    196, 225, 212, 168, 199, 233, 263, 243, 214, 228, 265, 213, 229, 230, 184, 240, 200, 264, 249, 215,
    241, 245, 216, 231, 247, 242, 244, 232, 248, 246,
)


UP, DOWN, ACROSS_Y, ACROSS_X = 0, 1, 2, 3
LEFT, RIGHT, PIECE = 0, 1, 2


class Product:
    def __init__(self, left, right, first, tall, route):
        self.left, self.right, self.first, self.tall, self.route = left, right, first, tall, route


SUMMED = -1


def weight_grad_kernel(products, left_count, *refs):
    count = len(products)
    refs = list(refs)

    def take(number):
        taken = refs[:number]
        del refs[:number]
        return taken

    lefts, rights = take(left_count), take(count - 3)
    left_far, right_far = take(FAR_LEFTS), take(len(FAR_RIGHTS))
    (
        order,
        held_at,
        grad_rows,
        pairs,
        lone,
        attn_sum,
        log_norm,
        bias_lines,
        in_bucket,
        resid_in,
        gain_one,
        resid_grad,
        gains,
    ) = take(13)
    weights = take(10)
    wholes, (vec_out, input_grad, encoder_grad, kv_both) = take(count - 1), take(4)
    kv_at = [product.left for product in products].index(SUMMED)
    wholes.insert(kv_at, kv_both.at[0])
    left_all, left_t = take(left_count), take(left_count)
    right_all, away, came, held, line_in = (take(count) for _ in range(5))
    rights += take(3)
    grad_packed, grad_landed, back_packed, back_landed, lines = take(5)
    attention_scratch = take(12)
    vec_in, vec_sums, vec_landed, weight_buffer, normed_grad = take(5)
    (
        left_send,
        left_own,
        left_recv,
        right_send,
        right_own,
        right_recv,
        pair_send,
        pair_recv,
        line_send,
        line_recv,
        out_send,
        out_recv,
        own_sem,
        vec_send,
        vec_recv,
        all_send,
        all_recv,
        all_own,
        kv_sem,
        weight_sem,
    ) = refs
    me, core = lax.axis_index("ctx"), lax.axis_index("wsh")
    peers = lax.axis_size("ctx")
    tokens = lefts[0].shape[0]
    x, y, z = lax.rem(me, 2), lax.rem(me // 2, 2), me // 4

    barrier = pltpu.get_barrier_semaphore()
    for step in range(1, peers):
        pl.semaphore_signal(
            barrier, inc=1, device_id=(lax.rem(me + step, peers), core), device_id_type=MESH
        )
    pl.semaphore_signal(barrier, inc=1, device_id=(me, 1 - core), device_id_type=MESH)
    for head in range(peers):
        cols = slice(head * HEAD_DIM, (head + 1) * HEAD_DIM)
        grad_packed[head] = jnp.concatenate(
            [grad_rows[:BLOCK, cols], grad_rows[BLOCK:, cols]], axis=1
        )
    pl.semaphore_wait(barrier, peers)

    def place(zz, yy, xx):
        return zz * 4 + yy * 2 + xx

    targets = {
        UP: place(lax.rem(z + 1, 4), y, x),
        DOWN: place(lax.rem(z + 3, 4), y, x),
        ACROSS_Y: place(z, 1 - y, x),
        ACROSS_X: place(z, y, 1 - x),
    }
    finish = []

    def remote(src, dst, send_sem, recv_sem, ctx, side):
        return pltpu.make_async_remote_copy(
            src_ref=src,
            dst_ref=dst,
            send_sem=send_sem,
            recv_sem=recv_sem,
            device_id=(ctx, side),
            device_id_type=MESH,
        )

    def launch(copy, only=None):
        if only is None:
            copy.start()
        else:
            pl.when(only)(copy.start)

    def arrived(ref, sem):
        remote(ref, ref, own_sem.at[0], sem, me, 1 - core).wait_recv()

    def left_here(ref, sem):
        finish.append(lambda: remote(ref, ref, sem, own_sem.at[0], me, 1 - core).wait_send())

    def lanes(ref, at, width):
        return ref.at[:, pl.ds(pl.multiple_of(at * width, 128), width)]

    def rows(ref, at, height):
        return ref.at[pl.ds(pl.multiple_of(at * height, 16), height)]

    def slot(ref, index):
        return ref.at[pl.ds(index * tokens, tokens)]

    def axes(product):
        along_x, along_y = (x, ACROSS_X), (y, ACROSS_Y)
        return (along_x, along_y) if product.first == BIT_X else (along_y, along_x)

    left_axis = {product.left: product for product in products}

    def local(src, dst, sem):
        copy = pltpu.make_async_copy(src, dst, sem)
        copy.start()
        return copy

    def send_left(at):
        half = left_all[at].shape[1]
        for index, ref in enumerate((lefts[at], left_far[at])):
            local(lanes(ref, core, half), slot(left_all[at], index), left_own.at[at])
            launch(remote(lanes(ref, 1 - core, half), slot(left_all[at], 2 + index), left_send.at[at], left_recv.at[at], me, 1 - core))
        left_here(left_all[at].at[: 2 * tokens], left_send.at[at])
        return left_all[at].at[: 2 * tokens], left_own.at[at]

    def send_right(at):
        (mine, way), _ = axes(products[at])
        half = right_all[at].shape[1]
        send_sem, recv_sem = right_send.at[at], right_recv.at[at]
        own, others = lanes(rights[at], mine, half), lanes(rights[at], 1 - mine, half)
        if products[at].left == SUMMED:
            launch(remote(others, right_all[at], send_sem, recv_sem.at[0], targets[way], core))
            left_here(right_all[at], send_sem)
            return None
        copies = [local(own, slot(right_all[at], 0), right_own.at[at])]
        launch(remote(own, slot(right_all[at], 2), send_sem, recv_sem.at[1], me, 1 - core))
        if at in FAR_RIGHTS:
            far = right_far[FAR_RIGHTS.index(at)]
            copies.append(local(far, slot(right_all[at], 1), right_own.at[at]))
            launch(remote(far, slot(right_all[at], 3), send_sem, recv_sem.at[2], me, 1 - core))
            left_here(right_all[at].at[: 2 * tokens], send_sem)
        else:
            launch(remote(others, slot(right_all[at], 1), send_sem, recv_sem.at[0], targets[way], core))
            left_here(right_all[at].at[: 3 * tokens], send_sem)
        return right_all[at].at[: len(copies) * tokens], right_own.at[at]

    def to_all(which, source, target):
        for step in range(1, peers):
            peer = lax.rem(me + step, peers)
            launch(remote(source.at[peer], target.at[me], all_send.at[which], all_recv.at[which], peer, core))
        own = local(source.at[me], target.at[me], all_own.at[which])
        left_here(source.at[1:], all_send.at[which])

        def wait():
            own.wait()
            arrived(target.at[1:], all_recv.at[which])

        return wait

    seen = set()
    owns = {}

    def send_operands(some):
        for at in some:
            left = products[at].left
            if left not in seen and left != SUMMED:
                seen.add(left)
                owns[LEFT, left] = send_left(left)
            owns[RIGHT, at] = send_right(at)

    def own_slots(key):
        ref, sem = owns[key]
        pltpu.make_async_copy(ref, ref, sem).wait()

    def vector_step(step):
        if step == 0:
            source, ctx, side = vec_in.at[1 - core], me, 1 - core
        else:
            source, ctx, side = vec_sums.at[step - 1], me ^ (1 << (step - 1)), core
        launch(remote(source, vec_landed.at[step], vec_send.at[step], vec_recv.at[step], ctx, side))
        left_here(source, vec_send.at[step])

    def vector_add(step):
        arrived(vec_landed.at[step], vec_recv.at[step])
        total = (vec_sums[step - 1] if step else vec_in[core]) + vec_landed[step]
        if step < 4:
            vec_sums[step] = total
            vector_step(step + 1)
        else:
            vec_out[...] = total

    def pass_on(at):
        if products[at].left == SUMMED or at in FAR_RIGHTS:
            return
        arrived(slot(right_all[at], 1), right_recv.at[at, 0])
        launch(remote(slot(right_all[at], 1), slot(right_all[at], 3), right_send.at[at], right_recv.at[at, 2], me, 1 - core))

    def multiply(at, out, half):
        product = products[at]
        left, right = left_t[product.left], right_all[at]
        height, width = out.shape
        step = 256 if height <= 256 else 128 if height % 256 else 256
        if product.tall:
            columns = pl.ds(pl.multiple_of(half * width, 128), width)

            def strip(index, carry):
                band = pl.ds(pl.multiple_of(index * 176, 16), 176)
                out[band, :] = plain_dot(left[band, :], right[:, columns]).astype(BF16)
                return carry

            lax.fori_loop(0, height // 176, strip, 0)
        else:
            band = pl.ds(pl.multiple_of(half * height, 16), height)

            def strip(index, carry):
                columns = pl.ds(pl.multiple_of(index * 256, 128), 256)
                out[:, columns] = plain_dot(left[band, :], right[:, columns]).astype(BF16)
                return carry

            lax.fori_loop(0, width // 256, strip, 0)
            if width % 256:
                out[:, width - 128 :] = plain_dot(left[band, :], right[:, width - 128 :]).astype(BF16)

    turned = set()

    def product_away(at):
        left = products[at].left
        _, (mine, way) = axes(products[at])
        if left == SUMMED:
            (first_mine, _), _ = axes(products[at])
            arrived(right_all[at], right_recv.at[at, 0])
            height = held[at].shape[0]
            for out, half in ((away[at], 1 - mine), (held[at], mine)):
                own = lanes(rows(rights[at], half, height), first_mine, held[at].shape[1])
                out[...] = (own[...].astype(F32) + rows(right_all[at], half, height)[...].astype(F32)).astype(BF16)
            launch(remote(away[at], came[at], pair_send.at[at], pair_recv.at[at], targets[way], core))
            left_here(away[at], pair_send.at[at])
            return
        if left not in turned:
            turned.add(left)
            arrived(left_all[left].at[2 * tokens :], left_recv.at[left])
            own_slots((LEFT, left))
            height = left_t[left].shape[0]

            def turn(index, carry):
                band = pl.ds(pl.multiple_of(index * 128, 128), 128)
                left_t[left][band, :] = jnp.transpose(left_all[left][:, band], (1, 0))
                return carry

            lax.fori_loop(0, height // 128, turn, 0)
        arrived(slot(right_all[at], 2), right_recv.at[at, 1])
        arrived(slot(right_all[at], 3), right_recv.at[at, 2])
        own_slots((RIGHT, at))
        multiply(at, away[at], 1 - mine)
        launch(remote(away[at], came[at], pair_send.at[at], pair_recv.at[at], targets[way], core))
        left_here(away[at], pair_send.at[at])
        multiply(at, held[at], mine)

    def add(into, more):
        into[...] = (into[...].astype(F32) + more[...].astype(F32)).astype(BF16)

    def add_pair(at):
        arrived(came[at], pair_recv.at[at])
        add(held[at], came[at])

    def line_step(at, step):
        height = held[at].shape[0] // 4
        for side, behind, chunk, way in (
            (0, z, lax.rem(z + 3 - step, 4), UP),
            (1, 3 - z, lax.rem(z + step + 1, 4), DOWN),
        ):
            recv_sem = line_recv.at[at, side, lax.rem(chunk + 2, 3) if side == 0 else lax.rem(chunk, 3)]
            landing = rows(line_in[at], chunk + 1 - side, height)

            def land(landing=landing, chunk=chunk, recv_sem=recv_sem):
                arrived(landing, recv_sem)
                add(rows(held[at], chunk, height), landing)

            pl.when(jnp.logical_and(behind > 0, behind <= step))(land)
            if step < 3:
                launch(
                    remote(
                        rows(held[at], chunk, height),
                        landing,
                        line_send.at[at],
                        recv_sem,
                        targets[way],
                        core,
                    ),
                    only=behind <= step,
                )
        if step == 3:
            left_here(held[at].at[: 3 * height], line_send.at[at])

    def own_piece(at):
        return rows(held[at], z, held[at].shape[0] // 4)

    def window(at, where):
        product = products[at]
        height, width = held[at].shape
        height //= 4
        xx, yy, zz = lax.rem(where, 2), lax.rem(where // 2, 2), where // 4
        one, two = (xx, yy) if product.first == BIT_X else (yy, xx)
        row, column = (zz, one * 2 + two) if product.tall else (two * 4 + zz, one)
        return wholes[at].at[
            pl.ds(pl.multiple_of(row * height, 16), height),
            pl.ds(pl.multiple_of(column * width, 128), width),
        ]

    def send(at, where, way, arrival, only=None, own=False):
        launch(
            remote(
                own_piece(at) if own else window(at, where),
                window(at, where),
                out_send.at[at, min(way, ACROSS_Y)],
                out_recv.at[at, arrival],
                targets[way],
                core,
            ),
            only,
        )

    def arrive(at, where, arrival, only=None):
        def act():
            arrived(window(at, where), out_recv.at[at, arrival])

        if only is None:
            act()
        else:
            pl.when(only)(act)

    def quarters(at, number):
        return wholes[at].at[: wholes[at].shape[0] // 4 * number]

    def near(way, zz):
        return place(zz, 1 - y, x) if way == ACROSS_Y else place(zz, y, 1 - x)

    def opposite(zz):
        return place(zz, 1 - y, 1 - x)

    def from_line(apart):
        return (
            (z >= apart, lax.rem(z + 4 - apart, 4), UP, jnp.logical_and(z >= apart, z < 3)),
            (z + apart <= 3, lax.rem(z + apart, 4), DOWN, jnp.logical_and(z + apart <= 3, z > 0)),
        )

    def line_sent(at, piece_groups):
        for number in (1, 2, 3):
            for way, here in ((UP, z == number - 1), (DOWN, z == 4 - number)):
                ref, sem = piece_groups(number), out_send.at[at, way]
                finish.append(
                    functools.partial(
                        pl.when(here),
                        lambda ref=ref, sem=sem: remote(ref, ref, sem, own_sem.at[0], me, 1 - core).wait_send(),
                    )
                )

    def gather_step(at, step):
        z_first, second, third = products[at].route
        if step == 0:
            owns[PIECE, at] = local(own_piece(at), window(at, me), own_sem.at[at])
            if at != kv_at:
                finish.append(owns[PIECE, at].wait)
            if z_first:
                send(at, me, UP, z, z < 3, own=True)
                send(at, me, DOWN, z, z > 0, own=True)
                send(at, me, second, 4 + z, own=True)
                send(at, me, third, 8, own=True)
                left_here(quarters(at, 3), out_send.at[at, ACROSS_Y])
                line_sent(at, lambda number: held[at].at[: held[at].shape[0] // 4 * number])
            else:
                send(at, me, second, 0, own=True)
                send(at, me, third, 1, own=True)
                send(at, me, UP, 4 + z, z < 3, own=True)
                send(at, me, DOWN, 4 + z, z > 0, own=True)
                left_here(held[at].at[: held[at].shape[0] // 4 * 3], out_send.at[at, ACROSS_Y])
                line_sent(at, lambda number: quarters(at, number))
        elif z_first:
            if step <= 3:
                for there, zz, way, on in from_line(step):
                    where = place(zz, y, x)
                    arrive(at, where, zz, there)
                    send(at, where, way, zz, on)
                    send(at, where, second, 4 + zz, there)
                    send(at, where, third, 8, there)
            elif step <= 7:
                zz = z ^ (step - 4)
                where = near(second, zz)
                arrive(at, where, 4 + zz)
                send(at, where, third, 8)
            elif step == 8:
                arrived(quarters(at, 2), out_recv.at[at, 8])
        else:
            if step == 1:
                where = near(second, z)
                arrive(at, where, 0)
                send(at, where, third, 2)
                send(at, where, UP, 4 + z, z < 3)
                send(at, where, DOWN, 4 + z, z > 0)
            elif step == 2:
                for arrival, where in ((1, near(third, z)), (2, opposite(z))):
                    arrive(at, where, arrival)
                    send(at, where, UP, 4 + z, z < 3)
                    send(at, where, DOWN, 4 + z, z > 0)
            elif step <= 5:
                for there, zz, way, on in from_line(step - 2):
                    pl.when(there)(
                        functools.partial(arrived, quarters(at, 1), out_recv.at[at, 4 + zz])
                    )
                    for where in (place(zz, y, x), near(second, zz), near(third, zz), opposite(zz)):
                        send(at, where, way, 4 + zz, on)

    def load_weight(index):
        return pltpu.make_async_copy(
            weights[index], weight_buffer.at[index % 2], weight_sem.at[index % 2]
        )

    def input_gradient():
        load_weight(0).start()
        for index in range(6):
            load_weight(index + 1).start()
            load_weight(index).wait()
            columns = lanes(normed_grad, core if index < 3 else 1 - core, normed_grad.shape[1] // 2)
            term = dot_nt(rights[count - 3 + index % 3][...], weight_buffer[index % 2])
            if index % 3:
                columns[...] += term
            else:
                columns[...] = term
        width = resid_in.shape[1]
        cotan, values = normed_grad[...], resid_in[...].astype(F32)
        rate = lax.rsqrt(jnp.mean(values * values, axis=1, keepdims=True) + EPSILON)
        scaled = cotan * gain_one[...]
        slope = jnp.mean(scaled * values, axis=1, keepdims=True)
        back = rate * scaled - values * (rate * rate * rate) * slope
        input_grad[...] = (resid_grad[...] + back).astype(BF16)
        gain_grad = jnp.sum(cotan * values * rate, axis=0, keepdims=True)
        column = jnp.zeros((BUCKETS, 1), F32)
        for apart in range(lines.shape[0]):
            sums = lines[apart : apart + 1, :TILE]
            if apart + 1 < lines.shape[0]:
                sums = sums + lines[apart + 1 : apart + 2, TILE:]
            column = column + jnp.sum(in_bucket[apart] * sums, axis=1, keepdims=True)
        place_at = lax.broadcasted_iota(jnp.int32, (BUCKETS, 128), 1)
        table = jnp.where(place_at == me, column, 0.0)
        for half in range(2):
            for index in range(4):
                start = (4 * half + index) * 128
                vec_in[half, index : index + 1, :] = gain_grad[:, start : start + 128]
            vec_in[half, 4:16, :] = gains[half]
            vec_in[half, 16:, :] = table[half * (BUCKETS // 2) : (half + 1) * (BUCKETS // 2)]
        vector_step(0)

    def encoder_gradient():
        own = kv_both[0, pl.ds(pl.multiple_of(me * encoder_grad.shape[0], 16), encoder_grad.shape[0]), :]
        width = own.shape[1] // 2
        for side in (0, 1):
            terms = []
            for index in (6 + 2 * side, 7 + 2 * side):
                if index < 9:
                    load_weight(index + 1).start()
                load_weight(index).wait()
                part = slice((index % 2) * width, (index % 2 + 1) * width)
                terms.append(dot_nt(own[:, part], weight_buffer[index % 2]))
            columns = lanes(encoder_grad, core if side == 0 else 1 - core, width // 2)
            columns[...] = (terms[0] + terms[1]).astype(BF16)

    later = {}

    def grads_leave():
        later[0] = to_all(0, grad_packed, grad_landed)

    def attention():
        later[0]()
        attend_back(
            order, held_at, pairs, lone, grad_landed, attn_sum, log_norm, bias_lines, back_packed, lines,
            *attention_scratch,
        )
        later[1] = to_all(1, back_packed, back_landed)

    def grads_return():
        later[1]()
        dq_ref, dk_ref, dv_ref = rights[count - 3 :]
        for pair in range(peers // 2):
            cols = slice(pair * 2 * HEAD_DIM, (pair + 1) * 2 * HEAD_DIM)
            dq_ref[:, cols], dk_ref[:, cols] = unpack_pair(back_landed, pair, slice(0, 2 * BLOCK))
            first, second = unpack_pair(back_landed, pair, slice(2 * BLOCK, 3 * BLOCK))
            dv_ref[:BLOCK, cols] = first
            dv_ref[BLOCK:, cols] = second

    def kv_gathered():
        owns[PIECE, kv_at].wait()
        launch(remote(kv_both.at[0], kv_both.at[1], kv_sem.at[0], kv_sem.at[1], me, 1 - core))
        left_here(kv_both.at[0], kv_sem.at[0])
        encoder_gradient()

    single = [grads_leave, attention, grads_return, input_gradient]
    single += [functools.partial(vector_add, step) for step in range(5)] + [kv_gathered]
    for code in SCHEDULE:
        stage, at = divmod(code, 16)
        if stage == 0:
            send_operands([at])
        elif stage == 1:
            pass_on(at)
        elif stage == 2:
            product_away(at)
        elif stage == 3:
            add_pair(at)
            line_step(at, 0)
        elif stage < 7:
            line_step(at, stage - 3)
        elif stage < 16:
            gather_step(at, stage - 7)
        else:
            single[at]()

    arrived(kv_both.at[1], kv_sem.at[1])
    for each in finish:
        each()


def weight_grads(products, lefts, rights, left_far, right_far, others, weights):
    count, peers = len(products), lax.axis_size("ctx")
    tokens = lefts[0].shape[0]
    length = others[5].shape[1]
    kv_at = [product.left for product in products].index(SUMMED)
    kv_rows, kv_width = rights[kv_at].shape
    spans = length // TILE
    dma = pltpu.SemaphoreType.DMA
    vmem = pltpu.VMEM
    width = HEADS * HEAD_DIM
    halves = [left.shape[1] // 2 for left in lefts]
    widths = [right.shape[1] for right in rights] + [width] * 3
    helds = []
    for product, right in zip(products, widths):
        height = kv_rows if product.left == SUMMED else halves[product.left]
        helds.append((height, right // 4) if product.tall else (height // 2, right // 2))
    lands = [vmem(shape, BF16) for shape in helds]
    chunk = (peers, BLOCK, 2 * HEAD_DIM)
    chunks = (peers, 3 * BLOCK, 2 * HEAD_DIM)
    smem_spec = pl.BlockSpec(memory_space=pltpu.SMEM)
    return pl.pallas_call(
        functools.partial(weight_grad_kernel, products, len(lefts)),
        out_shape=[
            jax.ShapeDtypeStruct((halves[product.left], right), BF16)
            for product, right in zip(products, widths)
            if product.left != SUMMED
        ]
        + [
            jax.ShapeDtypeStruct((32, 128), F32),
            jax.ShapeDtypeStruct((tokens, width), BF16),
            jax.ShapeDtypeStruct((kv_rows // peers, width), BF16),
            jax.ShapeDtypeStruct((2, kv_rows, kv_width), BF16),
        ],
        in_specs=[any_spec()] * len(lefts)
        + [vmem_spec() if product.left == SUMMED else any_spec() for product in products[: len(rights)]]
        + [any_spec()] * (len(left_far) + len(right_far))
        + [smem_spec] * 2
        + [vmem_spec()] * (len(others) - 2)
        + [any_spec()] * len(weights),
        out_specs=[any_spec()] * (count - 1) + [vmem_spec()] * 4,
        scratch_shapes=[vmem((4 * tokens, half), BF16) for half in halves]
        + [vmem((half, 4 * tokens), BF16) for half in halves]
        + [
            vmem((kv_rows if product.left == SUMMED else 4 * tokens, right // 2), BF16)
            for product, right in zip(products, widths)
        ]
        + lands * 3
        + [vmem((5 * height // 4, width_held), BF16) for height, width_held in helds]
        + [vmem((tokens, width), BF16)] * 3
        + [vmem(chunk, BF16), vmem(chunk, BF16), vmem(chunks, BF16), vmem(chunks, BF16)]
        + [vmem((spans, 2 * TILE), F32)]
        + [vmem((length, HEAD_DIM), BF16)] * 4
        + [vmem((HEAD_DIM, length), BF16)]
        + [vmem((spans, TILE, TILE), F32)] * 2
        + [vmem((length, HEAD_DIM), F32)] * 3
        + [vmem((1, length), F32), vmem((HEAD_DIM, length), F32)]
        + [
            vmem((2, 32, 128), F32),
            vmem((4, 32, 128), F32),
            vmem((5, 32, 128), F32),
            vmem((2,) + weights[0].shape, BF16),
            vmem((tokens, width), F32),
        ]
        + [
            dma((len(lefts),)),
            dma((len(lefts),)),
            dma((len(lefts),)),
            dma((count,)),
            dma((count,)),
            dma((count, 3)),
            dma((count,)),
            dma((count,)),
            dma((count,)),
            dma((count, 2, 3)),
            dma((count, 3)),
            dma((count, 9)),
            dma((count,)),
            dma((5,)),
            dma((5,)),
            dma((2,)),
            dma((2,)),
            dma((2,)),
            dma((2,)),
            dma((2,)),
        ],
        compiler_params=pltpu.CompilerParams(
            collective_id=5, has_side_effects=True, vmem_limit_bytes=60 * MIB
        ),
        name="weight_grads",
    )(*lefts, *rights, *left_far, *right_far, *others, *weights)


def on_device_by_heads(
    inputs,
    encoder,
    cotangent,
    block_order,
    bucket_of,
    self_gain,
    query_weight,
    key_weight,
    value_weight,
    out_weight,
    bias_table,
    cross_gain,
    cross_query,
    cross_key,
    cross_value,
    cross_out,
    mlp_gain,
    gate_weight,
    up_weight,
    down_weight,
):
    blocks = block_order.shape[0]
    block_ids = jnp.arange(blocks, dtype=jnp.int32)
    held_at = jnp.sum(
        jnp.where(block_order[None, :] == block_ids[:, None], block_ids[None, :], 0), axis=1
    )
    bucket_ids = jnp.arange(BUCKETS, dtype=jnp.int32)[None, :, None]
    bucket_tiles = (bucket_of.reshape(-1, 1, TILE) == bucket_ids).astype(F32)
    row = jnp.arange(8, dtype=jnp.int32)[:, None]
    small = jnp.where(
        row == 0, self_gain[None], jnp.where(row == 1, cross_gain[None], mlp_gain[None])
    ).astype(F32)
    table = jnp.pad(bias_table.astype(F32), ((0, 0), (0, 128 - HEADS)))
    sources = Weights(
        query=query_weight,
        key=key_weight,
        value=value_weight,
        out=out_weight,
        cross_key=cross_key,
        cross_value=cross_value,
        cross_query=cross_query,
        cross_out=cross_out,
        gate=gate_weight,
        up=up_weight,
        down=down_weight,
    )
    made, far, lent = layer(
        inputs[0], cotangent[0], encoder[0], small, table, bucket_tiles, held_at, block_order, sources
    )

    z_then_yx, z_then_xy, yx_then_z, xy_then_z = (
        (True, ACROSS_Y, ACROSS_X),
        (True, ACROSS_X, ACROSS_Y),
        (False, ACROSS_Y, ACROSS_X),
        (False, ACROSS_X, ACROSS_Y),
    )
    lefts = (
        made.normed_three, made.hidden, made.cross_mixed, made.normed_two, made.attended, made.normed_one
    )
    products = (
        Product(0, made.gate_grad, BIT_Y, False, z_then_yx),
        Product(1, cotangent[0], BIT_X, True, z_then_yx),
        Product(0, made.up_grad, BIT_Y, False, z_then_xy),
        Product(SUMMED, made.kv_part, BIT_Y, False, yx_then_z),
        Product(2, made.branch_two, BIT_X, False, z_then_xy),
        Product(3, made.cross_q_grad, BIT_X, False, z_then_xy),
        Product(4, made.branch_one, BIT_Y, False, z_then_xy),
        Product(5, None, BIT_X, False, yx_then_z),
        Product(5, None, BIT_X, False, yx_then_z),
        Product(5, None, BIT_X, False, z_then_yx),
    )
    *wholes, totals, input_grad, encoder_grad, cross_kv_both = weight_grads(
        products,
        lefts,
        [product.right for product in products[:7]],
        far[:FAR_LEFTS],
        far[FAR_LEFTS:],
        [
            block_order,
            held_at,
            made.dattn,
            made.pairs,
            made.lone,
            made.attn_sum,
            made.log_norm,
            made.bias_lines,
            bucket_tiles,
            inputs[0],
            made.gain_one,
            made.resid_grad,
            made.gain_grads,
        ],
        [query_weight, key_weight, value_weight, *lent[:3], cross_key, cross_value, *lent[3:]],
    )
    head_width = HEADS * HEAD_DIM
    cross_kv_rows = cross_kv_both.reshape(-1, 2 * head_width)
    sum_cross_key = left_contract(made.encoder_both, cross_kv_rows[:, :head_width])
    sum_cross_value = left_contract(made.encoder_both, cross_kv_rows[:, head_width:])
    (
        sum_gate,
        sum_down,
        sum_up,
        sum_cross_out,
        sum_cross_query,
        sum_out,
        sum_query,
        sum_key,
        sum_value,
    ) = (member.astype(F32) for member in wholes)
    sum_gain_one, sum_gain_two, sum_gain_three = (
        totals[4 * at : 4 * at + 4].reshape(-1) for at in range(3)
    )
    sum_table = totals[16:, :HEADS]
    return (
        made.result[None],
        input_grad[None],
        encoder_grad[None],
        sum_gain_one,
        sum_query,
        sum_key,
        sum_value,
        sum_out,
        sum_table,
        sum_gain_two,
        sum_cross_query,
        sum_cross_key,
        sum_cross_value,
        sum_cross_out,
        sum_gain_three,
        sum_gate,
        sum_up,
        sum_down,
    )


def solution(mesh):
    by_heads = mesh.shape["ctx"] == HEADS and mesh.shape["wsh"] == 2
    return jax.shard_map(
        on_device_by_heads if by_heads else on_device,
        mesh=mesh,
        in_specs=(
            P("wsh", "ctx", None),
            P("wsh", "ctx", None),
            P("wsh", "ctx", None),
            P(),
            P(),
            P("wsh"),
            P("wsh", None),
            P("wsh", None),
            P("wsh", None),
            P("wsh", None),
            P("wsh", None),
            P("wsh"),
            P("wsh", None),
            P("wsh", None),
            P("wsh", None),
            P("wsh", None),
            P("wsh"),
            P("wsh", None),
            P("wsh", None),
            P("wsh", None),
        ),
        out_specs=(
            P("wsh", "ctx", None),
            P("wsh", "ctx", None),
            P("wsh", "ctx", None),
            P("wsh"),
            P("wsh", None),
            P("wsh", None),
            P("wsh", None),
            P("wsh", None),
            P("wsh", None),
            P("wsh"),
            P("wsh", None),
            P("wsh", None),
            P("wsh", None),
            P("wsh", None),
            P("wsh"),
            P("wsh", None),
            P("wsh", None),
            P("wsh", None),
        ),
        check_vma=False,
    )
```
